32 devices in a mesh: seq: 4 (over z), fsdp: 8 (over y, x, core).
Axes of the slice: x: 2, y: 2, z: 4, core: 2. Of those that a mesh axis runs over, the one named last changes fastest.
Arguments:
- tokens: bfloat16 [16, 2048, 768], P('fsdp', 'seq'), may hold values from -6 to 6
- segment_ids: int32 [16, 2048], P('fsdp', 'seq'), may hold values from 0 to 64, as said below
- cotangent: bfloat16 [16, 2048, 768], P('fsdp', 'seq'), may hold values from -6 to 6
- w_qkv: float32 [768, 2304], P(('seq', 'fsdp')), may hold values from -0.21875 to 0.21875
- w_out: float32 [768, 768], P(('seq', 'fsdp')), may hold values from -0.875 to 0.875
- w_gate: float32 [768, 3072], P(('seq', 'fsdp')), may hold values from -0.21875 to 0.21875
- w_up: float32 [768, 3072], P(('seq', 'fsdp')), may hold values from -0.21875 to 0.21875
- w_down: float32 [3072, 768], P(('seq', 'fsdp')), may hold values from -0.15625 to 0.15625
- norm_params: float32 [4, 768], P(None, ('seq', 'fsdp')), may hold values from -0.5 to 2.4
- first_qkv: float32 [768, 2304], P(('seq', 'fsdp')), may hold values from -0.00021362305 to 0.00021362305
- first_out: float32 [768, 768], P(('seq', 'fsdp')), may hold values from -0.00021362305 to 0.00021362305
- first_gate: float32 [768, 3072], P(('seq', 'fsdp')), may hold values from -0.00021362305 to 0.00021362305
- first_up: float32 [768, 3072], P(('seq', 'fsdp')), may hold values from -0.00021362305 to 0.00021362305
- first_down: float32 [3072, 768], P(('seq', 'fsdp')), may hold values from -0.00021362305 to 0.00021362305
- first_norms: float32 [4, 768], P(None, ('seq', 'fsdp')), may hold values from -0.0008544922 to 0.0008544922
- second_qkv: float32 [768, 2304], P(('seq', 'fsdp')), may hold values from 5.2964664e-11 to 8.474346e-10
- second_out: float32 [768, 768], P(('seq', 'fsdp')), may hold values from 1.0592933e-11 to 8.474346e-11
- second_gate: float32 [768, 3072], P(('seq', 'fsdp')), may hold values from 5.2964664e-11 to 8.474346e-10
- second_up: float32 [768, 3072], P(('seq', 'fsdp')), may hold values from 5.2964664e-11 to 8.474346e-10
- second_down: float32 [3072, 768], P(('seq', 'fsdp')), may hold values from 5.2964664e-11 to 8.474346e-10
- second_norms: float32 [4, 768], P(None, ('seq', 'fsdp')), may hold values from 8.474346e-10 to 1.3558954e-08
Outputs:
- output: bfloat16 [16, 2048, 768], P('fsdp', 'seq')
- input_grad: float32 [16, 2048, 768], P('fsdp', 'seq')
- grad_qkv: float32 [768, 2304], P(('seq', 'fsdp'))
- grad_out: float32 [768, 768], P(('seq', 'fsdp'))
- grad_gate: float32 [768, 3072], P(('seq', 'fsdp'))
- grad_up: float32 [768, 3072], P(('seq', 'fsdp'))
- grad_down: float32 [3072, 768], P(('seq', 'fsdp'))
- grad_norms: float32 [4, 768], P(None, ('seq', 'fsdp'))
- new_qkv: float32 [768, 2304], P(('seq', 'fsdp'))
- new_out: float32 [768, 768], P(('seq', 'fsdp'))
- new_gate: float32 [768, 3072], P(('seq', 'fsdp'))
- new_up: float32 [768, 3072], P(('seq', 'fsdp'))
- new_down: float32 [3072, 768], P(('seq', 'fsdp'))
- new_norms: float32 [4, 768], P(None, ('seq', 'fsdp'))
- new_first_qkv: float32 [768, 2304], P(('seq', 'fsdp'))
- new_first_out: float32 [768, 768], P(('seq', 'fsdp'))
- new_first_gate: float32 [768, 3072], P(('seq', 'fsdp'))
- new_first_up: float32 [768, 3072], P(('seq', 'fsdp'))
- new_first_down: float32 [3072, 768], P(('seq', 'fsdp'))
- new_first_norms: float32 [4, 768], P(None, ('seq', 'fsdp'))
- new_second_qkv: float32 [768, 2304], P(('seq', 'fsdp'))
- new_second_out: float32 [768, 768], P(('seq', 'fsdp'))
- new_second_gate: float32 [768, 3072], P(('seq', 'fsdp'))
- new_second_up: float32 [768, 3072], P(('seq', 'fsdp'))
- new_second_down: float32 [3072, 768], P(('seq', 'fsdp'))
- new_second_norms: float32 [4, 768], P(None, ('seq', 'fsdp'))
- grad_norm: float32 [], replicated
The draws below stay inside these ranges and needn't reach their ends.
Inputs may be any that keep to these rules, and one draw needn't show every extreme that they name: `segment_ids`: within each sequence the ids start at 0 and rise by 0 or 1 from one position to the next, never above 64.
All inputs are finite; a program needn't handle non-finite values.
Results may differ from the reference program's by a relative error of at most 0.015.
Values may be sent and summed in bfloat16 or wider, within the bound.
A program may use at most 192 MiB of HBM per device.

```python
import math
import jax
import jax.numpy as jnp
from jax import lax

D = 768
HEADS = 12
HEAD_DIM = 64
FF = 3072
SEQ_LEN = 2048
SEQS_DEV = 2
STEP = 10
SEQS = 16
P_ALL = 9440256


def draw_tokens(key, part):
    key = jax.random.fold_in(key, 5)
    columns = jnp.arange(D, dtype=jnp.float32) / D
    col_scale = 0.5 + columns
    base = jax.random.truncated_normal(key, -4.0, 4.0, (SEQS, SEQ_LEN, D), jnp.float32)
    return (base * col_scale).astype(jnp.bfloat16)


def draw_norm_params(key, part):
    key = jax.random.fold_in(key, 7)
    key_jitter = jax.random.fold_in(key, 1)
    key_shift = jax.random.fold_in(key, 2)
    columns = jnp.arange(D, dtype=jnp.float32) / D
    rising = 0.6 + 1.2 * columns
    jitter = jax.random.uniform(key_jitter, (2, D), jnp.float32, 0.8, 1.2)
    gains = rising[None, :] * jitter
    shifts = jax.random.uniform(key_shift, (2, D), jnp.float32, -0.5, 0.5)
    return jnp.stack([gains[0], shifts[0], gains[1], shifts[1]]).astype(jnp.float32)


def draw_segment_ids(key, part):
    key = jax.random.fold_in(key, 11)
    key_rate, key_flag, key_pick = jax.random.split(key, 3)
    thresholds = jnp.array([512, 64, 8], dtype=jnp.int32)
    row_kind = jax.random.randint(key_rate, (SEQS,), 0, 3)
    row_limit = jnp.take(thresholds, row_kind)
    flags = jax.random.randint(key_flag, (SEQS, SEQ_LEN), 0, 4096) < row_limit[:, None]
    picked = jax.random.randint(key_pick, (SEQS // SEQS_DEV, 1), 0, SEQS_DEV)
    long_row = (jnp.arange(SEQS).reshape(SEQS // SEQS_DEV, SEQS_DEV) == picked).reshape(SEQS)
    positions = jnp.arange(SEQ_LEN)
    rim = SEQ_LEN // 32
    middle = (positions >= rim) & (positions < SEQ_LEN - rim)
    forced = (positions < rim) | (positions == SEQ_LEN - 1)
    flags = jnp.where(long_row[:, None] & middle[None, :], False, flags)
    flags = jnp.where(long_row[:, None] & forced[None, :], True, flags)
    flags = jnp.where(positions[None, :] == 0, True, flags)
    counted = jnp.cumsum(flags.astype(jnp.int32), axis=1) - 1
    return jnp.minimum(counted, rim).astype(jnp.int32)


def levels(rng, shape, shards, least, largest):
    def one(axis_at, blocks):
        heights = jax.random.uniform(jax.random.fold_in(jax.random.fold_in(rng, 6), axis_at), (blocks,), jnp.float32, least / len(shards), largest / len(shards))
        return jnp.repeat(jnp.exp(heights), shape[axis_at] // blocks).reshape((-1,) + (1,) * (len(shape) - axis_at - 1))

    level = one(*shards[0])
    for cut in shards[1:]:
        level = level * one(*cut)
    return level


def noise(key, dims, scale, most, cuts=(), kind=jnp.bfloat16):
    values = scale * jax.random.normal(key, dims, jnp.float32)
    if cuts:
        values = values * levels(key, dims, cuts, -0.22, 0.18)
    return jnp.clip(values, -most, most).astype(kind)


def setup_inputs(seed: int = 0) -> dict:
    splits = jax.random.split(jax.random.key(seed), 22)
    tokens = draw_tokens(jax.random.fold_in(splits[21], 71), 0)
    segment_ids = draw_segment_ids(jax.random.fold_in(splits[21], 71), 0)
    cotangent = noise(splits[2], (SEQS, SEQ_LEN, D), 1.0, 6.0, ((0, 8), (1, 4)))
    w_qkv = noise(splits[3], (D, 3 * D), D ** -0.5, 0.21875, ((0, 32),), jnp.float32)
    w_out = noise(splits[4], (D, D), (D // 16) ** -0.5, 0.875, ((0, 32),), jnp.float32)
    w_gate = noise(splits[5], (D, FF), D ** -0.5, 0.21875, ((0, 32),), jnp.float32)
    w_up = noise(splits[6], (D, FF), D ** -0.5, 0.21875, ((0, 32),), jnp.float32)
    w_down = noise(splits[7], (FF, D), (FF // 2) ** -0.5, 0.15625, ((0, 32),), jnp.float32)
    norm_params = draw_norm_params(jax.random.fold_in(splits[21], 71), 0)
    first_qkv = noise(splits[9], (D, 3 * D), (0.11 * P_ALL ** -0.5), 0.00021362305, ((0, 32),), jnp.float32)
    first_out = noise(splits[10], (D, D), (0.11 * P_ALL ** -0.5), 0.00021362305, ((0, 32),), jnp.float32)
    first_gate = noise(splits[11], (D, FF), (0.11 * P_ALL ** -0.5), 0.00021362305, ((0, 32),), jnp.float32)
    first_up = noise(splits[12], (D, FF), (0.11 * P_ALL ** -0.5), 0.00021362305, ((0, 32),), jnp.float32)
    first_down = noise(splits[13], (FF, D), (0.11 * P_ALL ** -0.5), 0.00021362305, ((0, 32),), jnp.float32)
    first_norms = noise(splits[14], (4, D), (0.44 * P_ALL ** -0.5), 0.0008544922, ((1, 32),), jnp.float32)
    second_qkv = jnp.clip(jnp.exp(math.log(8.474346224751628e-10) - 2.7725887 * jax.random.uniform(splits[15], (D, 3 * D), jnp.float32) ** levels(splits[15], (D, 3 * D), ((0, 32),), -0.2, 0.2)), 5.296466390469767e-11, 8.474346224751628e-10)
    second_out = jnp.clip(jnp.exp(math.log(8.474346224751628e-11) - 2.0794415 * jax.random.uniform(splits[16], (D, D), jnp.float32) ** levels(splits[16], (D, D), ((0, 32),), -0.2, 0.2)), 1.0592932780939535e-11, 8.474346224751628e-11)
    second_gate = jnp.clip(jnp.exp(math.log(8.474346224751628e-10) - 2.7725887 * jax.random.uniform(splits[17], (D, FF), jnp.float32) ** levels(splits[17], (D, FF), ((0, 32),), -0.2, 0.2)), 5.296466390469767e-11, 8.474346224751628e-10)
    second_up = jnp.clip(jnp.exp(math.log(8.474346224751628e-10) - 2.7725887 * jax.random.uniform(splits[18], (D, FF), jnp.float32) ** levels(splits[18], (D, FF), ((0, 32),), -0.2, 0.2)), 5.296466390469767e-11, 8.474346224751628e-10)
    second_down = jnp.clip(jnp.exp(math.log(8.474346224751628e-10) - 2.7725887 * jax.random.uniform(splits[19], (FF, D), jnp.float32) ** levels(splits[19], (FF, D), ((0, 32),), -0.2, 0.2)), 5.296466390469767e-11, 8.474346224751628e-10)
    second_norms = jnp.clip(jnp.exp(math.log(1.3558953959602604e-08) - 2.7725887 * jax.random.uniform(splits[20], (4, D), jnp.float32) ** levels(splits[20], (4, D), ((1, 32),), -0.2, 0.2)), 8.474346224751628e-10, 1.3558953959602604e-08)
    return {"tokens": tokens, "segment_ids": segment_ids, "cotangent": cotangent, "w_qkv": w_qkv, "w_out": w_out, "w_gate": w_gate, "w_up": w_up, "w_down": w_down, "norm_params": norm_params, "first_qkv": first_qkv, "first_out": first_out, "first_gate": first_gate, "first_up": first_up, "first_down": first_down, "first_norms": first_norms, "second_qkv": second_qkv, "second_out": second_out, "second_gate": second_gate, "second_up": second_up, "second_down": second_down, "second_norms": second_norms}


EPS_NORM = 1e-06
ROPE_BASE = 1000.0
MASKED_SCORE = -1e+30
MAX_NORM = 1.0
LEARN_RATE = 0.1
NORM_RATE = 0.6
BETA_ONE = 0.9
BETA_TWO = 0.999
ADAM_EPS = 1e-08
WEIGHT_DECAY = 0.01
PRECISE = lax.Precision.HIGHEST

@jax.custom_vjp
def low(v):
    return lax.optimization_barrier(v.astype(jnp.bfloat16)).astype(jnp.float32)

@jax.custom_vjp
def low_back(v):
    return v

def low_keep(v):
    return (low(v), None)

def low_pass(kept, grad):
    return (grad,)

def back_keep(v):
    return (v, None)

def back_low(kept, grad):
    return (low(grad),)
low.defvjp(low_keep, low_pass)
low_back.defvjp(back_keep, back_low)

def rotate(field, positions, sign_rot):
    shape_in = field.shape
    heads_view = field.reshape(shape_in[:-1] + (HEADS, HEAD_DIM))
    half_dim = HEAD_DIM // 2
    inverse = jnp.exp(jnp.arange(half_dim, dtype=jnp.float32) * (-2.0 * math.log(ROPE_BASE) / HEAD_DIM))
    angles = positions[:, None] * inverse[None, :]
    cosine = jnp.cos(angles)[:, None, :]
    sine = jnp.sin(angles)[:, None, :] * sign_rot
    first_half = heads_view[..., :half_dim]
    second_half = heads_view[..., half_dim:]
    turned = jnp.concatenate([first_half * cosine - second_half * sine, second_half * cosine + first_half * sine], -1)
    return turned.reshape(shape_in)

def layer_norm(resid, gain, shift):
    mean_row = lax.optimization_barrier(jnp.mean(resid, -1, keepdims=True))
    centered = resid - mean_row
    spread = lax.optimization_barrier(jnp.mean(centered * centered, -1, keepdims=True))
    return centered * lax.rsqrt(spread + EPS_NORM) * gain + shift

def layer_block(inputs, segments, lowered):
    low_qkv, low_out, low_gate, low_up, low_down, low_norms = lowered
    group_size, seq_len, model_width = inputs.shape
    positions = jnp.arange(seq_len).astype(jnp.float32)
    score_scale = 1.0 / math.sqrt(HEAD_DIM)
    projected = low_back(jnp.einsum('gld,de->gle', inputs, low_qkv, precision=PRECISE))
    query = low(rotate(projected[..., :model_width], positions, 1.0))
    key_rot = low(rotate(projected[..., model_width:2 * model_width], positions, 1.0))
    value_low = low(projected[..., 2 * model_width:])
    same_doc = segments[:, :, None] == segments[:, None, :]

    def split_heads(field):
        return field.reshape(group_size, seq_len, HEADS, HEAD_DIM).transpose(2, 0, 1, 3)

    def one_head(operands):
        query_head, key_head, value_head = operands
        raw_scores = jnp.einsum('gqd,gkd->gqk', query_head, key_head, precision=PRECISE)
        scores = jnp.where(same_doc, low_back(raw_scores * score_scale), MASKED_SCORE)
        row_max = lax.optimization_barrier(jnp.max(scores, -1, keepdims=True))
        exp_scores = jnp.exp(scores - row_max)
        attn_prob = low(exp_scores / lax.optimization_barrier(jnp.sum(exp_scores, -1, keepdims=True)))
        return jnp.einsum('gqk,gkd->gqd', attn_prob, value_head, precision=PRECISE)
    head_outs = lax.map(jax.checkpoint(one_head), (split_heads(query), split_heads(key_rot), split_heads(value_low)))
    attended = head_outs.transpose(1, 2, 0, 3).reshape(group_size, seq_len, model_width)
    attended = low(low_back(attended))
    attn_branch = low_back(jnp.einsum('gld,de->gle', attended, low_out, precision=PRECISE))
    hidden = layer_norm(inputs + attn_branch, low_norms[0], low_norms[1])
    hidden_low = low(hidden)
    gate_proj = low_back(jnp.einsum('gld,df->glf', hidden_low, low_gate, precision=PRECISE))
    up_proj = low_back(jnp.einsum('gld,df->glf', hidden_low, low_up, precision=PRECISE))
    mixed_low = low(jax.nn.silu(gate_proj) * up_proj)
    ff_branch = low_back(jnp.einsum('glf,fd->gld', mixed_low, low_down, precision=PRECISE))
    return layer_norm(hidden + ff_branch, low_norms[2], low_norms[3])

def adam_update(weight, gradient, moment_one, moment_two, decay_rate, step_rate, clip_factor):
    clipped = gradient * clip_factor
    first_new = BETA_ONE * moment_one + (1.0 - BETA_ONE) * clipped
    second_new = BETA_TWO * moment_two + (1.0 - BETA_TWO) * clipped * clipped
    first_fix = 1.0 - BETA_ONE ** STEP
    second_fix = 1.0 - BETA_TWO ** STEP
    direction = first_new / first_fix / (jnp.sqrt(second_new / second_fix) + ADAM_EPS) + decay_rate * weight
    return (weight - step_rate * direction, first_new, second_new)

def reference(tokens, segment_ids, cotangent, w_qkv, w_out, w_gate, w_up, w_down, norm_params, first_qkv, first_out, first_gate, first_up, first_down, first_norms, second_qkv, second_out, second_gate, second_up, second_down, second_norms):
    inputs = tokens.astype(jnp.float32)
    group_count = SEQS // 2
    seg_groups = segment_ids.reshape(group_count, 2, SEQ_LEN)

    def run_layer(inputs, p_qkv, p_out, p_gate, p_up, p_down, p_norms):
        lowered = (low(p_qkv), low(p_out), low(p_gate), low(p_up), low(p_down), low(p_norms))

        def seq_group(operands):
            group_in, group_seg = operands
            return layer_block(group_in, group_seg, lowered)
        outs = lax.map(jax.checkpoint(seq_group), (inputs.reshape(group_count, 2, SEQ_LEN, D), seg_groups))
        return outs.reshape(SEQS, SEQ_LEN, D)
    result, pullback = jax.vjp(run_layer, inputs, w_qkv, w_out, w_gate, w_up, w_down, norm_params)
    gradients = pullback(cotangent.astype(jnp.float32))
    input_grad = gradients[0]
    g_qkv, g_out, g_gate, g_up, g_down, g_norms = gradients[1:]
    squares_sum = jnp.sum(g_qkv * g_qkv) + jnp.sum(g_out * g_out) + jnp.sum(g_gate * g_gate) + jnp.sum(g_up * g_up) + jnp.sum(g_down * g_down) + jnp.sum(g_norms * g_norms)
    grad_norm = jnp.sqrt(squares_sum)
    clip_factor = jnp.minimum(1.0, MAX_NORM / (grad_norm + 1e-06))
    new_qkv, mom_qkv, sec_qkv = adam_update(w_qkv, g_qkv, first_qkv, second_qkv, WEIGHT_DECAY, LEARN_RATE, clip_factor)
    new_out, mom_out, sec_out = adam_update(w_out, g_out, first_out, second_out, WEIGHT_DECAY, LEARN_RATE, clip_factor)
    new_gate, mom_gate, sec_gate = adam_update(w_gate, g_gate, first_gate, second_gate, WEIGHT_DECAY, LEARN_RATE, clip_factor)
    new_up, mom_up, sec_up = adam_update(w_up, g_up, first_up, second_up, WEIGHT_DECAY, LEARN_RATE, clip_factor)
    new_down, mom_down, sec_down = adam_update(w_down, g_down, first_down, second_down, WEIGHT_DECAY, LEARN_RATE, clip_factor)
    new_norms, mom_norms, sec_norms = adam_update(norm_params, g_norms, first_norms, second_norms, 0.0, NORM_RATE, clip_factor)
    return (result.astype(jnp.bfloat16), input_grad, g_qkv, g_out, g_gate, g_up, g_down, g_norms, new_qkv, new_out, new_gate, new_up, new_down, new_norms, mom_qkv, mom_out, mom_gate, mom_up, mom_down, mom_norms, sec_qkv, sec_out, sec_gate, sec_up, sec_down, sec_norms, grad_norm)
```

```python
import functools
import math

import jax
import jax.numpy as jnp
from jax import lax
from jax.experimental import pallas as pl
from jax.experimental.pallas import tpu as pltpu
from jax.sharding import PartitionSpec as P

HEADS = 12
HEAD_DIM = 64
STEP = 10


EPS_NORM = 1e-06
ROPE_BASE = 1000.0
MASKED_SCORE = -1e30
MAX_NORM = 1.0
LEARN_RATE = 0.1
NORM_RATE = 0.6
BETA_ONE = 0.9
BETA_TWO = 0.999
ADAM_EPS = 1e-08
WEIGHT_DECAY = 0.01


def rotate(field, positions, sign_rot):
    shape_in = field.shape
    heads_view = field.reshape(shape_in[:-1] + (HEADS, HEAD_DIM))
    half_dim = HEAD_DIM // 2
    inverse = jnp.exp(
        jnp.arange(half_dim, dtype=jnp.float32) * (-2.0 * math.log(ROPE_BASE) / HEAD_DIM)
    )
    angles = positions[:, None] * inverse[None, :]
    cosine = jnp.cos(angles)[:, None, :]
    sine = jnp.sin(angles)[:, None, :] * sign_rot
    first_half = heads_view[..., :half_dim]
    second_half = heads_view[..., half_dim:]
    turned = jnp.concatenate(
        [first_half * cosine - second_half * sine, second_half * cosine + first_half * sine], -1
    )
    return turned.reshape(shape_in)


def normalize(resid, gain, shift):
    mean_row = jnp.mean(resid, -1, keepdims=True)
    centered = resid - mean_row
    inv_std = lax.rsqrt(jnp.mean(centered * centered, -1, keepdims=True) + EPS_NORM)
    normed = centered * inv_std
    return (normed * gain + shift, normed, inv_std)


def normalize_back(grad_in, normed, inv_std, gain):
    scaled = grad_in * gain
    return inv_std * (
        scaled
        - jnp.mean(scaled, -1, keepdims=True)
        - normed * jnp.mean(scaled * normed, -1, keepdims=True)
    )


def attend(query, keys, values, same_doc, score_scale):
    seq_count, local_len, model_width = query.shape

    def one_head(head_index, carried):
        out_all, log_sums = carried
        col_start = head_index * HEAD_DIM
        query_head = lax.dynamic_slice_in_dim(query, col_start, HEAD_DIM, 2)
        key_head = lax.dynamic_slice_in_dim(keys, col_start, HEAD_DIM, 2)
        value_head = lax.dynamic_slice_in_dim(values, col_start, HEAD_DIM, 2)
        raw_scores = jnp.einsum(
            "sqd,skd->sqk", query_head, key_head, preferred_element_type=jnp.float32
        )
        scores = jnp.where(same_doc, raw_scores * score_scale, MASKED_SCORE)
        row_max = jnp.max(scores, -1, keepdims=True)
        exp_scores = jnp.exp(scores - row_max)
        row_sums = jnp.sum(exp_scores, -1, keepdims=True)
        attn_prob = (exp_scores / row_sums).astype(jnp.bfloat16)
        head_out = jnp.einsum(
            "sqk,skd->sqd", attn_prob, value_head, preferred_element_type=jnp.float32
        )
        out_all = lax.dynamic_update_slice_in_dim(out_all, head_out, col_start, 2)
        log_sums = lax.dynamic_update_index_in_dim(
            log_sums, (row_max + jnp.log(row_sums))[..., 0], head_index, 0
        )
        return (out_all, log_sums)

    start_state = (
        jnp.zeros((seq_count, local_len, model_width), jnp.float32),
        jnp.zeros((HEADS, seq_count, local_len), jnp.float32),
    )
    return lax.fori_loop(0, HEADS, one_head, start_state)


def attend_back(query, keys, values, same_doc, log_sums, grad_attended, score_scale):
    seq_count, local_len, model_width = query.shape
    key_len = keys.shape[1]

    def one_head(head_index, carried):
        dq_all, dk_all, dv_all = carried
        col_start = head_index * HEAD_DIM
        query_head = lax.dynamic_slice_in_dim(query, col_start, HEAD_DIM, 2)
        key_head = lax.dynamic_slice_in_dim(keys, col_start, HEAD_DIM, 2)
        value_head = lax.dynamic_slice_in_dim(values, col_start, HEAD_DIM, 2)
        grad_head = lax.dynamic_slice_in_dim(grad_attended, col_start, HEAD_DIM, 2)
        head_sums = lax.dynamic_index_in_dim(log_sums, head_index, 0, keepdims=False)
        raw_scores = jnp.einsum(
            "sqd,skd->sqk", query_head, key_head, preferred_element_type=jnp.float32
        )
        scores = jnp.where(same_doc, raw_scores * score_scale, MASKED_SCORE)
        attn_prob = jnp.exp(scores - head_sums[..., None])
        grad_prob = jnp.einsum(
            "sqd,skd->sqk", grad_head, value_head, preferred_element_type=jnp.float32
        )
        dv_head = jnp.einsum(
            "sqk,sqd->skd",
            attn_prob.astype(jnp.bfloat16),
            grad_head,
            preferred_element_type=jnp.float32,
        )
        row_dots = jnp.sum(attn_prob * grad_prob, -1, keepdims=True)
        grad_scores = (attn_prob * (grad_prob - row_dots)).astype(jnp.bfloat16)
        dq_head = (
            jnp.einsum("sqk,skd->sqd", grad_scores, key_head, preferred_element_type=jnp.float32)
            * score_scale
        )
        dk_head = (
            jnp.einsum("sqk,sqd->skd", grad_scores, query_head, preferred_element_type=jnp.float32)
            * score_scale
        )
        dq_all = lax.dynamic_update_slice_in_dim(dq_all, dq_head, col_start, 2)
        dk_all = lax.dynamic_update_slice_in_dim(dk_all, dk_head, col_start, 2)
        dv_all = lax.dynamic_update_slice_in_dim(dv_all, dv_head, col_start, 2)
        return (dq_all, dk_all, dv_all)

    start_state = (
        jnp.zeros((seq_count, local_len, model_width), jnp.float32),
        jnp.zeros((seq_count, key_len, model_width), jnp.float32),
        jnp.zeros((seq_count, key_len, model_width), jnp.float32),
    )
    return lax.fori_loop(0, HEADS, one_head, start_state)


def adam_update(weight, gradient, moment_one, moment_two, decay_rate, step_rate, clip_factor):
    clipped = gradient * clip_factor
    first_new = BETA_ONE * moment_one + (1.0 - BETA_ONE) * clipped
    second_new = BETA_TWO * moment_two + (1.0 - BETA_TWO) * clipped * clipped
    first_fix = 1.0 - BETA_ONE**STEP
    second_fix = 1.0 - BETA_TWO**STEP
    direction = (
        first_new / first_fix / (jnp.sqrt(second_new / second_fix) + ADAM_EPS) + decay_rate * weight
    )
    return (weight - step_rate * direction, first_new, second_new)


def per_device(
    tokens,
    segment_ids,
    cotangent,
    w_qkv,
    w_out,
    w_gate,
    w_up,
    w_down,
    norm_params,
    first_qkv,
    first_out,
    first_gate,
    first_up,
    first_down,
    first_norms,
    second_qkv,
    second_out,
    second_gate,
    second_up,
    second_down,
    second_norms,
):
    seq_count, local_len, model_width = tokens.shape
    row_count = seq_count * local_len
    score_scale = 1.0 / math.sqrt(HEAD_DIM)
    lowered_qkv = w_qkv.astype(jnp.bfloat16)
    lowered_out = w_out.astype(jnp.bfloat16)
    lowered_gate = w_gate.astype(jnp.bfloat16)
    lowered_up = w_up.astype(jnp.bfloat16)
    lowered_down = w_down.astype(jnp.bfloat16)
    lowered_norms = norm_params.astype(jnp.bfloat16)
    full_qkv, full_out, full_gate, full_up, full_down, full_norms = (
        lax.all_gather(lowered_qkv, ("seq", "fsdp"), axis=0, tiled=True),
        lax.all_gather(lowered_out, ("seq", "fsdp"), axis=0, tiled=True),
        lax.all_gather(lowered_gate, ("seq", "fsdp"), axis=0, tiled=True),
        lax.all_gather(lowered_up, ("seq", "fsdp"), axis=0, tiled=True),
        lax.all_gather(lowered_down, ("seq", "fsdp"), axis=0, tiled=True),
        lax.all_gather(lowered_norms, ("seq", "fsdp"), axis=1, tiled=True),
    )
    gains = full_norms.astype(jnp.float32)
    gain_one, shift_one, gain_two, shift_two = (gains[0], gains[1], gains[2], gains[3])
    positions = (lax.axis_index("seq") * local_len + jnp.arange(local_len)).astype(jnp.float32)
    flat_rows = tokens.reshape(row_count, model_width)
    projected = jnp.dot(flat_rows, full_qkv, preferred_element_type=jnp.float32).reshape(
        seq_count, local_len, 3 * model_width
    )
    query = rotate(projected[..., :model_width], positions, 1.0).astype(jnp.bfloat16)
    keys_local = rotate(projected[..., model_width : 2 * model_width], positions, 1.0).astype(
        jnp.bfloat16
    )
    values_local = projected[..., 2 * model_width :].astype(jnp.bfloat16)
    keys_all, values_all, key_segments = (
        lax.all_gather(keys_local, "seq", axis=1, tiled=True),
        lax.all_gather(values_local, "seq", axis=1, tiled=True),
        lax.all_gather(segment_ids, "seq", axis=1, tiled=True),
    )
    same_doc = segment_ids[:, :, None] == key_segments[:, None, :]
    attended, log_sums = attend(query, keys_all, values_all, same_doc, score_scale)
    attended_low = attended.astype(jnp.bfloat16).reshape(row_count, model_width)
    resid_one = flat_rows.astype(jnp.float32) + jnp.dot(
        attended_low, full_out, preferred_element_type=jnp.float32
    )
    hidden, normed_one, inv_std_one = normalize(resid_one, gain_one, shift_one)
    hidden_low = hidden.astype(jnp.bfloat16)
    gate_proj = jnp.dot(hidden_low, full_gate, preferred_element_type=jnp.float32)
    up_proj = jnp.dot(hidden_low, full_up, preferred_element_type=jnp.float32)
    sigmoid_gate = jax.nn.sigmoid(gate_proj)
    silu_gate = gate_proj * sigmoid_gate
    mixed_low = (silu_gate * up_proj).astype(jnp.bfloat16)
    resid_two = hidden + jnp.dot(mixed_low, full_down, preferred_element_type=jnp.float32)
    result, normed_two, inv_std_two = normalize(resid_two, gain_two, shift_two)
    output = result.astype(jnp.bfloat16).reshape(seq_count, local_len, model_width)
    back_qkv, back_out, back_gate, back_up, back_down = (
        lax.all_gather(lowered_qkv, ("seq", "fsdp"), axis=0, tiled=True),
        lax.all_gather(lowered_out, ("seq", "fsdp"), axis=0, tiled=True),
        lax.all_gather(lowered_gate, ("seq", "fsdp"), axis=0, tiled=True),
        lax.all_gather(lowered_up, ("seq", "fsdp"), axis=0, tiled=True),
        lax.all_gather(lowered_down, ("seq", "fsdp"), axis=0, tiled=True),
    )
    grad_result = cotangent.reshape(row_count, model_width).astype(jnp.float32)
    d_gain_two = jnp.sum(grad_result * normed_two, 0)
    d_shift_two = jnp.sum(grad_result, 0)
    d_resid_two = normalize_back(grad_result, normed_two, inv_std_two, gain_two)
    d_ff_low = d_resid_two.astype(jnp.bfloat16)
    g_down = jnp.einsum("rf,rd->fd", mixed_low, d_ff_low, preferred_element_type=jnp.float32)
    d_mixed = jnp.einsum("rd,fd->rf", d_ff_low, back_down, preferred_element_type=jnp.float32)
    d_up_low = (d_mixed * silu_gate).astype(jnp.bfloat16)
    d_gate_low = (
        d_mixed * up_proj * sigmoid_gate * (1.0 + gate_proj * (1.0 - sigmoid_gate))
    ).astype(jnp.bfloat16)
    g_gate = jnp.einsum("rd,rf->df", hidden_low, d_gate_low, preferred_element_type=jnp.float32)
    g_up = jnp.einsum("rd,rf->df", hidden_low, d_up_low, preferred_element_type=jnp.float32)
    d_hidden = (
        d_resid_two
        + jnp.einsum("rf,df->rd", d_gate_low, back_gate, preferred_element_type=jnp.float32)
        + jnp.einsum("rf,df->rd", d_up_low, back_up, preferred_element_type=jnp.float32)
    )
    d_gain_one = jnp.sum(d_hidden * normed_one, 0)
    d_shift_one = jnp.sum(d_hidden, 0)
    d_resid_one = normalize_back(d_hidden, normed_one, inv_std_one, gain_one)
    d_branch_low = d_resid_one.astype(jnp.bfloat16)
    g_out = jnp.einsum("rd,re->de", attended_low, d_branch_low, preferred_element_type=jnp.float32)
    d_attended_low = (
        jnp.einsum("re,de->rd", d_branch_low, back_out, preferred_element_type=jnp.float32)
        .astype(jnp.bfloat16)
        .reshape(seq_count, local_len, model_width)
    )
    keys_back, values_back = (
        lax.all_gather(keys_local, "seq", axis=1, tiled=True),
        lax.all_gather(values_local, "seq", axis=1, tiled=True),
    )
    d_query, d_keys, d_values = attend_back(
        query, keys_back, values_back, same_doc, log_sums, d_attended_low, score_scale
    )
    d_keys_local, d_values_local = (
        lax.psum_scatter(
            d_keys.astype(jnp.bfloat16), "seq", scatter_dimension=1, tiled=True
        ).astype(jnp.float32),
        lax.psum_scatter(
            d_values.astype(jnp.bfloat16), "seq", scatter_dimension=1, tiled=True
        ).astype(jnp.float32),
    )
    d_projected_low = (
        jnp.concatenate(
            [
                rotate(d_query, positions, -1.0),
                rotate(d_keys_local, positions, -1.0),
                d_values_local,
            ],
            -1,
        )
        .astype(jnp.bfloat16)
        .reshape(row_count, 3 * model_width)
    )
    g_qkv = jnp.einsum("rd,re->de", flat_rows, d_projected_low, preferred_element_type=jnp.float32)
    input_grad = (
        d_resid_one
        + jnp.einsum("re,de->rd", d_projected_low, back_qkv, preferred_element_type=jnp.float32)
    ).reshape(seq_count, local_len, model_width)
    g_norms = jnp.stack([d_gain_one, d_shift_one, d_gain_two, d_shift_two])
    red_qkv, red_out, red_gate, red_up, red_down, red_norms = (
        lax.psum_scatter(g_qkv, ("seq", "fsdp"), scatter_dimension=0, tiled=True),
        lax.psum_scatter(g_out, ("seq", "fsdp"), scatter_dimension=0, tiled=True),
        lax.psum_scatter(g_gate, ("seq", "fsdp"), scatter_dimension=0, tiled=True),
        lax.psum_scatter(g_up, ("seq", "fsdp"), scatter_dimension=0, tiled=True),
        lax.psum_scatter(g_down, ("seq", "fsdp"), scatter_dimension=0, tiled=True),
        lax.psum_scatter(g_norms, ("seq", "fsdp"), scatter_dimension=1, tiled=True),
    )
    local_squares = (
        jnp.sum(red_qkv * red_qkv)
        + jnp.sum(red_out * red_out)
        + jnp.sum(red_gate * red_gate)
        + jnp.sum(red_up * red_up)
        + jnp.sum(red_down * red_down)
        + jnp.sum(red_norms * red_norms)
    )
    squares_sum = lax.psum(local_squares, ("seq", "fsdp"))
    grad_norm = jnp.sqrt(squares_sum)
    clip_factor = jnp.minimum(1.0, MAX_NORM / (grad_norm + 1e-06))
    new_qkv, mom_qkv, sec_qkv = adam_update(
        w_qkv, red_qkv, first_qkv, second_qkv, WEIGHT_DECAY, LEARN_RATE, clip_factor
    )
    new_out, mom_out, sec_out = adam_update(
        w_out, red_out, first_out, second_out, WEIGHT_DECAY, LEARN_RATE, clip_factor
    )
    new_gate, mom_gate, sec_gate = adam_update(
        w_gate, red_gate, first_gate, second_gate, WEIGHT_DECAY, LEARN_RATE, clip_factor
    )
    new_up, mom_up, sec_up = adam_update(
        w_up, red_up, first_up, second_up, WEIGHT_DECAY, LEARN_RATE, clip_factor
    )
    new_down, mom_down, sec_down = adam_update(
        w_down, red_down, first_down, second_down, WEIGHT_DECAY, LEARN_RATE, clip_factor
    )
    new_norms, mom_norms, sec_norms = adam_update(
        norm_params, red_norms, first_norms, second_norms, 0.0, NORM_RATE, clip_factor
    )
    return (
        output,
        input_grad,
        red_qkv,
        red_out,
        red_gate,
        red_up,
        red_down,
        red_norms,
        new_qkv,
        new_out,
        new_gate,
        new_up,
        new_down,
        new_norms,
        mom_qkv,
        mom_out,
        mom_gate,
        mom_up,
        mom_down,
        mom_norms,
        sec_qkv,
        sec_out,
        sec_gate,
        sec_up,
        sec_down,
        sec_norms,
        grad_norm,
    )


NT = (((1,), (1,)), ((), ()))
NN = (((1,), (0,)), ((), ()))
TN = (((0,), (0,)), ((), ()))
FAR = 1e30
CODE_BITS = 7
MESH_ID = pl.DeviceIdType.MESH


def dotf(left, right, dims=NN):
    return lax.dot_general(left, right, dims, preferred_element_type=jnp.float32)


def gather_kernel(seqs, bits, pieces, *refs):
    gate, up, qkv, out, norm, down = refs[:6]
    wide_all, down_all = refs[6:8]
    wide_two, down_two, wide_chip, down_chip = refs[8:12]
    core_send, core_recv, own_sem, line_send, line_recv, hop_send, hop_recv, swap_send, swap_recv = refs[12:]
    z = lax.axis_index("seq")
    f = lax.axis_index("fsdp")
    core = lax.rem(f, 2)
    chip = lax.div(f, 2)
    sibling = {"fsdp": f + 1 - 2 * core}

    def chip_at(mask):
        at = chip
        for b in range(bits):
            if mask & (1 << b):
                at = at + (1 - 2 * lax.rem(lax.div(chip, 1 << b), 2)) * (1 << b)
        return at

    def partner(b):
        return {"fsdp": 2 * chip_at(1 << b) + core}

    barrier = pltpu.get_barrier_semaphore()
    pl.semaphore_signal(barrier, inc=1, device_id=sibling, device_id_type=MESH_ID)
    for b in range(bits):
        pl.semaphore_signal(barrier, inc=1, device_id=partner(b), device_id_type=MESH_ID)

    for way in (1, seqs - 1):
        pl.semaphore_signal(barrier, inc=1, device_id={"seq": lax.rem(z + way, seqs)}, device_id_type=MESH_ID)
    rows = gate.shape[0]
    at = 0
    for part in (gate, up, qkv, out, norm):
        wide_two[core, :, at : at + part.shape[1]] = part[...]
        at += part.shape[1]
    down_two[core] = down[...]
    pl.semaphore_wait(barrier, 3 + bits)

    first = [
        pltpu.make_async_remote_copy(
            two.at[core], two.at[core], core_send.at[i], core_recv.at[i], device_id=sibling, device_id_type=MESH_ID
        )
        for i, two in enumerate((wide_two, down_two))
    ]
    for copy in first:
        copy.start()
    for copy in first:
        copy.wait()
    wide_chip[...] = wide_two[...].reshape(wide_chip.shape).astype(jnp.bfloat16)
    down_chip[...] = down_two[...].reshape(down_chip.shape).astype(jnp.bfloat16)
    own = [
        pltpu.make_async_copy(wide_chip, wide_all.at[z, chip], own_sem.at[0]),
        pltpu.make_async_copy(down_chip, down_all.at[z, chip], own_sem.at[1]),
    ]
    for copy in own:
        copy.start()

    def columns(p):
        source, offset, width, _ = pieces[p]
        half = (down_all if source else wide_all).shape[-1] // 2
        return pl.ds(pl.multiple_of(core * half + offset, 128), width)

    def block(p, zz, mask):
        return (down_all if pieces[p][0] else wide_all).at[zz, chip_at(mask), :, columns(p)]

    def own_block(p):
        return (down_chip if pieces[p][0] else wide_chip).at[:, columns(p)]

    def line_copy(p, zz, way, mine):
        return pltpu.make_async_remote_copy(
            own_block(p) if mine else block(p, zz, 0),
            block(p, zz, 0),
            line_send.at[p, way, zz],
            line_recv.at[p, zz],
            device_id={"seq": z + (1 if way else -1)},
            device_id_type=MESH_ID,
        )

    def hop_copy(p, zz, mask, b, mine):
        return pltpu.make_async_remote_copy(
            own_block(p) if mine else block(p, zz, mask),
            block(p, zz, mask),
            hop_send.at[p, zz, mask | (1 << b)],
            hop_recv.at[p, zz, mask | (1 << b)],
            device_id=partner(b),
            device_id_type=MESH_ID,
        )

    def swap_copy(p, zz, mask):
        return pltpu.make_async_remote_copy(
            block(p, zz, mask),
            block(p, zz, mask),
            swap_send.at[p, zz, mask],
            swap_recv.at[p, zz, mask],
            device_id=sibling,
            device_id_type=MESH_ID,
        )

    def level(p, mask):
        return max([i for i, b in enumerate(pieces[p][3]) if mask & (1 << b)], default=-1)

    def masks(p):
        return sorted(range(1 << bits), key=lambda mask: (level(p, mask), mask))

    def pass_on(p, zz, mask, mine=False):
        for b in pieces[p][3][level(p, mask) + 1 :]:
            hop_copy(p, zz, mask, b, mine).start()
        if not mine:
            swap_copy(p, zz, mask).start()

    def arrived(p, zz, mask):
        b = pieces[p][3][level(p, mask)]
        hop_copy(p, zz, mask & ~(1 << b), b, False).wait_recv()

    count = len(pieces)
    for p in range(count):

        @pl.when(z > 0)
        def _():
            line_copy(p, z, 0, True).start()

        @pl.when(z < seqs - 1)
        def _():
            line_copy(p, z, 1, True).start()

        pass_on(p, z, 0, True)

    def hops(zz):
        for level_at in range(bits):
            for p in range(count):
                for mask in masks(p):
                    if level(p, mask) == level_at:
                        arrived(p, zz, mask)
                        pass_on(p, zz, mask)

    for distance in range(1, seqs):
        for way in (1, 0):
            zz = z - distance if way else z + distance

            @pl.when((zz >= 0) & (zz < seqs))
            def _():
                for p in range(count):
                    line_copy(p, zz, way, False).wait_recv()

                    @pl.when((z < seqs - 1) if way else (z > 0))
                    def _():
                        line_copy(p, zz, way, False).start()

                    pass_on(p, zz, 0)

        for way in (1, 0):
            zz = z - distance + 1 if way else z + distance - 1
            if distance > 1 or way:

                @pl.when((zz >= 0) & (zz < seqs))
                def _():
                    hops(zz)

    for way in (1, 0):
        zz = z - seqs + 1 if way else z + seqs - 1

        @pl.when((zz >= 0) & (zz < seqs))
        def _():
            hops(zz)

    def finish(zz):
        for p in range(count):

            @pl.when((zz <= z) & (z < seqs - 1))
            def _():
                line_copy(p, zz, 1, False).wait_send()

            @pl.when((zz >= z) & (z > 0))
            def _():
                line_copy(p, zz, 0, False).wait_send()

            for mask in masks(p):
                for b in pieces[p][3][level(p, mask) + 1 :]:
                    hop_copy(p, zz, mask, b, False).wait_send()
                if mask:
                    swap_copy(p, zz, mask).wait()

            @pl.when(zz != z)
            def _():
                swap_copy(p, zz, 0).wait()

    lax.fori_loop(0, seqs, lambda zz, _: (finish(zz), 0)[1], 0)
    for copy in own:
        copy.wait()


def gather_all(mesh_shape, gate, up, qkv, out, norm, down):
    seqs, chips = mesh_shape["seq"], mesh_shape["fsdp"] // 2
    bits = chips.bit_length() - 1
    rows, rows_down = gate.shape[0], down.shape[0]
    wide = sum(part.shape[1] for part in (gate, up, qkv, out, norm))
    upward, downward = tuple(range(bits)), tuple(reversed(range(bits)))
    down_load = down.shape[1] // 2 * rows_down // rows
    cut = max(0, (wide // 2 + down_load) // 2 - down_load) // 128 * 128 + 128
    pieces = ((0, 0, cut, upward), (1, 0, down.shape[1] // 2, upward), (0, cut, wide // 2 - cut, downward))
    count = len(pieces)
    dma = pltpu.SemaphoreType.DMA
    any_space = pl.BlockSpec(memory_space=pl.ANY)
    vmem = pl.BlockSpec(memory_space=pltpu.VMEM)
    return pl.pallas_call(
        functools.partial(gather_kernel, seqs, bits, pieces),
        out_shape=[
            jax.ShapeDtypeStruct((seqs, chips, 2 * rows, wide), jnp.bfloat16),
            jax.ShapeDtypeStruct((seqs, chips, 2 * rows_down, down.shape[1]), jnp.bfloat16),
        ],
        in_specs=[vmem] * 6,
        out_specs=[any_space] * 2,
        scratch_shapes=[
            pltpu.VMEM((2, rows, wide), jnp.float32),
            pltpu.VMEM((2, rows_down, down.shape[1]), jnp.float32),
            pltpu.VMEM((2 * rows, wide), jnp.bfloat16),
            pltpu.VMEM((2 * rows_down, down.shape[1]), jnp.bfloat16),
            dma((2,)),
            dma((2,)),
            dma((2,)),
            dma((count, 2, seqs)),
            dma((count, seqs)),
            dma((count, seqs, chips)),
            dma((count, seqs, chips)),
            dma((count, seqs, chips)),
            dma((count, seqs, chips)),
        ],
        compiler_params=pltpu.CompilerParams(collective_id=0, has_side_effects=True, vmem_limit_bytes=48 << 20),
        name="gather_parameters",
    )(gate, up, qkv, out, norm, down)


def turn(field, cosine, sine):
    width = field.shape[-1]
    reps = width // cosine.shape[-1]
    cosine = jnp.concatenate([cosine] * reps, -1)
    sine = jnp.concatenate([sine] * reps, -1)
    lane = lax.broadcasted_iota(jnp.int32, field.shape, 1)
    half = HEAD_DIM // 2
    other = jnp.where(
        lax.rem(lane, HEAD_DIM) < half, pltpu.roll(field, width - half, 1), pltpu.roll(field, half, 1)
    )
    return field * cosine + other * sine


def project_kernel(x_ref, wq_ref, wk_ref, wv_ref, cos_ref, sin_ref, code_ref, q_ref, kv_ref):
    x, cosine, sine = x_ref[...], cos_ref[...], sin_ref[...]
    width = x.shape[-1]
    query = turn(dotf(x, wq_ref[...]), cosine, sine).astype(jnp.bfloat16)
    q_ref[...] = query * jnp.bfloat16(1.0 / math.sqrt(HEAD_DIM))
    kv_ref[:, :width] = turn(dotf(x, wk_ref[...]), cosine, sine).astype(jnp.bfloat16)
    kv_ref[:, width : 2 * width] = dotf(x, wv_ref[...]).astype(jnp.bfloat16)
    kv_ref[:, 2 * width :] = code_ref[...]


def project(x, wide, first, cosine, sine, code, block=256):
    rows, width = x.shape
    weight = lambda n: pl.BlockSpec((width, width), lambda i, n=n: (0, first + n))
    row = lambda cols: pl.BlockSpec((block, cols), lambda i: (i, 0))
    return pl.pallas_call(
        project_kernel,
        grid=(rows // block,),
        in_specs=[row(width), weight(0), weight(1), weight(2), row(128), row(128), row(128)],
        out_specs=[row(width), row(2 * width + 128)],
        out_shape=[
            jax.ShapeDtypeStruct((rows, width), jnp.bfloat16),
            jax.ShapeDtypeStruct((rows, 2 * width + 128), jnp.bfloat16),
        ],
        compiler_params=pltpu.CompilerParams(vmem_limit_bytes=48 << 20),
        name="project",
    )(x, wide, wide, wide, cosine, sine, code)


def attend_kernel(unit, chunk, q_ref, qc_ref, k0, kc0, v0, k1, kc1, v1, p_ref, o_ref, inv_ref, ka, vt, st_ref):
    part = k0.shape[0]
    keys = 2 * part
    rows = q_ref.shape[0]
    low_k = lax.broadcasted_iota(jnp.int32, (part, 128), 1) < HEAD_DIM
    for i, (k_ref, kc_ref, v_ref) in enumerate(((k0, kc0, v0), (k1, kc1, v1))):
        k, kc, v = k_ref[...], kc_ref[...], v_ref[...]
        one = jnp.ones_like(v)
        here = slice(i * part, (i + 1) * part)
        ka[0, here] = jnp.where(low_k, k, kc)
        ka[1, here] = jnp.where(low_k, kc, k)
        vt[0, :, here] = jnp.where(low_k, v, one).T
        vt[1, :, here] = jnp.where(low_k, one, v).T
    low_q = lax.broadcasted_iota(jnp.int32, (unit, 128), 1) < HEAD_DIM
    units = [(h, b) for b in range(rows // unit) for h in range(2)]
    results, before = {}, None
    for u, now in enumerate([*units, None]):
        if now is not None:
            h, b = now
            q, qc = q_ref[b * unit : (b + 1) * unit], qc_ref[b * unit : (b + 1) * unit]
            qa = jnp.where(low_q, q, qc) if h == 0 else jnp.where(low_q, qc, q)
        top = total = None
        for c in range(keys // chunk):
            here = slice(c * chunk, (c + 1) * chunk)
            if now is not None:
                s = dotf(ka[h, here], qa, NT)
                st_ref[u % 2, here] = s
                most = jnp.max(s.reshape(chunk // 8, 8, unit), axis=0)
                top = most if top is None else jnp.maximum(top, most)
            if before is not None:
                hb, bb, row_max = before
                p = jnp.exp(st_ref[(u - 1) % 2, here] - row_max).astype(jnp.bfloat16)
                p_ref[hb, here, bb * unit : (bb + 1) * unit] = p
                d = dotf(vt[hb, :, here], p)
                total = d if total is None else total + d
        if before is not None:
            results[before[:2]] = total.T
        before = None if now is None else (h, b, jnp.max(top, axis=0, keepdims=True))
    for b in range(rows // unit):
        r0, r1 = results[(0, b)], results[(1, b)]
        inv = 1.0 / pltpu.roll(jnp.where(low_q, r1, r0), HEAD_DIM, 1)
        inv_ref[b * unit : (b + 1) * unit] = inv
        o_ref[b * unit : (b + 1) * unit] = (jnp.where(low_q, r0, r1) * inv).astype(jnp.bfloat16)


def attend_pallas(q, qc, own, sib, unit=512, chunk=512):
    rows, width = q.shape
    pairs = width // 128
    part = own.shape[0]
    row = pl.BlockSpec((rows, 128), lambda j: (0, j))
    kv = [
        pl.BlockSpec((part, 128), lambda j: (0, j)),
        pl.BlockSpec((part, 128), lambda j: (0, 2 * pairs)),
        pl.BlockSpec((part, 128), lambda j: (0, pairs + j)),
    ]
    return pl.pallas_call(
        functools.partial(attend_kernel, unit, chunk),
        grid=(pairs,),
        in_specs=[row, pl.BlockSpec((rows, 128), lambda j: (0, 0)), *kv, *kv],
        out_specs=[pl.BlockSpec((2, 2 * part, rows), lambda j: (j, 0, 0)), row, row],
        out_shape=[
            jax.ShapeDtypeStruct((2 * pairs, 2 * part, rows), jnp.bfloat16),
            jax.ShapeDtypeStruct((rows, width), jnp.bfloat16),
            jax.ShapeDtypeStruct((rows, width), jnp.float32),
        ],
        scratch_shapes=[
            pltpu.VMEM((2, 2 * part, 128), jnp.bfloat16),
            pltpu.VMEM((2, 128, 2 * part), jnp.bfloat16),
            pltpu.VMEM((2, 2 * part, unit), jnp.float32),
        ],
        compiler_params=pltpu.CompilerParams(vmem_limit_bytes=56 << 20),
        name="attend",
    )(q, qc, own, own, own, sib, sib, sib)


def attend_back_kernel(q_ref, k0, v0, k1, v1, p_ref, o_ref, inv_ref, do_ref, dq_ref, own_ref, sib_ref, kt, va, dk, dv):
    part = k0.shape[0]
    unit = q_ref.shape[0]
    lane_k = lax.broadcasted_iota(jnp.int32, (part, 128), 1)

    @pl.when(pl.program_id(1) == 0)
    def _():
        for i, (k_ref, v_ref) in enumerate(((k0, v0), (k1, v1))):
            k, v = k_ref[...], v_ref[...]
            zero, one = jnp.zeros_like(v), jnp.ones_like(v)
            here = slice(i * part, (i + 1) * part)
            kt[0, :, here] = jnp.where(lane_k < HEAD_DIM, k, zero).T
            kt[1, :, here] = jnp.where(lane_k < HEAD_DIM, zero, k).T
            va[0, here] = jnp.where(lane_k < HEAD_DIM, v, jnp.where(lane_k < HEAD_DIM + 3, one, zero))
            va[1, here] = jnp.where(lane_k >= HEAD_DIM, v, jnp.where(lane_k < 3, one, zero))
        dk[...] = jnp.zeros_like(dk)
        dv[...] = jnp.zeros_like(dv)

    lane = lax.broadcasted_iota(jnp.int32, (unit, 128), 1)
    q = q_ref[...]
    dof = do_ref[...].astype(jnp.float32) * inv_ref[...]
    prod = dof * o_ref[...].astype(jnp.float32)
    dob = dof.astype(jnp.bfloat16)
    zero = jnp.zeros_like(dob)
    turned = None
    for h in range(2):
        mine = lane < HEAD_DIM if h == 0 else lane >= HEAD_DIM
        base = HEAD_DIM if h == 0 else 0
        d = -jnp.sum(jnp.where(mine, prod, 0.0), axis=1, keepdims=True)
        d1 = d.astype(jnp.bfloat16).astype(jnp.float32)
        d2 = (d - d1).astype(jnp.bfloat16).astype(jnp.float32)
        d3 = d - d1 - d2
        extra = jnp.where(
            lane == base, d1, jnp.where(lane == base + 1, d2, jnp.where(lane == base + 2, d3, 0.0))
        ).astype(jnp.bfloat16)
        p = p_ref[h]
        ds = (p.astype(jnp.float32) * dotf(va[h], jnp.where(mine, dob, extra), NT)).astype(jnp.bfloat16)
        dv[...] += dotf(p, jnp.where(mine, dob, zero))
        dk[...] += dotf(ds, jnp.where(mine, q, zero))
        new = dotf(kt[h], ds)
        turned = new if turned is None else turned + new
    dq_ref[...] = turned.T * (1.0 / math.sqrt(HEAD_DIM))

    @pl.when(pl.program_id(1) == pl.num_programs(1) - 1)
    def _():
        for i, total in enumerate((dk, dv)):
            own_ref[i] = total[:part]
            sib_ref[i] = total[part:].astype(jnp.bfloat16)


def attend_back_pallas(q, own, sib, p, o, inv, do, first, pairs, unit=512):
    rows, width = q.shape
    all_pairs = width // 128
    part = own.shape[0]
    row = pl.BlockSpec((unit, 128), lambda j, i: (i, j + first))
    kv = [
        pl.BlockSpec((part, 128), lambda j, i: (0, j + first)),
        pl.BlockSpec((part, 128), lambda j, i: (0, j + first + all_pairs)),
    ]
    return pl.pallas_call(
        attend_back_kernel,
        grid=(pairs, rows // unit),
        in_specs=[row, *kv, *kv, pl.BlockSpec((2, 2 * part, unit), lambda j, i: (j + first, 0, i)), row, row, row],
        out_specs=[
            pl.BlockSpec((unit, 128), lambda j, i: (i, j)),
            pl.BlockSpec((2, part, 128), lambda j, i: (0, 0, j)),
            pl.BlockSpec((2, part, 128), lambda j, i: (0, 0, j)),
        ],
        out_shape=[
            jax.ShapeDtypeStruct((rows, 128 * pairs), jnp.float32),
            jax.ShapeDtypeStruct((2, part, 128 * pairs), jnp.float32),
            jax.ShapeDtypeStruct((2, part, 128 * pairs), jnp.bfloat16),
        ],
        scratch_shapes=[
            pltpu.VMEM((2, 128, 2 * part), jnp.bfloat16),
            pltpu.VMEM((2, 2 * part, 128), jnp.bfloat16),
            pltpu.VMEM((2 * part, 128), jnp.float32),
            pltpu.VMEM((2 * part, 128), jnp.float32),
        ],
        compiler_params=pltpu.CompilerParams(vmem_limit_bytes=56 << 20),
        name="attend_back",
    )(q, own, own, sib, sib, p, o, inv, do)


def mean_row(field):
    return jnp.mean(field, -1, keepdims=True)


def middle_kernel(
    x_ref, att_ref, cot_ref, wo_ref, wg_ref, wu_ref, wd_ref, norms_ref,
    out_ref, dr_ref, branch_ref, datt_ref, hid_ref, mixed_ref, dgate_ref, dup_ref, dff_ref, sums_ref,
    silu_s, slope_s,
):
    gain_one, shift_one, gain_two, shift_two = (norms_ref[n : n + 1] for n in range(4))
    resid_one = x_ref[...].astype(jnp.float32) + dotf(att_ref[...], wo_ref[...])
    hidden, normed_one, inv_one = normalize(resid_one, gain_one, shift_one)
    hidden_low = hidden.astype(jnp.bfloat16)
    hid_ref[...] = hidden_low
    hidden_units = wd_ref.shape[0]
    step = 768
    cuts = [slice(n, n + step) for n in range(0, hidden_units, step)]
    resid_two = hidden
    for cut in cuts:
        gate = dotf(hidden_low, wg_ref[:, cut])
        up = dotf(hidden_low, wu_ref[:, cut])
        sig = jax.nn.sigmoid(gate)
        silu = gate * sig
        mixed = (silu * up).astype(jnp.bfloat16)
        silu_s[:, cut] = silu
        slope_s[:, cut] = up * sig * (1.0 + gate * (1.0 - sig))
        mixed_ref[:, cut] = mixed
        resid_two = resid_two + dotf(mixed, wd_ref[cut, :])
    result, normed_two, inv_two = normalize(resid_two, gain_two, shift_two)
    out_ref[...] = result.astype(jnp.bfloat16)
    dy = cot_ref[...].astype(jnp.float32)
    d_two = normalize_back(dy, normed_two, inv_two, gain_two)
    d_ff = d_two.astype(jnp.bfloat16)
    dff_ref[...] = d_ff
    d_hidden = d_two
    for cut in cuts:
        d_mixed = dotf(d_ff, wd_ref[cut, :], NT)
        d_up = (d_mixed * silu_s[:, cut]).astype(jnp.bfloat16)
        d_gate = (d_mixed * slope_s[:, cut]).astype(jnp.bfloat16)
        dup_ref[:, cut] = d_up
        dgate_ref[:, cut] = d_gate
        d_hidden = d_hidden + dotf(d_gate, wg_ref[:, cut], NT) + dotf(d_up, wu_ref[:, cut], NT)
    d_one = normalize_back(d_hidden, normed_one, inv_one, gain_one)
    dr_ref[...] = d_one
    branch = d_one.astype(jnp.bfloat16)
    branch_ref[...] = branch
    datt_ref[...] = dotf(branch, wo_ref[...], NT).astype(jnp.bfloat16)

    @pl.when(pl.program_id(0) == 0)
    def _():
        sums_ref[...] = jnp.zeros_like(sums_ref)

    for n, term in enumerate((d_hidden * normed_one, d_hidden, dy * normed_two, dy)):
        sums_ref[n : n + 1] += jnp.sum(term, 0, keepdims=True)


def middle(x, attended, cotangent, wide, down, norms, block=256):
    rows, width = x.shape
    units = down.shape[0]
    row = lambda cols: pl.BlockSpec((block, cols), lambda i: (i, 0))
    once = pl.Buffered(1)
    weight = lambda shape, n: pl.BlockSpec(shape, lambda i: (0, n), pipeline_mode=once)
    like = lambda cols, dtype: jax.ShapeDtypeStruct((rows, cols), dtype)
    low = jnp.bfloat16
    first_out = (2 * units + 3 * width) // width
    return pl.pallas_call(
        middle_kernel,
        grid=(rows // block,),
        in_specs=[
            row(width), row(width), row(width),
            weight((width, width), first_out), weight((width, units), 0), weight((width, units), 1),
            weight((units, width), 0), weight((8, width), 0),
        ],
        out_specs=[
            row(width), row(width), row(width), row(width), row(width), row(units), row(units), row(units), row(width),
            pl.BlockSpec((8, width), lambda i: (0, 0)),
        ],
        out_shape=[
            like(width, low), like(width, jnp.float32), like(width, low), like(width, low), like(width, low),
            like(units, low), like(units, low), like(units, low), like(width, low),
            jax.ShapeDtypeStruct((8, width), jnp.float32),
        ],
        scratch_shapes=[pltpu.VMEM((block, units), jnp.float32), pltpu.VMEM((block, units), jnp.float32)],
        compiler_params=pltpu.CompilerParams(vmem_limit_bytes=60 << 20),
        name="middle",
    )(x, attended, cotangent, wide, wide, wide, down, norms)


def grad_wide_kernel(tiles, core_ref, left_ref, right_ref, keep_ref, send_ref):
    value = dotf(left_ref[...], right_ref[...], TN).astype(jnp.bfloat16)

    @pl.when(pl.program_id(0) < tiles)
    def _():
        send_ref[...] = value

    @pl.when(pl.program_id(0) >= tiles)
    def _():
        keep_ref[...] = value


def grad_wide(core, left, right, tile=512):
    rows, width = left.shape
    half = right.shape[1] // 2
    tiles = half // tile
    like = jax.ShapeDtypeStruct((width, half), jnp.bfloat16)
    return pl.pallas_call(
        functools.partial(grad_wide_kernel, tiles),
        grid_spec=pltpu.PrefetchScalarGridSpec(
            num_scalar_prefetch=1,
            grid=(2 * tiles,),
            in_specs=[
                pl.BlockSpec((rows, width), lambda i, c: (0, 0)),
                pl.BlockSpec(
                    (rows, tile), lambda i, c: (0, lax.rem(c[0] + 1 + lax.div(i, tiles), 2) * tiles + lax.rem(i, tiles))
                ),
            ],
            out_specs=[
                pl.BlockSpec((width, tile), lambda i, c: (0, jnp.maximum(i - tiles, 0))),
                pl.BlockSpec((width, tile), lambda i, c: (0, jnp.minimum(i, tiles - 1))),
            ],
        ),
        out_shape=[like, like],
        compiler_params=pltpu.CompilerParams(vmem_limit_bytes=48 << 20),
        name="grad_wide",
    )(core, left, right)


def halves(value, core, keep_ref, send_ref):
    half = value.shape[1] // 2
    low, high = value[:, :half].astype(jnp.bfloat16), value[:, half:].astype(jnp.bfloat16)
    keep_ref[...] = jnp.where(core == 0, low, high)
    send_ref[...] = jnp.where(core == 0, high, low)


def grad_tall_kernel(core_ref, left_ref, right_ref, keep_ref, send_ref):
    halves(dotf(left_ref[...], right_ref[...], TN), core_ref[0], keep_ref, send_ref)


def grad_tall(core, left, right, tile=512):
    rows, height = left.shape
    width = right.shape[1]
    out = pl.BlockSpec((tile, width // 2), lambda i, c: (i, 0))
    like = jax.ShapeDtypeStruct((height, width // 2), jnp.bfloat16)
    return pl.pallas_call(
        grad_tall_kernel,
        grid_spec=pltpu.PrefetchScalarGridSpec(
            num_scalar_prefetch=1,
            grid=(height // tile,),
            in_specs=[
                pl.BlockSpec((rows, tile), lambda i, c: (0, i)),
                pl.BlockSpec((rows, width), lambda i, c: (0, 0)),
            ],
            out_specs=[out, out],
        ),
        out_shape=[like, like],
        compiler_params=pltpu.CompilerParams(vmem_limit_bytes=48 << 20),
        name="grad_tall",
    )(core, left, right)


def grad_out_kernel(core_ref, left_ref, right_ref, sums_ref, keep_ref, send_ref):
    value = dotf(left_ref[...], right_ref[...], TN)
    pad = jnp.zeros((NORM_COLS - sums_ref.shape[0], sums_ref.shape[1]), jnp.float32)
    norms = jnp.concatenate([sums_ref[...], pad], 0).T
    halves(jnp.concatenate([value, norms], 1), core_ref[0], keep_ref, send_ref)


def grad_out(core, left, right, sums):
    width = left.shape[1]
    full = lambda array: pl.BlockSpec(array.shape, lambda i, c: (0, 0))
    half = (width + NORM_COLS) // 2
    out = pl.BlockSpec((width, half), lambda i, c: (0, 0))
    like = jax.ShapeDtypeStruct((width, half), jnp.bfloat16)
    return pl.pallas_call(
        grad_out_kernel,
        grid_spec=pltpu.PrefetchScalarGridSpec(
            num_scalar_prefetch=1, grid=(1,), in_specs=[full(left), full(right), full(sums)], out_specs=[out, out]
        ),
        out_shape=[like, like],
        compiler_params=pltpu.CompilerParams(vmem_limit_bytes=48 << 20),
        name="grad_out",
    )(core, left, right, sums)


def grad_qkv_kernel(calls, core_ref, x_ref, cos_ref, sin_ref, *refs):
    parts = [refs[3 * n : 3 * n + 3] for n in range(calls)]
    dproj_ref, keep_ref, send_ref, total = refs[3 * calls :]
    join = lambda pieces: jnp.concatenate(pieces, -1)
    d_query = join([dq[...] for dq, _, _ in parts])
    d_keys = join([own[0] + got[0].astype(jnp.float32) for _, own, got in parts])
    d_values = join([own[1] + got[1].astype(jnp.float32) for _, own, got in parts])
    cosine, sine = cos_ref[...], -sin_ref[...]
    low = jnp.bfloat16
    d_projected = join(
        [turn(d_query, cosine, sine).astype(low), turn(d_keys, cosine, sine).astype(low), d_values.astype(low)]
    )
    dproj_ref[...] = d_projected
    new = dotf(x_ref[...], d_projected, TN)

    @pl.when(pl.program_id(0) == 0)
    def _():
        total[...] = new

    @pl.when(pl.program_id(0) > 0)
    def _():
        total[...] += new

    @pl.when(pl.program_id(0) == pl.num_programs(0) - 1)
    def _():
        halves(total[...], core_ref[0], keep_ref, send_ref)


def grad_qkv(core, x, cosine, sine, parts, block=256):
    rows, width = x.shape
    row = lambda cols: pl.BlockSpec((block, cols), lambda i, c: (i, 0))
    specs, arrays = [], []
    for d_query, own, got in parts:
        cols = d_query.shape[1]
        pair = pl.BlockSpec((2, block, cols), lambda i, c: (0, i, 0))
        specs += [row(cols), pair, pair]
        arrays += [d_query, own, got]
    half = pl.BlockSpec((width, 3 * width // 2), lambda i, c: (0, 0))
    like = jax.ShapeDtypeStruct((width, 3 * width // 2), jnp.bfloat16)
    return pl.pallas_call(
        functools.partial(grad_qkv_kernel, len(parts)),
        grid_spec=pltpu.PrefetchScalarGridSpec(
            num_scalar_prefetch=1,
            grid=(rows // block,),
            in_specs=[row(width), row(128), row(128), *specs],
            out_specs=[row(3 * width), half, half],
            scratch_shapes=[pltpu.VMEM((width, 3 * width), jnp.float32)],
        ),
        out_shape=[jax.ShapeDtypeStruct((rows, 3 * width), jnp.bfloat16), like, like],
        compiler_params=pltpu.CompilerParams(vmem_limit_bytes=56 << 20),
        name="grad_qkv",
    )(core, x, cosine, sine, *arrays)


def grad_input_kernel(dproj_ref, wq_ref, wk_ref, wv_ref, dr_ref, dx_ref):
    width = dr_ref.shape[1]
    total = dr_ref[...]
    for n, w_ref in enumerate((wq_ref, wk_ref, wv_ref)):
        total = total + dotf(dproj_ref[:, n * width : (n + 1) * width], w_ref[...], NT)
    dx_ref[...] = total.astype(jnp.bfloat16)


def grad_input(d_projected, wide, first, d_resid, block=256):
    rows, width = d_resid.shape
    weight = lambda n: pl.BlockSpec((width, width), lambda i, n=n: (0, first + n))
    row = lambda cols: pl.BlockSpec((block, cols), lambda i: (i, 0))
    return pl.pallas_call(
        grad_input_kernel,
        grid=(rows // block,),
        in_specs=[row(3 * width), weight(0), weight(1), weight(2), row(width)],
        out_specs=row(width),
        out_shape=jax.ShapeDtypeStruct((rows, width), jnp.bfloat16),
        compiler_params=pltpu.CompilerParams(vmem_limit_bytes=48 << 20),
        name="grad_input",
    )(d_projected, wide, wide, wide, d_resid)


NORM_COLS = 256
AXES = ("seq", "fsdp")


def pairs_of(shape, move):
    seqs, line = shape["seq"], shape["fsdp"]
    found = []
    for z in range(seqs):
        for f in range(line):
            to_z, to_chip, to_core = move(z, f // 2, f % 2)
            found.append((z * line + f, to_z * line + 2 * to_chip + to_core))
    return found


def send(array, pairs):
    return lax.ppermute(array, AXES, pairs)


def pick(array, index, axis):
    return lax.dynamic_index_in_dim(array, index, axis, keepdims=False)


def add_up(arrays):
    return sum(array.astype(jnp.float32) for array in arrays)


def reduce_scatter(shape, keep, away, downward):
    seqs, chips = shape["seq"], shape["fsdp"] // 2
    bits = chips.bit_length() - 1
    z = lax.axis_index("seq")
    f = lax.axis_index("fsdp")
    core, chip = f % 2, f // 2
    half = keep.shape[1]
    rows = keep.shape[0] // (seqs * chips)
    got = send(away, pairs_of(shape, lambda z, p, c: (z, p, 1 - c)))
    whole = [array.reshape((seqs,) + (2,) * bits + (rows, half)) for array in (keep, got)]
    left = list(reversed(range(bits)))
    for b in left if downward else range(bits):
        axis = 1 + sorted(left, reverse=True).index(b)
        left = [n for n in left if n != b]
        mine = (chip >> b) & 1
        away = add_up([pick(array, 1 - mine, axis) for array in whole]).astype(jnp.bfloat16)
        got = send(away, pairs_of(shape, lambda z, p, c: (z, p ^ (1 << b), c)))
        whole = [pick(array, mine, axis) for array in whole] + [got]
    terms = [add_up([pick(array, z, 0) for array in whole])]
    for k in range(1, seqs):
        away = add_up([pick(array, (z + k) % seqs, 0) for array in whole]).astype(jnp.bfloat16)
        terms.append(send(away, pairs_of(shape, lambda z, p, c: ((z + k) % seqs, p, c))))
    total = add_up(terms)
    mine, away = jnp.where(core == 0, 0, rows // 2), jnp.where(core == 0, rows // 2, 0)
    got = send(
        lax.dynamic_slice_in_dim(total, away, rows // 2, 0), pairs_of(shape, lambda z, p, c: (z, p, 1 - c))
    )
    mine = lax.dynamic_slice_in_dim(total, mine, rows // 2, 0)
    return jnp.where(core == 0, jnp.concatenate([mine, got], 1), jnp.concatenate([got, mine], 1))


def sum_all(shape, value):
    seqs, chips = shape["seq"], shape["fsdp"] // 2
    moves = [lambda z, p, c: (z, p, 1 - c)]
    b = 1
    while b < chips:
        moves.append(lambda z, p, c, b=b: (z, p ^ b, c))
        b *= 2
    b = 1
    while b < seqs:
        moves.append(lambda z, p, c, b=b: (z ^ b, p, c))
        b *= 2
    for move in moves:
        value = value + send(value, pairs_of(shape, move))
    return value


def seg_codes(segments):
    lane = jnp.arange(128) % HEAD_DIM
    low, high = lane < CODE_BITS, lane < 2 * CODE_BITS
    bit = (segments[:, None] >> jnp.where(low, lane, jnp.where(high, lane - CODE_BITS, 0))[None, :]) & 1
    query = jnp.where(low, bit, jnp.where(high, 1 - bit, 0))
    keys = jnp.where(low, 1 - bit, jnp.where(high, bit, 0)) * -FAR
    return query.astype(jnp.bfloat16), keys.astype(jnp.bfloat16)


def two_to_a_sequence(
    shape,
    tokens, segment_ids, cotangent,
    w_qkv, w_out, w_gate, w_up, w_down, norm_params,
    first_qkv, first_out, first_gate, first_up, first_down, first_norms,
    second_qkv, second_out, second_gate, second_up, second_down, second_norms,
):
    seqs = shape["seq"]
    seq_count, local_len, width = tokens.shape
    rows = seq_count * local_len
    group = seqs // seq_count
    units = w_gate.shape[1]
    z = lax.axis_index("seq")
    f = lax.axis_index("fsdp")
    core = f % 2

    def there(turn_at):
        def move(z, p, c):
            at = (c * seq_count + (z + turn_at) % seq_count) * group + z // seq_count
            return (at // 2, p, at % 2)

        return pairs_of(shape, move)

    out_pairs = [there(t) for t in range(seq_count)]
    back_pairs = [[(to, at) for at, to in pairs] for pairs in out_pairs]

    def to_sequences(array):
        return jnp.concatenate(
            [send(pick(array, (z + t) % seq_count, 0), out_pairs[t]) for t in range(seq_count)], 0
        )

    def from_sequences(array):
        got = jnp.stack(
            [send(array[t * local_len : (t + 1) * local_len], back_pairs[t]) for t in range(seq_count)]
        )
        return jnp.roll(got, z % seq_count, 0)

    x = to_sequences(tokens)
    segments = to_sequences(segment_ids)
    dy = to_sequences(cotangent)
    q_code, k_code = seg_codes(segments)
    at = z * 2 + core
    within = jnp.concatenate(
        [((at // group - t) % seq_count) * local_len + jnp.arange(local_len) for t in range(seq_count)]
    )
    positions = ((at % group) * rows + within).astype(jnp.float32)
    half_dim = HEAD_DIM // 2
    inverse = jnp.exp(jnp.arange(half_dim, dtype=jnp.float32) * (-2.0 * math.log(ROPE_BASE) / HEAD_DIM))
    angles = positions[:, None] * inverse[None, :]
    cosine, sine = jnp.cos(angles), jnp.sin(angles)
    cosine = jnp.concatenate([cosine] * 4, 1)
    sine = jnp.concatenate([-sine, sine, -sine, sine], 1)

    norm_rows = jnp.pad(norm_params.T, ((0, 0), (0, NORM_COLS - norm_params.shape[0])))
    wide, down = gather_all(shape, w_gate, w_up, w_qkv, w_out, norm_rows, w_down)
    wide = wide.reshape(width, wide.shape[-1])
    down = down.reshape(units, width)
    norms = jnp.pad(wide[:, -NORM_COLS : 4 - NORM_COLS].T.astype(jnp.float32), ((0, 4), (0, 0)))
    first_block = 2 * units // width

    sibling = pairs_of(shape, lambda z, p, c: (z, p, 1 - c))
    query, own = project(x, wide, first_block, cosine, sine, k_code)
    sib = send(own, sibling)
    probs, attended, inverse_sums = attend_pallas(query, q_code, own, sib)
    (
        result, d_resid_one, d_branch, d_attended, hidden_low, mixed, d_gate, d_up, d_ff, sums,
    ) = middle(x, attended, dy, wide, down, norms)
    output = from_sequences(result)

    core_id = core.astype(jnp.int32).reshape(1)
    scatter = functools.partial(reduce_scatter, shape)
    red_down = scatter(*grad_tall(core_id, mixed, d_ff), False)
    red_gate = scatter(*grad_wide(core_id, hidden_low, d_gate), True)
    red_up = scatter(*grad_wide(core_id, hidden_low, d_up), False)
    red_out = scatter(*grad_out(core_id, attended, d_branch, sums), True)
    red_norms = red_out[:, width : width + norm_params.shape[0]].T
    red_out = red_out[:, :width]

    parts = []
    for first, count in ((0, 2), (2, 2), (4, 2)):
        d_query, d_own, d_sib = attend_back_pallas(
            query, own, sib, probs, attended, inverse_sums, d_attended, first, count
        )
        parts.append((d_query, d_own, send(d_sib, sibling)))
    d_projected, keep, away = grad_qkv(core_id, x, cosine, sine, parts)
    red_qkv = scatter(keep, away, True)
    d_x = grad_input(d_projected, wide, first_block, d_resid_one)
    input_grad = from_sequences(d_x).astype(jnp.float32)

    reduced = (red_qkv, red_out, red_gate, red_up, red_down, red_norms)
    squares = sum(jnp.sum(grad * grad) for grad in reduced)
    grad_norm = jnp.sqrt(sum_all(shape, squares.reshape(1))[0])
    clip_factor = jnp.minimum(1.0, MAX_NORM / (grad_norm + 1e-06))
    weights = (w_qkv, w_out, w_gate, w_up, w_down, norm_params)
    firsts = (first_qkv, first_out, first_gate, first_up, first_down, first_norms)
    seconds = (second_qkv, second_out, second_gate, second_up, second_down, second_norms)
    updated = [
        adam_update(
            weight,
            grad,
            first,
            second,
            0.0 if weight is norm_params else WEIGHT_DECAY,
            NORM_RATE if weight is norm_params else LEARN_RATE,
            clip_factor,
        )
        for weight, grad, first, second in zip(weights, reduced, firsts, seconds)
    ]
    return (
        output,
        input_grad,
        *reduced,
        *(new for new, _, _ in updated),
        *(new for _, new, _ in updated),
        *(new for _, _, new in updated),
        grad_norm,
    )


def device_program(shape, *arrays):
    tokens, w_gate, w_down = arrays[0], arrays[5], arrays[7]
    seqs, line = shape["seq"], shape["fsdp"]
    seq_count, local_len, width = tokens.shape
    fits = (
        seqs == 2 * seq_count
        and line & (line - 1) == 0
        and line >= 4
        and (seq_count * local_len) % 512 == 0
        and w_gate.shape[0] % 8 == 0
        and w_down.shape[0] % 8 == 0
    )
    return two_to_a_sequence(shape, *arrays) if fits else per_device(*arrays)


def solution(mesh):
    return jax.shard_map(
        functools.partial(device_program, dict(mesh.shape)),
        mesh=mesh,
        in_specs=(
            P("fsdp", "seq", None),
            P("fsdp", "seq"),
            P("fsdp", "seq", None),
            P(("seq", "fsdp"), None),
            P(("seq", "fsdp"), None),
            P(("seq", "fsdp"), None),
            P(("seq", "fsdp"), None),
            P(("seq", "fsdp"), None),
            P(None, ("seq", "fsdp")),
            P(("seq", "fsdp"), None),
            P(("seq", "fsdp"), None),
            P(("seq", "fsdp"), None),
            P(("seq", "fsdp"), None),
            P(("seq", "fsdp"), None),
            P(None, ("seq", "fsdp")),
            P(("seq", "fsdp"), None),
            P(("seq", "fsdp"), None),
            P(("seq", "fsdp"), None),
            P(("seq", "fsdp"), None),
            P(("seq", "fsdp"), None),
            P(None, ("seq", "fsdp")),
        ),
        out_specs=(
            P("fsdp", "seq", None),
            P("fsdp", "seq", None),
            P(("seq", "fsdp"), None),
            P(("seq", "fsdp"), None),
            P(("seq", "fsdp"), None),
            P(("seq", "fsdp"), None),
            P(("seq", "fsdp"), None),
            P(None, ("seq", "fsdp")),
            P(("seq", "fsdp"), None),
            P(("seq", "fsdp"), None),
            P(("seq", "fsdp"), None),
            P(("seq", "fsdp"), None),
            P(("seq", "fsdp"), None),
            P(None, ("seq", "fsdp")),
            P(("seq", "fsdp"), None),
            P(("seq", "fsdp"), None),
            P(("seq", "fsdp"), None),
            P(("seq", "fsdp"), None),
            P(("seq", "fsdp"), None),
            P(None, ("seq", "fsdp")),
            P(("seq", "fsdp"), None),
            P(("seq", "fsdp"), None),
            P(("seq", "fsdp"), None),
            P(("seq", "fsdp"), None),
            P(("seq", "fsdp"), None),
            P(None, ("seq", "fsdp")),
            P(),
        ),
        check_vma=False,
    )
```

```python
import functools
import math

import jax
import jax.numpy as jnp
from jax import lax
from jax.experimental import pallas as pl
from jax.experimental.pallas import tpu as pltpu
from jax.sharding import PartitionSpec as P

HEADS = 12
HEAD_DIM = 64
STEP = 10


EPS_NORM = 1e-06
ROPE_BASE = 1000.0
MASKED_SCORE = -1e30
MAX_NORM = 1.0
LEARN_RATE = 0.1
NORM_RATE = 0.6
BETA_ONE = 0.9
BETA_TWO = 0.999
ADAM_EPS = 1e-08
WEIGHT_DECAY = 0.01


def rotate(field, positions, sign_rot):
    shape_in = field.shape
    heads_view = field.reshape(shape_in[:-1] + (HEADS, HEAD_DIM))
    half_dim = HEAD_DIM // 2
    inverse = jnp.exp(
        jnp.arange(half_dim, dtype=jnp.float32) * (-2.0 * math.log(ROPE_BASE) / HEAD_DIM)
    )
    angles = positions[:, None] * inverse[None, :]
    cosine = jnp.cos(angles)[:, None, :]
    sine = jnp.sin(angles)[:, None, :] * sign_rot
    first_half = heads_view[..., :half_dim]
    second_half = heads_view[..., half_dim:]
    turned = jnp.concatenate(
        [first_half * cosine - second_half * sine, second_half * cosine + first_half * sine], -1
    )
    return turned.reshape(shape_in)


def normalize(resid, gain, shift):
    mean_row = jnp.mean(resid, -1, keepdims=True)
    centered = resid - mean_row
    inv_std = lax.rsqrt(jnp.mean(centered * centered, -1, keepdims=True) + EPS_NORM)
    normed = centered * inv_std
    return (normed * gain + shift, normed, inv_std)


def normalize_back(grad_in, normed, inv_std, gain):
    scaled = grad_in * gain
    return inv_std * (
        scaled
        - jnp.mean(scaled, -1, keepdims=True)
        - normed * jnp.mean(scaled * normed, -1, keepdims=True)
    )


def attend(query, keys, values, same_doc, score_scale):
    seq_count, local_len, model_width = query.shape

    def one_head(head_index, carried):
        out_all, log_sums = carried
        col_start = head_index * HEAD_DIM
        query_head = lax.dynamic_slice_in_dim(query, col_start, HEAD_DIM, 2)
        key_head = lax.dynamic_slice_in_dim(keys, col_start, HEAD_DIM, 2)
        value_head = lax.dynamic_slice_in_dim(values, col_start, HEAD_DIM, 2)
        raw_scores = jnp.einsum(
            "sqd,skd->sqk", query_head, key_head, preferred_element_type=jnp.float32
        )
        scores = jnp.where(same_doc, raw_scores * score_scale, MASKED_SCORE)
        row_max = jnp.max(scores, -1, keepdims=True)
        exp_scores = jnp.exp(scores - row_max)
        row_sums = jnp.sum(exp_scores, -1, keepdims=True)
        attn_prob = (exp_scores / row_sums).astype(jnp.bfloat16)
        head_out = jnp.einsum(
            "sqk,skd->sqd", attn_prob, value_head, preferred_element_type=jnp.float32
        )
        out_all = lax.dynamic_update_slice_in_dim(out_all, head_out, col_start, 2)
        log_sums = lax.dynamic_update_index_in_dim(
            log_sums, (row_max + jnp.log(row_sums))[..., 0], head_index, 0
        )
        return (out_all, log_sums)

    start_state = (
        jnp.zeros((seq_count, local_len, model_width), jnp.float32),
        jnp.zeros((HEADS, seq_count, local_len), jnp.float32),
    )
    return lax.fori_loop(0, HEADS, one_head, start_state)


def attend_back(query, keys, values, same_doc, log_sums, grad_attended, score_scale):
    seq_count, local_len, model_width = query.shape
    key_len = keys.shape[1]

    def one_head(head_index, carried):
        dq_all, dk_all, dv_all = carried
        col_start = head_index * HEAD_DIM
        query_head = lax.dynamic_slice_in_dim(query, col_start, HEAD_DIM, 2)
        key_head = lax.dynamic_slice_in_dim(keys, col_start, HEAD_DIM, 2)
        value_head = lax.dynamic_slice_in_dim(values, col_start, HEAD_DIM, 2)
        grad_head = lax.dynamic_slice_in_dim(grad_attended, col_start, HEAD_DIM, 2)
        head_sums = lax.dynamic_index_in_dim(log_sums, head_index, 0, keepdims=False)
        raw_scores = jnp.einsum(
            "sqd,skd->sqk", query_head, key_head, preferred_element_type=jnp.float32
        )
        scores = jnp.where(same_doc, raw_scores * score_scale, MASKED_SCORE)
        attn_prob = jnp.exp(scores - head_sums[..., None])
        grad_prob = jnp.einsum(
            "sqd,skd->sqk", grad_head, value_head, preferred_element_type=jnp.float32
        )
        dv_head = jnp.einsum(
            "sqk,sqd->skd",
            attn_prob.astype(jnp.bfloat16),
            grad_head,
            preferred_element_type=jnp.float32,
        )
        row_dots = jnp.sum(attn_prob * grad_prob, -1, keepdims=True)
        grad_scores = (attn_prob * (grad_prob - row_dots)).astype(jnp.bfloat16)
        dq_head = (
            jnp.einsum("sqk,skd->sqd", grad_scores, key_head, preferred_element_type=jnp.float32)
            * score_scale
        )
        dk_head = (
            jnp.einsum("sqk,sqd->skd", grad_scores, query_head, preferred_element_type=jnp.float32)
            * score_scale
        )
        dq_all = lax.dynamic_update_slice_in_dim(dq_all, dq_head, col_start, 2)
        dk_all = lax.dynamic_update_slice_in_dim(dk_all, dk_head, col_start, 2)
        dv_all = lax.dynamic_update_slice_in_dim(dv_all, dv_head, col_start, 2)
        return (dq_all, dk_all, dv_all)

    start_state = (
        jnp.zeros((seq_count, local_len, model_width), jnp.float32),
        jnp.zeros((seq_count, key_len, model_width), jnp.float32),
        jnp.zeros((seq_count, key_len, model_width), jnp.float32),
    )
    return lax.fori_loop(0, HEADS, one_head, start_state)


def adam_update(weight, gradient, moment_one, moment_two, decay_rate, step_rate, clip_factor):
    clipped = gradient * clip_factor
    first_new = BETA_ONE * moment_one + (1.0 - BETA_ONE) * clipped
    second_new = BETA_TWO * moment_two + (1.0 - BETA_TWO) * clipped * clipped
    first_fix = 1.0 - BETA_ONE**STEP
    second_fix = 1.0 - BETA_TWO**STEP
    direction = (
        first_new / first_fix / (jnp.sqrt(second_new / second_fix) + ADAM_EPS) + decay_rate * weight
    )
    return (weight - step_rate * direction, first_new, second_new)


def per_device(
    tokens,
    segment_ids,
    cotangent,
    w_qkv,
    w_out,
    w_gate,
    w_up,
    w_down,
    norm_params,
    first_qkv,
    first_out,
    first_gate,
    first_up,
    first_down,
    first_norms,
    second_qkv,
    second_out,
    second_gate,
    second_up,
    second_down,
    second_norms,
):
    seq_count, local_len, model_width = tokens.shape
    row_count = seq_count * local_len
    score_scale = 1.0 / math.sqrt(HEAD_DIM)
    lowered_qkv = w_qkv.astype(jnp.bfloat16)
    lowered_out = w_out.astype(jnp.bfloat16)
    lowered_gate = w_gate.astype(jnp.bfloat16)
    lowered_up = w_up.astype(jnp.bfloat16)
    lowered_down = w_down.astype(jnp.bfloat16)
    lowered_norms = norm_params.astype(jnp.bfloat16)
    full_qkv, full_out, full_gate, full_up, full_down, full_norms = (
        lax.all_gather(lowered_qkv, ("seq", "fsdp"), axis=0, tiled=True),
        lax.all_gather(lowered_out, ("seq", "fsdp"), axis=0, tiled=True),
        lax.all_gather(lowered_gate, ("seq", "fsdp"), axis=0, tiled=True),
        lax.all_gather(lowered_up, ("seq", "fsdp"), axis=0, tiled=True),
        lax.all_gather(lowered_down, ("seq", "fsdp"), axis=0, tiled=True),
        lax.all_gather(lowered_norms, ("seq", "fsdp"), axis=1, tiled=True),
    )
    gains = full_norms.astype(jnp.float32)
    gain_one, shift_one, gain_two, shift_two = (gains[0], gains[1], gains[2], gains[3])
    positions = (lax.axis_index("seq") * local_len + jnp.arange(local_len)).astype(jnp.float32)
    flat_rows = tokens.reshape(row_count, model_width)
    projected = jnp.dot(flat_rows, full_qkv, preferred_element_type=jnp.float32).reshape(
        seq_count, local_len, 3 * model_width
    )
    query = rotate(projected[..., :model_width], positions, 1.0).astype(jnp.bfloat16)
    keys_local = rotate(projected[..., model_width : 2 * model_width], positions, 1.0).astype(
        jnp.bfloat16
    )
    values_local = projected[..., 2 * model_width :].astype(jnp.bfloat16)
    keys_all, values_all, key_segments = (
        lax.all_gather(keys_local, "seq", axis=1, tiled=True),
        lax.all_gather(values_local, "seq", axis=1, tiled=True),
        lax.all_gather(segment_ids, "seq", axis=1, tiled=True),
    )
    same_doc = segment_ids[:, :, None] == key_segments[:, None, :]
    attended, log_sums = attend(query, keys_all, values_all, same_doc, score_scale)
    attended_low = attended.astype(jnp.bfloat16).reshape(row_count, model_width)
    resid_one = flat_rows.astype(jnp.float32) + jnp.dot(
        attended_low, full_out, preferred_element_type=jnp.float32
    )
    hidden, normed_one, inv_std_one = normalize(resid_one, gain_one, shift_one)
    hidden_low = hidden.astype(jnp.bfloat16)
    gate_proj = jnp.dot(hidden_low, full_gate, preferred_element_type=jnp.float32)
    up_proj = jnp.dot(hidden_low, full_up, preferred_element_type=jnp.float32)
    sigmoid_gate = jax.nn.sigmoid(gate_proj)
    silu_gate = gate_proj * sigmoid_gate
    mixed_low = (silu_gate * up_proj).astype(jnp.bfloat16)
    resid_two = hidden + jnp.dot(mixed_low, full_down, preferred_element_type=jnp.float32)
    result, normed_two, inv_std_two = normalize(resid_two, gain_two, shift_two)
    output = result.astype(jnp.bfloat16).reshape(seq_count, local_len, model_width)
    back_qkv, back_out, back_gate, back_up, back_down = (
        lax.all_gather(lowered_qkv, ("seq", "fsdp"), axis=0, tiled=True),
        lax.all_gather(lowered_out, ("seq", "fsdp"), axis=0, tiled=True),
        lax.all_gather(lowered_gate, ("seq", "fsdp"), axis=0, tiled=True),
        lax.all_gather(lowered_up, ("seq", "fsdp"), axis=0, tiled=True),
        lax.all_gather(lowered_down, ("seq", "fsdp"), axis=0, tiled=True),
    )
    grad_result = cotangent.reshape(row_count, model_width).astype(jnp.float32)
    d_gain_two = jnp.sum(grad_result * normed_two, 0)
    d_shift_two = jnp.sum(grad_result, 0)
    d_resid_two = normalize_back(grad_result, normed_two, inv_std_two, gain_two)
    d_ff_low = d_resid_two.astype(jnp.bfloat16)
    g_down = jnp.einsum("rf,rd->fd", mixed_low, d_ff_low, preferred_element_type=jnp.float32)
    d_mixed = jnp.einsum("rd,fd->rf", d_ff_low, back_down, preferred_element_type=jnp.float32)
    d_up_low = (d_mixed * silu_gate).astype(jnp.bfloat16)
    d_gate_low = (
        d_mixed * up_proj * sigmoid_gate * (1.0 + gate_proj * (1.0 - sigmoid_gate))
    ).astype(jnp.bfloat16)
    g_gate = jnp.einsum("rd,rf->df", hidden_low, d_gate_low, preferred_element_type=jnp.float32)
    g_up = jnp.einsum("rd,rf->df", hidden_low, d_up_low, preferred_element_type=jnp.float32)
    d_hidden = (
        d_resid_two
        + jnp.einsum("rf,df->rd", d_gate_low, back_gate, preferred_element_type=jnp.float32)
        + jnp.einsum("rf,df->rd", d_up_low, back_up, preferred_element_type=jnp.float32)
    )
    d_gain_one = jnp.sum(d_hidden * normed_one, 0)
    d_shift_one = jnp.sum(d_hidden, 0)
    d_resid_one = normalize_back(d_hidden, normed_one, inv_std_one, gain_one)
    d_branch_low = d_resid_one.astype(jnp.bfloat16)
    g_out = jnp.einsum("rd,re->de", attended_low, d_branch_low, preferred_element_type=jnp.float32)
    d_attended_low = (
        jnp.einsum("re,de->rd", d_branch_low, back_out, preferred_element_type=jnp.float32)
        .astype(jnp.bfloat16)
        .reshape(seq_count, local_len, model_width)
    )
    keys_back, values_back = (
        lax.all_gather(keys_local, "seq", axis=1, tiled=True),
        lax.all_gather(values_local, "seq", axis=1, tiled=True),
    )
    d_query, d_keys, d_values = attend_back(
        query, keys_back, values_back, same_doc, log_sums, d_attended_low, score_scale
    )
    d_keys_local, d_values_local = (
        lax.psum_scatter(
            d_keys.astype(jnp.bfloat16), "seq", scatter_dimension=1, tiled=True
        ).astype(jnp.float32),
        lax.psum_scatter(
            d_values.astype(jnp.bfloat16), "seq", scatter_dimension=1, tiled=True
        ).astype(jnp.float32),
    )
    d_projected_low = (
        jnp.concatenate(
            [
                rotate(d_query, positions, -1.0),
                rotate(d_keys_local, positions, -1.0),
                d_values_local,
            ],
            -1,
        )
        .astype(jnp.bfloat16)
        .reshape(row_count, 3 * model_width)
    )
    g_qkv = jnp.einsum("rd,re->de", flat_rows, d_projected_low, preferred_element_type=jnp.float32)
    input_grad = (
        d_resid_one
        + jnp.einsum("re,de->rd", d_projected_low, back_qkv, preferred_element_type=jnp.float32)
    ).reshape(seq_count, local_len, model_width)
    g_norms = jnp.stack([d_gain_one, d_shift_one, d_gain_two, d_shift_two])
    red_qkv, red_out, red_gate, red_up, red_down, red_norms = (
        lax.psum_scatter(g_qkv, ("seq", "fsdp"), scatter_dimension=0, tiled=True),
        lax.psum_scatter(g_out, ("seq", "fsdp"), scatter_dimension=0, tiled=True),
        lax.psum_scatter(g_gate, ("seq", "fsdp"), scatter_dimension=0, tiled=True),
        lax.psum_scatter(g_up, ("seq", "fsdp"), scatter_dimension=0, tiled=True),
        lax.psum_scatter(g_down, ("seq", "fsdp"), scatter_dimension=0, tiled=True),
        lax.psum_scatter(g_norms, ("seq", "fsdp"), scatter_dimension=1, tiled=True),
    )
    local_squares = (
        jnp.sum(red_qkv * red_qkv)
        + jnp.sum(red_out * red_out)
        + jnp.sum(red_gate * red_gate)
        + jnp.sum(red_up * red_up)
        + jnp.sum(red_down * red_down)
        + jnp.sum(red_norms * red_norms)
    )
    squares_sum = lax.psum(local_squares, ("seq", "fsdp"))
    grad_norm = jnp.sqrt(squares_sum)
    clip_factor = jnp.minimum(1.0, MAX_NORM / (grad_norm + 1e-06))
    new_qkv, mom_qkv, sec_qkv = adam_update(
        w_qkv, red_qkv, first_qkv, second_qkv, WEIGHT_DECAY, LEARN_RATE, clip_factor
    )
    new_out, mom_out, sec_out = adam_update(
        w_out, red_out, first_out, second_out, WEIGHT_DECAY, LEARN_RATE, clip_factor
    )
    new_gate, mom_gate, sec_gate = adam_update(
        w_gate, red_gate, first_gate, second_gate, WEIGHT_DECAY, LEARN_RATE, clip_factor
    )
    new_up, mom_up, sec_up = adam_update(
        w_up, red_up, first_up, second_up, WEIGHT_DECAY, LEARN_RATE, clip_factor
    )
    new_down, mom_down, sec_down = adam_update(
        w_down, red_down, first_down, second_down, WEIGHT_DECAY, LEARN_RATE, clip_factor
    )
    new_norms, mom_norms, sec_norms = adam_update(
        norm_params, red_norms, first_norms, second_norms, 0.0, NORM_RATE, clip_factor
    )
    return (
        output,
        input_grad,
        red_qkv,
        red_out,
        red_gate,
        red_up,
        red_down,
        red_norms,
        new_qkv,
        new_out,
        new_gate,
        new_up,
        new_down,
        new_norms,
        mom_qkv,
        mom_out,
        mom_gate,
        mom_up,
        mom_down,
        mom_norms,
        sec_qkv,
        sec_out,
        sec_gate,
        sec_up,
        sec_down,
        sec_norms,
        grad_norm,
    )


NT = (((1,), (1,)), ((), ()))
NN = (((1,), (0,)), ((), ()))
TN = (((0,), (0,)), ((), ()))
FAR = 1e30
CODE_BITS = 7
MESH_ID = pl.DeviceIdType.MESH


def dotf(left, right, dims=NN):
    return lax.dot_general(left, right, dims, preferred_element_type=jnp.float32)


def gather_kernel(seqs, bits, pieces, *refs):
    gate, up, qkv, out, norm, down = refs[:6]
    wide_all, down_all = refs[6:8]
    wide_two, down_two, wide_chip, down_chip = refs[8:12]
    core_send, core_recv, own_sem, line_send, line_recv, hop_send, hop_recv, swap_send, swap_recv = refs[12:]
    z = lax.axis_index("seq")
    f = lax.axis_index("fsdp")
    core = lax.rem(f, 2)
    chip = lax.div(f, 2)
    sibling = {"fsdp": f + 1 - 2 * core}

    def chip_at(mask):
        at = chip
        for b in range(bits):
            if mask & (1 << b):
                at = at + (1 - 2 * lax.rem(lax.div(chip, 1 << b), 2)) * (1 << b)
        return at

    def partner(b):
        return {"fsdp": 2 * chip_at(1 << b) + core}

    barrier = pltpu.get_barrier_semaphore()
    pl.semaphore_signal(barrier, inc=1, device_id=sibling, device_id_type=MESH_ID)
    for b in range(bits):
        pl.semaphore_signal(barrier, inc=1, device_id=partner(b), device_id_type=MESH_ID)

    for way in (1, seqs - 1):
        pl.semaphore_signal(barrier, inc=1, device_id={"seq": lax.rem(z + way, seqs)}, device_id_type=MESH_ID)
    rows = gate.shape[0]
    at = 0
    for part in (gate, up, qkv, out, norm):
        wide_two[core, :, at : at + part.shape[1]] = part[...]
        at += part.shape[1]
    down_two[core] = down[...]
    pl.semaphore_wait(barrier, 3 + bits)

    first = [
        pltpu.make_async_remote_copy(
            two.at[core], two.at[core], core_send.at[i], core_recv.at[i], device_id=sibling, device_id_type=MESH_ID
        )
        for i, two in enumerate((wide_two, down_two))
    ]
    for copy in first:
        copy.start()
    for copy in first:
        copy.wait()
    wide_chip[...] = wide_two[...].reshape(wide_chip.shape).astype(jnp.bfloat16)
    down_chip[...] = down_two[...].reshape(down_chip.shape).astype(jnp.bfloat16)
    own = [
        pltpu.make_async_copy(wide_chip, wide_all.at[z, chip], own_sem.at[0]),
        pltpu.make_async_copy(down_chip, down_all.at[z, chip], own_sem.at[1]),
    ]
    for copy in own:
        copy.start()

    def columns(p):
        source, offset, width, _ = pieces[p]
        half = (down_all if source else wide_all).shape[-1] // 2
        return pl.ds(pl.multiple_of(core * half + offset, 128), width)

    def block(p, zz, mask):
        return (down_all if pieces[p][0] else wide_all).at[zz, chip_at(mask), :, columns(p)]

    def own_block(p):
        return (down_chip if pieces[p][0] else wide_chip).at[:, columns(p)]

    def line_copy(p, zz, way, mine):
        return pltpu.make_async_remote_copy(
            own_block(p) if mine else block(p, zz, 0),
            block(p, zz, 0),
            line_send.at[p, way, zz],
            line_recv.at[p, zz],
            device_id={"seq": z + (1 if way else -1)},
            device_id_type=MESH_ID,
        )

    def hop_copy(p, zz, mask, b, mine):
        return pltpu.make_async_remote_copy(
            own_block(p) if mine else block(p, zz, mask),
            block(p, zz, mask),
            hop_send.at[p, zz, mask | (1 << b)],
            hop_recv.at[p, zz, mask | (1 << b)],
            device_id=partner(b),
            device_id_type=MESH_ID,
        )

    def swap_copy(p, zz, mask):
        return pltpu.make_async_remote_copy(
            block(p, zz, mask),
            block(p, zz, mask),
            swap_send.at[p, zz, mask],
            swap_recv.at[p, zz, mask],
            device_id=sibling,
            device_id_type=MESH_ID,
        )

    def level(p, mask):
        return max([i for i, b in enumerate(pieces[p][3]) if mask & (1 << b)], default=-1)

    def masks(p):
        return sorted(range(1 << bits), key=lambda mask: (level(p, mask), mask))

    def pass_on(p, zz, mask, mine=False):
        for b in pieces[p][3][level(p, mask) + 1 :]:
            hop_copy(p, zz, mask, b, mine).start()
        if not mine:
            swap_copy(p, zz, mask).start()

    def arrived(p, zz, mask):
        b = pieces[p][3][level(p, mask)]
        hop_copy(p, zz, mask & ~(1 << b), b, False).wait_recv()

    count = len(pieces)
    for p in range(count):

        @pl.when(z > 0)
        def _():
            line_copy(p, z, 0, True).start()

        @pl.when(z < seqs - 1)
        def _():
            line_copy(p, z, 1, True).start()

        pass_on(p, z, 0, True)

    def hops(zz):
        for level_at in range(bits):
            for p in range(count):
                for mask in masks(p):
                    if level(p, mask) == level_at:
                        arrived(p, zz, mask)
                        pass_on(p, zz, mask)

    for distance in range(1, seqs):
        for way in (1, 0):
            zz = z - distance if way else z + distance

            @pl.when((zz >= 0) & (zz < seqs))
            def _():
                for p in range(count):
                    line_copy(p, zz, way, False).wait_recv()

                    @pl.when((z < seqs - 1) if way else (z > 0))
                    def _():
                        line_copy(p, zz, way, False).start()

                    pass_on(p, zz, 0)

        for way in (1, 0):
            zz = z - distance + 1 if way else z + distance - 1
            if distance > 1 or way:

                @pl.when((zz >= 0) & (zz < seqs))
                def _():
                    hops(zz)

    for way in (1, 0):
        zz = z - seqs + 1 if way else z + seqs - 1

        @pl.when((zz >= 0) & (zz < seqs))
        def _():
            hops(zz)

    def finish(zz):
        for p in range(count):

            @pl.when((zz <= z) & (z < seqs - 1))
            def _():
                line_copy(p, zz, 1, False).wait_send()

            @pl.when((zz >= z) & (z > 0))
            def _():
                line_copy(p, zz, 0, False).wait_send()

            for mask in masks(p):
                for b in pieces[p][3][level(p, mask) + 1 :]:
                    hop_copy(p, zz, mask, b, False).wait_send()
                if mask:
                    swap_copy(p, zz, mask).wait()

            @pl.when(zz != z)
            def _():
                swap_copy(p, zz, 0).wait()

    lax.fori_loop(0, seqs, lambda zz, _: (finish(zz), 0)[1], 0)
    for copy in own:
        copy.wait()


def gather_all(mesh_shape, gate, up, qkv, out, norm, down):
    seqs, chips = mesh_shape["seq"], mesh_shape["fsdp"] // 2
    bits = chips.bit_length() - 1
    rows, rows_down = gate.shape[0], down.shape[0]
    wide = sum(part.shape[1] for part in (gate, up, qkv, out, norm))
    upward, downward = tuple(range(bits)), tuple(reversed(range(bits)))
    down_load = down.shape[1] // 2 * rows_down // rows
    cut = max(0, (wide // 2 + down_load) // 2 - down_load) // 128 * 128 + 128
    pieces = ((0, 0, cut, upward), (1, 0, down.shape[1] // 2, upward), (0, cut, wide // 2 - cut, downward))
    count = len(pieces)
    dma = pltpu.SemaphoreType.DMA
    any_space = pl.BlockSpec(memory_space=pl.ANY)
    vmem = pl.BlockSpec(memory_space=pltpu.VMEM)
    return pl.pallas_call(
        functools.partial(gather_kernel, seqs, bits, pieces),
        out_shape=[
            jax.ShapeDtypeStruct((seqs, chips, 2 * rows, wide), jnp.bfloat16),
            jax.ShapeDtypeStruct((seqs, chips, 2 * rows_down, down.shape[1]), jnp.bfloat16),
        ],
        in_specs=[vmem] * 6,
        out_specs=[any_space] * 2,
        scratch_shapes=[
            pltpu.VMEM((2, rows, wide), jnp.float32),
            pltpu.VMEM((2, rows_down, down.shape[1]), jnp.float32),
            pltpu.VMEM((2 * rows, wide), jnp.bfloat16),
            pltpu.VMEM((2 * rows_down, down.shape[1]), jnp.bfloat16),
            dma((2,)),
            dma((2,)),
            dma((2,)),
            dma((count, 2, seqs)),
            dma((count, seqs)),
            dma((count, seqs, chips)),
            dma((count, seqs, chips)),
            dma((count, seqs, chips)),
            dma((count, seqs, chips)),
        ],
        compiler_params=pltpu.CompilerParams(collective_id=0, has_side_effects=True, vmem_limit_bytes=48 << 20),
        name="gather_parameters",
    )(gate, up, qkv, out, norm, down)


def place():
    f = lax.axis_index("fsdp")
    return lax.axis_index("seq"), lax.div(f, 2), lax.rem(f, 2)


def chip_at(chip, mask):
    at, b = chip, 0
    while mask >> b:
        if (mask >> b) & 1:
            at = at + (1 - 2 * lax.rem(lax.div(chip, 1 << b), 2)) * (1 << b)
        b += 1
    return at


def greet(seqs, bits):
    z, chip, core = place()
    barrier = pltpu.get_barrier_semaphore()
    peers = [{"fsdp": 2 * chip + 1 - core}]
    peers += [{"fsdp": 2 * chip_at(chip, 1 << b) + core} for b in range(bits)]
    peers += [{"seq": lax.rem(z + k, seqs)} for k in range(1, seqs)]
    for peer in peers:
        pl.semaphore_signal(barrier, inc=1, device_id=peer, device_id_type=MESH_ID)
    pl.semaphore_wait(barrier, len(peers))


def hop_masks(order, stage):
    gone = sum(1 << b for b in order[:stage])
    return [m for m in range(1 << len(order)) if (m >> order[stage]) & 1 and not m & gone]


def hop_slot(order, stage, mask):
    return [m ^ (1 << order[stage]) for m in hop_masks(order, stage)].index(mask)


def reducer_scratch(seqs, bits, pieces, rows, width):
    dma = pltpu.SemaphoreType.DMA
    chips = 1 << bits
    low = jnp.bfloat16
    hops = [
        pltpu.VMEM((seqs, len(hop_masks(order, stage)), rows, cols), low)
        for _, cols, order in pieces
        for stage in range(bits)
    ]
    most = max(1, chips // 2)
    return [
        pltpu.VMEM((seqs, chips, rows, width), low),
        pltpu.VMEM((seqs, rows, width), low),
        pltpu.VMEM((2, rows // 2, width), jnp.float32),
        pltpu.VMEM((rows // 2, width), jnp.float32),
        dma((2, seqs, chips)),
        dma((2, len(pieces), bits, seqs, most)),
        dma((2, seqs)),
        dma((2,)),
        *hops,
    ]


def reducer(seqs, bits, pieces, away, keep, got, line, halves_ref, swapped, core_sem, hop_sem, line_sem, swap_sem, *hops):
    z, chip, core = place()
    rows = keep.shape[2]
    half = rows // 2
    sibling = {"fsdp": 2 * chip + 1 - core}
    masks = range(1 << bits)
    hop = lambda p, stage: hops[p * bits + stage]

    def remote(source, target, sems, index, device):
        return pltpu.make_async_remote_copy(
            source, target, sems.at[(0, *index)], sems.at[(1, *index)], device_id=device, device_id_type=MESH_ID
        )

    def core_copy(zz, mask):
        at = chip_at(chip, mask)
        return remote(away.at[zz, at], got.at[zz, at], core_sem, (zz, at), sibling)

    def hop_copy(p, stage, zz, mask):
        start, cols, order = pieces[p]
        slot = hop_slot(order, stage, mask ^ (1 << order[stage]))
        return remote(
            got.at[zz, chip_at(chip, mask), :, pl.ds(start, cols)],
            hop(p, stage).at[zz, slot],
            hop_sem,
            (p, stage, zz, slot),
            {"fsdp": 2 * chip_at(chip, 1 << order[stage]) + core},
        )

    def line_copy(zz, source):
        return remote(got.at[zz, chip], line.at[source], line_sem, (source,), {"seq": zz})

    def total(p, zz, mask, stages):
        start, cols, order = pieces[p]
        at = chip_at(chip, mask)
        where = (zz, at, slice(None), pl.ds(start, cols))
        value = keep[where].astype(jnp.float32) + got[where].astype(jnp.float32)
        for stage in range(stages):
            value = value + hop(p, stage)[zz, hop_slot(order, stage, mask)].astype(jnp.float32)
        return value

    def start():
        for k in range(1, seqs + 1):
            zz = lax.rem(z + k, seqs)
            for mask in reversed(masks):
                core_copy(zz, mask).start()

    def come(p, stage, zz):
        for mask in hop_masks(pieces[p][2], stage):
            hop_copy(p, stage, zz, mask).wait_recv()

    def stage_of(stage, zz):
        if stage == 0:
            for mask in masks:
                core_copy(zz, mask).wait_recv()
        for p, (first, cols, order) in enumerate(pieces):
            if stage:
                come(p, stage - 1, zz)
            for mask in hop_masks(order, stage):
                got[zz, chip_at(chip, mask), :, pl.ds(first, cols)] = total(p, zz, mask, stage).astype(jnp.bfloat16)
                hop_copy(p, stage, zz, mask).start()

    def line_of(zz):
        for p, (first, cols, _) in enumerate(pieces):
            come(p, bits - 1, zz)
            got[zz, chip, :, pl.ds(first, cols)] = total(p, zz, 0, bits).astype(jnp.bfloat16)
        line_copy(zz, z).start()

    def finish():
        for p in range(len(pieces)):
            come(p, bits - 1, z)
        for k in range(1, seqs):
            source = lax.rem(z + k, seqs)
            line_copy(z, source).wait_recv()
        for p, (first, cols, _) in enumerate(pieces):
            value = total(p, z, 0, bits)
            for k in range(1, seqs):
                value = value + line[lax.rem(z + k, seqs), :, pl.ds(first, cols)].astype(jnp.float32)
            halves_ref[0, :, pl.ds(first, cols)] = value[:half]
            halves_ref[1, :, pl.ds(first, cols)] = value[half:]
        swap = remote(halves_ref.at[1 - core], swapped, swap_sem, (), sibling)
        swap.start()
        for zz in range(seqs):
            for mask in masks:
                core_copy(zz, mask).wait_send()
            for p, (_, _, order) in enumerate(pieces):
                for stage in range(bits):
                    for mask in hop_masks(order, stage):
                        hop_copy(p, stage, zz, mask).wait_send()
        for k in range(1, seqs):
            line_copy(lax.rem(z + k, seqs), z).wait_send()
        swap.wait()

    def own(k):
        return lax.rem(z + k, seqs)

    return start, stage_of, line_of, finish, own


def attend_back_kernel(
    seqs, bits, pieces, plan,
    q_ref, k0, v0, k1, v1, p_ref, o_ref, inv_ref, do_ref, keep_hbm, away_hbm,
    dq_ref, own_ref, sib_ref, sum_ref,
    kt, va, dk, dv, sib, sib_sem, keep, keep_sem, *shared,
):
    part = k0.shape[0]
    unit = q_ref.shape[0]
    j, i = pl.program_id(0), pl.program_id(1)
    count = pl.num_programs(1)
    step = j * count + i
    z, chip, core = place()
    lane_k = lax.broadcasted_iota(jnp.int32, (part, 128), 1)
    start, stage_of, line_of, finish, own = reducer(seqs, bits, pieces, away_hbm, keep, *shared)
    keep_copy = pltpu.make_async_copy(keep_hbm, keep, keep_sem)

    def sib_copy(pair):
        return pltpu.make_async_remote_copy(
            sib.at[lax.rem(pair, 2)],
            sib_ref.at[:, :, pl.ds(pl.multiple_of(pair * 128, 128), 128)],
            sib_sem.at[0, pair],
            sib_sem.at[1, pair],
            device_id={"fsdp": 2 * chip + 1 - core},
            device_id_type=MESH_ID,
        )

    @pl.when(step == 0)
    def _():
        keep_copy.start()
        greet(seqs, bits)
        start()
        keep_copy.wait()

    for at, tasks in plan.items():

        @pl.when(step == at)
        def _():
            for kind, k in tasks:
                if kind < bits:
                    stage_of(kind, own(k))
                else:
                    line_of(own(k))

    @pl.when(i == 0)
    def _():
        for n, (k_ref, v_ref) in enumerate(((k0, v0), (k1, v1))):
            k, v = k_ref[...], v_ref[...]
            zero, one = jnp.zeros_like(v), jnp.ones_like(v)
            here = slice(n * part, (n + 1) * part)
            kt[0, :, here] = jnp.where(lane_k < HEAD_DIM, k, zero).T
            kt[1, :, here] = jnp.where(lane_k < HEAD_DIM, zero, k).T
            va[0, here] = jnp.where(lane_k < HEAD_DIM, v, jnp.where(lane_k < HEAD_DIM + 3, one, zero))
            va[1, here] = jnp.where(lane_k >= HEAD_DIM, v, jnp.where(lane_k < 3, one, zero))
        dk[...] = jnp.zeros_like(dk)
        dv[...] = jnp.zeros_like(dv)

    lane = lax.broadcasted_iota(jnp.int32, (unit, 128), 1)
    q = q_ref[...]
    dof = do_ref[...].astype(jnp.float32) * inv_ref[...]
    prod = dof * o_ref[...].astype(jnp.float32)
    dob = dof.astype(jnp.bfloat16)
    zero = jnp.zeros_like(dob)
    turned = None
    for h in range(2):
        mine = lane < HEAD_DIM if h == 0 else lane >= HEAD_DIM
        base = HEAD_DIM if h == 0 else 0
        d = -jnp.sum(jnp.where(mine, prod, 0.0), axis=1, keepdims=True)
        d1 = d.astype(jnp.bfloat16).astype(jnp.float32)
        d2 = (d - d1).astype(jnp.bfloat16).astype(jnp.float32)
        d3 = d - d1 - d2
        extra = jnp.where(
            lane == base, d1, jnp.where(lane == base + 1, d2, jnp.where(lane == base + 2, d3, 0.0))
        ).astype(jnp.bfloat16)
        p = p_ref[h]
        ds = (p.astype(jnp.float32) * dotf(va[h], jnp.where(mine, dob, extra), NT)).astype(jnp.bfloat16)
        dv[...] += dotf(p, jnp.where(mine, dob, zero))
        dk[...] += dotf(ds, jnp.where(mine, q, zero))
        new = dotf(kt[h], ds)
        turned = new if turned is None else turned + new
    dq_ref[...] = turned.T * (1.0 / math.sqrt(HEAD_DIM))

    @pl.when(i == count - 1)
    def _():
        @pl.when(j >= 2)
        def _():
            sib_copy(j - 2).wait_send()

        for n, total in enumerate((dk, dv)):
            own_ref[n] = total[:part]
            sib[lax.rem(j, 2), n] = total[part:].astype(jnp.bfloat16)
        sib_copy(j).start()

    @pl.when(step == pl.num_programs(0) * count - 1)
    def _():
        finish()
        halves_ref, swapped = shared[2], shared[3]
        sum_ref[core] = halves_ref[core]
        sum_ref[1 - core] = swapped[...]
        pairs = pl.num_programs(0)
        for back in (1, 0):
            sib_copy(pairs - 1 - back).wait_send()
        lax.fori_loop(0, pairs, lambda pair, _: (sib_copy(pair).wait_recv(), 0)[1], 0)


def attend_back_pallas(shape, q, own, sib, p, o, inv, do, keep, away, plan, unit=512):
    seqs, bits = shape["seq"], (shape["fsdp"] // 2).bit_length() - 1
    rows, width = q.shape
    pairs = width // 128
    part = own.shape[0]
    low = jnp.bfloat16
    keep, away = (array.reshape(seqs, 1 << bits, -1, array.shape[1]) for array in (keep, away))
    sum_rows, sum_cols = keep.shape[2:]
    pieces = halves_of(sum_cols, bits)
    row = pl.BlockSpec((unit, 128), lambda j, i: (i, j))
    kv = [
        pl.BlockSpec((part, 128), lambda j, i: (0, j)),
        pl.BlockSpec((part, 128), lambda j, i: (0, j + pairs)),
    ]
    any_space = pl.BlockSpec(memory_space=pl.ANY)
    dma = pltpu.SemaphoreType.DMA
    return pl.pallas_call(
        functools.partial(attend_back_kernel, seqs, bits, pieces, plan),
        grid=(pairs, rows // unit),
        in_specs=[
            row, *kv, *kv, pl.BlockSpec((2, 2 * part, unit), lambda j, i: (j, 0, i)), row, row, row, any_space, any_space
        ],
        out_specs=[
            row,
            pl.BlockSpec((2, part, 128), lambda j, i: (0, 0, j)),
            any_space,
            pl.BlockSpec((2, sum_rows // 2, sum_cols), lambda j, i: (0, 0, 0)),
        ],
        out_shape=[
            jax.ShapeDtypeStruct((rows, width), jnp.float32),
            jax.ShapeDtypeStruct((2, part, width), jnp.float32),
            jax.ShapeDtypeStruct((2, part, width), low),
            jax.ShapeDtypeStruct((2, sum_rows // 2, sum_cols), jnp.float32),
        ],
        scratch_shapes=[
            pltpu.VMEM((2, 128, 2 * part), low),
            pltpu.VMEM((2, 2 * part, 128), low),
            pltpu.VMEM((2 * part, 128), jnp.float32),
            pltpu.VMEM((2 * part, 128), jnp.float32),
            pltpu.VMEM((2, 2, part, 128), low),
            dma((2, pairs)),
            pltpu.VMEM(keep.shape, low),
            dma,
            *reducer_scratch(seqs, bits, pieces, sum_rows, sum_cols),
        ],
        compiler_params=pltpu.CompilerParams(
            collective_id=1, has_side_effects=True, vmem_limit_bytes=62 << 20
        ),
        name="attend_back",
    )(q, own, own, sib, sib, p, o, inv, do, keep, away)


def halves_of(cols, bits):
    cut = cols // 256 * 128
    return ((0, cut, tuple(range(bits))), (cut, cols - cut, tuple(reversed(range(bits)))))


def turn(field, cosine, sine):
    width = field.shape[-1]
    reps = width // cosine.shape[-1]
    cosine = jnp.concatenate([cosine] * reps, -1)
    sine = jnp.concatenate([sine] * reps, -1)
    lane = lax.broadcasted_iota(jnp.int32, field.shape, 1)
    half = HEAD_DIM // 2
    other = jnp.where(
        lax.rem(lane, HEAD_DIM) < half, pltpu.roll(field, width - half, 1), pltpu.roll(field, half, 1)
    )
    return field * cosine + other * sine


def project_kernel(x_ref, wq_ref, wk_ref, wv_ref, cos_ref, sin_ref, code_ref, q_ref, kv_ref):
    x, cosine, sine = x_ref[...], cos_ref[...], sin_ref[...]
    width = x.shape[-1]
    query = turn(dotf(x, wq_ref[...]), cosine, sine).astype(jnp.bfloat16)
    q_ref[...] = query * jnp.bfloat16(1.0 / math.sqrt(HEAD_DIM))
    kv_ref[:, :width] = turn(dotf(x, wk_ref[...]), cosine, sine).astype(jnp.bfloat16)
    kv_ref[:, width : 2 * width] = dotf(x, wv_ref[...]).astype(jnp.bfloat16)
    kv_ref[:, 2 * width :] = code_ref[...]


def project(x, wide, first, cosine, sine, code, block=256):
    rows, width = x.shape
    weight = lambda n: pl.BlockSpec((width, width), lambda i, n=n: (0, first + n))
    row = lambda cols: pl.BlockSpec((block, cols), lambda i: (i, 0))
    return pl.pallas_call(
        project_kernel,
        grid=(rows // block,),
        in_specs=[row(width), weight(0), weight(1), weight(2), row(128), row(128), row(128)],
        out_specs=[row(width), row(2 * width + 128)],
        out_shape=[
            jax.ShapeDtypeStruct((rows, width), jnp.bfloat16),
            jax.ShapeDtypeStruct((rows, 2 * width + 128), jnp.bfloat16),
        ],
        compiler_params=pltpu.CompilerParams(vmem_limit_bytes=48 << 20),
        name="project",
    )(x, wide, wide, wide, cosine, sine, code)


def attend_kernel(unit, chunk, q_ref, qc_ref, k0, kc0, v0, k1, kc1, v1, p_ref, o_ref, inv_ref, ka, vt, st_ref):
    part = k0.shape[0]
    keys = 2 * part
    rows = q_ref.shape[0]
    low_k = lax.broadcasted_iota(jnp.int32, (part, 128), 1) < HEAD_DIM
    for i, (k_ref, kc_ref, v_ref) in enumerate(((k0, kc0, v0), (k1, kc1, v1))):
        k, kc, v = k_ref[...], kc_ref[...], v_ref[...]
        one = jnp.ones_like(v)
        here = slice(i * part, (i + 1) * part)
        ka[0, here] = jnp.where(low_k, k, kc)
        ka[1, here] = jnp.where(low_k, kc, k)
        vt[0, :, here] = jnp.where(low_k, v, one).T
        vt[1, :, here] = jnp.where(low_k, one, v).T
    low_q = lax.broadcasted_iota(jnp.int32, (unit, 128), 1) < HEAD_DIM
    units = [(h, b) for b in range(rows // unit) for h in range(2)]
    results, before = {}, None
    for u, now in enumerate([*units, None]):
        if now is not None:
            h, b = now
            q, qc = q_ref[b * unit : (b + 1) * unit], qc_ref[b * unit : (b + 1) * unit]
            qa = jnp.where(low_q, q, qc) if h == 0 else jnp.where(low_q, qc, q)
        top = total = None
        for c in range(keys // chunk):
            here = slice(c * chunk, (c + 1) * chunk)
            if now is not None:
                s = dotf(ka[h, here], qa, NT)
                st_ref[u % 2, here] = s
                most = jnp.max(s.reshape(chunk // 8, 8, unit), axis=0)
                top = most if top is None else jnp.maximum(top, most)
            if before is not None:
                hb, bb, row_max = before
                p = jnp.exp(st_ref[(u - 1) % 2, here] - row_max).astype(jnp.bfloat16)
                p_ref[hb, here, bb * unit : (bb + 1) * unit] = p
                d = dotf(vt[hb, :, here], p)
                total = d if total is None else total + d
        if before is not None:
            results[before[:2]] = total.T
        before = None if now is None else (h, b, jnp.max(top, axis=0, keepdims=True))
    for b in range(rows // unit):
        r0, r1 = results[(0, b)], results[(1, b)]
        inv = 1.0 / pltpu.roll(jnp.where(low_q, r1, r0), HEAD_DIM, 1)
        inv_ref[b * unit : (b + 1) * unit] = inv
        o_ref[b * unit : (b + 1) * unit] = (jnp.where(low_q, r0, r1) * inv).astype(jnp.bfloat16)


def attend_pallas(q, qc, own, sib, unit=512, chunk=512):
    rows, width = q.shape
    pairs = width // 128
    part = own.shape[0]
    row = pl.BlockSpec((rows, 128), lambda j: (0, j))
    kv = [
        pl.BlockSpec((part, 128), lambda j: (0, j)),
        pl.BlockSpec((part, 128), lambda j: (0, 2 * pairs)),
        pl.BlockSpec((part, 128), lambda j: (0, pairs + j)),
    ]
    return pl.pallas_call(
        functools.partial(attend_kernel, unit, chunk),
        grid=(pairs,),
        in_specs=[row, pl.BlockSpec((rows, 128), lambda j: (0, 0)), *kv, *kv],
        out_specs=[pl.BlockSpec((2, 2 * part, rows), lambda j: (j, 0, 0)), row, row],
        out_shape=[
            jax.ShapeDtypeStruct((2 * pairs, 2 * part, rows), jnp.bfloat16),
            jax.ShapeDtypeStruct((rows, width), jnp.bfloat16),
            jax.ShapeDtypeStruct((rows, width), jnp.float32),
        ],
        scratch_shapes=[
            pltpu.VMEM((2, 2 * part, 128), jnp.bfloat16),
            pltpu.VMEM((2, 128, 2 * part), jnp.bfloat16),
            pltpu.VMEM((2, 2 * part, unit), jnp.float32),
        ],
        compiler_params=pltpu.CompilerParams(vmem_limit_bytes=56 << 20),
        name="attend",
    )(q, qc, own, own, own, sib, sib, sib)


def mean_row(field):
    return jnp.mean(field, -1, keepdims=True)


def middle_kernel(
    x_ref, att_ref, cot_ref, wo_ref, wg_ref, wu_ref, wd_ref, norms_ref,
    out_ref, dr_ref, branch_ref, datt_ref, hid_ref, mixed_ref, dgate_ref, dup_ref, dff_ref, sums_ref,
    silu_s, slope_s,
):
    gain_one, shift_one, gain_two, shift_two = (norms_ref[n : n + 1] for n in range(4))
    resid_one = x_ref[...].astype(jnp.float32) + dotf(att_ref[...], wo_ref[...])
    hidden, normed_one, inv_one = normalize(resid_one, gain_one, shift_one)
    hidden_low = hidden.astype(jnp.bfloat16)
    hid_ref[...] = hidden_low
    hidden_units = wd_ref.shape[0]
    step = 768
    cuts = [slice(n, n + step) for n in range(0, hidden_units, step)]
    resid_two = hidden
    for cut in cuts:
        gate = dotf(hidden_low, wg_ref[:, cut])
        up = dotf(hidden_low, wu_ref[:, cut])
        sig = jax.nn.sigmoid(gate)
        silu = gate * sig
        mixed = (silu * up).astype(jnp.bfloat16)
        silu_s[:, cut] = silu
        slope_s[:, cut] = up * sig * (1.0 + gate * (1.0 - sig))
        mixed_ref[:, cut] = mixed
        resid_two = resid_two + dotf(mixed, wd_ref[cut, :])
    result, normed_two, inv_two = normalize(resid_two, gain_two, shift_two)
    out_ref[...] = result.astype(jnp.bfloat16)
    dy = cot_ref[...].astype(jnp.float32)
    d_two = normalize_back(dy, normed_two, inv_two, gain_two)
    d_ff = d_two.astype(jnp.bfloat16)
    dff_ref[...] = d_ff
    d_hidden = d_two
    for cut in cuts:
        d_mixed = dotf(d_ff, wd_ref[cut, :], NT)
        d_up = (d_mixed * silu_s[:, cut]).astype(jnp.bfloat16)
        d_gate = (d_mixed * slope_s[:, cut]).astype(jnp.bfloat16)
        dup_ref[:, cut] = d_up
        dgate_ref[:, cut] = d_gate
        d_hidden = d_hidden + dotf(d_gate, wg_ref[:, cut], NT) + dotf(d_up, wu_ref[:, cut], NT)
    d_one = normalize_back(d_hidden, normed_one, inv_one, gain_one)
    dr_ref[...] = d_one
    branch = d_one.astype(jnp.bfloat16)
    branch_ref[...] = branch
    datt_ref[...] = dotf(branch, wo_ref[...], NT).astype(jnp.bfloat16)

    @pl.when(pl.program_id(0) == 0)
    def _():
        sums_ref[...] = jnp.zeros_like(sums_ref)

    for n, term in enumerate((d_hidden * normed_one, d_hidden, dy * normed_two, dy)):
        sums_ref[n : n + 1] += jnp.sum(term, 0, keepdims=True)


def middle(x, attended, cotangent, wide, down, norms, block=256):
    rows, width = x.shape
    units = down.shape[0]
    row = lambda cols: pl.BlockSpec((block, cols), lambda i: (i, 0))
    once = pl.Buffered(1)
    weight = lambda shape, n: pl.BlockSpec(shape, lambda i: (0, n), pipeline_mode=once)
    like = lambda cols, dtype: jax.ShapeDtypeStruct((rows, cols), dtype)
    low = jnp.bfloat16
    first_out = (2 * units + 3 * width) // width
    return pl.pallas_call(
        middle_kernel,
        grid=(rows // block,),
        in_specs=[
            row(width), row(width), row(width),
            weight((width, width), first_out), weight((width, units), 0), weight((width, units), 1),
            weight((units, width), 0), weight((8, width), 0),
        ],
        out_specs=[
            row(width), row(width), row(width), row(width), row(width), row(units), row(units), row(units), row(width),
            pl.BlockSpec((8, width), lambda i: (0, 0)),
        ],
        out_shape=[
            like(width, low), like(width, jnp.float32), like(width, low), like(width, low), like(width, low),
            like(units, low), like(units, low), like(units, low), like(width, low),
            jax.ShapeDtypeStruct((8, width), jnp.float32),
        ],
        scratch_shapes=[pltpu.VMEM((block, units), jnp.float32), pltpu.VMEM((block, units), jnp.float32)],
        compiler_params=pltpu.CompilerParams(vmem_limit_bytes=60 << 20),
        name="middle",
    )(x, attended, cotangent, wide, wide, wide, down, norms)


def grad_wide_kernel(tiles, core_ref, left_ref, right_ref, *refs):
    keep_ref, send_ref = refs[-2:]
    value = dotf(left_ref[...], right_ref[...], TN).astype(jnp.bfloat16)

    @pl.when(pl.program_id(0) < tiles)
    def _():
        send_ref[...] = value

    @pl.when(pl.program_id(0) >= tiles)
    def _():
        keep_ref[...] = value


def grad_wide(core, left, right, held, offset, tile=512):
    rows, width = left.shape
    half = right.shape[1] // 2
    tiles = half // tile
    first = offset // tile
    like = jax.ShapeDtypeStruct(held[0].shape, jnp.bfloat16)
    return pl.pallas_call(
        functools.partial(grad_wide_kernel, tiles),
        grid_spec=pltpu.PrefetchScalarGridSpec(
            num_scalar_prefetch=1,
            grid=(2 * tiles,),
            in_specs=[
                pl.BlockSpec((rows, width), lambda i, c: (0, 0)),
                pl.BlockSpec(
                    (rows, tile), lambda i, c: (0, lax.rem(c[0] + 1 + lax.div(i, tiles), 2) * tiles + lax.rem(i, tiles))
                ),
                pl.BlockSpec(memory_space=pl.ANY),
                pl.BlockSpec(memory_space=pl.ANY),
            ],
            out_specs=[
                pl.BlockSpec((width, tile), lambda i, c: (0, first + jnp.maximum(i - tiles, 0))),
                pl.BlockSpec((width, tile), lambda i, c: (0, first + jnp.minimum(i, tiles - 1))),
            ],
        ),
        out_shape=[like, like],
        input_output_aliases={3: 0, 4: 1},
        compiler_params=pltpu.CompilerParams(vmem_limit_bytes=48 << 20),
        name="grad_wide",
    )(core, left, right, *held)


def halves(value, core, keep_ref, send_ref):
    half = value.shape[1] // 2
    low, high = value[:, :half].astype(jnp.bfloat16), value[:, half:].astype(jnp.bfloat16)
    keep_ref[...] = jnp.where(core == 0, low, high)
    send_ref[...] = jnp.where(core == 0, high, low)


def grad_tall_kernel(rows, core_ref, left_ref, right_ref, keep_ref, send_ref):
    value = dotf(left_ref[...], right_ref[...], TN)
    half = value.shape[1] // 2
    turns = keep_ref.shape[1] // half
    core = core_ref[0]
    for n, part in enumerate((value[:, :half], value[:, half:])):
        wide = jnp.concatenate(
            [
                jnp.concatenate([part[(b * turns + a) * rows : (b * turns + a + 1) * rows] for a in range(turns)], 1)
                for b in range(part.shape[0] // (turns * rows))
            ],
            0,
        ).astype(jnp.bfloat16)

        @pl.when(core == n)
        def _():
            keep_ref[...] = wide

        @pl.when(core != n)
        def _():
            send_ref[...] = wide


def grad_tall(core, left, right, rows, cols, tile=384):
    depth, height = left.shape
    width = right.shape[1]
    devices = height // (rows * (height // width))
    fold = height // (devices * rows)
    tile_rows = tile // fold
    out = pl.BlockSpec((tile_rows, fold * width // 2), lambda i, c: (i, 0))
    like = jax.ShapeDtypeStruct((height // fold, cols), jnp.bfloat16)
    return pl.pallas_call(
        functools.partial(grad_tall_kernel, rows),
        grid_spec=pltpu.PrefetchScalarGridSpec(
            num_scalar_prefetch=1,
            grid=(height // tile,),
            in_specs=[
                pl.BlockSpec((depth, tile), lambda i, c: (0, i)),
                pl.BlockSpec((depth, width), lambda i, c: (0, 0)),
            ],
            out_specs=[out, out],
        ),
        out_shape=[like, like],
        compiler_params=pltpu.CompilerParams(vmem_limit_bytes=48 << 20),
        name="grad_tall",
    )(core, left, right)


def grad_out_kernel(core_ref, left_ref, right_ref, sums_ref, _keep, _send, keep_ref, send_ref):
    value = dotf(left_ref[...], right_ref[...], TN)
    pad = jnp.zeros((NORM_COLS - sums_ref.shape[0], sums_ref.shape[1]), jnp.float32)
    norms = jnp.concatenate([sums_ref[...], pad], 0).T
    halves(jnp.concatenate([value, norms], 1), core_ref[0], keep_ref, send_ref)


def grad_out(core, left, right, sums, held, offset):
    width = left.shape[1]
    full = lambda array: pl.BlockSpec(array.shape, lambda i, c: (0, 0))
    half = (width + NORM_COLS) // 2
    out = pl.BlockSpec((width, half), lambda i, c: (0, offset // half))
    like = jax.ShapeDtypeStruct(held[0].shape, jnp.bfloat16)
    any_space = pl.BlockSpec(memory_space=pl.ANY)
    return pl.pallas_call(
        grad_out_kernel,
        grid_spec=pltpu.PrefetchScalarGridSpec(
            num_scalar_prefetch=1,
            grid=(1,),
            in_specs=[full(left), full(right), full(sums), any_space, any_space],
            out_specs=[out, out],
        ),
        out_shape=[like, like],
        input_output_aliases={4: 0, 5: 1},
        compiler_params=pltpu.CompilerParams(vmem_limit_bytes=48 << 20),
        name="grad_out",
    )(core, left, right, sums, *held)


def grad_qkv_kernel(calls, core_ref, x_ref, cos_ref, sin_ref, *refs):
    parts = [refs[3 * n : 3 * n + 3] for n in range(calls)]
    dproj_ref, keep_ref, send_ref, total = refs[3 * calls :]
    join = lambda pieces: jnp.concatenate(pieces, -1)
    d_query = join([dq[...] for dq, _, _ in parts])
    d_keys = join([own[0] + got[0].astype(jnp.float32) for _, own, got in parts])
    d_values = join([own[1] + got[1].astype(jnp.float32) for _, own, got in parts])
    cosine, sine = cos_ref[...], -sin_ref[...]
    low = jnp.bfloat16
    d_projected = join(
        [turn(d_query, cosine, sine).astype(low), turn(d_keys, cosine, sine).astype(low), d_values.astype(low)]
    )
    dproj_ref[...] = d_projected
    new = dotf(x_ref[...], d_projected, TN)

    @pl.when(pl.program_id(0) == 0)
    def _():
        total[...] = new

    @pl.when(pl.program_id(0) > 0)
    def _():
        total[...] += new

    @pl.when(pl.program_id(0) == pl.num_programs(0) - 1)
    def _():
        halves(total[...], core_ref[0], keep_ref, send_ref)


def grad_qkv(core, x, cosine, sine, parts, block=256):
    rows, width = x.shape
    row = lambda cols: pl.BlockSpec((block, cols), lambda i, c: (i, 0))
    specs, arrays = [], []
    for d_query, own, got in parts:
        cols = d_query.shape[1]
        pair = pl.BlockSpec((2, block, cols), lambda i, c: (0, i, 0))
        specs += [row(cols), pair, pair]
        arrays += [d_query, own, got]
    half = pl.BlockSpec((width, 3 * width // 2), lambda i, c: (0, 0))
    like = jax.ShapeDtypeStruct((width, 3 * width // 2), jnp.bfloat16)
    return pl.pallas_call(
        functools.partial(grad_qkv_kernel, len(parts)),
        grid_spec=pltpu.PrefetchScalarGridSpec(
            num_scalar_prefetch=1,
            grid=(rows // block,),
            in_specs=[row(width), row(128), row(128), *specs],
            out_specs=[row(3 * width), half, half],
            scratch_shapes=[pltpu.VMEM((width, 3 * width), jnp.float32)],
        ),
        out_shape=[jax.ShapeDtypeStruct((rows, 3 * width), jnp.bfloat16), like, like],
        compiler_params=pltpu.CompilerParams(vmem_limit_bytes=56 << 20),
        name="grad_qkv",
    )(core, x, cosine, sine, *arrays)


def grad_input_kernel(dproj_ref, wq_ref, wk_ref, wv_ref, dr_ref, dx_ref):
    width = dr_ref.shape[1]
    total = dr_ref[...]
    for n, w_ref in enumerate((wq_ref, wk_ref, wv_ref)):
        total = total + dotf(dproj_ref[:, n * width : (n + 1) * width], w_ref[...], NT)
    dx_ref[...] = total.astype(jnp.bfloat16)


def grad_input(d_projected, wide, first, d_resid, block=256):
    rows, width = d_resid.shape
    weight = lambda n: pl.BlockSpec((width, width), lambda i, n=n: (0, first + n))
    row = lambda cols: pl.BlockSpec((block, cols), lambda i: (i, 0))
    return pl.pallas_call(
        grad_input_kernel,
        grid=(rows // block,),
        in_specs=[row(3 * width), weight(0), weight(1), weight(2), row(width)],
        out_specs=row(width),
        out_shape=jax.ShapeDtypeStruct((rows, width), jnp.bfloat16),
        compiler_params=pltpu.CompilerParams(vmem_limit_bytes=48 << 20),
        name="grad_input",
    )(d_projected, wide, wide, wide, d_resid)


NORM_COLS = 256
PLAN = {1: ((0, 1),), 2: ((0, 2),), 4: ((0, 3), (1, 1)), 6: ((0, 0), (1, 2)), 8: ((1, 3), (2, 1)), 9: ((2, 2),), 10: ((1, 0),), 11: ((2, 3),)}
AXES = ("seq", "fsdp")


def pairs_of(shape, move):
    seqs, line = shape["seq"], shape["fsdp"]
    found = []
    for z in range(seqs):
        for f in range(line):
            to_z, to_chip, to_core = move(z, f // 2, f % 2)
            found.append((z * line + f, to_z * line + 2 * to_chip + to_core))
    return found


def send(array, pairs):
    return lax.ppermute(array, AXES, pairs)


def pick(array, index, axis):
    return lax.dynamic_index_in_dim(array, index, axis, keepdims=False)


def add_up(arrays):
    return sum(array.astype(jnp.float32) for array in arrays)


def reduce_scatter(shape, keep, away, downward):
    seqs, chips = shape["seq"], shape["fsdp"] // 2
    bits = chips.bit_length() - 1
    z = lax.axis_index("seq")
    f = lax.axis_index("fsdp")
    core, chip = f % 2, f // 2
    half = keep.shape[1]
    rows = keep.shape[0] // (seqs * chips)
    got = send(away, pairs_of(shape, lambda z, p, c: (z, p, 1 - c)))
    whole = [array.reshape((seqs,) + (2,) * bits + (rows, half)) for array in (keep, got)]
    left = list(reversed(range(bits)))
    for b in left if downward else range(bits):
        axis = 1 + sorted(left, reverse=True).index(b)
        left = [n for n in left if n != b]
        mine = (chip >> b) & 1
        away = add_up([pick(array, 1 - mine, axis) for array in whole]).astype(jnp.bfloat16)
        got = send(away, pairs_of(shape, lambda z, p, c: (z, p ^ (1 << b), c)))
        whole = [pick(array, mine, axis) for array in whole] + [got]
    terms = [add_up([pick(array, z, 0) for array in whole])]
    for k in range(1, seqs):
        away = add_up([pick(array, (z + k) % seqs, 0) for array in whole]).astype(jnp.bfloat16)
        terms.append(send(away, pairs_of(shape, lambda z, p, c: ((z + k) % seqs, p, c))))
    total = add_up(terms)
    mine, away = jnp.where(core == 0, 0, rows // 2), jnp.where(core == 0, rows // 2, 0)
    got = send(
        lax.dynamic_slice_in_dim(total, away, rows // 2, 0), pairs_of(shape, lambda z, p, c: (z, p, 1 - c))
    )
    mine = lax.dynamic_slice_in_dim(total, mine, rows // 2, 0)
    return jnp.where(core == 0, jnp.concatenate([mine, got], 1), jnp.concatenate([got, mine], 1))


def sum_all(shape, value):
    seqs, chips = shape["seq"], shape["fsdp"] // 2
    moves = [lambda z, p, c: (z, p, 1 - c)]
    b = 1
    while b < chips:
        moves.append(lambda z, p, c, b=b: (z, p ^ b, c))
        b *= 2
    b = 1
    while b < seqs:
        moves.append(lambda z, p, c, b=b: (z ^ b, p, c))
        b *= 2
    for move in moves:
        value = value + send(value, pairs_of(shape, move))
    return value


def seg_codes(segments):
    lane = jnp.arange(128) % HEAD_DIM
    low, high = lane < CODE_BITS, lane < 2 * CODE_BITS
    bit = (segments[:, None] >> jnp.where(low, lane, jnp.where(high, lane - CODE_BITS, 0))[None, :]) & 1
    query = jnp.where(low, bit, jnp.where(high, 1 - bit, 0))
    keys = jnp.where(low, 1 - bit, jnp.where(high, bit, 0)) * -FAR
    return query.astype(jnp.bfloat16), keys.astype(jnp.bfloat16)


def two_to_a_sequence(
    shape,
    tokens, segment_ids, cotangent,
    w_qkv, w_out, w_gate, w_up, w_down, norm_params,
    first_qkv, first_out, first_gate, first_up, first_down, first_norms,
    second_qkv, second_out, second_gate, second_up, second_down, second_norms,
):
    seqs = shape["seq"]
    seq_count, local_len, width = tokens.shape
    rows = seq_count * local_len
    group = seqs // seq_count
    units = w_gate.shape[1]
    z = lax.axis_index("seq")
    f = lax.axis_index("fsdp")
    core = f % 2

    def there(turn_at):
        def move(z, p, c):
            at = (c * seq_count + (z + turn_at) % seq_count) * group + z // seq_count
            return (at // 2, p, at % 2)

        return pairs_of(shape, move)

    out_pairs = [there(t) for t in range(seq_count)]
    back_pairs = [[(to, at) for at, to in pairs] for pairs in out_pairs]

    def to_sequences(array):
        return jnp.concatenate(
            [send(pick(array, (z + t) % seq_count, 0), out_pairs[t]) for t in range(seq_count)], 0
        )

    def from_sequences(array):
        got = jnp.stack(
            [send(array[t * local_len : (t + 1) * local_len], back_pairs[t]) for t in range(seq_count)]
        )
        return jnp.roll(got, z % seq_count, 0)

    x = to_sequences(tokens)
    segments = to_sequences(segment_ids)
    dy = to_sequences(cotangent)
    q_code, k_code = seg_codes(segments)
    at = z * 2 + core
    within = jnp.concatenate(
        [((at // group - t) % seq_count) * local_len + jnp.arange(local_len) for t in range(seq_count)]
    )
    positions = ((at % group) * rows + within).astype(jnp.float32)
    half_dim = HEAD_DIM // 2
    inverse = jnp.exp(jnp.arange(half_dim, dtype=jnp.float32) * (-2.0 * math.log(ROPE_BASE) / HEAD_DIM))
    angles = positions[:, None] * inverse[None, :]
    cosine, sine = jnp.cos(angles), jnp.sin(angles)
    cosine = jnp.concatenate([cosine] * 4, 1)
    sine = jnp.concatenate([-sine, sine, -sine, sine], 1)

    norm_rows = jnp.pad(norm_params.T, ((0, 0), (0, NORM_COLS - norm_params.shape[0])))
    wide, down = gather_all(shape, w_gate, w_up, w_qkv, w_out, norm_rows, w_down)
    wide = wide.reshape(width, wide.shape[-1])
    down = down.reshape(units, width)
    norms = jnp.pad(wide[:, -NORM_COLS : 4 - NORM_COLS].T.astype(jnp.float32), ((0, 4), (0, 0)))
    first_block = 2 * units // width

    sibling = pairs_of(shape, lambda z, p, c: (z, p, 1 - c))
    query, own = project(x, wide, first_block, cosine, sine, k_code)
    sib = send(own, sibling)
    probs, attended, inverse_sums = attend_pallas(query, q_code, own, sib)
    (
        result, d_resid_one, d_branch, d_attended, hidden_low, mixed, d_gate, d_up, d_ff, sums,
    ) = middle(x, attended, dy, wide, down, norms)
    output = from_sequences(result)

    core_id = core.astype(jnp.int32).reshape(1)
    scatter = functools.partial(reduce_scatter, shape)
    own_rows = w_gate.shape[0]
    half_tall, half_wide, half_out = units * width // 2 // width, units // 2, (width + NORM_COLS) // 2
    cols = half_tall + 2 * half_wide + half_out
    held = grad_tall(core_id, mixed, d_ff, own_rows, cols)
    held = grad_wide(core_id, hidden_low, d_gate, held, half_tall)
    held = grad_wide(core_id, hidden_low, d_up, held, half_tall + half_wide)
    held = grad_out(core_id, attended, d_branch, sums, held, half_tall + 2 * half_wide)
    d_query, d_own, d_got, reduced_sums = attend_back_pallas(
        shape, query, own, sib, probs, attended, inverse_sums, d_attended, *held, PLAN
    )
    parts = [(d_query, d_own, d_got)]
    columns = lambda first, count: jnp.concatenate([reduced_sums[n, :, first : first + count] for n in range(2)], 1)
    red_down = jnp.concatenate(
        [
            reduced_sums[n, :, :half_tall].reshape(own_rows, -1, width // 2).transpose(1, 0, 2).reshape(-1, width // 2)
            for n in range(2)
        ],
        1,
    )
    red_gate = columns(half_tall, half_wide)
    red_up = columns(half_tall + half_wide, half_wide)
    red_out = columns(half_tall + 2 * half_wide, half_out)
    red_norms = red_out[:, width : width + norm_params.shape[0]].T
    red_out = red_out[:, :width]

    d_projected, keep, away = grad_qkv(core_id, x, cosine, sine, parts)
    red_qkv = scatter(keep, away, True)
    d_x = grad_input(d_projected, wide, first_block, d_resid_one)
    input_grad = from_sequences(d_x).astype(jnp.float32)

    reduced = (red_qkv, red_out, red_gate, red_up, red_down, red_norms)
    squares = sum(jnp.sum(grad * grad) for grad in reduced)
    grad_norm = jnp.sqrt(sum_all(shape, squares.reshape(1))[0])
    clip_factor = jnp.minimum(1.0, MAX_NORM / (grad_norm + 1e-06))
    weights = (w_qkv, w_out, w_gate, w_up, w_down, norm_params)
    firsts = (first_qkv, first_out, first_gate, first_up, first_down, first_norms)
    seconds = (second_qkv, second_out, second_gate, second_up, second_down, second_norms)
    updated = [
        adam_update(
            weight,
            grad,
            first,
            second,
            0.0 if weight is norm_params else WEIGHT_DECAY,
            NORM_RATE if weight is norm_params else LEARN_RATE,
            clip_factor,
        )
        for weight, grad, first, second in zip(weights, reduced, firsts, seconds)
    ]
    return (
        output,
        input_grad,
        *reduced,
        *(new for new, _, _ in updated),
        *(new for _, new, _ in updated),
        *(new for _, _, new in updated),
        grad_norm,
    )


def device_program(shape, *arrays):
    tokens, w_gate, w_down = arrays[0], arrays[5], arrays[7]
    seqs, line = shape["seq"], shape["fsdp"]
    seq_count, local_len, width = tokens.shape
    fits = (
        seqs == 2 * seq_count
        and line & (line - 1) == 0
        and line >= 4
        and (seq_count * local_len) % 512 == 0
        and w_gate.shape[0] % 8 == 0
        and w_down.shape[0] % 8 == 0
    )
    return two_to_a_sequence(shape, *arrays) if fits else per_device(*arrays)


def solution(mesh):
    return jax.shard_map(
        functools.partial(device_program, dict(mesh.shape)),
        mesh=mesh,
        in_specs=(
            P("fsdp", "seq", None),
            P("fsdp", "seq"),
            P("fsdp", "seq", None),
            P(("seq", "fsdp"), None),
            P(("seq", "fsdp"), None),
            P(("seq", "fsdp"), None),
            P(("seq", "fsdp"), None),
            P(("seq", "fsdp"), None),
            P(None, ("seq", "fsdp")),
            P(("seq", "fsdp"), None),
            P(("seq", "fsdp"), None),
            P(("seq", "fsdp"), None),
            P(("seq", "fsdp"), None),
            P(("seq", "fsdp"), None),
            P(None, ("seq", "fsdp")),
            P(("seq", "fsdp"), None),
            P(("seq", "fsdp"), None),
            P(("seq", "fsdp"), None),
            P(("seq", "fsdp"), None),
            P(("seq", "fsdp"), None),
            P(None, ("seq", "fsdp")),
        ),
        out_specs=(
            P("fsdp", "seq", None),
            P("fsdp", "seq", None),
            P(("seq", "fsdp"), None),
            P(("seq", "fsdp"), None),
            P(("seq", "fsdp"), None),
            P(("seq", "fsdp"), None),
            P(("seq", "fsdp"), None),
            P(None, ("seq", "fsdp")),
            P(("seq", "fsdp"), None),
            P(("seq", "fsdp"), None),
            P(("seq", "fsdp"), None),
            P(("seq", "fsdp"), None),
            P(("seq", "fsdp"), None),
            P(None, ("seq", "fsdp")),
            P(("seq", "fsdp"), None),
            P(("seq", "fsdp"), None),
            P(("seq", "fsdp"), None),
            P(("seq", "fsdp"), None),
            P(("seq", "fsdp"), None),
            P(None, ("seq", "fsdp")),
            P(("seq", "fsdp"), None),
            P(("seq", "fsdp"), None),
            P(("seq", "fsdp"), None),
            P(("seq", "fsdp"), None),
            P(("seq", "fsdp"), None),
            P(None, ("seq", "fsdp")),
            P(),
        ),
        check_vma=False,
    )
```

```python
import functools
import math

import jax
import jax.numpy as jnp
from jax import lax
from jax.experimental import pallas as pl
from jax.experimental.pallas import tpu as pltpu
from jax.sharding import PartitionSpec as P

HEADS = 12
HEAD_DIM = 64
STEP = 10


EPS_NORM = 1e-06
ROPE_BASE = 1000.0
MASKED_SCORE = -1e30
MAX_NORM = 1.0
LEARN_RATE = 0.1
NORM_RATE = 0.6
BETA_ONE = 0.9
BETA_TWO = 0.999
ADAM_EPS = 1e-08
WEIGHT_DECAY = 0.01


def rotate(field, positions, sign_rot):
    shape_in = field.shape
    heads_view = field.reshape(shape_in[:-1] + (HEADS, HEAD_DIM))
    half_dim = HEAD_DIM // 2
    inverse = jnp.exp(
        jnp.arange(half_dim, dtype=jnp.float32) * (-2.0 * math.log(ROPE_BASE) / HEAD_DIM)
    )
    angles = positions[:, None] * inverse[None, :]
    cosine = jnp.cos(angles)[:, None, :]
    sine = jnp.sin(angles)[:, None, :] * sign_rot
    first_half = heads_view[..., :half_dim]
    second_half = heads_view[..., half_dim:]
    turned = jnp.concatenate(
        [first_half * cosine - second_half * sine, second_half * cosine + first_half * sine], -1
    )
    return turned.reshape(shape_in)


def normalize(resid, gain, shift):
    mean_row = jnp.mean(resid, -1, keepdims=True)
    centered = resid - mean_row
    inv_std = lax.rsqrt(jnp.mean(centered * centered, -1, keepdims=True) + EPS_NORM)
    normed = centered * inv_std
    return (normed * gain + shift, normed, inv_std)


def normalize_back(grad_in, normed, inv_std, gain):
    scaled = grad_in * gain
    return inv_std * (
        scaled
        - jnp.mean(scaled, -1, keepdims=True)
        - normed * jnp.mean(scaled * normed, -1, keepdims=True)
    )


def attend(query, keys, values, same_doc, score_scale):
    seq_count, local_len, model_width = query.shape

    def one_head(head_index, carried):
        out_all, log_sums = carried
        col_start = head_index * HEAD_DIM
        query_head = lax.dynamic_slice_in_dim(query, col_start, HEAD_DIM, 2)
        key_head = lax.dynamic_slice_in_dim(keys, col_start, HEAD_DIM, 2)
        value_head = lax.dynamic_slice_in_dim(values, col_start, HEAD_DIM, 2)
        raw_scores = jnp.einsum(
            "sqd,skd->sqk", query_head, key_head, preferred_element_type=jnp.float32
        )
        scores = jnp.where(same_doc, raw_scores * score_scale, MASKED_SCORE)
        row_max = jnp.max(scores, -1, keepdims=True)
        exp_scores = jnp.exp(scores - row_max)
        row_sums = jnp.sum(exp_scores, -1, keepdims=True)
        attn_prob = (exp_scores / row_sums).astype(jnp.bfloat16)
        head_out = jnp.einsum(
            "sqk,skd->sqd", attn_prob, value_head, preferred_element_type=jnp.float32
        )
        out_all = lax.dynamic_update_slice_in_dim(out_all, head_out, col_start, 2)
        log_sums = lax.dynamic_update_index_in_dim(
            log_sums, (row_max + jnp.log(row_sums))[..., 0], head_index, 0
        )
        return (out_all, log_sums)

    start_state = (
        jnp.zeros((seq_count, local_len, model_width), jnp.float32),
        jnp.zeros((HEADS, seq_count, local_len), jnp.float32),
    )
    return lax.fori_loop(0, HEADS, one_head, start_state)


def attend_back(query, keys, values, same_doc, log_sums, grad_attended, score_scale):
    seq_count, local_len, model_width = query.shape
    key_len = keys.shape[1]

    def one_head(head_index, carried):
        dq_all, dk_all, dv_all = carried
        col_start = head_index * HEAD_DIM
        query_head = lax.dynamic_slice_in_dim(query, col_start, HEAD_DIM, 2)
        key_head = lax.dynamic_slice_in_dim(keys, col_start, HEAD_DIM, 2)
        value_head = lax.dynamic_slice_in_dim(values, col_start, HEAD_DIM, 2)
        grad_head = lax.dynamic_slice_in_dim(grad_attended, col_start, HEAD_DIM, 2)
        head_sums = lax.dynamic_index_in_dim(log_sums, head_index, 0, keepdims=False)
        raw_scores = jnp.einsum(
            "sqd,skd->sqk", query_head, key_head, preferred_element_type=jnp.float32
        )
        scores = jnp.where(same_doc, raw_scores * score_scale, MASKED_SCORE)
        attn_prob = jnp.exp(scores - head_sums[..., None])
        grad_prob = jnp.einsum(
            "sqd,skd->sqk", grad_head, value_head, preferred_element_type=jnp.float32
        )
        dv_head = jnp.einsum(
            "sqk,sqd->skd",
            attn_prob.astype(jnp.bfloat16),
            grad_head,
            preferred_element_type=jnp.float32,
        )
        row_dots = jnp.sum(attn_prob * grad_prob, -1, keepdims=True)
        grad_scores = (attn_prob * (grad_prob - row_dots)).astype(jnp.bfloat16)
        dq_head = (
            jnp.einsum("sqk,skd->sqd", grad_scores, key_head, preferred_element_type=jnp.float32)
            * score_scale
        )
        dk_head = (
            jnp.einsum("sqk,sqd->skd", grad_scores, query_head, preferred_element_type=jnp.float32)
            * score_scale
        )
        dq_all = lax.dynamic_update_slice_in_dim(dq_all, dq_head, col_start, 2)
        dk_all = lax.dynamic_update_slice_in_dim(dk_all, dk_head, col_start, 2)
        dv_all = lax.dynamic_update_slice_in_dim(dv_all, dv_head, col_start, 2)
        return (dq_all, dk_all, dv_all)

    start_state = (
        jnp.zeros((seq_count, local_len, model_width), jnp.float32),
        jnp.zeros((seq_count, key_len, model_width), jnp.float32),
        jnp.zeros((seq_count, key_len, model_width), jnp.float32),
    )
    return lax.fori_loop(0, HEADS, one_head, start_state)


def adam_update(weight, gradient, moment_one, moment_two, decay_rate, step_rate, clip_factor):
    clipped = gradient * clip_factor
    first_new = BETA_ONE * moment_one + (1.0 - BETA_ONE) * clipped
    second_new = BETA_TWO * moment_two + (1.0 - BETA_TWO) * clipped * clipped
    first_fix = 1.0 - BETA_ONE**STEP
    second_fix = 1.0 - BETA_TWO**STEP
    direction = (
        first_new / first_fix / (jnp.sqrt(second_new / second_fix) + ADAM_EPS) + decay_rate * weight
    )
    return (weight - step_rate * direction, first_new, second_new)


def per_device(
    tokens,
    segment_ids,
    cotangent,
    w_qkv,
    w_out,
    w_gate,
    w_up,
    w_down,
    norm_params,
    first_qkv,
    first_out,
    first_gate,
    first_up,
    first_down,
    first_norms,
    second_qkv,
    second_out,
    second_gate,
    second_up,
    second_down,
    second_norms,
):
    seq_count, local_len, model_width = tokens.shape
    row_count = seq_count * local_len
    score_scale = 1.0 / math.sqrt(HEAD_DIM)
    lowered_qkv = w_qkv.astype(jnp.bfloat16)
    lowered_out = w_out.astype(jnp.bfloat16)
    lowered_gate = w_gate.astype(jnp.bfloat16)
    lowered_up = w_up.astype(jnp.bfloat16)
    lowered_down = w_down.astype(jnp.bfloat16)
    lowered_norms = norm_params.astype(jnp.bfloat16)
    full_qkv, full_out, full_gate, full_up, full_down, full_norms = (
        lax.all_gather(lowered_qkv, ("seq", "fsdp"), axis=0, tiled=True),
        lax.all_gather(lowered_out, ("seq", "fsdp"), axis=0, tiled=True),
        lax.all_gather(lowered_gate, ("seq", "fsdp"), axis=0, tiled=True),
        lax.all_gather(lowered_up, ("seq", "fsdp"), axis=0, tiled=True),
        lax.all_gather(lowered_down, ("seq", "fsdp"), axis=0, tiled=True),
        lax.all_gather(lowered_norms, ("seq", "fsdp"), axis=1, tiled=True),
    )
    gains = full_norms.astype(jnp.float32)
    gain_one, shift_one, gain_two, shift_two = (gains[0], gains[1], gains[2], gains[3])
    positions = (lax.axis_index("seq") * local_len + jnp.arange(local_len)).astype(jnp.float32)
    flat_rows = tokens.reshape(row_count, model_width)
    projected = jnp.dot(flat_rows, full_qkv, preferred_element_type=jnp.float32).reshape(
        seq_count, local_len, 3 * model_width
    )
    query = rotate(projected[..., :model_width], positions, 1.0).astype(jnp.bfloat16)
    keys_local = rotate(projected[..., model_width : 2 * model_width], positions, 1.0).astype(
        jnp.bfloat16
    )
    values_local = projected[..., 2 * model_width :].astype(jnp.bfloat16)
    keys_all, values_all, key_segments = (
        lax.all_gather(keys_local, "seq", axis=1, tiled=True),
        lax.all_gather(values_local, "seq", axis=1, tiled=True),
        lax.all_gather(segment_ids, "seq", axis=1, tiled=True),
    )
    same_doc = segment_ids[:, :, None] == key_segments[:, None, :]
    attended, log_sums = attend(query, keys_all, values_all, same_doc, score_scale)
    attended_low = attended.astype(jnp.bfloat16).reshape(row_count, model_width)
    resid_one = flat_rows.astype(jnp.float32) + jnp.dot(
        attended_low, full_out, preferred_element_type=jnp.float32
    )
    hidden, normed_one, inv_std_one = normalize(resid_one, gain_one, shift_one)
    hidden_low = hidden.astype(jnp.bfloat16)
    gate_proj = jnp.dot(hidden_low, full_gate, preferred_element_type=jnp.float32)
    up_proj = jnp.dot(hidden_low, full_up, preferred_element_type=jnp.float32)
    sigmoid_gate = jax.nn.sigmoid(gate_proj)
    silu_gate = gate_proj * sigmoid_gate
    mixed_low = (silu_gate * up_proj).astype(jnp.bfloat16)
    resid_two = hidden + jnp.dot(mixed_low, full_down, preferred_element_type=jnp.float32)
    result, normed_two, inv_std_two = normalize(resid_two, gain_two, shift_two)
    output = result.astype(jnp.bfloat16).reshape(seq_count, local_len, model_width)
    back_qkv, back_out, back_gate, back_up, back_down = (
        lax.all_gather(lowered_qkv, ("seq", "fsdp"), axis=0, tiled=True),
        lax.all_gather(lowered_out, ("seq", "fsdp"), axis=0, tiled=True),
        lax.all_gather(lowered_gate, ("seq", "fsdp"), axis=0, tiled=True),
        lax.all_gather(lowered_up, ("seq", "fsdp"), axis=0, tiled=True),
        lax.all_gather(lowered_down, ("seq", "fsdp"), axis=0, tiled=True),
    )
    grad_result = cotangent.reshape(row_count, model_width).astype(jnp.float32)
    d_gain_two = jnp.sum(grad_result * normed_two, 0)
    d_shift_two = jnp.sum(grad_result, 0)
    d_resid_two = normalize_back(grad_result, normed_two, inv_std_two, gain_two)
    d_ff_low = d_resid_two.astype(jnp.bfloat16)
    g_down = jnp.einsum("rf,rd->fd", mixed_low, d_ff_low, preferred_element_type=jnp.float32)
    d_mixed = jnp.einsum("rd,fd->rf", d_ff_low, back_down, preferred_element_type=jnp.float32)
    d_up_low = (d_mixed * silu_gate).astype(jnp.bfloat16)
    d_gate_low = (
        d_mixed * up_proj * sigmoid_gate * (1.0 + gate_proj * (1.0 - sigmoid_gate))
    ).astype(jnp.bfloat16)
    g_gate = jnp.einsum("rd,rf->df", hidden_low, d_gate_low, preferred_element_type=jnp.float32)
    g_up = jnp.einsum("rd,rf->df", hidden_low, d_up_low, preferred_element_type=jnp.float32)
    d_hidden = (
        d_resid_two
        + jnp.einsum("rf,df->rd", d_gate_low, back_gate, preferred_element_type=jnp.float32)
        + jnp.einsum("rf,df->rd", d_up_low, back_up, preferred_element_type=jnp.float32)
    )
    d_gain_one = jnp.sum(d_hidden * normed_one, 0)
    d_shift_one = jnp.sum(d_hidden, 0)
    d_resid_one = normalize_back(d_hidden, normed_one, inv_std_one, gain_one)
    d_branch_low = d_resid_one.astype(jnp.bfloat16)
    g_out = jnp.einsum("rd,re->de", attended_low, d_branch_low, preferred_element_type=jnp.float32)
    d_attended_low = (
        jnp.einsum("re,de->rd", d_branch_low, back_out, preferred_element_type=jnp.float32)
        .astype(jnp.bfloat16)
        .reshape(seq_count, local_len, model_width)
    )
    keys_back, values_back = (
        lax.all_gather(keys_local, "seq", axis=1, tiled=True),
        lax.all_gather(values_local, "seq", axis=1, tiled=True),
    )
    d_query, d_keys, d_values = attend_back(
        query, keys_back, values_back, same_doc, log_sums, d_attended_low, score_scale
    )
    d_keys_local, d_values_local = (
        lax.psum_scatter(
            d_keys.astype(jnp.bfloat16), "seq", scatter_dimension=1, tiled=True
        ).astype(jnp.float32),
        lax.psum_scatter(
            d_values.astype(jnp.bfloat16), "seq", scatter_dimension=1, tiled=True
        ).astype(jnp.float32),
    )
    d_projected_low = (
        jnp.concatenate(
            [
                rotate(d_query, positions, -1.0),
                rotate(d_keys_local, positions, -1.0),
                d_values_local,
            ],
            -1,
        )
        .astype(jnp.bfloat16)
        .reshape(row_count, 3 * model_width)
    )
    g_qkv = jnp.einsum("rd,re->de", flat_rows, d_projected_low, preferred_element_type=jnp.float32)
    input_grad = (
        d_resid_one
        + jnp.einsum("re,de->rd", d_projected_low, back_qkv, preferred_element_type=jnp.float32)
    ).reshape(seq_count, local_len, model_width)
    g_norms = jnp.stack([d_gain_one, d_shift_one, d_gain_two, d_shift_two])
    red_qkv, red_out, red_gate, red_up, red_down, red_norms = (
        lax.psum_scatter(g_qkv, ("seq", "fsdp"), scatter_dimension=0, tiled=True),
        lax.psum_scatter(g_out, ("seq", "fsdp"), scatter_dimension=0, tiled=True),
        lax.psum_scatter(g_gate, ("seq", "fsdp"), scatter_dimension=0, tiled=True),
        lax.psum_scatter(g_up, ("seq", "fsdp"), scatter_dimension=0, tiled=True),
        lax.psum_scatter(g_down, ("seq", "fsdp"), scatter_dimension=0, tiled=True),
        lax.psum_scatter(g_norms, ("seq", "fsdp"), scatter_dimension=1, tiled=True),
    )
    local_squares = (
        jnp.sum(red_qkv * red_qkv)
        + jnp.sum(red_out * red_out)
        + jnp.sum(red_gate * red_gate)
        + jnp.sum(red_up * red_up)
        + jnp.sum(red_down * red_down)
        + jnp.sum(red_norms * red_norms)
    )
    squares_sum = lax.psum(local_squares, ("seq", "fsdp"))
    grad_norm = jnp.sqrt(squares_sum)
    clip_factor = jnp.minimum(1.0, MAX_NORM / (grad_norm + 1e-06))
    new_qkv, mom_qkv, sec_qkv = adam_update(
        w_qkv, red_qkv, first_qkv, second_qkv, WEIGHT_DECAY, LEARN_RATE, clip_factor
    )
    new_out, mom_out, sec_out = adam_update(
        w_out, red_out, first_out, second_out, WEIGHT_DECAY, LEARN_RATE, clip_factor
    )
    new_gate, mom_gate, sec_gate = adam_update(
        w_gate, red_gate, first_gate, second_gate, WEIGHT_DECAY, LEARN_RATE, clip_factor
    )
    new_up, mom_up, sec_up = adam_update(
        w_up, red_up, first_up, second_up, WEIGHT_DECAY, LEARN_RATE, clip_factor
    )
    new_down, mom_down, sec_down = adam_update(
        w_down, red_down, first_down, second_down, WEIGHT_DECAY, LEARN_RATE, clip_factor
    )
    new_norms, mom_norms, sec_norms = adam_update(
        norm_params, red_norms, first_norms, second_norms, 0.0, NORM_RATE, clip_factor
    )
    return (
        output,
        input_grad,
        red_qkv,
        red_out,
        red_gate,
        red_up,
        red_down,
        red_norms,
        new_qkv,
        new_out,
        new_gate,
        new_up,
        new_down,
        new_norms,
        mom_qkv,
        mom_out,
        mom_gate,
        mom_up,
        mom_down,
        mom_norms,
        sec_qkv,
        sec_out,
        sec_gate,
        sec_up,
        sec_down,
        sec_norms,
        grad_norm,
    )


NT = (((1,), (1,)), ((), ()))
NN = (((1,), (0,)), ((), ()))
TN = (((0,), (0,)), ((), ()))
FAR = 1e30
CODE_BITS = 7
MESH_ID = pl.DeviceIdType.MESH


def dotf(left, right, dims=NN):
    return lax.dot_general(left, right, dims, preferred_element_type=jnp.float32)


def gather_kernel(seqs, bits, pieces, *refs):
    gate, up, qkv, out, norm, down = refs[:6]
    wide_all, down_all = refs[6:8]
    wide_two, down_two, wide_chip, down_chip = refs[8:12]
    core_send, core_recv, own_sem, line_send, line_recv, hop_send, hop_recv, swap_send, swap_recv = refs[12:]
    z = lax.axis_index("seq")
    f = lax.axis_index("fsdp")
    core = lax.rem(f, 2)
    chip = lax.div(f, 2)
    sibling = {"fsdp": f + 1 - 2 * core}

    def chip_at(mask):
        at = chip
        for b in range(bits):
            if mask & (1 << b):
                at = at + (1 - 2 * lax.rem(lax.div(chip, 1 << b), 2)) * (1 << b)
        return at

    def partner(b):
        return {"fsdp": 2 * chip_at(1 << b) + core}

    barrier = pltpu.get_barrier_semaphore()
    pl.semaphore_signal(barrier, inc=1, device_id=sibling, device_id_type=MESH_ID)
    for b in range(bits):
        pl.semaphore_signal(barrier, inc=1, device_id=partner(b), device_id_type=MESH_ID)

    for way in (1, seqs - 1):
        pl.semaphore_signal(barrier, inc=1, device_id={"seq": lax.rem(z + way, seqs)}, device_id_type=MESH_ID)
    rows = gate.shape[0]
    at = 0
    for part in (gate, up, qkv, out, norm):
        wide_two[core, :, at : at + part.shape[1]] = part[...]
        at += part.shape[1]
    down_two[core] = down[...]
    pl.semaphore_wait(barrier, 3 + bits)

    first = [
        pltpu.make_async_remote_copy(
            two.at[core], two.at[core], core_send.at[i], core_recv.at[i], device_id=sibling, device_id_type=MESH_ID
        )
        for i, two in enumerate((wide_two, down_two))
    ]
    for copy in first:
        copy.start()
    for copy in first:
        copy.wait()
    wide_chip[...] = wide_two[...].reshape(wide_chip.shape).astype(jnp.bfloat16)
    down_chip[...] = down_two[...].reshape(down_chip.shape).astype(jnp.bfloat16)
    own = [
        pltpu.make_async_copy(wide_chip, wide_all.at[z, chip], own_sem.at[0]),
        pltpu.make_async_copy(down_chip, down_all.at[z, chip], own_sem.at[1]),
    ]
    for copy in own:
        copy.start()

    def columns(p):
        source, offset, width, _ = pieces[p]
        half = (down_all if source else wide_all).shape[-1] // 2
        return pl.ds(pl.multiple_of(core * half + offset, 128), width)

    def block(p, zz, mask):
        return (down_all if pieces[p][0] else wide_all).at[zz, chip_at(mask), :, columns(p)]

    def own_block(p):
        return (down_chip if pieces[p][0] else wide_chip).at[:, columns(p)]

    def line_copy(p, zz, way, mine):
        return pltpu.make_async_remote_copy(
            own_block(p) if mine else block(p, zz, 0),
            block(p, zz, 0),
            line_send.at[p, way, zz],
            line_recv.at[p, zz],
            device_id={"seq": z + (1 if way else -1)},
            device_id_type=MESH_ID,
        )

    def hop_copy(p, zz, mask, b, mine):
        return pltpu.make_async_remote_copy(
            own_block(p) if mine else block(p, zz, mask),
            block(p, zz, mask),
            hop_send.at[p, zz, mask | (1 << b)],
            hop_recv.at[p, zz, mask | (1 << b)],
            device_id=partner(b),
            device_id_type=MESH_ID,
        )

    def swap_copy(p, zz, mask):
        return pltpu.make_async_remote_copy(
            block(p, zz, mask),
            block(p, zz, mask),
            swap_send.at[p, zz, mask],
            swap_recv.at[p, zz, mask],
            device_id=sibling,
            device_id_type=MESH_ID,
        )

    def level(p, mask):
        return max([i for i, b in enumerate(pieces[p][3]) if mask & (1 << b)], default=-1)

    def masks(p):
        return sorted(range(1 << bits), key=lambda mask: (level(p, mask), mask))

    def pass_on(p, zz, mask, mine=False):
        for b in pieces[p][3][level(p, mask) + 1 :]:
            hop_copy(p, zz, mask, b, mine).start()
        if not mine:
            swap_copy(p, zz, mask).start()

    def arrived(p, zz, mask):
        b = pieces[p][3][level(p, mask)]
        hop_copy(p, zz, mask & ~(1 << b), b, False).wait_recv()

    count = len(pieces)
    for p in range(count):

        @pl.when(z > 0)
        def _():
            line_copy(p, z, 0, True).start()

        @pl.when(z < seqs - 1)
        def _():
            line_copy(p, z, 1, True).start()

        pass_on(p, z, 0, True)

    def hops(zz):
        for level_at in range(bits):
            for p in range(count):
                for mask in masks(p):
                    if level(p, mask) == level_at:
                        arrived(p, zz, mask)
                        pass_on(p, zz, mask)

    for distance in range(1, seqs):
        for way in (1, 0):
            zz = z - distance if way else z + distance

            @pl.when((zz >= 0) & (zz < seqs))
            def _():
                for p in range(count):
                    line_copy(p, zz, way, False).wait_recv()

                    @pl.when((z < seqs - 1) if way else (z > 0))
                    def _():
                        line_copy(p, zz, way, False).start()

                    pass_on(p, zz, 0)

        for way in (1, 0):
            zz = z - distance + 1 if way else z + distance - 1
            if distance > 1 or way:

                @pl.when((zz >= 0) & (zz < seqs))
                def _():
                    hops(zz)

    for way in (1, 0):
        zz = z - seqs + 1 if way else z + seqs - 1

        @pl.when((zz >= 0) & (zz < seqs))
        def _():
            hops(zz)

    def finish(zz):
        for p in range(count):

            @pl.when((zz <= z) & (z < seqs - 1))
            def _():
                line_copy(p, zz, 1, False).wait_send()

            @pl.when((zz >= z) & (z > 0))
            def _():
                line_copy(p, zz, 0, False).wait_send()

            for mask in masks(p):
                for b in pieces[p][3][level(p, mask) + 1 :]:
                    hop_copy(p, zz, mask, b, False).wait_send()
                if mask:
                    swap_copy(p, zz, mask).wait()

            @pl.when(zz != z)
            def _():
                swap_copy(p, zz, 0).wait()

    lax.fori_loop(0, seqs, lambda zz, _: (finish(zz), 0)[1], 0)
    for copy in own:
        copy.wait()


def gather_all(mesh_shape, gate, up, qkv, out, norm, down):
    seqs, chips = mesh_shape["seq"], mesh_shape["fsdp"] // 2
    bits = chips.bit_length() - 1
    rows, rows_down = gate.shape[0], down.shape[0]
    wide = sum(part.shape[1] for part in (gate, up, qkv, out, norm))
    upward, downward = tuple(range(bits)), tuple(reversed(range(bits)))
    down_load = down.shape[1] // 2 * rows_down // rows
    cut = max(0, (wide // 2 + down_load) // 2 - down_load) // 128 * 128 + 128
    pieces = ((0, 0, cut, upward), (1, 0, down.shape[1] // 2, upward), (0, cut, wide // 2 - cut, downward))
    count = len(pieces)
    dma = pltpu.SemaphoreType.DMA
    any_space = pl.BlockSpec(memory_space=pl.ANY)
    vmem = pl.BlockSpec(memory_space=pltpu.VMEM)
    return pl.pallas_call(
        functools.partial(gather_kernel, seqs, bits, pieces),
        out_shape=[
            jax.ShapeDtypeStruct((seqs, chips, 2 * rows, wide), jnp.bfloat16),
            jax.ShapeDtypeStruct((seqs, chips, 2 * rows_down, down.shape[1]), jnp.bfloat16),
        ],
        in_specs=[vmem] * 6,
        out_specs=[any_space] * 2,
        scratch_shapes=[
            pltpu.VMEM((2, rows, wide), jnp.float32),
            pltpu.VMEM((2, rows_down, down.shape[1]), jnp.float32),
            pltpu.VMEM((2 * rows, wide), jnp.bfloat16),
            pltpu.VMEM((2 * rows_down, down.shape[1]), jnp.bfloat16),
            dma((2,)),
            dma((2,)),
            dma((2,)),
            dma((count, 2, seqs)),
            dma((count, seqs)),
            dma((count, seqs, chips)),
            dma((count, seqs, chips)),
            dma((count, seqs, chips)),
            dma((count, seqs, chips)),
        ],
        compiler_params=pltpu.CompilerParams(collective_id=0, has_side_effects=True, vmem_limit_bytes=48 << 20),
        name="gather_parameters",
    )(gate, up, qkv, out, norm, down)


def place():
    f = lax.axis_index("fsdp")
    return lax.axis_index("seq"), lax.div(f, 2), lax.rem(f, 2)


def chip_at(chip, mask):
    at, b = chip, 0
    while mask >> b:
        if (mask >> b) & 1:
            at = at + (1 - 2 * lax.rem(lax.div(chip, 1 << b), 2)) * (1 << b)
        b += 1
    return at


def greet(peers):
    barrier = pltpu.get_barrier_semaphore()
    for peer in peers:
        pl.semaphore_signal(barrier, inc=1, device_id=peer, device_id_type=MESH_ID)
    pl.semaphore_wait(barrier, len(peers))


def column_peers(seqs):
    z, chip, core = place()
    return [{"seq": lax.rem(z + k, seqs), "fsdp": 2 * chip + c} for k in range(1, seqs) for c in range(2)]


def plane_peers(line):
    f = lax.axis_index("fsdp")
    return [{"fsdp": lax.rem(f + k, line)} for k in range(1, line)]


def sum_peers(bits):
    z, chip, core = place()
    return [{"fsdp": 2 * chip + 1 - core}] + [{"fsdp": 2 * chip_at(chip, 1 << b) + core} for b in range(bits)]


def returns(seqs, seq_count, source, target, sems, rows):
    z, chip, core = place()
    group = seqs // seq_count
    at = z * 2 + core
    number = lax.div(at, group)
    slot = lax.rem(number, seq_count)
    to_core = lax.div(number, seq_count)
    local_len = target.shape[1]
    subs = local_len // rows

    def copies(n):
        t, sub = divmod(n, subs)
        to_z = lax.rem(at, group) * seq_count + lax.rem(slot - t + seq_count, seq_count)
        mine = (to_z == z) & (to_core == core)
        here = target.at[slot, pl.ds(sub * rows, rows)]
        remote = pltpu.make_async_remote_copy(
            source(n), here, sems.at[0, n], sems.at[1, slot * subs + sub],
            device_id={"seq": to_z, "fsdp": 2 * chip + to_core}, device_id_type=MESH_ID,
        )
        return mine, remote, pltpu.make_async_copy(source(n), here, sems.at[2, n])

    def begin(n):
        mine, remote, local = copies(n)

        @pl.when(mine)
        def _():
            local.start()

        @pl.when(jnp.logical_not(mine))
        def _():
            remote.start()

    def end():
        for n in range(seq_count * subs):
            mine, remote, local = copies(n)

            @pl.when(mine)
            def _():
                local.wait()

            @pl.when(jnp.logical_not(mine))
            def _():
                remote.wait_send()

        for s in range(seq_count):
            came = (core * seq_count + s) * group + lax.div(z, seq_count)
            other = jnp.logical_not((lax.div(came, 2) == z) & (lax.rem(came, 2) == core))
            for sub in range(subs):

                @pl.when(other)
                def _():
                    here = target.at[s, pl.ds(sub * rows, rows)]
                    pltpu.make_async_remote_copy(
                        source(0), here, sems.at[0, 0], sems.at[1, s * subs + sub],
                        device_id={"seq": z, "fsdp": 2 * chip + 1 - core}, device_id_type=MESH_ID,
                    ).wait_recv()

    return begin, end


def hop_masks(order, stage):
    gone = sum(1 << b for b in order[:stage])
    return [m for m in range(1 << len(order)) if (m >> order[stage]) & 1 and not m & gone]


def hop_slot(order, stage, mask):
    return [m ^ (1 << order[stage]) for m in hop_masks(order, stage)].index(mask)


def reducer_scratch(seqs, bits, pieces, rows, width):
    dma = pltpu.SemaphoreType.DMA
    chips = 1 << bits
    low = jnp.bfloat16
    hops = [
        pltpu.VMEM((seqs, len(hop_masks(order, stage)), rows, cols), low)
        for _, cols, order in pieces
        for stage in range(bits)
    ]
    most = max(1, chips // 2)
    return [
        pltpu.VMEM((seqs, chips, rows, width), low),
        pltpu.VMEM((seqs, rows, width), low),
        pltpu.VMEM((2, rows // 2, width), jnp.float32),
        pltpu.VMEM((rows // 2, width), jnp.float32),
        dma((2, seqs, chips)),
        dma((2, len(pieces), bits, seqs, most)),
        dma((2, seqs)),
        dma((2,)),
        *hops,
    ]


def reducer(seqs, bits, pieces, away, keep, got, line, halves_ref, swapped, core_sem, hop_sem, line_sem, swap_sem, *hops):
    z, chip, core = place()
    rows = keep.shape[2]
    half = rows // 2
    sibling = {"fsdp": 2 * chip + 1 - core}
    masks = range(1 << bits)
    hop = lambda p, stage: hops[p * bits + stage]

    def remote(source, target, sems, index, device):
        return pltpu.make_async_remote_copy(
            source, target, sems.at[(0, *index)], sems.at[(1, *index)], device_id=device, device_id_type=MESH_ID
        )

    def core_copy(zz, mask):
        at = chip_at(chip, mask)
        return remote(away.at[zz, at], got.at[zz, at], core_sem, (zz, at), sibling)

    def hop_copy(p, stage, zz, mask):
        start, cols, order = pieces[p]
        slot = hop_slot(order, stage, mask ^ (1 << order[stage]))
        return remote(
            got.at[zz, chip_at(chip, mask), :, pl.ds(start, cols)],
            hop(p, stage).at[zz, slot],
            hop_sem,
            (p, stage, zz, slot),
            {"fsdp": 2 * chip_at(chip, 1 << order[stage]) + core},
        )

    def line_copy(zz, source):
        return remote(got.at[zz, chip], line.at[source], line_sem, (source,), {"seq": zz})

    def total(p, zz, mask, stages):
        start, cols, order = pieces[p]
        at = chip_at(chip, mask)
        where = (zz, at, slice(None), pl.ds(start, cols))
        value = keep[where].astype(jnp.float32) + got[where].astype(jnp.float32)
        for stage in range(stages):
            value = value + hop(p, stage)[zz, hop_slot(order, stage, mask)].astype(jnp.float32)
        return value

    def start():
        for k in range(1, seqs + 1):
            zz = lax.rem(z + k, seqs)
            for mask in reversed(masks):
                core_copy(zz, mask).start()

    def come(p, stage, zz):
        for mask in hop_masks(pieces[p][2], stage):
            hop_copy(p, stage, zz, mask).wait_recv()

    def stage_of(stage, zz):
        if stage == 0:
            for mask in masks:
                core_copy(zz, mask).wait_recv()
        for p, (first, cols, order) in enumerate(pieces):
            if stage:
                come(p, stage - 1, zz)
            for mask in hop_masks(order, stage):
                got[zz, chip_at(chip, mask), :, pl.ds(first, cols)] = total(p, zz, mask, stage).astype(jnp.bfloat16)
                hop_copy(p, stage, zz, mask).start()

    def line_of(zz):
        for p, (first, cols, _) in enumerate(pieces):
            come(p, bits - 1, zz)
            got[zz, chip, :, pl.ds(first, cols)] = total(p, zz, 0, bits).astype(jnp.bfloat16)
        line_copy(zz, z).start()

    def finish():
        for p in range(len(pieces)):
            come(p, bits - 1, z)
        for k in range(1, seqs):
            source = lax.rem(z + k, seqs)
            line_copy(z, source).wait_recv()
        for p, (first, cols, _) in enumerate(pieces):
            value = total(p, z, 0, bits)
            for k in range(1, seqs):
                value = value + line[lax.rem(z + k, seqs), :, pl.ds(first, cols)].astype(jnp.float32)
            halves_ref[0, :, pl.ds(first, cols)] = value[:half]
            halves_ref[1, :, pl.ds(first, cols)] = value[half:]
        swap = remote(halves_ref.at[1 - core], swapped, swap_sem, (), sibling)
        swap.start()
        for zz in range(seqs):
            for mask in masks:
                core_copy(zz, mask).wait_send()
            for p, (_, _, order) in enumerate(pieces):
                for stage in range(bits):
                    for mask in hop_masks(order, stage):
                        hop_copy(p, stage, zz, mask).wait_send()
        for k in range(1, seqs):
            line_copy(lax.rem(z + k, seqs), z).wait_send()
        swap.wait()

    def own(k):
        return lax.rem(z + k, seqs)

    return start, stage_of, line_of, finish, own


def attend_back_kernel(
    seqs, bits, pieces, plan,
    q_ref, k0, v0, k1, v1, p_ref, o_ref, inv_ref, do_ref, keep_hbm, away_hbm, result_hbm,
    dq_ref, own_ref, sib_ref, sum_ref, output_hbm,
    kt, va, dk, dv, sib, sib_sem, keep, keep_sem, back_sem, *shared,
):
    part = k0.shape[0]
    unit = q_ref.shape[0]
    j, i = pl.program_id(0), pl.program_id(1)
    count = pl.num_programs(1)
    step = j * count + i
    z, chip, core = place()
    lane_k = lax.broadcasted_iota(jnp.int32, (part, 128), 1)
    start, stage_of, line_of, finish, own = reducer(seqs, bits, pieces, away_hbm, keep, *shared)
    keep_copy = pltpu.make_async_copy(keep_hbm, keep, keep_sem)
    seq_count, local_len = output_hbm.shape[:2]
    back_begin, back_end = returns(
        seqs, seq_count, lambda n: result_hbm.at[pl.ds(n * local_len, local_len)], output_hbm, back_sem, local_len
    )

    def sib_copy(pair):
        return pltpu.make_async_remote_copy(
            sib.at[lax.rem(pair, 2)],
            sib_ref.at[:, :, pl.ds(pl.multiple_of(pair * 128, 128), 128)],
            sib_sem.at[0, pair],
            sib_sem.at[1, pair],
            device_id={"fsdp": 2 * chip + 1 - core},
            device_id_type=MESH_ID,
        )

    @pl.when(step == 0)
    def _():
        keep_copy.start()
        greet(sum_peers(bits) + column_peers(seqs))
        start()
        for n in range(seq_count):
            back_begin(n)
        keep_copy.wait()

    for at, tasks in plan.items():

        @pl.when(step == at)
        def _():
            for kind, k in tasks:
                if kind < bits:
                    stage_of(kind, own(k))
                else:
                    line_of(own(k))

    @pl.when(i == 0)
    def _():
        for n, (k_ref, v_ref) in enumerate(((k0, v0), (k1, v1))):
            k, v = k_ref[...], v_ref[...]
            zero, one = jnp.zeros_like(v), jnp.ones_like(v)
            here = slice(n * part, (n + 1) * part)
            kt[0, :, here] = jnp.where(lane_k < HEAD_DIM, k, zero).T
            kt[1, :, here] = jnp.where(lane_k < HEAD_DIM, zero, k).T
            va[0, here] = jnp.where(lane_k < HEAD_DIM, v, jnp.where(lane_k < HEAD_DIM + 3, one, zero))
            va[1, here] = jnp.where(lane_k >= HEAD_DIM, v, jnp.where(lane_k < 3, one, zero))
        dk[...] = jnp.zeros_like(dk)
        dv[...] = jnp.zeros_like(dv)

    lane = lax.broadcasted_iota(jnp.int32, (unit, 128), 1)
    q = q_ref[...]
    dof = do_ref[...].astype(jnp.float32) * inv_ref[...]
    prod = dof * o_ref[...].astype(jnp.float32)
    dob = dof.astype(jnp.bfloat16)
    zero = jnp.zeros_like(dob)
    turned = None
    for h in range(2):
        mine = lane < HEAD_DIM if h == 0 else lane >= HEAD_DIM
        base = HEAD_DIM if h == 0 else 0
        d = -jnp.sum(jnp.where(mine, prod, 0.0), axis=1, keepdims=True)
        d1 = d.astype(jnp.bfloat16).astype(jnp.float32)
        d2 = (d - d1).astype(jnp.bfloat16).astype(jnp.float32)
        d3 = d - d1 - d2
        extra = jnp.where(
            lane == base, d1, jnp.where(lane == base + 1, d2, jnp.where(lane == base + 2, d3, 0.0))
        ).astype(jnp.bfloat16)
        p = p_ref[h]
        ds = (p.astype(jnp.float32) * dotf(va[h], jnp.where(mine, dob, extra), NT)).astype(jnp.bfloat16)
        dv[...] += dotf(p, jnp.where(mine, dob, zero))
        dk[...] += dotf(ds, jnp.where(mine, q, zero))
        new = dotf(kt[h], ds)
        turned = new if turned is None else turned + new
    dq_ref[...] = turned.T * (1.0 / math.sqrt(HEAD_DIM))

    @pl.when(i == count - 1)
    def _():
        @pl.when(j >= 2)
        def _():
            sib_copy(j - 2).wait_send()

        for n, total in enumerate((dk, dv)):
            own_ref[n] = total[:part]
            sib[lax.rem(j, 2), n] = total[part:].astype(jnp.bfloat16)
        sib_copy(j).start()

    @pl.when(step == pl.num_programs(0) * count - 1)
    def _():
        finish()
        back_end()
        halves_ref, swapped = shared[2], shared[3]
        sum_ref[core] = halves_ref[core]
        sum_ref[1 - core] = swapped[...]
        pairs = pl.num_programs(0)
        for back in (1, 0):
            sib_copy(pairs - 1 - back).wait_send()
        lax.fori_loop(0, pairs, lambda pair, _: (sib_copy(pair).wait_recv(), 0)[1], 0)


def attend_back_pallas(shape, q, own, sib, p, o, inv, do, keep, away, result, seq_count, plan, unit=512):
    seqs, bits = shape["seq"], (shape["fsdp"] // 2).bit_length() - 1
    rows, width = q.shape
    pairs = width // 128
    part = own.shape[0]
    low = jnp.bfloat16
    keep, away = (array.reshape(seqs, 1 << bits, -1, array.shape[1]) for array in (keep, away))
    sum_rows, sum_cols = keep.shape[2:]
    pieces = halves_of(sum_cols, bits)
    row = pl.BlockSpec((unit, 128), lambda j, i: (i, j))
    kv = [
        pl.BlockSpec((part, 128), lambda j, i: (0, j)),
        pl.BlockSpec((part, 128), lambda j, i: (0, j + pairs)),
    ]
    any_space = pl.BlockSpec(memory_space=pl.ANY)
    dma = pltpu.SemaphoreType.DMA
    return pl.pallas_call(
        functools.partial(attend_back_kernel, seqs, bits, pieces, plan),
        grid=(pairs, rows // unit),
        in_specs=[
            row, *kv, *kv, pl.BlockSpec((2, 2 * part, unit), lambda j, i: (j, 0, i)), row, row, row,
            any_space, any_space, any_space,
        ],
        out_specs=[
            row,
            pl.BlockSpec((2, part, 128), lambda j, i: (0, 0, j)),
            any_space,
            pl.BlockSpec((2, sum_rows // 2, sum_cols), lambda j, i: (0, 0, 0)),
            any_space,
        ],
        out_shape=[
            jax.ShapeDtypeStruct((rows, width), jnp.float32),
            jax.ShapeDtypeStruct((2, part, width), jnp.float32),
            jax.ShapeDtypeStruct((2, part, width), low),
            jax.ShapeDtypeStruct((2, sum_rows // 2, sum_cols), jnp.float32),
            jax.ShapeDtypeStruct((seq_count, rows // seq_count, width), low),
        ],
        scratch_shapes=[
            pltpu.VMEM((2, 128, 2 * part), low),
            pltpu.VMEM((2, 2 * part, 128), low),
            pltpu.VMEM((2 * part, 128), jnp.float32),
            pltpu.VMEM((2 * part, 128), jnp.float32),
            pltpu.VMEM((2, 2, part, 128), low),
            dma((2, pairs)),
            pltpu.VMEM(keep.shape, low),
            dma,
            dma((3, seq_count)),
            *reducer_scratch(seqs, bits, pieces, sum_rows, sum_cols),
        ],
        compiler_params=pltpu.CompilerParams(
            collective_id=1, has_side_effects=True, vmem_limit_bytes=62 << 20
        ),
        name="attend_back",
    )(q, own, own, sib, sib, p, o, inv, do, keep, away, result)


def tail_kernel(
    seqs, bits, pieces,
    cos_ref, sin_ref, dq_ref, own_ref, got_ref, wq_ref, wk_ref, wv_ref, dr_ref, x_ref, sum_ref,
    back_ref, qsum_ref, square_ref,
    dproj, dx, keep, away, plane, line_sum, back_sem, plane_sem, total_sem, *shared,
):
    z, chip, core = place()
    f = 2 * chip + core
    line = 2 << bits
    block, width = dr_ref.shape
    i = pl.program_id(0)
    blocks = dx.shape[0]
    low = jnp.bfloat16
    start, stage_of, line_of, finish, own = reducer(seqs, bits, pieces, away, keep, *shared)
    back_begin, back_end = returns(seqs, back_ref.shape[0], lambda n: dx.at[n], back_ref, back_sem, block)

    @pl.when(i == 0)
    def _():
        greet(plane_peers(line) + column_peers(seqs))

    cosine, sine = cos_ref[...], -sin_ref[...]
    grads = (
        turn(dq_ref[...], cosine, sine).astype(low),
        turn(own_ref[0] + got_ref[0].astype(jnp.float32), cosine, sine).astype(low),
        (own_ref[1] + got_ref[1].astype(jnp.float32)).astype(low),
    )
    value = dr_ref[...]
    rows = pl.ds(pl.multiple_of(i * block, block), block)
    for n, (grad, w_ref) in enumerate(zip(grads, (wq_ref, wk_ref, wv_ref))):
        dproj[rows, n * width : (n + 1) * width] = grad
        value = value + dotf(grad, w_ref[...], NT)
    dx[i] = value.astype(low)
    for n in range(blocks):

        @pl.when(i == n)
        def _():
            back_begin(n)

    @pl.when(i == blocks - 1)
    def _():
        half = keep.shape[-1]
        tile = 384
        for target, side in ((away, 1 - core), (keep, core)):
            for n in range(half // tile):
                cols = pl.ds(pl.multiple_of(side * half + n * tile, 128), tile)
                grad = dotf(x_ref[...], dproj[:, cols], TN).astype(low)
                target[:, :, :, n * tile : (n + 1) * tile] = grad.reshape(target.shape[:3] + (tile,))
            if target is away:
                start()
        order = [*range(1, seqs), 0]
        for k in order:
            stage_of(0, own(k))
        for stage in range(1, bits):
            for k in order:
                stage_of(stage, own(k))
        for k in order[:-1]:
            line_of(own(k))
        finish()
        halves_ref, swapped = shared[2], shared[3]
        qsum_ref[core] = halves_ref[core]
        qsum_ref[1 - core] = swapped[...]
        squares = jnp.sum(jnp.square(sum_ref[...])) + jnp.sum(jnp.square(qsum_ref[...]))
        plane[f] = jnp.zeros(plane.shape[1:], jnp.float32) + squares

        def plane_copy(to, source):
            return pltpu.make_async_remote_copy(
                plane.at[source], plane.at[source], plane_sem.at[0, to], plane_sem.at[1, source],
                device_id={"fsdp": to}, device_id_type=MESH_ID,
            )

        def total_copy(to, source):
            return pltpu.make_async_remote_copy(
                line_sum.at[source], line_sum.at[source], total_sem.at[0, to], total_sem.at[1, source],
                device_id={"seq": to}, device_id_type=MESH_ID,
            )

        for k in range(1, line):
            plane_copy(lax.rem(f + k, line), f).start()
        for k in range(1, line):
            plane_copy(lax.rem(f + k, line), lax.rem(f + k, line)).wait_recv()
        line_sum[z] = sum(plane[n] for n in range(line))
        for k in range(1, seqs):
            total_copy(lax.rem(z + k, seqs), z).start()
        for k in range(1, seqs):
            total_copy(lax.rem(z + k, seqs), lax.rem(z + k, seqs)).wait_recv()
        square_ref[...] = sum(line_sum[n] for n in range(seqs))
        for k in range(1, line):
            plane_copy(lax.rem(f + k, line), f).wait_send()
        for k in range(1, seqs):
            total_copy(lax.rem(z + k, seqs), z).wait_send()
        back_end()


def tail(shape, cosine, sine, d_query, own, got, wide, first, d_resid, x, sums, seq_count, block=256):
    seqs, line = shape["seq"], shape["fsdp"]
    bits = (line // 2).bit_length() - 1
    rows, width = x.shape
    low = jnp.bfloat16
    sum_rows, sum_cols = width // (seqs * line // 2), 3 * width // 2
    pieces = halves_of(sum_cols, bits)
    dma = pltpu.SemaphoreType.DMA
    row = lambda cols: pl.BlockSpec((block, cols), lambda i: (i, 0))
    pair = pl.BlockSpec((2, block, width), lambda i: (0, i, 0))
    once = pl.Buffered(1)
    weight = lambda n: pl.BlockSpec((width, width), lambda i, n=n: (0, first + n), pipeline_mode=once)
    blocks = rows // block
    return pl.pallas_call(
        functools.partial(tail_kernel, seqs, bits, pieces),
        grid=(blocks,),
        in_specs=[
            row(128), row(128), row(width), pair, pair, weight(0), weight(1), weight(2), row(width),
            pl.BlockSpec(x.shape, lambda i: (0, 0), pipeline_mode=once),
            pl.BlockSpec(sums.shape, lambda i: (0, 0, 0), pipeline_mode=once),
        ],
        out_specs=[
            pl.BlockSpec(memory_space=pl.ANY),
            pl.BlockSpec((2, sum_rows // 2, sum_cols), lambda i: (0, 0, 0)),
            pl.BlockSpec((8, 128), lambda i: (0, 0)),
        ],
        out_shape=[
            jax.ShapeDtypeStruct((seq_count, rows // seq_count, width), low),
            jax.ShapeDtypeStruct((2, sum_rows // 2, sum_cols), jnp.float32),
            jax.ShapeDtypeStruct((8, 128), jnp.float32),
        ],
        scratch_shapes=[
            pltpu.VMEM((rows, 3 * width), low),
            pltpu.VMEM((blocks, block, width), low),
            pltpu.VMEM((seqs, 1 << bits, sum_rows, sum_cols), low),
            pltpu.VMEM((seqs, 1 << bits, sum_rows, sum_cols), low),
            pltpu.VMEM((line, 8, 128), jnp.float32),
            pltpu.VMEM((seqs, 8, 128), jnp.float32),
            dma((3, blocks)),
            dma((2, line)),
            dma((2, seqs)),
            *reducer_scratch(seqs, bits, pieces, sum_rows, sum_cols),
        ],
        compiler_params=pltpu.CompilerParams(collective_id=2, has_side_effects=True, vmem_limit_bytes=60 << 20),
        name="tail",
    )(cosine, sine, d_query, own, got, wide, wide, wide, d_resid, x, sums)


def adam_kernel(sum_ref, qsum_ref, square_ref, back_ref, *refs):
    states, outs = refs[:18], refs[18:]
    back_out, norm_out = outs[24:]
    back_out[...] = back_ref[...].astype(jnp.float32)
    norm = jnp.sqrt(square_ref[0:1, 0:1])
    norm_out[...] = norm
    clip = jnp.minimum(1.0, MAX_NORM / (norm + 1e-06))
    rows, units = states[2].shape
    width = states[1].shape[1]
    tall, wide, out = units // 2, units // 2, (width + NORM_COLS) // 2
    at = tall + 2 * wide
    take = lambda first, count: jnp.concatenate([sum_ref[n, :, first : first + count] for n in range(2)], 1)
    fold = states[4].shape[0] // rows
    red_out = take(at, out)
    norms = red_out[:, width : width + 128].T[: states[5].shape[0]]
    grads = (
        jnp.concatenate([qsum_ref[0], qsum_ref[1]], 1),
        red_out[:, :width],
        take(tall, wide),
        take(tall + wide, wide),
        jnp.concatenate(
            [
                jnp.concatenate([sum_ref[n, :, a * (width // 2) : (a + 1) * (width // 2)] for n in range(2)], 1)
                for a in range(fold)
            ],
            0,
        ),
        norms,
    )
    for n, grad in enumerate(grads):
        rates = (0.0, NORM_RATE) if n == 5 else (WEIGHT_DECAY, LEARN_RATE)
        outs[n][...] = grad
        new, first, second = adam_update(
            states[n][...], grad, states[6 + n][...], states[12 + n][...], *rates, clip
        )
        outs[6 + n][...] = new
        outs[12 + n][...] = first
        outs[18 + n][...] = second


def adam(sums, qsums, squares, back, states):
    like = lambda array: jax.ShapeDtypeStruct(array.shape, jnp.float32)
    vmem = pl.BlockSpec(memory_space=pltpu.VMEM)
    outs = [like(array) for array in states[:6]] * 4
    outs += [like(back), jax.ShapeDtypeStruct((1, 1), jnp.float32)]
    return pl.pallas_call(
        adam_kernel,
        in_specs=[vmem] * (4 + len(states)),
        out_specs=[vmem] * len(outs),
        out_shape=outs,
        compiler_params=pltpu.CompilerParams(vmem_limit_bytes=56 << 20),
        name="adam",
    )(sums, qsums, squares, back, *states)


def halves_of(cols, bits):
    cut = cols // 256 * 128
    return ((0, cut, tuple(range(bits))), (cut, cols - cut, tuple(reversed(range(bits)))))


def turn(field, cosine, sine):
    width = field.shape[-1]
    reps = width // cosine.shape[-1]
    cosine = jnp.concatenate([cosine] * reps, -1)
    sine = jnp.concatenate([sine] * reps, -1)
    lane = lax.broadcasted_iota(jnp.int32, field.shape, 1)
    half = HEAD_DIM // 2
    other = jnp.where(
        lax.rem(lane, HEAD_DIM) < half, pltpu.roll(field, width - half, 1), pltpu.roll(field, half, 1)
    )
    return field * cosine + other * sine


def project_kernel(x_ref, wq_ref, wk_ref, wv_ref, cos_ref, sin_ref, code_ref, q_ref, kv_ref):
    x, cosine, sine = x_ref[...], cos_ref[...], sin_ref[...]
    width = x.shape[-1]
    query = turn(dotf(x, wq_ref[...]), cosine, sine).astype(jnp.bfloat16)
    q_ref[...] = query * jnp.bfloat16(1.0 / math.sqrt(HEAD_DIM))
    kv_ref[:, :width] = turn(dotf(x, wk_ref[...]), cosine, sine).astype(jnp.bfloat16)
    kv_ref[:, width : 2 * width] = dotf(x, wv_ref[...]).astype(jnp.bfloat16)
    kv_ref[:, 2 * width :] = code_ref[...]


def project(x, wide, first, cosine, sine, code, block=256):
    rows, width = x.shape
    weight = lambda n: pl.BlockSpec((width, width), lambda i, n=n: (0, first + n))
    row = lambda cols: pl.BlockSpec((block, cols), lambda i: (i, 0))
    return pl.pallas_call(
        project_kernel,
        grid=(rows // block,),
        in_specs=[row(width), weight(0), weight(1), weight(2), row(128), row(128), row(128)],
        out_specs=[row(width), row(2 * width + 128)],
        out_shape=[
            jax.ShapeDtypeStruct((rows, width), jnp.bfloat16),
            jax.ShapeDtypeStruct((rows, 2 * width + 128), jnp.bfloat16),
        ],
        compiler_params=pltpu.CompilerParams(vmem_limit_bytes=48 << 20),
        name="project",
    )(x, wide, wide, wide, cosine, sine, code)


def attend_kernel(unit, chunk, q_ref, qc_ref, k0, kc0, v0, k1, kc1, v1, p_ref, o_ref, inv_ref, ka, vt, st_ref):
    part = k0.shape[0]
    keys = 2 * part
    rows = q_ref.shape[0]
    low_k = lax.broadcasted_iota(jnp.int32, (part, 128), 1) < HEAD_DIM
    for i, (k_ref, kc_ref, v_ref) in enumerate(((k0, kc0, v0), (k1, kc1, v1))):
        k, kc, v = k_ref[...], kc_ref[...], v_ref[...]
        one = jnp.ones_like(v)
        here = slice(i * part, (i + 1) * part)
        ka[0, here] = jnp.where(low_k, k, kc)
        ka[1, here] = jnp.where(low_k, kc, k)
        vt[0, :, here] = jnp.where(low_k, v, one).T
        vt[1, :, here] = jnp.where(low_k, one, v).T
    low_q = lax.broadcasted_iota(jnp.int32, (unit, 128), 1) < HEAD_DIM
    units = [(h, b) for b in range(rows // unit) for h in range(2)]
    results, before = {}, None
    for u, now in enumerate([*units, None]):
        if now is not None:
            h, b = now
            q, qc = q_ref[b * unit : (b + 1) * unit], qc_ref[b * unit : (b + 1) * unit]
            qa = jnp.where(low_q, q, qc) if h == 0 else jnp.where(low_q, qc, q)
        top = total = None
        for c in range(keys // chunk):
            here = slice(c * chunk, (c + 1) * chunk)
            if now is not None:
                s = dotf(ka[h, here], qa, NT)
                st_ref[u % 2, here] = s
                most = jnp.max(s.reshape(chunk // 8, 8, unit), axis=0)
                top = most if top is None else jnp.maximum(top, most)
            if before is not None:
                hb, bb, row_max = before
                p = jnp.exp(st_ref[(u - 1) % 2, here] - row_max).astype(jnp.bfloat16)
                p_ref[hb, here, bb * unit : (bb + 1) * unit] = p
                d = dotf(vt[hb, :, here], p)
                total = d if total is None else total + d
        if before is not None:
            results[before[:2]] = total.T
        before = None if now is None else (h, b, jnp.max(top, axis=0, keepdims=True))
    for b in range(rows // unit):
        r0, r1 = results[(0, b)], results[(1, b)]
        inv = 1.0 / pltpu.roll(jnp.where(low_q, r1, r0), HEAD_DIM, 1)
        inv_ref[b * unit : (b + 1) * unit] = inv
        o_ref[b * unit : (b + 1) * unit] = (jnp.where(low_q, r0, r1) * inv).astype(jnp.bfloat16)


def attend_pallas(q, qc, own, sib, unit=512, chunk=512):
    rows, width = q.shape
    pairs = width // 128
    part = own.shape[0]
    row = pl.BlockSpec((rows, 128), lambda j: (0, j))
    kv = [
        pl.BlockSpec((part, 128), lambda j: (0, j)),
        pl.BlockSpec((part, 128), lambda j: (0, 2 * pairs)),
        pl.BlockSpec((part, 128), lambda j: (0, pairs + j)),
    ]
    return pl.pallas_call(
        functools.partial(attend_kernel, unit, chunk),
        grid=(pairs,),
        in_specs=[row, pl.BlockSpec((rows, 128), lambda j: (0, 0)), *kv, *kv],
        out_specs=[pl.BlockSpec((2, 2 * part, rows), lambda j: (j, 0, 0)), row, row],
        out_shape=[
            jax.ShapeDtypeStruct((2 * pairs, 2 * part, rows), jnp.bfloat16),
            jax.ShapeDtypeStruct((rows, width), jnp.bfloat16),
            jax.ShapeDtypeStruct((rows, width), jnp.float32),
        ],
        scratch_shapes=[
            pltpu.VMEM((2, 2 * part, 128), jnp.bfloat16),
            pltpu.VMEM((2, 128, 2 * part), jnp.bfloat16),
            pltpu.VMEM((2, 2 * part, unit), jnp.float32),
        ],
        compiler_params=pltpu.CompilerParams(vmem_limit_bytes=56 << 20),
        name="attend",
    )(q, qc, own, own, own, sib, sib, sib)


def mean_row(field):
    return jnp.mean(field, -1, keepdims=True)


def middle_kernel(
    x_ref, att_ref, cot_ref, wo_ref, wg_ref, wu_ref, wd_ref, norms_ref,
    out_ref, dr_ref, branch_ref, datt_ref, hid_ref, mixed_ref, dgate_ref, dup_ref, dff_ref, sums_ref,
    silu_s, slope_s,
):
    gain_one, shift_one, gain_two, shift_two = (norms_ref[n : n + 1] for n in range(4))
    resid_one = x_ref[...].astype(jnp.float32) + dotf(att_ref[...], wo_ref[...])
    hidden, normed_one, inv_one = normalize(resid_one, gain_one, shift_one)
    hidden_low = hidden.astype(jnp.bfloat16)
    hid_ref[...] = hidden_low
    hidden_units = wd_ref.shape[0]
    step = 768
    cuts = [slice(n, n + step) for n in range(0, hidden_units, step)]
    resid_two = hidden
    for cut in cuts:
        gate = dotf(hidden_low, wg_ref[:, cut])
        up = dotf(hidden_low, wu_ref[:, cut])
        sig = jax.nn.sigmoid(gate)
        silu = gate * sig
        mixed = (silu * up).astype(jnp.bfloat16)
        silu_s[:, cut] = silu
        slope_s[:, cut] = up * sig * (1.0 + gate * (1.0 - sig))
        mixed_ref[:, cut] = mixed
        resid_two = resid_two + dotf(mixed, wd_ref[cut, :])
    result, normed_two, inv_two = normalize(resid_two, gain_two, shift_two)
    out_ref[...] = result.astype(jnp.bfloat16)
    dy = cot_ref[...].astype(jnp.float32)
    d_two = normalize_back(dy, normed_two, inv_two, gain_two)
    d_ff = d_two.astype(jnp.bfloat16)
    dff_ref[...] = d_ff
    d_hidden = d_two
    for cut in cuts:
        d_mixed = dotf(d_ff, wd_ref[cut, :], NT)
        d_up = (d_mixed * silu_s[:, cut]).astype(jnp.bfloat16)
        d_gate = (d_mixed * slope_s[:, cut]).astype(jnp.bfloat16)
        dup_ref[:, cut] = d_up
        dgate_ref[:, cut] = d_gate
        d_hidden = d_hidden + dotf(d_gate, wg_ref[:, cut], NT) + dotf(d_up, wu_ref[:, cut], NT)
    d_one = normalize_back(d_hidden, normed_one, inv_one, gain_one)
    dr_ref[...] = d_one
    branch = d_one.astype(jnp.bfloat16)
    branch_ref[...] = branch
    datt_ref[...] = dotf(branch, wo_ref[...], NT).astype(jnp.bfloat16)

    @pl.when(pl.program_id(0) == 0)
    def _():
        sums_ref[...] = jnp.zeros_like(sums_ref)

    for n, term in enumerate((d_hidden * normed_one, d_hidden, dy * normed_two, dy)):
        sums_ref[n : n + 1] += jnp.sum(term, 0, keepdims=True)


def middle(x, attended, cotangent, wide, down, norms, block=256):
    rows, width = x.shape
    units = down.shape[0]
    row = lambda cols: pl.BlockSpec((block, cols), lambda i: (i, 0))
    once = pl.Buffered(1)
    weight = lambda shape, n: pl.BlockSpec(shape, lambda i: (0, n), pipeline_mode=once)
    like = lambda cols, dtype: jax.ShapeDtypeStruct((rows, cols), dtype)
    low = jnp.bfloat16
    first_out = (2 * units + 3 * width) // width
    return pl.pallas_call(
        middle_kernel,
        grid=(rows // block,),
        in_specs=[
            row(width), row(width), row(width),
            weight((width, width), first_out), weight((width, units), 0), weight((width, units), 1),
            weight((units, width), 0), weight((8, width), 0),
        ],
        out_specs=[
            row(width), row(width), row(width), row(width), row(width), row(units), row(units), row(units), row(width),
            pl.BlockSpec((8, width), lambda i: (0, 0)),
        ],
        out_shape=[
            like(width, low), like(width, jnp.float32), like(width, low), like(width, low), like(width, low),
            like(units, low), like(units, low), like(units, low), like(width, low),
            jax.ShapeDtypeStruct((8, width), jnp.float32),
        ],
        scratch_shapes=[pltpu.VMEM((block, units), jnp.float32), pltpu.VMEM((block, units), jnp.float32)],
        compiler_params=pltpu.CompilerParams(vmem_limit_bytes=60 << 20),
        name="middle",
    )(x, attended, cotangent, wide, wide, wide, down, norms)


def grad_wide_kernel(tiles, core_ref, left_ref, right_ref, *refs):
    keep_ref, send_ref = refs[-2:]
    value = dotf(left_ref[...], right_ref[...], TN).astype(jnp.bfloat16)

    @pl.when(pl.program_id(0) < tiles)
    def _():
        send_ref[...] = value

    @pl.when(pl.program_id(0) >= tiles)
    def _():
        keep_ref[...] = value


def grad_wide(core, left, right, held, offset, tile=512):
    rows, width = left.shape
    half = right.shape[1] // 2
    tiles = half // tile
    first = offset // tile
    like = jax.ShapeDtypeStruct(held[0].shape, jnp.bfloat16)
    return pl.pallas_call(
        functools.partial(grad_wide_kernel, tiles),
        grid_spec=pltpu.PrefetchScalarGridSpec(
            num_scalar_prefetch=1,
            grid=(2 * tiles,),
            in_specs=[
                pl.BlockSpec((rows, width), lambda i, c: (0, 0)),
                pl.BlockSpec(
                    (rows, tile), lambda i, c: (0, lax.rem(c[0] + 1 + lax.div(i, tiles), 2) * tiles + lax.rem(i, tiles))
                ),
                pl.BlockSpec(memory_space=pl.ANY),
                pl.BlockSpec(memory_space=pl.ANY),
            ],
            out_specs=[
                pl.BlockSpec((width, tile), lambda i, c: (0, first + jnp.maximum(i - tiles, 0))),
                pl.BlockSpec((width, tile), lambda i, c: (0, first + jnp.minimum(i, tiles - 1))),
            ],
        ),
        out_shape=[like, like],
        input_output_aliases={3: 0, 4: 1},
        compiler_params=pltpu.CompilerParams(vmem_limit_bytes=48 << 20),
        name="grad_wide",
    )(core, left, right, *held)


def halves(value, core, keep_ref, send_ref):
    half = value.shape[1] // 2
    low, high = value[:, :half].astype(jnp.bfloat16), value[:, half:].astype(jnp.bfloat16)
    keep_ref[...] = jnp.where(core == 0, low, high)
    send_ref[...] = jnp.where(core == 0, high, low)


def grad_tall_kernel(rows, core_ref, left_ref, right_ref, keep_ref, send_ref):
    value = dotf(left_ref[...], right_ref[...], TN)
    half = value.shape[1] // 2
    turns = keep_ref.shape[1] // half
    core = core_ref[0]
    for n, part in enumerate((value[:, :half], value[:, half:])):
        wide = jnp.concatenate(
            [
                jnp.concatenate([part[(b * turns + a) * rows : (b * turns + a + 1) * rows] for a in range(turns)], 1)
                for b in range(part.shape[0] // (turns * rows))
            ],
            0,
        ).astype(jnp.bfloat16)

        @pl.when(core == n)
        def _():
            keep_ref[...] = wide

        @pl.when(core != n)
        def _():
            send_ref[...] = wide


def grad_tall(core, left, right, rows, cols, tile=384):
    depth, height = left.shape
    width = right.shape[1]
    devices = height // (rows * (height // width))
    fold = height // (devices * rows)
    tile_rows = tile // fold
    out = pl.BlockSpec((tile_rows, fold * width // 2), lambda i, c: (i, 0))
    like = jax.ShapeDtypeStruct((height // fold, cols), jnp.bfloat16)
    return pl.pallas_call(
        functools.partial(grad_tall_kernel, rows),
        grid_spec=pltpu.PrefetchScalarGridSpec(
            num_scalar_prefetch=1,
            grid=(height // tile,),
            in_specs=[
                pl.BlockSpec((depth, tile), lambda i, c: (0, i)),
                pl.BlockSpec((depth, width), lambda i, c: (0, 0)),
            ],
            out_specs=[out, out],
        ),
        out_shape=[like, like],
        compiler_params=pltpu.CompilerParams(vmem_limit_bytes=48 << 20),
        name="grad_tall",
    )(core, left, right)


def grad_out_kernel(core_ref, left_ref, right_ref, sums_ref, _keep, _send, keep_ref, send_ref):
    value = dotf(left_ref[...], right_ref[...], TN)
    pad = jnp.zeros((NORM_COLS - sums_ref.shape[0], sums_ref.shape[1]), jnp.float32)
    norms = jnp.concatenate([sums_ref[...], pad], 0).T
    halves(jnp.concatenate([value, norms], 1), core_ref[0], keep_ref, send_ref)


def grad_out(core, left, right, sums, held, offset):
    width = left.shape[1]
    full = lambda array: pl.BlockSpec(array.shape, lambda i, c: (0, 0))
    half = (width + NORM_COLS) // 2
    out = pl.BlockSpec((width, half), lambda i, c: (0, offset // half))
    like = jax.ShapeDtypeStruct(held[0].shape, jnp.bfloat16)
    any_space = pl.BlockSpec(memory_space=pl.ANY)
    return pl.pallas_call(
        grad_out_kernel,
        grid_spec=pltpu.PrefetchScalarGridSpec(
            num_scalar_prefetch=1,
            grid=(1,),
            in_specs=[full(left), full(right), full(sums), any_space, any_space],
            out_specs=[out, out],
        ),
        out_shape=[like, like],
        input_output_aliases={4: 0, 5: 1},
        compiler_params=pltpu.CompilerParams(vmem_limit_bytes=48 << 20),
        name="grad_out",
    )(core, left, right, sums, *held)


NORM_COLS = 256
PLAN = {1: ((0, 1),), 2: ((0, 2),), 4: ((0, 3), (1, 1)), 6: ((0, 0), (1, 2)), 8: ((1, 3), (2, 1)), 9: ((2, 2),), 10: ((1, 0),), 11: ((2, 3),)}
AXES = ("seq", "fsdp")


def pairs_of(shape, move):
    seqs, line = shape["seq"], shape["fsdp"]
    found = []
    for z in range(seqs):
        for f in range(line):
            to_z, to_chip, to_core = move(z, f // 2, f % 2)
            found.append((z * line + f, to_z * line + 2 * to_chip + to_core))
    return found


def send(array, pairs):
    return lax.ppermute(array, AXES, pairs)


def pick(array, index, axis):
    return lax.dynamic_index_in_dim(array, index, axis, keepdims=False)


def seg_codes(segments):
    lane = jnp.arange(128) % HEAD_DIM
    low, high = lane < CODE_BITS, lane < 2 * CODE_BITS
    bit = (segments[:, None] >> jnp.where(low, lane, jnp.where(high, lane - CODE_BITS, 0))[None, :]) & 1
    query = jnp.where(low, bit, jnp.where(high, 1 - bit, 0))
    keys = jnp.where(low, 1 - bit, jnp.where(high, bit, 0)) * -FAR
    return query.astype(jnp.bfloat16), keys.astype(jnp.bfloat16)


def two_to_a_sequence(
    shape,
    tokens, segment_ids, cotangent,
    w_qkv, w_out, w_gate, w_up, w_down, norm_params,
    first_qkv, first_out, first_gate, first_up, first_down, first_norms,
    second_qkv, second_out, second_gate, second_up, second_down, second_norms,
):
    seqs = shape["seq"]
    seq_count, local_len, width = tokens.shape
    rows = seq_count * local_len
    group = seqs // seq_count
    units = w_gate.shape[1]
    z = lax.axis_index("seq")
    f = lax.axis_index("fsdp")
    core = f % 2

    def there(turn_at):
        def move(z, p, c):
            at = (c * seq_count + (z + turn_at) % seq_count) * group + z // seq_count
            return (at // 2, p, at % 2)

        return pairs_of(shape, move)

    out_pairs = [there(t) for t in range(seq_count)]

    def to_sequences(array):
        return jnp.concatenate(
            [send(pick(array, (z + t) % seq_count, 0), out_pairs[t]) for t in range(seq_count)], 0
        )

    x = to_sequences(tokens)
    segments = to_sequences(segment_ids)
    dy = to_sequences(cotangent)
    q_code, k_code = seg_codes(segments)
    at = z * 2 + core
    within = jnp.concatenate(
        [((at // group - t) % seq_count) * local_len + jnp.arange(local_len) for t in range(seq_count)]
    )
    positions = ((at % group) * rows + within).astype(jnp.float32)
    half_dim = HEAD_DIM // 2
    inverse = jnp.exp(jnp.arange(half_dim, dtype=jnp.float32) * (-2.0 * math.log(ROPE_BASE) / HEAD_DIM))
    angles = positions[:, None] * inverse[None, :]
    cosine, sine = jnp.cos(angles), jnp.sin(angles)
    cosine = jnp.concatenate([cosine] * 4, 1)
    sine = jnp.concatenate([-sine, sine, -sine, sine], 1)

    norm_rows = jnp.pad(norm_params.T, ((0, 0), (0, NORM_COLS - norm_params.shape[0])))
    wide, down = gather_all(shape, w_gate, w_up, w_qkv, w_out, norm_rows, w_down)
    wide = wide.reshape(width, wide.shape[-1])
    down = down.reshape(units, width)
    norms = jnp.pad(wide[:, -NORM_COLS : 4 - NORM_COLS].T.astype(jnp.float32), ((0, 4), (0, 0)))
    first_block = 2 * units // width

    sibling = pairs_of(shape, lambda z, p, c: (z, p, 1 - c))
    query, own = project(x, wide, first_block, cosine, sine, k_code)
    sib = send(own, sibling)
    probs, attended, inverse_sums = attend_pallas(query, q_code, own, sib)
    (
        result, d_resid_one, d_branch, d_attended, hidden_low, mixed, d_gate, d_up, d_ff, sums,
    ) = middle(x, attended, dy, wide, down, norms)

    core_id = core.astype(jnp.int32).reshape(1)
    own_rows = w_gate.shape[0]
    half_tall, half_wide, half_out = units * width // 2 // width, units // 2, (width + NORM_COLS) // 2
    cols = half_tall + 2 * half_wide + half_out
    held = grad_tall(core_id, mixed, d_ff, own_rows, cols)
    held = grad_wide(core_id, hidden_low, d_gate, held, half_tall)
    held = grad_wide(core_id, hidden_low, d_up, held, half_tall + half_wide)
    held = grad_out(core_id, attended, d_branch, sums, held, half_tall + 2 * half_wide)
    d_query, d_own, d_got, reduced_sums, output = attend_back_pallas(
        shape, query, own, sib, probs, attended, inverse_sums, d_attended, *held, result, seq_count, PLAN
    )
    back, qkv_sums, squares = tail(
        shape, cosine, sine, d_query, d_own, d_got, wide, first_block, d_resid_one, x, reduced_sums, seq_count
    )
    states = (
        w_qkv, w_out, w_gate, w_up, w_down, norm_params,
        first_qkv, first_out, first_gate, first_up, first_down, first_norms,
        second_qkv, second_out, second_gate, second_up, second_down, second_norms,
    )
    *updated, input_grad, grad_norm = adam(reduced_sums, qkv_sums, squares, back, states)
    return (output, input_grad, *updated, grad_norm.reshape(()))


def device_program(shape, *arrays):
    tokens, w_gate, w_down = arrays[0], arrays[5], arrays[7]
    seqs, line = shape["seq"], shape["fsdp"]
    seq_count, local_len, width = tokens.shape
    fits = (
        seqs == 2 * seq_count
        and line & (line - 1) == 0
        and line >= 4
        and (seq_count * local_len) % 512 == 0
        and w_gate.shape[0] % 8 == 0
        and w_down.shape[0] % 8 == 0
    )
    return two_to_a_sequence(shape, *arrays) if fits else per_device(*arrays)


def solution(mesh):
    return jax.shard_map(
        functools.partial(device_program, dict(mesh.shape)),
        mesh=mesh,
        in_specs=(
            P("fsdp", "seq", None),
            P("fsdp", "seq"),
            P("fsdp", "seq", None),
            P(("seq", "fsdp"), None),
            P(("seq", "fsdp"), None),
            P(("seq", "fsdp"), None),
            P(("seq", "fsdp"), None),
            P(("seq", "fsdp"), None),
            P(None, ("seq", "fsdp")),
            P(("seq", "fsdp"), None),
            P(("seq", "fsdp"), None),
            P(("seq", "fsdp"), None),
            P(("seq", "fsdp"), None),
            P(("seq", "fsdp"), None),
            P(None, ("seq", "fsdp")),
            P(("seq", "fsdp"), None),
            P(("seq", "fsdp"), None),
            P(("seq", "fsdp"), None),
            P(("seq", "fsdp"), None),
            P(("seq", "fsdp"), None),
            P(None, ("seq", "fsdp")),
        ),
        out_specs=(
            P("fsdp", "seq", None),
            P("fsdp", "seq", None),
            P(("seq", "fsdp"), None),
            P(("seq", "fsdp"), None),
            P(("seq", "fsdp"), None),
            P(("seq", "fsdp"), None),
            P(("seq", "fsdp"), None),
            P(None, ("seq", "fsdp")),
            P(("seq", "fsdp"), None),
            P(("seq", "fsdp"), None),
            P(("seq", "fsdp"), None),
            P(("seq", "fsdp"), None),
            P(("seq", "fsdp"), None),
            P(None, ("seq", "fsdp")),
            P(("seq", "fsdp"), None),
            P(("seq", "fsdp"), None),
            P(("seq", "fsdp"), None),
            P(("seq", "fsdp"), None),
            P(("seq", "fsdp"), None),
            P(None, ("seq", "fsdp")),
            P(("seq", "fsdp"), None),
            P(("seq", "fsdp"), None),
            P(("seq", "fsdp"), None),
            P(("seq", "fsdp"), None),
            P(("seq", "fsdp"), None),
            P(None, ("seq", "fsdp")),
            P(),
        ),
        check_vma=False,
    )
```

```python
import functools
import math

import jax
import jax.numpy as jnp
from jax import lax
from jax.experimental import pallas as pl
from jax.experimental.pallas import tpu as pltpu
from jax.sharding import PartitionSpec as P

HEADS = 12
HEAD_DIM = 64
STEP = 10


EPS_NORM = 1e-06
ROPE_BASE = 1000.0
MASKED_SCORE = -1e30
MAX_NORM = 1.0
LEARN_RATE = 0.1
NORM_RATE = 0.6
BETA_ONE = 0.9
BETA_TWO = 0.999
ADAM_EPS = 1e-08
WEIGHT_DECAY = 0.01


def rotate(field, positions, sign_rot):
    shape_in = field.shape
    heads_view = field.reshape(shape_in[:-1] + (HEADS, HEAD_DIM))
    half_dim = HEAD_DIM // 2
    inverse = jnp.exp(
        jnp.arange(half_dim, dtype=jnp.float32) * (-2.0 * math.log(ROPE_BASE) / HEAD_DIM)
    )
    angles = positions[:, None] * inverse[None, :]
    cosine = jnp.cos(angles)[:, None, :]
    sine = jnp.sin(angles)[:, None, :] * sign_rot
    first_half = heads_view[..., :half_dim]
    second_half = heads_view[..., half_dim:]
    turned = jnp.concatenate(
        [first_half * cosine - second_half * sine, second_half * cosine + first_half * sine], -1
    )
    return turned.reshape(shape_in)


def normalize(resid, gain, shift):
    mean_row = jnp.mean(resid, -1, keepdims=True)
    centered = resid - mean_row
    inv_std = lax.rsqrt(jnp.mean(centered * centered, -1, keepdims=True) + EPS_NORM)
    normed = centered * inv_std
    return (normed * gain + shift, normed, inv_std)


def normalize_back(grad_in, normed, inv_std, gain):
    scaled = grad_in * gain
    return inv_std * (
        scaled
        - jnp.mean(scaled, -1, keepdims=True)
        - normed * jnp.mean(scaled * normed, -1, keepdims=True)
    )


def attend(query, keys, values, same_doc, score_scale):
    seq_count, local_len, model_width = query.shape

    def one_head(head_index, carried):
        out_all, log_sums = carried
        col_start = head_index * HEAD_DIM
        query_head = lax.dynamic_slice_in_dim(query, col_start, HEAD_DIM, 2)
        key_head = lax.dynamic_slice_in_dim(keys, col_start, HEAD_DIM, 2)
        value_head = lax.dynamic_slice_in_dim(values, col_start, HEAD_DIM, 2)
        raw_scores = jnp.einsum(
            "sqd,skd->sqk", query_head, key_head, preferred_element_type=jnp.float32
        )
        scores = jnp.where(same_doc, raw_scores * score_scale, MASKED_SCORE)
        row_max = jnp.max(scores, -1, keepdims=True)
        exp_scores = jnp.exp(scores - row_max)
        row_sums = jnp.sum(exp_scores, -1, keepdims=True)
        attn_prob = (exp_scores / row_sums).astype(jnp.bfloat16)
        head_out = jnp.einsum(
            "sqk,skd->sqd", attn_prob, value_head, preferred_element_type=jnp.float32
        )
        out_all = lax.dynamic_update_slice_in_dim(out_all, head_out, col_start, 2)
        log_sums = lax.dynamic_update_index_in_dim(
            log_sums, (row_max + jnp.log(row_sums))[..., 0], head_index, 0
        )
        return (out_all, log_sums)

    start_state = (
        jnp.zeros((seq_count, local_len, model_width), jnp.float32),
        jnp.zeros((HEADS, seq_count, local_len), jnp.float32),
    )
    return lax.fori_loop(0, HEADS, one_head, start_state)


def attend_back(query, keys, values, same_doc, log_sums, grad_attended, score_scale):
    seq_count, local_len, model_width = query.shape
    key_len = keys.shape[1]

    def one_head(head_index, carried):
        dq_all, dk_all, dv_all = carried
        col_start = head_index * HEAD_DIM
        query_head = lax.dynamic_slice_in_dim(query, col_start, HEAD_DIM, 2)
        key_head = lax.dynamic_slice_in_dim(keys, col_start, HEAD_DIM, 2)
        value_head = lax.dynamic_slice_in_dim(values, col_start, HEAD_DIM, 2)
        grad_head = lax.dynamic_slice_in_dim(grad_attended, col_start, HEAD_DIM, 2)
        head_sums = lax.dynamic_index_in_dim(log_sums, head_index, 0, keepdims=False)
        raw_scores = jnp.einsum(
            "sqd,skd->sqk", query_head, key_head, preferred_element_type=jnp.float32
        )
        scores = jnp.where(same_doc, raw_scores * score_scale, MASKED_SCORE)
        attn_prob = jnp.exp(scores - head_sums[..., None])
        grad_prob = jnp.einsum(
            "sqd,skd->sqk", grad_head, value_head, preferred_element_type=jnp.float32
        )
        dv_head = jnp.einsum(
            "sqk,sqd->skd",
            attn_prob.astype(jnp.bfloat16),
            grad_head,
            preferred_element_type=jnp.float32,
        )
        row_dots = jnp.sum(attn_prob * grad_prob, -1, keepdims=True)
        grad_scores = (attn_prob * (grad_prob - row_dots)).astype(jnp.bfloat16)
        dq_head = (
            jnp.einsum("sqk,skd->sqd", grad_scores, key_head, preferred_element_type=jnp.float32)
            * score_scale
        )
        dk_head = (
            jnp.einsum("sqk,sqd->skd", grad_scores, query_head, preferred_element_type=jnp.float32)
            * score_scale
        )
        dq_all = lax.dynamic_update_slice_in_dim(dq_all, dq_head, col_start, 2)
        dk_all = lax.dynamic_update_slice_in_dim(dk_all, dk_head, col_start, 2)
        dv_all = lax.dynamic_update_slice_in_dim(dv_all, dv_head, col_start, 2)
        return (dq_all, dk_all, dv_all)

    start_state = (
        jnp.zeros((seq_count, local_len, model_width), jnp.float32),
        jnp.zeros((seq_count, key_len, model_width), jnp.float32),
        jnp.zeros((seq_count, key_len, model_width), jnp.float32),
    )
    return lax.fori_loop(0, HEADS, one_head, start_state)


def adam_update(weight, gradient, moment_one, moment_two, decay_rate, step_rate, clip_factor):
    clipped = gradient * clip_factor
    first_new = BETA_ONE * moment_one + (1.0 - BETA_ONE) * clipped
    second_new = BETA_TWO * moment_two + (1.0 - BETA_TWO) * clipped * clipped
    first_fix = 1.0 - BETA_ONE**STEP
    second_fix = 1.0 - BETA_TWO**STEP
    direction = (
        first_new / first_fix / (jnp.sqrt(second_new / second_fix) + ADAM_EPS) + decay_rate * weight
    )
    return (weight - step_rate * direction, first_new, second_new)


def per_device(
    tokens,
    segment_ids,
    cotangent,
    w_qkv,
    w_out,
    w_gate,
    w_up,
    w_down,
    norm_params,
    first_qkv,
    first_out,
    first_gate,
    first_up,
    first_down,
    first_norms,
    second_qkv,
    second_out,
    second_gate,
    second_up,
    second_down,
    second_norms,
):
    seq_count, local_len, model_width = tokens.shape
    row_count = seq_count * local_len
    score_scale = 1.0 / math.sqrt(HEAD_DIM)
    lowered_qkv = w_qkv.astype(jnp.bfloat16)
    lowered_out = w_out.astype(jnp.bfloat16)
    lowered_gate = w_gate.astype(jnp.bfloat16)
    lowered_up = w_up.astype(jnp.bfloat16)
    lowered_down = w_down.astype(jnp.bfloat16)
    lowered_norms = norm_params.astype(jnp.bfloat16)
    full_qkv, full_out, full_gate, full_up, full_down, full_norms = (
        lax.all_gather(lowered_qkv, ("seq", "fsdp"), axis=0, tiled=True),
        lax.all_gather(lowered_out, ("seq", "fsdp"), axis=0, tiled=True),
        lax.all_gather(lowered_gate, ("seq", "fsdp"), axis=0, tiled=True),
        lax.all_gather(lowered_up, ("seq", "fsdp"), axis=0, tiled=True),
        lax.all_gather(lowered_down, ("seq", "fsdp"), axis=0, tiled=True),
        lax.all_gather(lowered_norms, ("seq", "fsdp"), axis=1, tiled=True),
    )
    gains = full_norms.astype(jnp.float32)
    gain_one, shift_one, gain_two, shift_two = (gains[0], gains[1], gains[2], gains[3])
    positions = (lax.axis_index("seq") * local_len + jnp.arange(local_len)).astype(jnp.float32)
    flat_rows = tokens.reshape(row_count, model_width)
    projected = jnp.dot(flat_rows, full_qkv, preferred_element_type=jnp.float32).reshape(
        seq_count, local_len, 3 * model_width
    )
    query = rotate(projected[..., :model_width], positions, 1.0).astype(jnp.bfloat16)
    keys_local = rotate(projected[..., model_width : 2 * model_width], positions, 1.0).astype(
        jnp.bfloat16
    )
    values_local = projected[..., 2 * model_width :].astype(jnp.bfloat16)
    keys_all, values_all, key_segments = (
        lax.all_gather(keys_local, "seq", axis=1, tiled=True),
        lax.all_gather(values_local, "seq", axis=1, tiled=True),
        lax.all_gather(segment_ids, "seq", axis=1, tiled=True),
    )
    same_doc = segment_ids[:, :, None] == key_segments[:, None, :]
    attended, log_sums = attend(query, keys_all, values_all, same_doc, score_scale)
    attended_low = attended.astype(jnp.bfloat16).reshape(row_count, model_width)
    resid_one = flat_rows.astype(jnp.float32) + jnp.dot(
        attended_low, full_out, preferred_element_type=jnp.float32
    )
    hidden, normed_one, inv_std_one = normalize(resid_one, gain_one, shift_one)
    hidden_low = hidden.astype(jnp.bfloat16)
    gate_proj = jnp.dot(hidden_low, full_gate, preferred_element_type=jnp.float32)
    up_proj = jnp.dot(hidden_low, full_up, preferred_element_type=jnp.float32)
    sigmoid_gate = jax.nn.sigmoid(gate_proj)
    silu_gate = gate_proj * sigmoid_gate
    mixed_low = (silu_gate * up_proj).astype(jnp.bfloat16)
    resid_two = hidden + jnp.dot(mixed_low, full_down, preferred_element_type=jnp.float32)
    result, normed_two, inv_std_two = normalize(resid_two, gain_two, shift_two)
    output = result.astype(jnp.bfloat16).reshape(seq_count, local_len, model_width)
    back_qkv, back_out, back_gate, back_up, back_down = (
        lax.all_gather(lowered_qkv, ("seq", "fsdp"), axis=0, tiled=True),
        lax.all_gather(lowered_out, ("seq", "fsdp"), axis=0, tiled=True),
        lax.all_gather(lowered_gate, ("seq", "fsdp"), axis=0, tiled=True),
        lax.all_gather(lowered_up, ("seq", "fsdp"), axis=0, tiled=True),
        lax.all_gather(lowered_down, ("seq", "fsdp"), axis=0, tiled=True),
    )
    grad_result = cotangent.reshape(row_count, model_width).astype(jnp.float32)
    d_gain_two = jnp.sum(grad_result * normed_two, 0)
    d_shift_two = jnp.sum(grad_result, 0)
    d_resid_two = normalize_back(grad_result, normed_two, inv_std_two, gain_two)
    d_ff_low = d_resid_two.astype(jnp.bfloat16)
    g_down = jnp.einsum("rf,rd->fd", mixed_low, d_ff_low, preferred_element_type=jnp.float32)
    d_mixed = jnp.einsum("rd,fd->rf", d_ff_low, back_down, preferred_element_type=jnp.float32)
    d_up_low = (d_mixed * silu_gate).astype(jnp.bfloat16)
    d_gate_low = (
        d_mixed * up_proj * sigmoid_gate * (1.0 + gate_proj * (1.0 - sigmoid_gate))
    ).astype(jnp.bfloat16)
    g_gate = jnp.einsum("rd,rf->df", hidden_low, d_gate_low, preferred_element_type=jnp.float32)
    g_up = jnp.einsum("rd,rf->df", hidden_low, d_up_low, preferred_element_type=jnp.float32)
    d_hidden = (
        d_resid_two
        + jnp.einsum("rf,df->rd", d_gate_low, back_gate, preferred_element_type=jnp.float32)
        + jnp.einsum("rf,df->rd", d_up_low, back_up, preferred_element_type=jnp.float32)
    )
    d_gain_one = jnp.sum(d_hidden * normed_one, 0)
    d_shift_one = jnp.sum(d_hidden, 0)
    d_resid_one = normalize_back(d_hidden, normed_one, inv_std_one, gain_one)
    d_branch_low = d_resid_one.astype(jnp.bfloat16)
    g_out = jnp.einsum("rd,re->de", attended_low, d_branch_low, preferred_element_type=jnp.float32)
    d_attended_low = (
        jnp.einsum("re,de->rd", d_branch_low, back_out, preferred_element_type=jnp.float32)
        .astype(jnp.bfloat16)
        .reshape(seq_count, local_len, model_width)
    )
    keys_back, values_back = (
        lax.all_gather(keys_local, "seq", axis=1, tiled=True),
        lax.all_gather(values_local, "seq", axis=1, tiled=True),
    )
    d_query, d_keys, d_values = attend_back(
        query, keys_back, values_back, same_doc, log_sums, d_attended_low, score_scale
    )
    d_keys_local, d_values_local = (
        lax.psum_scatter(
            d_keys.astype(jnp.bfloat16), "seq", scatter_dimension=1, tiled=True
        ).astype(jnp.float32),
        lax.psum_scatter(
            d_values.astype(jnp.bfloat16), "seq", scatter_dimension=1, tiled=True
        ).astype(jnp.float32),
    )
    d_projected_low = (
        jnp.concatenate(
            [
                rotate(d_query, positions, -1.0),
                rotate(d_keys_local, positions, -1.0),
                d_values_local,
            ],
            -1,
        )
        .astype(jnp.bfloat16)
        .reshape(row_count, 3 * model_width)
    )
    g_qkv = jnp.einsum("rd,re->de", flat_rows, d_projected_low, preferred_element_type=jnp.float32)
    input_grad = (
        d_resid_one
        + jnp.einsum("re,de->rd", d_projected_low, back_qkv, preferred_element_type=jnp.float32)
    ).reshape(seq_count, local_len, model_width)
    g_norms = jnp.stack([d_gain_one, d_shift_one, d_gain_two, d_shift_two])
    red_qkv, red_out, red_gate, red_up, red_down, red_norms = (
        lax.psum_scatter(g_qkv, ("seq", "fsdp"), scatter_dimension=0, tiled=True),
        lax.psum_scatter(g_out, ("seq", "fsdp"), scatter_dimension=0, tiled=True),
        lax.psum_scatter(g_gate, ("seq", "fsdp"), scatter_dimension=0, tiled=True),
        lax.psum_scatter(g_up, ("seq", "fsdp"), scatter_dimension=0, tiled=True),
        lax.psum_scatter(g_down, ("seq", "fsdp"), scatter_dimension=0, tiled=True),
        lax.psum_scatter(g_norms, ("seq", "fsdp"), scatter_dimension=1, tiled=True),
    )
    local_squares = (
        jnp.sum(red_qkv * red_qkv)
        + jnp.sum(red_out * red_out)
        + jnp.sum(red_gate * red_gate)
        + jnp.sum(red_up * red_up)
        + jnp.sum(red_down * red_down)
        + jnp.sum(red_norms * red_norms)
    )
    squares_sum = lax.psum(local_squares, ("seq", "fsdp"))
    grad_norm = jnp.sqrt(squares_sum)
    clip_factor = jnp.minimum(1.0, MAX_NORM / (grad_norm + 1e-06))
    new_qkv, mom_qkv, sec_qkv = adam_update(
        w_qkv, red_qkv, first_qkv, second_qkv, WEIGHT_DECAY, LEARN_RATE, clip_factor
    )
    new_out, mom_out, sec_out = adam_update(
        w_out, red_out, first_out, second_out, WEIGHT_DECAY, LEARN_RATE, clip_factor
    )
    new_gate, mom_gate, sec_gate = adam_update(
        w_gate, red_gate, first_gate, second_gate, WEIGHT_DECAY, LEARN_RATE, clip_factor
    )
    new_up, mom_up, sec_up = adam_update(
        w_up, red_up, first_up, second_up, WEIGHT_DECAY, LEARN_RATE, clip_factor
    )
    new_down, mom_down, sec_down = adam_update(
        w_down, red_down, first_down, second_down, WEIGHT_DECAY, LEARN_RATE, clip_factor
    )
    new_norms, mom_norms, sec_norms = adam_update(
        norm_params, red_norms, first_norms, second_norms, 0.0, NORM_RATE, clip_factor
    )
    return (
        output,
        input_grad,
        red_qkv,
        red_out,
        red_gate,
        red_up,
        red_down,
        red_norms,
        new_qkv,
        new_out,
        new_gate,
        new_up,
        new_down,
        new_norms,
        mom_qkv,
        mom_out,
        mom_gate,
        mom_up,
        mom_down,
        mom_norms,
        sec_qkv,
        sec_out,
        sec_gate,
        sec_up,
        sec_down,
        sec_norms,
        grad_norm,
    )


NT = (((1,), (1,)), ((), ()))
NN = (((1,), (0,)), ((), ()))
TN = (((0,), (0,)), ((), ()))
FAR = 1e30
CODE_BITS = 7
MESH_ID = pl.DeviceIdType.MESH


def dotf(left, right, dims=NN):
    return lax.dot_general(left, right, dims, preferred_element_type=jnp.float32)


def place():
    f = lax.axis_index("fsdp")
    return lax.axis_index("seq"), lax.div(f, 2), lax.rem(f, 2)


def chip_at(chip, mask):
    at, b = chip, 0
    while mask >> b:
        if (mask >> b) & 1:
            at = at + (1 - 2 * lax.rem(lax.div(chip, 1 << b), 2)) * (1 << b)
        b += 1
    return at


def greet(peers):
    barrier = pltpu.get_barrier_semaphore()
    for peer in peers:
        pl.semaphore_signal(barrier, inc=1, device_id=peer, device_id_type=MESH_ID)
    pl.semaphore_wait(barrier, len(peers))


def column_peers(seqs):
    z, chip, core = place()
    return [{"seq": lax.rem(z + k, seqs), "fsdp": 2 * chip + c} for k in range(1, seqs) for c in range(2)]


def plane_peers(line):
    f = lax.axis_index("fsdp")
    return [{"fsdp": lax.rem(f + k, line)} for k in range(1, line)]


def sum_peers(bits):
    z, chip, core = place()
    return [{"fsdp": 2 * chip + 1 - core}] + [{"fsdp": 2 * chip_at(chip, 1 << b) + core} for b in range(bits)]


def departs(seqs, seq_count, source, target, sems, subs=1):
    z, chip, core = place()
    group = seqs // seq_count

    def copies(s, sub):
        at = (core * seq_count + s) * group + lax.div(z, seq_count)
        to_z, to_core = lax.div(at, 2), lax.rem(at, 2)
        n = lax.rem(z, seq_count) * subs + sub
        remote = pltpu.make_async_remote_copy(
            source(s, sub), target(n), sems.at[0, s * subs + sub], sems.at[1, n],
            device_id={"seq": to_z, "fsdp": 2 * chip + to_core}, device_id_type=MESH_ID,
        )
        return (to_z == z) & (to_core == core), remote, pltpu.make_async_copy(source(s, sub), target(n), sems.at[2, n])

    def begin():
        for sub in range(subs):
            for s in range(seq_count):
                mine, remote, local = copies(s, sub)

                @pl.when(mine)
                def _():
                    local.start()

                @pl.when(jnp.logical_not(mine))
                def _():
                    remote.start()

    def came(n):
        at = z * 2 + core
        from_z = lax.rem(at, group) * seq_count + lax.div(n, subs)
        mine = (from_z == z) & (lax.div(lax.div(at, group), seq_count) == core)

        @pl.when(mine)
        def _():
            pltpu.make_async_copy(source(0, 0), target(n), sems.at[2, n]).wait()

        @pl.when(jnp.logical_not(mine))
        def _():
            pltpu.make_async_remote_copy(
                source(0, 0), target(n), sems.at[0, 0], sems.at[1, n],
                device_id={"seq": z, "fsdp": 2 * chip + 1 - core}, device_id_type=MESH_ID,
            ).wait_recv()

    def sent():
        for sub in range(subs):
            for s in range(seq_count):
                mine, remote, _ = copies(s, sub)

                @pl.when(jnp.logical_not(mine))
                def _():
                    remote.wait_send()

    return begin, came, sent


def returns(seqs, seq_count, source, target, sems, rows):
    z, chip, core = place()
    group = seqs // seq_count
    at = z * 2 + core
    number = lax.div(at, group)
    slot = lax.rem(number, seq_count)
    to_core = lax.div(number, seq_count)
    local_len = target.shape[1]
    subs = local_len // rows

    def copies(n):
        t, sub = divmod(n, subs)
        to_z = lax.rem(at, group) * seq_count + t
        mine = (to_z == z) & (to_core == core)
        here = target.at[slot, pl.ds(sub * rows, rows)]
        remote = pltpu.make_async_remote_copy(
            source(n), here, sems.at[0, n], sems.at[1, slot * subs + sub],
            device_id={"seq": to_z, "fsdp": 2 * chip + to_core}, device_id_type=MESH_ID,
        )
        return mine, remote, pltpu.make_async_copy(source(n), here, sems.at[2, n])

    def begin(n):
        mine, remote, local = copies(n)

        @pl.when(mine)
        def _():
            local.start()

        @pl.when(jnp.logical_not(mine))
        def _():
            remote.start()

    def end():
        for n in range(seq_count * subs):
            mine, remote, local = copies(n)

            @pl.when(mine)
            def _():
                local.wait()

            @pl.when(jnp.logical_not(mine))
            def _():
                remote.wait_send()

        for s in range(seq_count):
            came = (core * seq_count + s) * group + lax.div(z, seq_count)
            other = jnp.logical_not((lax.div(came, 2) == z) & (lax.rem(came, 2) == core))
            for sub in range(subs):

                @pl.when(other)
                def _():
                    here = target.at[s, pl.ds(sub * rows, rows)]
                    pltpu.make_async_remote_copy(
                        source(0), here, sems.at[0, 0], sems.at[1, s * subs + sub],
                        device_id={"seq": z, "fsdp": 2 * chip + 1 - core}, device_id_type=MESH_ID,
                    ).wait_recv()

    return begin, end


def line_peers(seqs):
    z = lax.axis_index("seq")
    return [{"seq": lax.rem(z + way, seqs)} for way in (1, seqs - 1)]


def gatherer_scratch(seqs, bits, count):
    dma = pltpu.SemaphoreType.DMA
    chips = 1 << bits
    return [
        dma((count, 2, seqs)),
        dma((count, seqs)),
        dma((count, seqs, chips)),
        dma((count, seqs, chips)),
        dma((count, seqs, chips)),
        dma((count, seqs, chips)),
    ]


def gatherer(seqs, bits, pieces, wholes, line_send, line_recv, hop_send, hop_recv, swap_send, swap_recv):
    z, chip, core = place()

    def block(p, zz, mask):
        which, offset, width, _ = pieces[p]
        half = wholes[which].shape[-1] // 2
        return wholes[which].at[zz, chip_at(chip, mask), :, pl.ds(pl.multiple_of(core * half + offset, 128), width)]

    def line_copy(p, zz, way):
        return pltpu.make_async_remote_copy(
            block(p, zz, 0), block(p, zz, 0), line_send.at[p, way, zz], line_recv.at[p, zz],
            device_id={"seq": z + (1 if way else -1)}, device_id_type=MESH_ID,
        )

    def hop_copy(p, zz, mask, b):
        to = mask | (1 << b)
        return pltpu.make_async_remote_copy(
            block(p, zz, mask), block(p, zz, mask), hop_send.at[p, zz, to], hop_recv.at[p, zz, to],
            device_id={"fsdp": 2 * chip_at(chip, 1 << b) + core}, device_id_type=MESH_ID,
        )

    def swap_copy(p, zz, mask):
        return pltpu.make_async_remote_copy(
            block(p, zz, mask), block(p, zz, mask), swap_send.at[p, zz, mask], swap_recv.at[p, zz, mask],
            device_id={"fsdp": 2 * chip + 1 - core}, device_id_type=MESH_ID,
        )

    def level(p, mask):
        return max([i for i, b in enumerate(pieces[p][3]) if mask & (1 << b)], default=-1)

    def later(p, mask):
        return pieces[p][3][level(p, mask) + 1 :]

    masks = range(1 << bits)

    def pass_on(p, zz, mask, mine=False):
        for b in later(p, mask):
            hop_copy(p, zz, mask, b).start()
        if not mine:
            swap_copy(p, zz, mask).start()

    def own_line(which):
        for p in which:

            @pl.when(z > 0)
            def _():
                line_copy(p, z, 0).start()

            @pl.when(z < seqs - 1)
            def _():
                line_copy(p, z, 1).start()

    def own_hops(which):
        for p in which:
            pass_on(p, z, 0, True)

    def both(distance, task):
        for way in (1, 0) if distance else (1,):
            zz = z - distance if way else z + distance
            pl.when((zz >= 0) & (zz < seqs))(functools.partial(task, zz, way))

    def line(which, distance):
        def task(zz, way):
            for p in which:
                line_copy(p, zz, way).wait_recv()

                @pl.when((z < seqs - 1) if way else (z > 0))
                def _():
                    line_copy(p, zz, way).start()

                pass_on(p, zz, 0)

        both(distance, task)

    def hops(which, distance, levels=range(bits)):
        def task(zz, way):
            for at in levels:
                for p in which:
                    for mask in masks:
                        if level(p, mask) == at:
                            b = pieces[p][3][at]
                            hop_copy(p, zz, mask & ~(1 << b), b).wait_recv()
                            pass_on(p, zz, mask)

        both(distance, task)

    def finish_line(which):
        def task(zz, _):
            for p in which:

                @pl.when((zz <= z) & (z < seqs - 1))
                def _():
                    line_copy(p, zz, 1).wait_send()

                @pl.when((zz >= z) & (z > 0))
                def _():
                    line_copy(p, zz, 0).wait_send()

            return 0

        lax.fori_loop(0, seqs, task, 0)

    def finish_hops(which, distance):
        def task(zz, _):
            for p in which:
                for mask in masks:
                    for b in later(p, mask):
                        hop_copy(p, zz, mask, b).wait_send()
                    if mask or distance:
                        swap_copy(p, zz, mask).wait()

        both(distance, task)

    return own_line, own_hops, line, hops, finish_line, finish_hops


def first_gather_kernel(seqs, bits, pieces, early, *refs):
    tokens, segments, gate, up, qkv, out, norm, down = refs[:8]
    x_out, segments_out, qkv_all, rest_all, down_all = refs[8:13]
    qkv_two, rest_two, down_two, qkv_chip, rest_chip, down_chip, core_sem, own_sem, token_sem, segment_sem = refs[13:23]
    z, chip, core = place()
    wholes = (qkv_all, rest_all, down_all)
    chips = (qkv_chip, rest_chip, down_chip)
    own_line, own_hops, line, hops, finish_line, finish_hops = gatherer(seqs, bits, pieces, wholes, *refs[23:])
    seq_count = tokens.shape[0]
    token_begin, token_came, token_sent = departs(
        seqs, seq_count, lambda s, _: tokens.at[s], lambda n: x_out.at[n], token_sem
    )
    segment_begin, segment_came, segment_sent = departs(
        seqs, seq_count, lambda s, _: segments.at[s], lambda n: segments_out.at[n], segment_sem
    )
    greet(sum_peers(bits) + column_peers(seqs))
    segment_begin()
    at = 0
    for part in (gate, up, out, norm):
        rest_two[core, :, at : at + part.shape[1]] = part[...]
        at += part.shape[1]
    qkv_two[core] = qkv[...]
    down_two[core] = down[...]
    twos = (qkv_two, rest_two, down_two)
    first = [
        pltpu.make_async_remote_copy(
            two.at[core], two.at[core], core_sem.at[0, i], core_sem.at[1, i],
            device_id={"fsdp": 2 * chip + 1 - core}, device_id_type=MESH_ID,
        )
        for i, two in enumerate(twos)
    ]
    for copy in first:
        copy.start()
    own = [
        pltpu.make_async_copy(chip_ref, whole.at[z, chip], own_sem.at[i])
        for i, (chip_ref, whole) in enumerate(zip(chips, wholes))
    ]
    for i, copy in enumerate(first):
        copy.wait()
        chips[i][...] = twos[i][...].reshape(chips[i].shape).astype(jnp.bfloat16)
        own[i].start()
    rest = [p for p in range(len(pieces)) if p not in early]
    own[0].wait()
    own_line(early)
    own_hops(early)
    own[1].wait()
    own[2].wait()
    own_hops(rest)
    for distance in range(1, seqs):
        line(early, distance)
        if distance == seqs - 2:
            token_begin()
        hops(early, distance - 1)
    hops(rest, 0)
    hops(early, seqs - 1)
    finish_line(early)
    for distance in range(seqs):
        finish_hops(early, distance)
    finish_hops(rest, 0)
    for n in range(seq_count):
        token_came(n)
        segment_came(n)
    token_sent()
    segment_sent()


def gather_pieces(bits, qkv, rest, down, rows):
    upward, downward = tuple(range(bits)), tuple(reversed(range(bits)))
    cut = qkv // 512 * 128
    load = down.shape[1] // 2 * down.shape[0] // rows
    other = max(128, ((rest // 2 + load) // 2 - load) // 128 * 128)
    return (
        (0, 0, cut, upward),
        (0, cut, qkv // 2 - cut, downward),
        (1, 0, other, upward),
        (2, 0, down.shape[1] // 2, upward),
        (1, other, rest // 2 - other, downward),
    )


def first_gather(shape, tokens, segments, gate, up, qkv, out, norm, down):
    seqs, chips = shape["seq"], shape["fsdp"] // 2
    bits = chips.bit_length() - 1
    rows, rows_down = gate.shape[0], down.shape[0]
    rest = sum(part.shape[1] for part in (gate, up, out, norm))
    pieces = gather_pieces(bits, qkv.shape[1], rest, down, rows)
    seq_count = tokens.shape[0]
    dma = pltpu.SemaphoreType.DMA
    low = jnp.bfloat16
    any_space = pl.BlockSpec(memory_space=pl.ANY)
    vmem = pl.BlockSpec(memory_space=pltpu.VMEM)
    forms = ((rows, qkv.shape[1]), (rows, rest), (rows_down, down.shape[1]))
    *outs, = pl.pallas_call(
        functools.partial(first_gather_kernel, seqs, bits, pieces, (0, 1)),
        out_shape=[
            jax.ShapeDtypeStruct(tokens.shape, low),
            jax.ShapeDtypeStruct(segments.shape, jnp.int32),
            *(jax.ShapeDtypeStruct((seqs, chips, 2 * n, cols), low) for n, cols in forms),
        ],
        in_specs=[any_space, any_space, *[vmem] * 6],
        out_specs=[any_space] * 5,
        scratch_shapes=[
            *(pltpu.VMEM((2, *form), jnp.float32) for form in forms),
            *(pltpu.VMEM((2 * n, cols), low) for n, cols in forms),
            dma((2, 3)),
            dma((3,)),
            dma((3, seq_count)),
            dma((3, seq_count)),
            *gatherer_scratch(seqs, bits, len(pieces)),
        ],
        compiler_params=pltpu.CompilerParams(collective_id=0, has_side_effects=True, vmem_limit_bytes=48 << 20),
        name="first_gather",
    )(tokens, segments, gate, up, qkv, out, norm, down)
    return outs, pieces[2:]


def hop_masks(order, stage):
    gone = sum(1 << b for b in order[:stage])
    return [m for m in range(1 << len(order)) if (m >> order[stage]) & 1 and not m & gone]


def hop_slot(order, stage, mask):
    return [m ^ (1 << order[stage]) for m in hop_masks(order, stage)].index(mask)


def reducer_scratch(seqs, bits, pieces, rows, width):
    dma = pltpu.SemaphoreType.DMA
    chips = 1 << bits
    low = jnp.bfloat16
    hops = [
        pltpu.VMEM((seqs, len(hop_masks(order, stage)), rows, cols), low)
        for _, cols, order in pieces
        for stage in range(bits)
    ]
    most = max(1, chips // 2)
    return [
        pltpu.VMEM((seqs, chips, rows, width), low),
        pltpu.VMEM((seqs, rows, width), low),
        pltpu.VMEM((2, rows // 2, width), jnp.float32),
        pltpu.VMEM((rows // 2, width), jnp.float32),
        dma((2, seqs, chips)),
        dma((2, len(pieces), bits, seqs, most)),
        dma((2, seqs)),
        dma((2,)),
        *hops,
    ]


def reducer(seqs, bits, pieces, away, keep, got, line, halves_ref, swapped, core_sem, hop_sem, line_sem, swap_sem, *hops):
    z, chip, core = place()
    rows = keep.shape[2]
    half = rows // 2
    sibling = {"fsdp": 2 * chip + 1 - core}
    masks = range(1 << bits)
    hop = lambda p, stage: hops[p * bits + stage]

    def remote(source, target, sems, index, device):
        return pltpu.make_async_remote_copy(
            source, target, sems.at[(0, *index)], sems.at[(1, *index)], device_id=device, device_id_type=MESH_ID
        )

    def core_copy(zz, mask):
        at = chip_at(chip, mask)
        return remote(away.at[zz, at], got.at[zz, at], core_sem, (zz, at), sibling)

    def hop_copy(p, stage, zz, mask):
        start, cols, order = pieces[p]
        slot = hop_slot(order, stage, mask ^ (1 << order[stage]))
        return remote(
            got.at[zz, chip_at(chip, mask), :, pl.ds(start, cols)],
            hop(p, stage).at[zz, slot],
            hop_sem,
            (p, stage, zz, slot),
            {"fsdp": 2 * chip_at(chip, 1 << order[stage]) + core},
        )

    def line_copy(zz, source):
        return remote(got.at[zz, chip], line.at[source], line_sem, (source,), {"seq": zz})

    def total(p, zz, mask, stages):
        start, cols, order = pieces[p]
        at = chip_at(chip, mask)
        where = (zz, at, slice(None), pl.ds(start, cols))
        value = keep[where].astype(jnp.float32) + got[where].astype(jnp.float32)
        for stage in range(stages):
            value = value + hop(p, stage)[zz, hop_slot(order, stage, mask)].astype(jnp.float32)
        return value

    def start():
        for k in range(1, seqs + 1):
            zz = lax.rem(z + k, seqs)
            for mask in reversed(masks):
                core_copy(zz, mask).start()

    def come(p, stage, zz):
        for mask in hop_masks(pieces[p][2], stage):
            hop_copy(p, stage, zz, mask).wait_recv()

    def stage_of(stage, zz):
        if stage == 0:
            for mask in masks:
                core_copy(zz, mask).wait_recv()
        for p, (first, cols, order) in enumerate(pieces):
            if stage:
                come(p, stage - 1, zz)
            for mask in hop_masks(order, stage):
                got[zz, chip_at(chip, mask), :, pl.ds(first, cols)] = total(p, zz, mask, stage).astype(jnp.bfloat16)
                hop_copy(p, stage, zz, mask).start()

    def line_of(zz):
        for p, (first, cols, _) in enumerate(pieces):
            come(p, bits - 1, zz)
            got[zz, chip, :, pl.ds(first, cols)] = total(p, zz, 0, bits).astype(jnp.bfloat16)
        line_copy(zz, z).start()

    def finish():
        for p in range(len(pieces)):
            come(p, bits - 1, z)
        for k in range(1, seqs):
            source = lax.rem(z + k, seqs)
            line_copy(z, source).wait_recv()
        for p, (first, cols, _) in enumerate(pieces):
            value = total(p, z, 0, bits)
            for k in range(1, seqs):
                value = value + line[lax.rem(z + k, seqs), :, pl.ds(first, cols)].astype(jnp.float32)
            halves_ref[0, :, pl.ds(first, cols)] = value[:half]
            halves_ref[1, :, pl.ds(first, cols)] = value[half:]
        swap = remote(halves_ref.at[1 - core], swapped, swap_sem, (), sibling)
        swap.start()
        for zz in range(seqs):
            for mask in masks:
                core_copy(zz, mask).wait_send()
            for p, (_, _, order) in enumerate(pieces):
                for stage in range(bits):
                    for mask in hop_masks(order, stage):
                        hop_copy(p, stage, zz, mask).wait_send()
        for k in range(1, seqs):
            line_copy(lax.rem(z + k, seqs), z).wait_send()
        swap.wait()

    def own(k):
        return lax.rem(z + k, seqs)

    return start, stage_of, line_of, finish, own


def attend_back_kernel(
    seqs, bits, pieces, plan,
    q_ref, k0, v0, k1, v1, p_ref, o_ref, inv_ref, do_ref, keep_hbm, away_hbm, result_hbm,
    dq_ref, own_ref, sib_ref, sum_ref, output_hbm,
    kt, va, dk, dv, sib, sib_sem, keep, keep_sem, back_sem, *shared,
):
    part = k0.shape[0]
    unit = q_ref.shape[0]
    j, i = pl.program_id(0), pl.program_id(1)
    count = pl.num_programs(1)
    step = j * count + i
    z, chip, core = place()
    lane_k = lax.broadcasted_iota(jnp.int32, (part, 128), 1)
    start, stage_of, line_of, finish, own = reducer(seqs, bits, pieces, away_hbm, keep, *shared)
    keep_copy = pltpu.make_async_copy(keep_hbm, keep, keep_sem)
    seq_count, local_len = output_hbm.shape[:2]
    back_begin, back_end = returns(
        seqs, seq_count, lambda n: result_hbm.at[pl.ds(n * local_len, local_len)], output_hbm, back_sem, local_len
    )

    def sib_copy(pair):
        return pltpu.make_async_remote_copy(
            sib.at[lax.rem(pair, 2)],
            sib_ref.at[:, :, pl.ds(pl.multiple_of(pair * 128, 128), 128)],
            sib_sem.at[0, pair],
            sib_sem.at[1, pair],
            device_id={"fsdp": 2 * chip + 1 - core},
            device_id_type=MESH_ID,
        )

    @pl.when(step == 0)
    def _():
        keep_copy.start()
        greet(sum_peers(bits) + column_peers(seqs))
        start()
        for n in range(seq_count):
            back_begin(n)
        keep_copy.wait()

    for at, tasks in plan.items():

        @pl.when(step == at)
        def _():
            for kind, k in tasks:
                if kind < bits:
                    stage_of(kind, own(k))
                else:
                    line_of(own(k))

    @pl.when(i == 0)
    def _():
        for n, (k_ref, v_ref) in enumerate(((k0, v0), (k1, v1))):
            k, v = k_ref[...], v_ref[...]
            zero, one = jnp.zeros_like(v), jnp.ones_like(v)
            here = slice(n * part, (n + 1) * part)
            kt[0, :, here] = jnp.where(lane_k < HEAD_DIM, k, zero).T
            kt[1, :, here] = jnp.where(lane_k < HEAD_DIM, zero, k).T
            va[0, here] = jnp.where(lane_k < HEAD_DIM, v, jnp.where(lane_k < HEAD_DIM + 3, one, zero))
            va[1, here] = jnp.where(lane_k >= HEAD_DIM, v, jnp.where(lane_k < 3, one, zero))
        dk[...] = jnp.zeros_like(dk)
        dv[...] = jnp.zeros_like(dv)

    lane = lax.broadcasted_iota(jnp.int32, (unit, 128), 1)
    q = q_ref[...]
    dof = do_ref[...].astype(jnp.float32) * inv_ref[...]
    prod = dof * o_ref[...].astype(jnp.float32)
    dob = dof.astype(jnp.bfloat16)
    zero = jnp.zeros_like(dob)
    turned = None
    for h in range(2):
        mine = lane < HEAD_DIM if h == 0 else lane >= HEAD_DIM
        base = HEAD_DIM if h == 0 else 0
        d = -jnp.sum(jnp.where(mine, prod, 0.0), axis=1, keepdims=True)
        d1 = d.astype(jnp.bfloat16).astype(jnp.float32)
        d2 = (d - d1).astype(jnp.bfloat16).astype(jnp.float32)
        d3 = d - d1 - d2
        extra = jnp.where(
            lane == base, d1, jnp.where(lane == base + 1, d2, jnp.where(lane == base + 2, d3, 0.0))
        ).astype(jnp.bfloat16)
        p = p_ref[h]
        ds = (p.astype(jnp.float32) * dotf(va[h], jnp.where(mine, dob, extra), NT)).astype(jnp.bfloat16)
        dv[...] += dotf(p, jnp.where(mine, dob, zero))
        dk[...] += dotf(ds, jnp.where(mine, q, zero))
        new = dotf(kt[h], ds)
        turned = new if turned is None else turned + new
    dq_ref[...] = turned.T * (1.0 / math.sqrt(HEAD_DIM))

    @pl.when(i == count - 1)
    def _():
        @pl.when(j >= 2)
        def _():
            sib_copy(j - 2).wait_send()

        for n, total in enumerate((dk, dv)):
            own_ref[n] = total[:part]
            sib[lax.rem(j, 2), n] = total[part:].astype(jnp.bfloat16)
        sib_copy(j).start()

    @pl.when(step == pl.num_programs(0) * count - 1)
    def _():
        finish()
        back_end()
        halves_ref, swapped = shared[2], shared[3]
        sum_ref[core] = halves_ref[core]
        sum_ref[1 - core] = swapped[...]
        pairs = pl.num_programs(0)
        for back in (1, 0):
            sib_copy(pairs - 1 - back).wait_send()
        lax.fori_loop(0, pairs, lambda pair, _: (sib_copy(pair).wait_recv(), 0)[1], 0)


def attend_back_pallas(shape, q, own, sib, p, o, inv, do, keep, away, result, seq_count, plan, unit=512):
    seqs, bits = shape["seq"], (shape["fsdp"] // 2).bit_length() - 1
    rows, width = q.shape
    pairs = width // 128
    part = own.shape[0]
    low = jnp.bfloat16
    keep, away = (array.reshape(seqs, 1 << bits, -1, array.shape[1]) for array in (keep, away))
    sum_rows, sum_cols = keep.shape[2:]
    pieces = halves_of(sum_cols, bits)
    row = pl.BlockSpec((unit, 128), lambda j, i: (i, j))
    kv = [
        pl.BlockSpec((part, 128), lambda j, i: (0, 2 * j)),
        pl.BlockSpec((part, 128), lambda j, i: (0, 2 * j + 1)),
    ]
    any_space = pl.BlockSpec(memory_space=pl.ANY)
    dma = pltpu.SemaphoreType.DMA
    return pl.pallas_call(
        functools.partial(attend_back_kernel, seqs, bits, pieces, plan),
        grid=(pairs, rows // unit),
        in_specs=[
            row, *kv, *kv, pl.BlockSpec((2, 2 * part, unit), lambda j, i: (j, 0, i)), row, row, row,
            any_space, any_space, any_space,
        ],
        out_specs=[
            row,
            pl.BlockSpec((2, part, 128), lambda j, i: (0, 0, j)),
            any_space,
            pl.BlockSpec((2, sum_rows // 2, sum_cols), lambda j, i: (0, 0, 0)),
            any_space,
        ],
        out_shape=[
            jax.ShapeDtypeStruct((rows, width), jnp.float32),
            jax.ShapeDtypeStruct((2, part, width), jnp.float32),
            jax.ShapeDtypeStruct((2, part, width), low),
            jax.ShapeDtypeStruct((2, sum_rows // 2, sum_cols), jnp.float32),
            jax.ShapeDtypeStruct((seq_count, rows // seq_count, width), low),
        ],
        scratch_shapes=[
            pltpu.VMEM((2, 128, 2 * part), low),
            pltpu.VMEM((2, 2 * part, 128), low),
            pltpu.VMEM((2 * part, 128), jnp.float32),
            pltpu.VMEM((2 * part, 128), jnp.float32),
            pltpu.VMEM((2, 2, part, 128), low),
            dma((2, pairs)),
            pltpu.VMEM(keep.shape, low),
            dma,
            dma((3, seq_count)),
            *reducer_scratch(seqs, bits, pieces, sum_rows, sum_cols),
        ],
        compiler_params=pltpu.CompilerParams(
            collective_id=1, has_side_effects=True, vmem_limit_bytes=62 << 20
        ),
        name="attend_back",
    )(q, own, own, sib, sib, p, o, inv, do, keep, away, result)


def tail_kernel(
    seqs, bits, pieces,
    cos_ref, sin_ref, dq_ref, own_ref, got_ref, wq_ref, wk_ref, wv_ref, dr_ref, x_ref, sum_ref,
    back_ref, qsum_ref, square_ref,
    dproj, dx, keep, away, plane, line_sum, back_sem, plane_sem, total_sem, *shared,
):
    z, chip, core = place()
    f = 2 * chip + core
    line = 2 << bits
    block, width = dr_ref.shape
    i = pl.program_id(0)
    blocks = dx.shape[0]
    low = jnp.bfloat16
    start, stage_of, line_of, finish, own = reducer(seqs, bits, pieces, away, keep, *shared)
    back_begin, back_end = returns(seqs, back_ref.shape[0], lambda n: dx.at[n], back_ref, back_sem, block)

    @pl.when(i == 0)
    def _():
        greet(plane_peers(line) + column_peers(seqs))

    cosine, sine = cos_ref[...], -sin_ref[...]
    grads = (
        turn(dq_ref[...], cosine, sine).astype(low),
        turn(own_ref[0] + got_ref[0].astype(jnp.float32), cosine, sine).astype(low),
        (own_ref[1] + got_ref[1].astype(jnp.float32)).astype(low),
    )
    value = dr_ref[...]
    rows = pl.ds(pl.multiple_of(i * block, block), block)
    for n, (grad, w_ref) in enumerate(zip(grads, (wq_ref, wk_ref, wv_ref))):
        dproj[rows, n * width : (n + 1) * width] = grad
        value = value + dotf(grad, w_ref[...], NT)
    dx[i] = value.astype(low)
    for n in range(blocks):

        @pl.when(i == n)
        def _():
            back_begin(n)

    @pl.when(i == blocks - 1)
    def _():
        half = keep.shape[-1]
        tile = 384
        for target, side in ((away, 1 - core), (keep, core)):
            for n in range(half // tile):
                cols = pl.ds(pl.multiple_of(side * half + n * tile, 128), tile)
                grad = dotf(x_ref[...], dproj[:, cols], TN).astype(low)
                target[:, :, :, n * tile : (n + 1) * tile] = grad.reshape(target.shape[:3] + (tile,))
            if target is away:
                start()
        order = [*range(1, seqs), 0]
        for k in order:
            stage_of(0, own(k))
        for stage in range(1, bits):
            for k in order:
                stage_of(stage, own(k))
        for k in order[:-1]:
            line_of(own(k))
        finish()
        halves_ref, swapped = shared[2], shared[3]
        qsum_ref[core] = halves_ref[core]
        qsum_ref[1 - core] = swapped[...]
        squares = jnp.sum(jnp.square(sum_ref[...])) + jnp.sum(jnp.square(qsum_ref[...]))
        plane[f] = jnp.zeros(plane.shape[1:], jnp.float32) + squares

        def plane_copy(to, source):
            return pltpu.make_async_remote_copy(
                plane.at[source], plane.at[source], plane_sem.at[0, to], plane_sem.at[1, source],
                device_id={"fsdp": to}, device_id_type=MESH_ID,
            )

        def total_copy(to, source):
            return pltpu.make_async_remote_copy(
                line_sum.at[source], line_sum.at[source], total_sem.at[0, to], total_sem.at[1, source],
                device_id={"seq": to}, device_id_type=MESH_ID,
            )

        for k in range(1, line):
            plane_copy(lax.rem(f + k, line), f).start()
        for k in range(1, line):
            plane_copy(lax.rem(f + k, line), lax.rem(f + k, line)).wait_recv()
        line_sum[z] = sum(plane[n] for n in range(line))
        for k in range(1, seqs):
            total_copy(lax.rem(z + k, seqs), z).start()
        for k in range(1, seqs):
            total_copy(lax.rem(z + k, seqs), lax.rem(z + k, seqs)).wait_recv()
        square_ref[...] = sum(line_sum[n] for n in range(seqs))
        for k in range(1, line):
            plane_copy(lax.rem(f + k, line), f).wait_send()
        for k in range(1, seqs):
            total_copy(lax.rem(z + k, seqs), z).wait_send()
        back_end()


def tail(shape, cosine, sine, d_query, own, got, wide, first, d_resid, x, sums, seq_count, block=256):
    seqs, line = shape["seq"], shape["fsdp"]
    bits = (line // 2).bit_length() - 1
    rows, width = x.shape
    low = jnp.bfloat16
    sum_rows, sum_cols = width // (seqs * line // 2), 3 * width // 2
    pieces = halves_of(sum_cols, bits)
    dma = pltpu.SemaphoreType.DMA
    row = lambda cols: pl.BlockSpec((block, cols), lambda i: (i, 0))
    pair = pl.BlockSpec((2, block, width), lambda i: (0, i, 0))
    once = pl.Buffered(1)
    weight = lambda n: pl.BlockSpec((width, width), lambda i, n=n: (0, first + n), pipeline_mode=once)
    blocks = rows // block
    return pl.pallas_call(
        functools.partial(tail_kernel, seqs, bits, pieces),
        grid=(blocks,),
        in_specs=[
            row(128), row(128), row(width), pair, pair, weight(0), weight(1), weight(2), row(width),
            pl.BlockSpec(x.shape, lambda i: (0, 0), pipeline_mode=once),
            pl.BlockSpec(sums.shape, lambda i: (0, 0, 0), pipeline_mode=once),
        ],
        out_specs=[
            pl.BlockSpec(memory_space=pl.ANY),
            pl.BlockSpec((2, sum_rows // 2, sum_cols), lambda i: (0, 0, 0)),
            pl.BlockSpec((8, 128), lambda i: (0, 0)),
        ],
        out_shape=[
            jax.ShapeDtypeStruct((seq_count, rows // seq_count, width), low),
            jax.ShapeDtypeStruct((2, sum_rows // 2, sum_cols), jnp.float32),
            jax.ShapeDtypeStruct((8, 128), jnp.float32),
        ],
        scratch_shapes=[
            pltpu.VMEM((rows, 3 * width), low),
            pltpu.VMEM((blocks, block, width), low),
            pltpu.VMEM((seqs, 1 << bits, sum_rows, sum_cols), low),
            pltpu.VMEM((seqs, 1 << bits, sum_rows, sum_cols), low),
            pltpu.VMEM((line, 8, 128), jnp.float32),
            pltpu.VMEM((seqs, 8, 128), jnp.float32),
            dma((3, blocks)),
            dma((2, line)),
            dma((2, seqs)),
            *reducer_scratch(seqs, bits, pieces, sum_rows, sum_cols),
        ],
        compiler_params=pltpu.CompilerParams(collective_id=2, has_side_effects=True, vmem_limit_bytes=60 << 20),
        name="tail",
    )(cosine, sine, d_query, own, got, wide, wide, wide, d_resid, x, sums)


def adam_kernel(sum_ref, qsum_ref, square_ref, back_ref, *refs):
    states, outs = refs[:18], refs[18:]
    back_out, norm_out = outs[24:]
    back_out[...] = back_ref[...].astype(jnp.float32)
    norm = jnp.sqrt(square_ref[0:1, 0:1])
    norm_out[...] = norm
    clip = jnp.minimum(1.0, MAX_NORM / (norm + 1e-06))
    rows, units = states[2].shape
    width = states[1].shape[1]
    tall, wide, out = units // 2, units // 2, (width + NORM_COLS) // 2
    at = tall + 2 * wide
    take = lambda first, count: jnp.concatenate([sum_ref[n, :, first : first + count] for n in range(2)], 1)
    fold = states[4].shape[0] // rows
    red_out = take(at, out)
    norms = red_out[:, width : width + 128].T[: states[5].shape[0]]
    grads = (
        jnp.concatenate([qsum_ref[0], qsum_ref[1]], 1),
        red_out[:, :width],
        take(tall, wide),
        take(tall + wide, wide),
        jnp.concatenate(
            [
                jnp.concatenate([sum_ref[n, :, a * (width // 2) : (a + 1) * (width // 2)] for n in range(2)], 1)
                for a in range(fold)
            ],
            0,
        ),
        norms,
    )
    for n, grad in enumerate(grads):
        rates = (0.0, NORM_RATE) if n == 5 else (WEIGHT_DECAY, LEARN_RATE)
        outs[n][...] = grad
        new, first, second = adam_update(
            states[n][...], grad, states[6 + n][...], states[12 + n][...], *rates, clip
        )
        outs[6 + n][...] = new
        outs[12 + n][...] = first
        outs[18 + n][...] = second


def adam(sums, qsums, squares, back, states):
    like = lambda array: jax.ShapeDtypeStruct(array.shape, jnp.float32)
    vmem = pl.BlockSpec(memory_space=pltpu.VMEM)
    outs = [like(array) for array in states[:6]] * 4
    outs += [like(back), jax.ShapeDtypeStruct((1, 1), jnp.float32)]
    return pl.pallas_call(
        adam_kernel,
        in_specs=[vmem] * (4 + len(states)),
        out_specs=[vmem] * len(outs),
        out_shape=outs,
        compiler_params=pltpu.CompilerParams(vmem_limit_bytes=56 << 20),
        name="adam",
    )(sums, qsums, squares, back, *states)


def halves_of(cols, bits):
    cut = cols // 256 * 128
    return ((0, cut, tuple(range(bits))), (cut, cols - cut, tuple(reversed(range(bits)))))


def turn(field, cosine, sine):
    width = field.shape[-1]
    reps = width // cosine.shape[-1]
    cosine = jnp.concatenate([cosine] * reps, -1)
    sine = jnp.concatenate([sine] * reps, -1)
    lane = lax.broadcasted_iota(jnp.int32, field.shape, 1)
    half = HEAD_DIM // 2
    other = jnp.where(
        lax.rem(lane, HEAD_DIM) < half, pltpu.roll(field, width - half, 1), pltpu.roll(field, half, 1)
    )
    return field * cosine + other * sine


def project_kernel(x_ref, wq_ref, wk_ref, wv_ref, cos_ref, sin_ref, code_ref, q_ref, kv_ref):
    x, cosine, sine = x_ref[...], cos_ref[...], sin_ref[...]
    width = x.shape[-1]
    query = turn(dotf(x, wq_ref[...]), cosine, sine).astype(jnp.bfloat16)
    q_ref[...] = query * jnp.bfloat16(1.0 / math.sqrt(HEAD_DIM))
    keys = turn(dotf(x, wk_ref[...]), cosine, sine).astype(jnp.bfloat16)
    values = dotf(x, wv_ref[...]).astype(jnp.bfloat16)
    for at in range(0, width, 128):
        kv_ref[:, 2 * at : 2 * at + 128] = keys[:, at : at + 128]
        kv_ref[:, 2 * at + 128 : 2 * at + 256] = values[:, at : at + 128]
    kv_ref[:, 2 * width :] = code_ref[...]


def project(x, wide, first, cosine, sine, code, block=256):
    rows, width = x.shape
    weight = lambda n: pl.BlockSpec((width, width), lambda i, n=n: (0, first + n))
    row = lambda cols: pl.BlockSpec((block, cols), lambda i: (i, 0))
    return pl.pallas_call(
        project_kernel,
        grid=(rows // block,),
        in_specs=[row(width), weight(0), weight(1), weight(2), row(128), row(128), row(128)],
        out_specs=[row(width), row(2 * width + 128)],
        out_shape=[
            jax.ShapeDtypeStruct((rows, width), jnp.bfloat16),
            jax.ShapeDtypeStruct((rows, 2 * width + 128), jnp.bfloat16),
        ],
        compiler_params=pltpu.CompilerParams(vmem_limit_bytes=48 << 20),
        name="project",
    )(x, wide, wide, wide, cosine, sine, code)


def attend_kernel(seqs, bits, pieces, plan, unit, chunk, q_ref, qc_ref, own_ref, code_ref, own_hbm, *refs):
    p_ref, o_ref, inv_ref, sib_hbm, rest_all, down_all = refs[2:8]
    ka, vt, st_ref, sib, kv_sem, keep_sem = refs[8:14]
    own_line, own_hops, line, hops, finish_line, finish_hops = gatherer(
        seqs, bits, pieces, (None, rest_all, down_all), *refs[14:]
    )
    z, chip, core = place()
    part, rows = own_ref.shape[0], q_ref.shape[0]
    keys = 2 * part
    j, pairs = pl.program_id(0), pl.num_programs(0)
    step = j * pl.num_programs(1) + pl.program_id(1)
    which = range(len(pieces))

    def kv_copy(first, count, n):
        cols = pl.ds(pl.multiple_of(first, 128), count)
        return pltpu.make_async_remote_copy(
            own_hbm.at[:, cols], sib.at[:, cols], kv_sem.at[0, n], kv_sem.at[1, n],
            device_id={"fsdp": 2 * chip + 1 - core}, device_id_type=MESH_ID,
        )

    code_copy = kv_copy(256 * pairs, 128, pairs)
    pair_copy = lambda n: kv_copy(256 * n, 256, n)

    def carry(distance, level=None):
        if level is None:
            line(which, distance)
        else:
            hops(which, distance, (level,))

    @pl.when(step == 0)
    def _():
        greet(sum_peers(bits) + line_peers(seqs))
        code_copy.start()
        pair_copy(0).start()
        own_line(which)
        lax.fori_loop(1, pairs, lambda n, _: (pair_copy(n).start(), 0)[1], 0)
        code_copy.wait_recv()

    for at in [at for at in plan if at is not None]:

        @pl.when(step == at)
        def _():
            for task in plan[at]:
                carry(*task)

    low_k = lax.broadcasted_iota(jnp.int32, (part, 128), 1) < HEAD_DIM

    @pl.when(pl.program_id(1) == 0)
    def _():
        pair_copy(j).wait_recv()
        sides = (
            (own_ref[:, :128], code_ref[...], own_ref[:, 128:]),
            (
                sib[:, pl.ds(pl.multiple_of(256 * j, 128), 128)],
                sib[:, sib.shape[1] - 128 :],
                sib[:, pl.ds(pl.multiple_of(256 * j + 128, 128), 128)],
            ),
        )
        for i, (k, kc, v) in enumerate(sides):
            one = jnp.ones_like(v)
            here = slice(i * part, (i + 1) * part)
            ka[0, here] = jnp.where(low_k, k, kc)
            ka[1, here] = jnp.where(low_k, kc, k)
            vt[0, :, here] = jnp.where(low_k, v, one).T
            vt[1, :, here] = jnp.where(low_k, one, v).T

    low_q = lax.broadcasted_iota(jnp.int32, (unit, 128), 1) < HEAD_DIM
    units = [(h, b) for b in range(rows // unit) for h in range(2)]
    results, before = {}, None
    for u, now in enumerate([*units, None]):
        if now is not None:
            h, b = now
            q, qc = q_ref[b * unit : (b + 1) * unit], qc_ref[b * unit : (b + 1) * unit]
            qa = jnp.where(low_q, q, qc) if h == 0 else jnp.where(low_q, qc, q)
        top = total = None
        for c in range(keys // chunk):
            here = slice(c * chunk, (c + 1) * chunk)
            if now is not None:
                s = dotf(ka[h, here], qa, NT)
                st_ref[u % 2, here] = s
                most = jnp.max(s.reshape(chunk // 8, 8, unit), axis=0)
                top = most if top is None else jnp.maximum(top, most)
            if before is not None:
                hb, bb, row_max = before
                p = jnp.exp(st_ref[(u - 1) % 2, here] - row_max).astype(jnp.bfloat16)
                p_ref[hb, here, bb * unit : (bb + 1) * unit] = p
                d = dotf(vt[hb, :, here], p)
                total = d if total is None else total + d
        if before is not None:
            results[before[:2]] = total.T
        before = None if now is None else (h, b, jnp.max(top, axis=0, keepdims=True))
    for b in range(rows // unit):
        r0, r1 = results[(0, b)], results[(1, b)]
        inv = 1.0 / pltpu.roll(jnp.where(low_q, r1, r0), HEAD_DIM, 1)
        inv_ref[b * unit : (b + 1) * unit] = inv
        o_ref[b * unit : (b + 1) * unit] = (jnp.where(low_q, r0, r1) * inv).astype(jnp.bfloat16)

    @pl.when(step == pairs * pl.num_programs(1) - 1)
    def _():
        keep = pltpu.make_async_copy(sib, sib_hbm, keep_sem)
        keep.start()
        for task in plan[None]:
            carry(*task)
        finish_line(which)
        for distance in range(1, seqs):
            finish_hops(which, distance)
        code_copy.wait_send()
        lax.fori_loop(0, pairs, lambda n, _: (pair_copy(n).wait_send(), 0)[1], 0)
        keep.wait()


def attend_pallas(shape, pieces, plan, q, qc, own, rest_all, down_all, unit=512, chunk=512, block=512):
    seqs, bits = shape["seq"], (shape["fsdp"] // 2).bit_length() - 1
    rows, width = q.shape
    pairs = width // 128
    part = own.shape[0]
    low = jnp.bfloat16
    row = pl.BlockSpec((block, 128), lambda j, i: (i, j))
    any_space = pl.BlockSpec(memory_space=pl.ANY)
    dma = pltpu.SemaphoreType.DMA
    like = lambda array: jax.ShapeDtypeStruct(array.shape, array.dtype)

    return pl.pallas_call(
        functools.partial(attend_kernel, seqs, bits, pieces, plan, unit, chunk),
        grid=(pairs, rows // block),
        in_specs=[
            row,
            pl.BlockSpec((block, 128), lambda j, i: (i, 0)),
            pl.BlockSpec((part, 256), lambda j, i: (0, j)),
            pl.BlockSpec((part, 128), lambda j, i: (0, 2 * pairs)),
            any_space,
            any_space,
            any_space,
        ],
        out_specs=[pl.BlockSpec((2, 2 * part, block), lambda j, i: (j, 0, i)), row, row, any_space, any_space, any_space],
        out_shape=[
            jax.ShapeDtypeStruct((2 * pairs, 2 * part, rows), low),
            jax.ShapeDtypeStruct((rows, width), low),
            jax.ShapeDtypeStruct((rows, width), jnp.float32),
            like(own),
            like(rest_all),
            like(down_all),
        ],
        input_output_aliases={5: 4, 6: 5},
        scratch_shapes=[
            pltpu.VMEM((2, 2 * part, 128), low),
            pltpu.VMEM((2, 128, 2 * part), low),
            pltpu.VMEM((2, 2 * part, unit), jnp.float32),
            pltpu.VMEM(own.shape, low),
            dma((2, pairs + 1)),
            dma,
            *gatherer_scratch(seqs, bits, len(pieces)),
        ],
        compiler_params=pltpu.CompilerParams(collective_id=3, has_side_effects=True, vmem_limit_bytes=58 << 20),
        name="attend",
    )(q, qc, own, own, own, rest_all, down_all)


def mean_row(field):
    return jnp.mean(field, -1, keepdims=True)


def middle_kernel(
    seqs, seq_count, x_ref, att_ref, cot_hbm, wo_ref, wg_ref, wu_ref, wd_ref, norms_ref,
    out_ref, dr_ref, branch_ref, datt_ref, hid_ref, mixed_ref, dgate_ref, dup_ref, dff_ref, sums_ref,
    silu_s, slope_s, dy_s, dy_sem,
):
    blocks, block = dy_s.shape[:2]
    subs = blocks // seq_count
    begin, came, sent = departs(
        seqs, seq_count, lambda s, sub: cot_hbm.at[s, pl.ds(sub * block, block)], lambda n: dy_s.at[n], dy_sem, subs
    )

    @pl.when(pl.program_id(0) == 0)
    def _():
        greet(column_peers(seqs))
        begin()

    gain_one, shift_one, gain_two, shift_two = (norms_ref[n : n + 1] for n in range(4))
    resid_one = x_ref[...].astype(jnp.float32) + dotf(att_ref[...], wo_ref[...])
    hidden, normed_one, inv_one = normalize(resid_one, gain_one, shift_one)
    hidden_low = hidden.astype(jnp.bfloat16)
    hid_ref[...] = hidden_low
    hidden_units = wd_ref.shape[0]
    step = 768
    cuts = [slice(n, n + step) for n in range(0, hidden_units, step)]
    resid_two = hidden
    for cut in cuts:
        gate = dotf(hidden_low, wg_ref[:, cut])
        up = dotf(hidden_low, wu_ref[:, cut])
        sig = jax.nn.sigmoid(gate)
        silu = gate * sig
        mixed = (silu * up).astype(jnp.bfloat16)
        silu_s[:, cut] = silu
        slope_s[:, cut] = up * sig * (1.0 + gate * (1.0 - sig))
        mixed_ref[:, cut] = mixed
        resid_two = resid_two + dotf(mixed, wd_ref[cut, :])
    result, normed_two, inv_two = normalize(resid_two, gain_two, shift_two)
    out_ref[...] = result.astype(jnp.bfloat16)
    now = row_order(seq_count, subs, pl.program_id(0))
    came(now)
    dy = dy_s[now].astype(jnp.float32)
    d_two = normalize_back(dy, normed_two, inv_two, gain_two)
    d_ff = d_two.astype(jnp.bfloat16)
    dff_ref[...] = d_ff
    d_hidden = d_two
    for cut in cuts:
        d_mixed = dotf(d_ff, wd_ref[cut, :], NT)
        d_up = (d_mixed * silu_s[:, cut]).astype(jnp.bfloat16)
        d_gate = (d_mixed * slope_s[:, cut]).astype(jnp.bfloat16)
        dup_ref[:, cut] = d_up
        dgate_ref[:, cut] = d_gate
        d_hidden = d_hidden + dotf(d_gate, wg_ref[:, cut], NT) + dotf(d_up, wu_ref[:, cut], NT)
    d_one = normalize_back(d_hidden, normed_one, inv_one, gain_one)
    dr_ref[...] = d_one
    branch = d_one.astype(jnp.bfloat16)
    branch_ref[...] = branch
    datt_ref[...] = dotf(branch, wo_ref[...], NT).astype(jnp.bfloat16)

    @pl.when(pl.program_id(0) == 0)
    def _():
        sums_ref[...] = jnp.zeros_like(sums_ref)

    for n, term in enumerate((d_hidden * normed_one, d_hidden, dy * normed_two, dy)):
        sums_ref[n : n + 1] += jnp.sum(term, 0, keepdims=True)

    @pl.when(pl.program_id(0) == blocks - 1)
    def _():
        sent()


def row_order(seq_count, subs, step):
    return lax.rem(step, seq_count) * subs + lax.div(step, seq_count)


def middle(shape, x, attended, cotangent, rest, down, norms, block=256):
    rows, width = x.shape
    units = down.shape[0]
    seq_count, local_len = cotangent.shape[:2]
    subs = local_len // block
    row = lambda cols: pl.BlockSpec((block, cols), lambda i: (row_order(seq_count, subs, i), 0))
    once = pl.Buffered(1)
    weight = lambda shape, n: pl.BlockSpec(shape, lambda i: (0, n), pipeline_mode=once)
    like = lambda cols, dtype: jax.ShapeDtypeStruct((rows, cols), dtype)
    low = jnp.bfloat16
    return pl.pallas_call(
        functools.partial(middle_kernel, shape["seq"], seq_count),
        grid=(rows // block,),
        in_specs=[
            row(width), row(width), pl.BlockSpec(memory_space=pl.ANY),
            weight((width, width), 2 * units // width), weight((width, units), 0), weight((width, units), 1),
            weight((units, width), 0), weight((8, width), 0),
        ],
        out_specs=[
            row(width), row(width), row(width), row(width), row(width), row(units), row(units), row(units), row(width),
            pl.BlockSpec((8, width), lambda i: (0, 0)),
        ],
        out_shape=[
            like(width, low), like(width, jnp.float32), like(width, low), like(width, low), like(width, low),
            like(units, low), like(units, low), like(units, low), like(width, low),
            jax.ShapeDtypeStruct((8, width), jnp.float32),
        ],
        scratch_shapes=[
            pltpu.VMEM((block, units), jnp.float32),
            pltpu.VMEM((block, units), jnp.float32),
            pltpu.VMEM((rows // block, block, width), low),
            pltpu.SemaphoreType.DMA((3, rows // block)),
        ],
        compiler_params=pltpu.CompilerParams(collective_id=4, has_side_effects=True, vmem_limit_bytes=61 << 20),
        name="middle",
    )(x, attended, cotangent, rest, rest, rest, down, norms)


def grad_wide_kernel(tiles, core_ref, left_ref, right_ref, *refs):
    keep_ref, send_ref = refs[-2:]
    value = dotf(left_ref[...], right_ref[...], TN).astype(jnp.bfloat16)

    @pl.when(pl.program_id(0) < tiles)
    def _():
        send_ref[...] = value

    @pl.when(pl.program_id(0) >= tiles)
    def _():
        keep_ref[...] = value


def grad_wide(core, left, right, held, offset, tile=512):
    rows, width = left.shape
    half = right.shape[1] // 2
    tiles = half // tile
    first = offset // tile
    like = jax.ShapeDtypeStruct(held[0].shape, jnp.bfloat16)
    return pl.pallas_call(
        functools.partial(grad_wide_kernel, tiles),
        grid_spec=pltpu.PrefetchScalarGridSpec(
            num_scalar_prefetch=1,
            grid=(2 * tiles,),
            in_specs=[
                pl.BlockSpec((rows, width), lambda i, c: (0, 0)),
                pl.BlockSpec(
                    (rows, tile), lambda i, c: (0, lax.rem(c[0] + 1 + lax.div(i, tiles), 2) * tiles + lax.rem(i, tiles))
                ),
                pl.BlockSpec(memory_space=pl.ANY),
                pl.BlockSpec(memory_space=pl.ANY),
            ],
            out_specs=[
                pl.BlockSpec((width, tile), lambda i, c: (0, first + jnp.maximum(i - tiles, 0))),
                pl.BlockSpec((width, tile), lambda i, c: (0, first + jnp.minimum(i, tiles - 1))),
            ],
        ),
        out_shape=[like, like],
        input_output_aliases={3: 0, 4: 1},
        compiler_params=pltpu.CompilerParams(vmem_limit_bytes=48 << 20),
        name="grad_wide",
    )(core, left, right, *held)


def halves(value, core, keep_ref, send_ref):
    half = value.shape[1] // 2
    low, high = value[:, :half].astype(jnp.bfloat16), value[:, half:].astype(jnp.bfloat16)
    keep_ref[...] = jnp.where(core == 0, low, high)
    send_ref[...] = jnp.where(core == 0, high, low)


def grad_tall_kernel(rows, core_ref, left_ref, right_ref, keep_ref, send_ref):
    value = dotf(left_ref[...], right_ref[...], TN)
    half = value.shape[1] // 2
    turns = keep_ref.shape[1] // half
    core = core_ref[0]
    for n, part in enumerate((value[:, :half], value[:, half:])):
        wide = jnp.concatenate(
            [
                jnp.concatenate([part[(b * turns + a) * rows : (b * turns + a + 1) * rows] for a in range(turns)], 1)
                for b in range(part.shape[0] // (turns * rows))
            ],
            0,
        ).astype(jnp.bfloat16)

        @pl.when(core == n)
        def _():
            keep_ref[...] = wide

        @pl.when(core != n)
        def _():
            send_ref[...] = wide


def grad_tall(core, left, right, rows, cols, tile=384):
    depth, height = left.shape
    width = right.shape[1]
    devices = height // (rows * (height // width))
    fold = height // (devices * rows)
    tile_rows = tile // fold
    out = pl.BlockSpec((tile_rows, fold * width // 2), lambda i, c: (i, 0))
    like = jax.ShapeDtypeStruct((height // fold, cols), jnp.bfloat16)
    return pl.pallas_call(
        functools.partial(grad_tall_kernel, rows),
        grid_spec=pltpu.PrefetchScalarGridSpec(
            num_scalar_prefetch=1,
            grid=(height // tile,),
            in_specs=[
                pl.BlockSpec((depth, tile), lambda i, c: (0, i)),
                pl.BlockSpec((depth, width), lambda i, c: (0, 0)),
            ],
            out_specs=[out, out],
        ),
        out_shape=[like, like],
        compiler_params=pltpu.CompilerParams(vmem_limit_bytes=48 << 20),
        name="grad_tall",
    )(core, left, right)


def grad_out_kernel(core_ref, left_ref, right_ref, sums_ref, _keep, _send, keep_ref, send_ref):
    value = dotf(left_ref[...], right_ref[...], TN)
    pad = jnp.zeros((NORM_COLS - sums_ref.shape[0], sums_ref.shape[1]), jnp.float32)
    norms = jnp.concatenate([sums_ref[...], pad], 0).T
    halves(jnp.concatenate([value, norms], 1), core_ref[0], keep_ref, send_ref)


def grad_out(core, left, right, sums, held, offset):
    width = left.shape[1]
    full = lambda array: pl.BlockSpec(array.shape, lambda i, c: (0, 0))
    half = (width + NORM_COLS) // 2
    out = pl.BlockSpec((width, half), lambda i, c: (0, offset // half))
    like = jax.ShapeDtypeStruct(held[0].shape, jnp.bfloat16)
    any_space = pl.BlockSpec(memory_space=pl.ANY)
    return pl.pallas_call(
        grad_out_kernel,
        grid_spec=pltpu.PrefetchScalarGridSpec(
            num_scalar_prefetch=1,
            grid=(1,),
            in_specs=[full(left), full(right), full(sums), any_space, any_space],
            out_specs=[out, out],
        ),
        out_shape=[like, like],
        input_output_aliases={4: 0, 5: 1},
        compiler_params=pltpu.CompilerParams(vmem_limit_bytes=48 << 20),
        name="grad_out",
    )(core, left, right, sums, *held)


NORM_COLS = 256
PLAN = {1: ((0, 1),), 2: ((0, 2),), 4: ((0, 3), (1, 1)), 6: ((0, 0), (1, 2)), 8: ((1, 3), (2, 1)), 9: ((2, 2),), 10: ((1, 0),), 11: ((2, 3),)}
GATHER_PLAN = {3: ((1,),), 5: ((1, 0),), 6: ((2,),), 7: ((1, 1),), 8: ((2, 0),), 9: ((3,),), 10: ((2, 1),), 11: ((3, 0),), None: ((3, 1),)}


def seg_codes(segments):
    lane = jnp.arange(128) % HEAD_DIM
    low, high = lane < CODE_BITS, lane < 2 * CODE_BITS
    bit = (segments[:, None] >> jnp.where(low, lane, jnp.where(high, lane - CODE_BITS, 0))[None, :]) & 1
    query = jnp.where(low, bit, jnp.where(high, 1 - bit, 0))
    keys = jnp.where(low, 1 - bit, jnp.where(high, bit, 0)) * -FAR
    return query.astype(jnp.bfloat16), keys.astype(jnp.bfloat16)


def two_to_a_sequence(
    shape,
    tokens, segment_ids, cotangent,
    w_qkv, w_out, w_gate, w_up, w_down, norm_params,
    first_qkv, first_out, first_gate, first_up, first_down, first_norms,
    second_qkv, second_out, second_gate, second_up, second_down, second_norms,
):
    seqs = shape["seq"]
    seq_count, local_len, width = tokens.shape
    rows = seq_count * local_len
    group = seqs // seq_count
    units = w_gate.shape[1]
    z = lax.axis_index("seq")
    core = lax.axis_index("fsdp") % 2

    norm_rows = jnp.pad(norm_params.T, ((0, 0), (0, NORM_COLS - norm_params.shape[0])))
    (x, segments, qkv_all, rest_all, down_all), pieces = first_gather(
        shape, tokens, segment_ids.reshape(seq_count, 1, local_len), w_gate, w_up, w_qkv, w_out, norm_rows, w_down
    )
    x = x.reshape(rows, width)
    w_all = qkv_all.reshape(width, 3 * width)
    q_code, k_code = seg_codes(segments.reshape(rows))
    positions = ((z * 2 + core) % group * rows + jnp.arange(rows)).astype(jnp.float32)
    half_dim = HEAD_DIM // 2
    inverse = jnp.exp(jnp.arange(half_dim, dtype=jnp.float32) * (-2.0 * math.log(ROPE_BASE) / HEAD_DIM))
    angles = positions[:, None] * inverse[None, :]
    cosine, sine = jnp.cos(angles), jnp.sin(angles)
    cosine = jnp.concatenate([cosine] * 4, 1)
    sine = jnp.concatenate([-sine, sine, -sine, sine], 1)

    query, own = project(x, w_all, 0, cosine, sine, k_code)
    probs, attended, inverse_sums, sib, rest_all, down_all = attend_pallas(
        shape, pieces, GATHER_PLAN, query, q_code, own, rest_all, down_all
    )
    rest = rest_all.reshape(width, rest_all.shape[-1])
    down = down_all.reshape(units, width)
    norms = jnp.pad(rest[:, -NORM_COLS : 4 - NORM_COLS].T.astype(jnp.float32), ((0, 4), (0, 0)))
    (
        result, d_resid_one, d_branch, d_attended, hidden_low, mixed, d_gate, d_up, d_ff, sums,
    ) = middle(shape, x, attended, cotangent, rest, down, norms)

    core_id = core.astype(jnp.int32).reshape(1)
    own_rows = w_gate.shape[0]
    half_tall, half_wide, half_out = units * width // 2 // width, units // 2, (width + NORM_COLS) // 2
    cols = half_tall + 2 * half_wide + half_out
    held = grad_tall(core_id, mixed, d_ff, own_rows, cols)
    held = grad_wide(core_id, hidden_low, d_gate, held, half_tall)
    held = grad_wide(core_id, hidden_low, d_up, held, half_tall + half_wide)
    held = grad_out(core_id, attended, d_branch, sums, held, half_tall + 2 * half_wide)
    d_query, d_own, d_got, reduced_sums, output = attend_back_pallas(
        shape, query, own, sib, probs, attended, inverse_sums, d_attended, *held, result, seq_count, PLAN
    )
    back, qkv_sums, squares = tail(
        shape, cosine, sine, d_query, d_own, d_got, w_all, 0, d_resid_one, x, reduced_sums, seq_count
    )
    states = (
        w_qkv, w_out, w_gate, w_up, w_down, norm_params,
        first_qkv, first_out, first_gate, first_up, first_down, first_norms,
        second_qkv, second_out, second_gate, second_up, second_down, second_norms,
    )
    *updated, input_grad, grad_norm = adam(reduced_sums, qkv_sums, squares, back, states)
    return (output, input_grad, *updated, grad_norm.reshape(()))


def device_program(shape, *arrays):
    tokens, w_gate, w_down = arrays[0], arrays[5], arrays[7]
    seqs, line = shape["seq"], shape["fsdp"]
    seq_count, local_len, width = tokens.shape
    fits = (
        seqs == 2 * seq_count
        and line & (line - 1) == 0
        and line >= 4
        and (seq_count * local_len) % 512 == 0
        and w_gate.shape[0] % 8 == 0
        and w_down.shape[0] % 8 == 0
    )
    return two_to_a_sequence(shape, *arrays) if fits else per_device(*arrays)


def solution(mesh):
    return jax.shard_map(
        functools.partial(device_program, dict(mesh.shape)),
        mesh=mesh,
        in_specs=(
            P("fsdp", "seq", None),
            P("fsdp", "seq"),
            P("fsdp", "seq", None),
            P(("seq", "fsdp"), None),
            P(("seq", "fsdp"), None),
            P(("seq", "fsdp"), None),
            P(("seq", "fsdp"), None),
            P(("seq", "fsdp"), None),
            P(None, ("seq", "fsdp")),
            P(("seq", "fsdp"), None),
            P(("seq", "fsdp"), None),
            P(("seq", "fsdp"), None),
            P(("seq", "fsdp"), None),
            P(("seq", "fsdp"), None),
            P(None, ("seq", "fsdp")),
            P(("seq", "fsdp"), None),
            P(("seq", "fsdp"), None),
            P(("seq", "fsdp"), None),
            P(("seq", "fsdp"), None),
            P(("seq", "fsdp"), None),
            P(None, ("seq", "fsdp")),
        ),
        out_specs=(
            P("fsdp", "seq", None),
            P("fsdp", "seq", None),
            P(("seq", "fsdp"), None),
            P(("seq", "fsdp"), None),
            P(("seq", "fsdp"), None),
            P(("seq", "fsdp"), None),
            P(("seq", "fsdp"), None),
            P(None, ("seq", "fsdp")),
            P(("seq", "fsdp"), None),
            P(("seq", "fsdp"), None),
            P(("seq", "fsdp"), None),
            P(("seq", "fsdp"), None),
            P(("seq", "fsdp"), None),
            P(None, ("seq", "fsdp")),
            P(("seq", "fsdp"), None),
            P(("seq", "fsdp"), None),
            P(("seq", "fsdp"), None),
            P(("seq", "fsdp"), None),
            P(("seq", "fsdp"), None),
            P(None, ("seq", "fsdp")),
            P(("seq", "fsdp"), None),
            P(("seq", "fsdp"), None),
            P(("seq", "fsdp"), None),
            P(("seq", "fsdp"), None),
            P(("seq", "fsdp"), None),
            P(None, ("seq", "fsdp")),
            P(),
        ),
        check_vma=False,
    )
```

```python
import functools
import math

import jax
import jax.numpy as jnp
from jax import lax
from jax.experimental import pallas as pl
from jax.experimental.pallas import tpu as pltpu
from jax.sharding import PartitionSpec as P

HEADS = 12
HEAD_DIM = 64
STEP = 10


EPS_NORM = 1e-06
ROPE_BASE = 1000.0
MASKED_SCORE = -1e30
MAX_NORM = 1.0
LEARN_RATE = 0.1
NORM_RATE = 0.6
BETA_ONE = 0.9
BETA_TWO = 0.999
ADAM_EPS = 1e-08
WEIGHT_DECAY = 0.01


def rotate(field, positions, sign_rot):
    shape_in = field.shape
    heads_view = field.reshape(shape_in[:-1] + (HEADS, HEAD_DIM))
    half_dim = HEAD_DIM // 2
    inverse = jnp.exp(
        jnp.arange(half_dim, dtype=jnp.float32) * (-2.0 * math.log(ROPE_BASE) / HEAD_DIM)
    )
    angles = positions[:, None] * inverse[None, :]
    cosine = jnp.cos(angles)[:, None, :]
    sine = jnp.sin(angles)[:, None, :] * sign_rot
    first_half = heads_view[..., :half_dim]
    second_half = heads_view[..., half_dim:]
    turned = jnp.concatenate(
        [first_half * cosine - second_half * sine, second_half * cosine + first_half * sine], -1
    )
    return turned.reshape(shape_in)


def normalize(resid, gain, shift):
    mean_row = jnp.mean(resid, -1, keepdims=True)
    centered = resid - mean_row
    inv_std = lax.rsqrt(jnp.mean(centered * centered, -1, keepdims=True) + EPS_NORM)
    normed = centered * inv_std
    return (normed * gain + shift, normed, inv_std)


def normalize_back(grad_in, normed, inv_std, gain):
    scaled = grad_in * gain
    return inv_std * (
        scaled
        - jnp.mean(scaled, -1, keepdims=True)
        - normed * jnp.mean(scaled * normed, -1, keepdims=True)
    )


def attend(query, keys, values, same_doc, score_scale):
    seq_count, local_len, model_width = query.shape

    def one_head(head_index, carried):
        out_all, log_sums = carried
        col_start = head_index * HEAD_DIM
        query_head = lax.dynamic_slice_in_dim(query, col_start, HEAD_DIM, 2)
        key_head = lax.dynamic_slice_in_dim(keys, col_start, HEAD_DIM, 2)
        value_head = lax.dynamic_slice_in_dim(values, col_start, HEAD_DIM, 2)
        raw_scores = jnp.einsum(
            "sqd,skd->sqk", query_head, key_head, preferred_element_type=jnp.float32
        )
        scores = jnp.where(same_doc, raw_scores * score_scale, MASKED_SCORE)
        row_max = jnp.max(scores, -1, keepdims=True)
        exp_scores = jnp.exp(scores - row_max)
        row_sums = jnp.sum(exp_scores, -1, keepdims=True)
        attn_prob = (exp_scores / row_sums).astype(jnp.bfloat16)
        head_out = jnp.einsum(
            "sqk,skd->sqd", attn_prob, value_head, preferred_element_type=jnp.float32
        )
        out_all = lax.dynamic_update_slice_in_dim(out_all, head_out, col_start, 2)
        log_sums = lax.dynamic_update_index_in_dim(
            log_sums, (row_max + jnp.log(row_sums))[..., 0], head_index, 0
        )
        return (out_all, log_sums)

    start_state = (
        jnp.zeros((seq_count, local_len, model_width), jnp.float32),
        jnp.zeros((HEADS, seq_count, local_len), jnp.float32),
    )
    return lax.fori_loop(0, HEADS, one_head, start_state)


def attend_back(query, keys, values, same_doc, log_sums, grad_attended, score_scale):
    seq_count, local_len, model_width = query.shape
    key_len = keys.shape[1]

    def one_head(head_index, carried):
        dq_all, dk_all, dv_all = carried
        col_start = head_index * HEAD_DIM
        query_head = lax.dynamic_slice_in_dim(query, col_start, HEAD_DIM, 2)
        key_head = lax.dynamic_slice_in_dim(keys, col_start, HEAD_DIM, 2)
        value_head = lax.dynamic_slice_in_dim(values, col_start, HEAD_DIM, 2)
        grad_head = lax.dynamic_slice_in_dim(grad_attended, col_start, HEAD_DIM, 2)
        head_sums = lax.dynamic_index_in_dim(log_sums, head_index, 0, keepdims=False)
        raw_scores = jnp.einsum(
            "sqd,skd->sqk", query_head, key_head, preferred_element_type=jnp.float32
        )
        scores = jnp.where(same_doc, raw_scores * score_scale, MASKED_SCORE)
        attn_prob = jnp.exp(scores - head_sums[..., None])
        grad_prob = jnp.einsum(
            "sqd,skd->sqk", grad_head, value_head, preferred_element_type=jnp.float32
        )
        dv_head = jnp.einsum(
            "sqk,sqd->skd",
            attn_prob.astype(jnp.bfloat16),
            grad_head,
            preferred_element_type=jnp.float32,
        )
        row_dots = jnp.sum(attn_prob * grad_prob, -1, keepdims=True)
        grad_scores = (attn_prob * (grad_prob - row_dots)).astype(jnp.bfloat16)
        dq_head = (
            jnp.einsum("sqk,skd->sqd", grad_scores, key_head, preferred_element_type=jnp.float32)
            * score_scale
        )
        dk_head = (
            jnp.einsum("sqk,sqd->skd", grad_scores, query_head, preferred_element_type=jnp.float32)
            * score_scale
        )
        dq_all = lax.dynamic_update_slice_in_dim(dq_all, dq_head, col_start, 2)
        dk_all = lax.dynamic_update_slice_in_dim(dk_all, dk_head, col_start, 2)
        dv_all = lax.dynamic_update_slice_in_dim(dv_all, dv_head, col_start, 2)
        return (dq_all, dk_all, dv_all)

    start_state = (
        jnp.zeros((seq_count, local_len, model_width), jnp.float32),
        jnp.zeros((seq_count, key_len, model_width), jnp.float32),
        jnp.zeros((seq_count, key_len, model_width), jnp.float32),
    )
    return lax.fori_loop(0, HEADS, one_head, start_state)


def adam_update(weight, gradient, moment_one, moment_two, decay_rate, step_rate, clip_factor):
    clipped = gradient * clip_factor
    first_new = BETA_ONE * moment_one + (1.0 - BETA_ONE) * clipped
    second_new = BETA_TWO * moment_two + (1.0 - BETA_TWO) * clipped * clipped
    first_fix = 1.0 - BETA_ONE**STEP
    second_fix = 1.0 - BETA_TWO**STEP
    direction = (
        first_new / first_fix / (jnp.sqrt(second_new / second_fix) + ADAM_EPS) + decay_rate * weight
    )
    return (weight - step_rate * direction, first_new, second_new)


def per_device(
    tokens,
    segment_ids,
    cotangent,
    w_qkv,
    w_out,
    w_gate,
    w_up,
    w_down,
    norm_params,
    first_qkv,
    first_out,
    first_gate,
    first_up,
    first_down,
    first_norms,
    second_qkv,
    second_out,
    second_gate,
    second_up,
    second_down,
    second_norms,
):
    seq_count, local_len, model_width = tokens.shape
    row_count = seq_count * local_len
    score_scale = 1.0 / math.sqrt(HEAD_DIM)
    lowered_qkv = w_qkv.astype(jnp.bfloat16)
    lowered_out = w_out.astype(jnp.bfloat16)
    lowered_gate = w_gate.astype(jnp.bfloat16)
    lowered_up = w_up.astype(jnp.bfloat16)
    lowered_down = w_down.astype(jnp.bfloat16)
    lowered_norms = norm_params.astype(jnp.bfloat16)
    full_qkv, full_out, full_gate, full_up, full_down, full_norms = (
        lax.all_gather(lowered_qkv, ("seq", "fsdp"), axis=0, tiled=True),
        lax.all_gather(lowered_out, ("seq", "fsdp"), axis=0, tiled=True),
        lax.all_gather(lowered_gate, ("seq", "fsdp"), axis=0, tiled=True),
        lax.all_gather(lowered_up, ("seq", "fsdp"), axis=0, tiled=True),
        lax.all_gather(lowered_down, ("seq", "fsdp"), axis=0, tiled=True),
        lax.all_gather(lowered_norms, ("seq", "fsdp"), axis=1, tiled=True),
    )
    gains = full_norms.astype(jnp.float32)
    gain_one, shift_one, gain_two, shift_two = (gains[0], gains[1], gains[2], gains[3])
    positions = (lax.axis_index("seq") * local_len + jnp.arange(local_len)).astype(jnp.float32)
    flat_rows = tokens.reshape(row_count, model_width)
    projected = jnp.dot(flat_rows, full_qkv, preferred_element_type=jnp.float32).reshape(
        seq_count, local_len, 3 * model_width
    )
    query = rotate(projected[..., :model_width], positions, 1.0).astype(jnp.bfloat16)
    keys_local = rotate(projected[..., model_width : 2 * model_width], positions, 1.0).astype(
        jnp.bfloat16
    )
    values_local = projected[..., 2 * model_width :].astype(jnp.bfloat16)
    keys_all, values_all, key_segments = (
        lax.all_gather(keys_local, "seq", axis=1, tiled=True),
        lax.all_gather(values_local, "seq", axis=1, tiled=True),
        lax.all_gather(segment_ids, "seq", axis=1, tiled=True),
    )
    same_doc = segment_ids[:, :, None] == key_segments[:, None, :]
    attended, log_sums = attend(query, keys_all, values_all, same_doc, score_scale)
    attended_low = attended.astype(jnp.bfloat16).reshape(row_count, model_width)
    resid_one = flat_rows.astype(jnp.float32) + jnp.dot(
        attended_low, full_out, preferred_element_type=jnp.float32
    )
    hidden, normed_one, inv_std_one = normalize(resid_one, gain_one, shift_one)
    hidden_low = hidden.astype(jnp.bfloat16)
    gate_proj = jnp.dot(hidden_low, full_gate, preferred_element_type=jnp.float32)
    up_proj = jnp.dot(hidden_low, full_up, preferred_element_type=jnp.float32)
    sigmoid_gate = jax.nn.sigmoid(gate_proj)
    silu_gate = gate_proj * sigmoid_gate
    mixed_low = (silu_gate * up_proj).astype(jnp.bfloat16)
    resid_two = hidden + jnp.dot(mixed_low, full_down, preferred_element_type=jnp.float32)
    result, normed_two, inv_std_two = normalize(resid_two, gain_two, shift_two)
    output = result.astype(jnp.bfloat16).reshape(seq_count, local_len, model_width)
    back_qkv, back_out, back_gate, back_up, back_down = (
        lax.all_gather(lowered_qkv, ("seq", "fsdp"), axis=0, tiled=True),
        lax.all_gather(lowered_out, ("seq", "fsdp"), axis=0, tiled=True),
        lax.all_gather(lowered_gate, ("seq", "fsdp"), axis=0, tiled=True),
        lax.all_gather(lowered_up, ("seq", "fsdp"), axis=0, tiled=True),
        lax.all_gather(lowered_down, ("seq", "fsdp"), axis=0, tiled=True),
    )
    grad_result = cotangent.reshape(row_count, model_width).astype(jnp.float32)
    d_gain_two = jnp.sum(grad_result * normed_two, 0)
    d_shift_two = jnp.sum(grad_result, 0)
    d_resid_two = normalize_back(grad_result, normed_two, inv_std_two, gain_two)
    d_ff_low = d_resid_two.astype(jnp.bfloat16)
    g_down = jnp.einsum("rf,rd->fd", mixed_low, d_ff_low, preferred_element_type=jnp.float32)
    d_mixed = jnp.einsum("rd,fd->rf", d_ff_low, back_down, preferred_element_type=jnp.float32)
    d_up_low = (d_mixed * silu_gate).astype(jnp.bfloat16)
    d_gate_low = (
        d_mixed * up_proj * sigmoid_gate * (1.0 + gate_proj * (1.0 - sigmoid_gate))
    ).astype(jnp.bfloat16)
    g_gate = jnp.einsum("rd,rf->df", hidden_low, d_gate_low, preferred_element_type=jnp.float32)
    g_up = jnp.einsum("rd,rf->df", hidden_low, d_up_low, preferred_element_type=jnp.float32)
    d_hidden = (
        d_resid_two
        + jnp.einsum("rf,df->rd", d_gate_low, back_gate, preferred_element_type=jnp.float32)
        + jnp.einsum("rf,df->rd", d_up_low, back_up, preferred_element_type=jnp.float32)
    )
    d_gain_one = jnp.sum(d_hidden * normed_one, 0)
    d_shift_one = jnp.sum(d_hidden, 0)
    d_resid_one = normalize_back(d_hidden, normed_one, inv_std_one, gain_one)
    d_branch_low = d_resid_one.astype(jnp.bfloat16)
    g_out = jnp.einsum("rd,re->de", attended_low, d_branch_low, preferred_element_type=jnp.float32)
    d_attended_low = (
        jnp.einsum("re,de->rd", d_branch_low, back_out, preferred_element_type=jnp.float32)
        .astype(jnp.bfloat16)
        .reshape(seq_count, local_len, model_width)
    )
    keys_back, values_back = (
        lax.all_gather(keys_local, "seq", axis=1, tiled=True),
        lax.all_gather(values_local, "seq", axis=1, tiled=True),
    )
    d_query, d_keys, d_values = attend_back(
        query, keys_back, values_back, same_doc, log_sums, d_attended_low, score_scale
    )
    d_keys_local, d_values_local = (
        lax.psum_scatter(
            d_keys.astype(jnp.bfloat16), "seq", scatter_dimension=1, tiled=True
        ).astype(jnp.float32),
        lax.psum_scatter(
            d_values.astype(jnp.bfloat16), "seq", scatter_dimension=1, tiled=True
        ).astype(jnp.float32),
    )
    d_projected_low = (
        jnp.concatenate(
            [
                rotate(d_query, positions, -1.0),
                rotate(d_keys_local, positions, -1.0),
                d_values_local,
            ],
            -1,
        )
        .astype(jnp.bfloat16)
        .reshape(row_count, 3 * model_width)
    )
    g_qkv = jnp.einsum("rd,re->de", flat_rows, d_projected_low, preferred_element_type=jnp.float32)
    input_grad = (
        d_resid_one
        + jnp.einsum("re,de->rd", d_projected_low, back_qkv, preferred_element_type=jnp.float32)
    ).reshape(seq_count, local_len, model_width)
    g_norms = jnp.stack([d_gain_one, d_shift_one, d_gain_two, d_shift_two])
    red_qkv, red_out, red_gate, red_up, red_down, red_norms = (
        lax.psum_scatter(g_qkv, ("seq", "fsdp"), scatter_dimension=0, tiled=True),
        lax.psum_scatter(g_out, ("seq", "fsdp"), scatter_dimension=0, tiled=True),
        lax.psum_scatter(g_gate, ("seq", "fsdp"), scatter_dimension=0, tiled=True),
        lax.psum_scatter(g_up, ("seq", "fsdp"), scatter_dimension=0, tiled=True),
        lax.psum_scatter(g_down, ("seq", "fsdp"), scatter_dimension=0, tiled=True),
        lax.psum_scatter(g_norms, ("seq", "fsdp"), scatter_dimension=1, tiled=True),
    )
    local_squares = (
        jnp.sum(red_qkv * red_qkv)
        + jnp.sum(red_out * red_out)
        + jnp.sum(red_gate * red_gate)
        + jnp.sum(red_up * red_up)
        + jnp.sum(red_down * red_down)
        + jnp.sum(red_norms * red_norms)
    )
    squares_sum = lax.psum(local_squares, ("seq", "fsdp"))
    grad_norm = jnp.sqrt(squares_sum)
    clip_factor = jnp.minimum(1.0, MAX_NORM / (grad_norm + 1e-06))
    new_qkv, mom_qkv, sec_qkv = adam_update(
        w_qkv, red_qkv, first_qkv, second_qkv, WEIGHT_DECAY, LEARN_RATE, clip_factor
    )
    new_out, mom_out, sec_out = adam_update(
        w_out, red_out, first_out, second_out, WEIGHT_DECAY, LEARN_RATE, clip_factor
    )
    new_gate, mom_gate, sec_gate = adam_update(
        w_gate, red_gate, first_gate, second_gate, WEIGHT_DECAY, LEARN_RATE, clip_factor
    )
    new_up, mom_up, sec_up = adam_update(
        w_up, red_up, first_up, second_up, WEIGHT_DECAY, LEARN_RATE, clip_factor
    )
    new_down, mom_down, sec_down = adam_update(
        w_down, red_down, first_down, second_down, WEIGHT_DECAY, LEARN_RATE, clip_factor
    )
    new_norms, mom_norms, sec_norms = adam_update(
        norm_params, red_norms, first_norms, second_norms, 0.0, NORM_RATE, clip_factor
    )
    return (
        output,
        input_grad,
        red_qkv,
        red_out,
        red_gate,
        red_up,
        red_down,
        red_norms,
        new_qkv,
        new_out,
        new_gate,
        new_up,
        new_down,
        new_norms,
        mom_qkv,
        mom_out,
        mom_gate,
        mom_up,
        mom_down,
        mom_norms,
        sec_qkv,
        sec_out,
        sec_gate,
        sec_up,
        sec_down,
        sec_norms,
        grad_norm,
    )


NT = (((1,), (1,)), ((), ()))
NN = (((1,), (0,)), ((), ()))
TN = (((0,), (0,)), ((), ()))
FAR = 1e30
CODE_BITS = 7
MESH_ID = pl.DeviceIdType.MESH


def dotf(left, right, dims=NN):
    return lax.dot_general(left, right, dims, preferred_element_type=jnp.float32)


def place():
    f = lax.axis_index("fsdp")
    return lax.axis_index("seq"), lax.div(f, 2), lax.rem(f, 2)


def chip_at(chip, mask):
    at, b = chip, 0
    while mask >> b:
        if (mask >> b) & 1:
            at = at + (1 - 2 * lax.rem(lax.div(chip, 1 << b), 2)) * (1 << b)
        b += 1
    return at


def greet(peers):
    barrier = pltpu.get_barrier_semaphore()
    for peer in peers:
        pl.semaphore_signal(barrier, inc=1, device_id=peer, device_id_type=MESH_ID)
    pl.semaphore_wait(barrier, len(peers))


def column_peers(seqs):
    z, chip, core = place()
    return [{"seq": lax.rem(z + k, seqs), "fsdp": 2 * chip + c} for k in range(1, seqs) for c in range(2)]


def plane_peers(line):
    f = lax.axis_index("fsdp")
    return [{"fsdp": lax.rem(f + k, line)} for k in range(1, line)]


def sum_peers(bits):
    z, chip, core = place()
    return [{"fsdp": 2 * chip + 1 - core}] + [{"fsdp": 2 * chip_at(chip, 1 << b) + core} for b in range(bits)]


def departs(seqs, seq_count, source, target, sems, subs=1):
    z, chip, core = place()
    group = seqs // seq_count

    def copies(s, sub):
        at = (core * seq_count + s) * group + lax.div(z, seq_count)
        to_z, to_core = lax.div(at, 2), lax.rem(at, 2)
        n = lax.rem(z, seq_count) * subs + sub
        remote = pltpu.make_async_remote_copy(
            source(s, sub), target(n), sems.at[0, s * subs + sub], sems.at[1, n],
            device_id={"seq": to_z, "fsdp": 2 * chip + to_core}, device_id_type=MESH_ID,
        )
        return (to_z == z) & (to_core == core), remote, pltpu.make_async_copy(source(s, sub), target(n), sems.at[2, n])

    def begin():
        for sub in range(subs):
            for s in range(seq_count):
                mine, remote, local = copies(s, sub)

                @pl.when(mine)
                def _():
                    local.start()

                @pl.when(jnp.logical_not(mine))
                def _():
                    remote.start()

    def came(n):
        at = z * 2 + core
        from_z = lax.rem(at, group) * seq_count + lax.div(n, subs)
        mine = (from_z == z) & (lax.div(lax.div(at, group), seq_count) == core)

        @pl.when(mine)
        def _():
            pltpu.make_async_copy(source(0, 0), target(n), sems.at[2, n]).wait()

        @pl.when(jnp.logical_not(mine))
        def _():
            pltpu.make_async_remote_copy(
                source(0, 0), target(n), sems.at[0, 0], sems.at[1, n],
                device_id={"seq": z, "fsdp": 2 * chip + 1 - core}, device_id_type=MESH_ID,
            ).wait_recv()

    def sent():
        for sub in range(subs):
            for s in range(seq_count):
                mine, remote, _ = copies(s, sub)

                @pl.when(jnp.logical_not(mine))
                def _():
                    remote.wait_send()

    return begin, came, sent


def returns(seqs, seq_count, source, target, sems, rows):
    z, chip, core = place()
    group = seqs // seq_count
    at = z * 2 + core
    number = lax.div(at, group)
    slot = lax.rem(number, seq_count)
    to_core = lax.div(number, seq_count)
    local_len = target.shape[1]
    subs = local_len // rows

    def copies(n):
        t, sub = divmod(n, subs)
        to_z = lax.rem(at, group) * seq_count + t
        mine = (to_z == z) & (to_core == core)
        here = target.at[slot, pl.ds(sub * rows, rows)]
        remote = pltpu.make_async_remote_copy(
            source(n), here, sems.at[0, n], sems.at[1, slot * subs + sub],
            device_id={"seq": to_z, "fsdp": 2 * chip + to_core}, device_id_type=MESH_ID,
        )
        return mine, remote, pltpu.make_async_copy(source(n), here, sems.at[2, n])

    def begin(n):
        mine, remote, local = copies(n)

        @pl.when(mine)
        def _():
            local.start()

        @pl.when(jnp.logical_not(mine))
        def _():
            remote.start()

    def end():
        for n in range(seq_count * subs):
            mine, remote, local = copies(n)

            @pl.when(mine)
            def _():
                local.wait()

            @pl.when(jnp.logical_not(mine))
            def _():
                remote.wait_send()

        for s in range(seq_count):
            came = (core * seq_count + s) * group + lax.div(z, seq_count)
            other = jnp.logical_not((lax.div(came, 2) == z) & (lax.rem(came, 2) == core))
            for sub in range(subs):

                @pl.when(other)
                def _():
                    here = target.at[s, pl.ds(sub * rows, rows)]
                    pltpu.make_async_remote_copy(
                        source(0), here, sems.at[0, 0], sems.at[1, s * subs + sub],
                        device_id={"seq": z, "fsdp": 2 * chip + 1 - core}, device_id_type=MESH_ID,
                    ).wait_recv()

    return begin, end


def line_peers(seqs):
    z = lax.axis_index("seq")
    return [{"seq": lax.rem(z + way, seqs)} for way in (1, seqs - 1)]


def gatherer_scratch(seqs, bits, count):
    dma = pltpu.SemaphoreType.DMA
    chips = 1 << bits
    return [
        dma((count, 2, seqs)),
        dma((count, seqs)),
        dma((count, seqs, chips)),
        dma((count, seqs, chips)),
        dma((count, seqs, chips)),
        dma((count, seqs, chips)),
    ]


def gatherer(seqs, bits, pieces, wholes, line_send, line_recv, hop_send, hop_recv, swap_send, swap_recv):
    z, chip, core = place()

    def block(p, zz, mask):
        which, offset, width, _ = pieces[p]
        half = wholes[which].shape[-1] // 2
        return wholes[which].at[zz, chip_at(chip, mask), :, pl.ds(pl.multiple_of(core * half + offset, 128), width)]

    def line_copy(p, zz, way):
        return pltpu.make_async_remote_copy(
            block(p, zz, 0), block(p, zz, 0), line_send.at[p, way, zz], line_recv.at[p, zz],
            device_id={"seq": z + (1 if way else -1)}, device_id_type=MESH_ID,
        )

    def hop_copy(p, zz, mask, b):
        to = mask | (1 << b)
        return pltpu.make_async_remote_copy(
            block(p, zz, mask), block(p, zz, mask), hop_send.at[p, zz, to], hop_recv.at[p, zz, to],
            device_id={"fsdp": 2 * chip_at(chip, 1 << b) + core}, device_id_type=MESH_ID,
        )

    def swap_copy(p, zz, mask):
        return pltpu.make_async_remote_copy(
            block(p, zz, mask), block(p, zz, mask), swap_send.at[p, zz, mask], swap_recv.at[p, zz, mask],
            device_id={"fsdp": 2 * chip + 1 - core}, device_id_type=MESH_ID,
        )

    def level(p, mask):
        return max([i for i, b in enumerate(pieces[p][3]) if mask & (1 << b)], default=-1)

    def later(p, mask):
        return pieces[p][3][level(p, mask) + 1 :]

    masks = range(1 << bits)

    def pass_on(p, zz, mask, mine=False):
        for b in later(p, mask):
            hop_copy(p, zz, mask, b).start()
        if not mine:
            swap_copy(p, zz, mask).start()

    def own_line(which):
        for p in which:

            @pl.when(z > 0)
            def _():
                line_copy(p, z, 0).start()

            @pl.when(z < seqs - 1)
            def _():
                line_copy(p, z, 1).start()

    def own_hops(which):
        for p in which:
            pass_on(p, z, 0, True)

    def both(distance, task):
        for way in (1, 0) if distance else (1,):
            zz = z - distance if way else z + distance
            pl.when((zz >= 0) & (zz < seqs))(functools.partial(task, zz, way))

    def line(which, distance):
        def task(zz, way):
            for p in which:
                line_copy(p, zz, way).wait_recv()

                @pl.when((z < seqs - 1) if way else (z > 0))
                def _():
                    line_copy(p, zz, way).start()

                pass_on(p, zz, 0)

        both(distance, task)

    def hops(which, distance, levels=range(bits)):
        def task(zz, way):
            for at in levels:
                for p in which:
                    for mask in masks:
                        if level(p, mask) == at:
                            b = pieces[p][3][at]
                            hop_copy(p, zz, mask & ~(1 << b), b).wait_recv()
                            pass_on(p, zz, mask)

        both(distance, task)

    def finish_line(which):
        def task(zz, _):
            for p in which:

                @pl.when((zz <= z) & (z < seqs - 1))
                def _():
                    line_copy(p, zz, 1).wait_send()

                @pl.when((zz >= z) & (z > 0))
                def _():
                    line_copy(p, zz, 0).wait_send()

            return 0

        lax.fori_loop(0, seqs, task, 0)

    def finish_hops(which, distance):
        def task(zz, _):
            for p in which:
                for mask in masks:
                    for b in later(p, mask):
                        hop_copy(p, zz, mask, b).wait_send()
                    if mask or distance:
                        swap_copy(p, zz, mask).wait()

        both(distance, task)

    return own_line, own_hops, line, hops, finish_line, finish_hops


def first_gather_kernel(seqs, bits, pieces, early, *refs):
    tokens, segments, gate, up, qkv, out, norm, down = refs[:8]
    x_out, segments_out, qkv_all, rest_all, down_all = refs[8:13]
    qkv_two, rest_two, down_two, qkv_chip, rest_chip, down_chip, core_sem, own_sem, token_sem, segment_sem = refs[13:23]
    z, chip, core = place()
    wholes = (qkv_all, rest_all, down_all)
    chips = (qkv_chip, rest_chip, down_chip)
    own_line, own_hops, line, hops, finish_line, finish_hops = gatherer(seqs, bits, pieces, wholes, *refs[23:])
    seq_count = tokens.shape[0]
    token_begin, token_came, token_sent = departs(
        seqs, seq_count, lambda s, _: tokens.at[s], lambda n: x_out.at[n], token_sem
    )
    segment_begin, segment_came, segment_sent = departs(
        seqs, seq_count, lambda s, _: segments.at[s], lambda n: segments_out.at[n], segment_sem
    )
    greet(sum_peers(bits) + column_peers(seqs))
    segment_begin()
    at = 0
    for part in (gate, up, out, norm):
        rest_two[core, :, at : at + part.shape[1]] = part[...]
        at += part.shape[1]
    qkv_two[core] = qkv[...]
    down_two[core] = down[...]
    twos = (qkv_two, rest_two, down_two)
    first = [
        pltpu.make_async_remote_copy(
            two.at[core], two.at[core], core_sem.at[0, i], core_sem.at[1, i],
            device_id={"fsdp": 2 * chip + 1 - core}, device_id_type=MESH_ID,
        )
        for i, two in enumerate(twos)
    ]
    for copy in first:
        copy.start()
    own = [
        pltpu.make_async_copy(chip_ref, whole.at[z, chip], own_sem.at[i])
        for i, (chip_ref, whole) in enumerate(zip(chips, wholes))
    ]
    for i, copy in enumerate(first):
        copy.wait()
        chips[i][...] = twos[i][...].reshape(chips[i].shape).astype(jnp.bfloat16)
        own[i].start()
    rest = [p for p in range(len(pieces)) if p not in early]
    own[0].wait()
    own_line(early)
    own_hops(early)
    own[1].wait()
    own[2].wait()
    own_hops(rest)
    for distance in range(1, seqs):
        line(early, distance)
        if distance == 1:
            token_begin()
        hops(early, distance - 1)
    hops(rest, 0)
    hops(early, seqs - 1)
    finish_line(early)
    for distance in range(seqs):
        finish_hops(early, distance)
    finish_hops(rest, 0)
    for n in range(seq_count):
        token_came(n)
        segment_came(n)
    token_sent()
    segment_sent()


def gather_pieces(bits, qkv, rest, down, rows):
    upward, downward = tuple(range(bits)), tuple(reversed(range(bits)))
    cut = qkv // 512 * 128
    load = down.shape[1] // 2 * down.shape[0] // rows
    other = max(128, ((rest // 2 + load) // 2 - load) // 128 * 128)
    return (
        (0, 0, cut, upward),
        (0, cut, qkv // 2 - cut, downward),
        (1, 0, other, upward),
        (2, 0, down.shape[1] // 2, upward),
        (1, other, rest // 2 - other, downward),
    )


def first_gather(shape, tokens, segments, gate, up, qkv, out, norm, down):
    seqs, chips = shape["seq"], shape["fsdp"] // 2
    bits = chips.bit_length() - 1
    rows, rows_down = gate.shape[0], down.shape[0]
    rest = sum(part.shape[1] for part in (gate, up, out, norm))
    pieces = gather_pieces(bits, qkv.shape[1], rest, down, rows)
    seq_count = tokens.shape[0]
    dma = pltpu.SemaphoreType.DMA
    low = jnp.bfloat16
    any_space = pl.BlockSpec(memory_space=pl.ANY)
    vmem = pl.BlockSpec(memory_space=pltpu.VMEM)
    forms = ((rows, qkv.shape[1]), (rows, rest), (rows_down, down.shape[1]))
    *outs, = pl.pallas_call(
        functools.partial(first_gather_kernel, seqs, bits, pieces, (0, 1)),
        out_shape=[
            jax.ShapeDtypeStruct(tokens.shape, low),
            jax.ShapeDtypeStruct(segments.shape, jnp.int32),
            *(jax.ShapeDtypeStruct((seqs, chips, 2 * n, cols), low) for n, cols in forms),
        ],
        in_specs=[any_space, any_space, *[vmem] * 6],
        out_specs=[any_space] * 5,
        scratch_shapes=[
            *(pltpu.VMEM((2, *form), jnp.float32) for form in forms),
            *(pltpu.VMEM((2 * n, cols), low) for n, cols in forms),
            dma((2, 3)),
            dma((3,)),
            dma((3, seq_count)),
            dma((3, seq_count)),
            *gatherer_scratch(seqs, bits, len(pieces)),
        ],
        compiler_params=pltpu.CompilerParams(collective_id=0, has_side_effects=True, vmem_limit_bytes=48 << 20),
        name="first_gather",
    )(tokens, segments, gate, up, qkv, out, norm, down)
    return outs, pieces[2:]


def hop_masks(order, stage):
    gone = sum(1 << b for b in order[:stage])
    return [m for m in range(1 << len(order)) if (m >> order[stage]) & 1 and not m & gone]


def hop_slot(order, stage, mask):
    return [m ^ (1 << order[stage]) for m in hop_masks(order, stage)].index(mask)


def z_low(zm):
    return (zm & -zm).bit_length() - 1


def span(pieces, group):
    return pieces[group[0]][0], sum(pieces[p][1] for p in group)


def reducer_scratch(seqs, bits, pieces, groups, rows, width):
    dma = pltpu.SemaphoreType.DMA
    low = jnp.bfloat16
    line_bits = seqs.bit_length() - 1
    hops = [
        pltpu.VMEM((seqs, len(hop_masks(order, stage)), rows, cols), low)
        for _, cols, order in pieces
        for stage in range(bits)
    ]
    lines = [
        pltpu.VMEM((seqs >> (k + 1), rows, span(pieces, group)[1]), low) for group in groups for k in range(line_bits)
    ]
    most = 1 << (bits - 1)
    return [
        pltpu.VMEM((2, rows // 2, width), jnp.float32),
        pltpu.VMEM((rows // 2, width), jnp.float32),
        dma((2, seqs, 1 << bits)),
        dma((2, len(pieces), bits, seqs, most)),
        dma((2, len(groups), line_bits, seqs)),
        dma((2,)),
        *hops,
        *lines,
    ]


def reducer(seqs, bits, pieces, groups, away, keep, got, halves_ref, swapped, core_sem, hop_sem, line_sem, swap_sem, *buffers):
    z, chip, core = place()
    rows = keep.shape[2]
    half = rows // 2
    line_bits = seqs.bit_length() - 1
    sibling = {"fsdp": 2 * chip + 1 - core}
    masks = range(1 << bits)
    hop = lambda p, stage: buffers[p * bits + stage]
    line = lambda g, k: buffers[len(pieces) * bits + g * line_bits + k]

    def remote(source, target, sems, index, device):
        return pltpu.make_async_remote_copy(
            source, target, sems.at[(0, *index)], sems.at[(1, *index)], device_id=device, device_id_type=MESH_ID
        )

    def core_copy(zm, mask):
        at = (chip_at(z, zm), chip_at(chip, mask))
        return remote(away.at[at], got.at[at], core_sem, (zm, mask), sibling)

    def hop_copy(p, stage, zm, mask):
        first, cols, order = pieces[p]
        slot = hop_slot(order, stage, mask ^ (1 << order[stage]))
        return remote(
            got.at[chip_at(z, zm), chip_at(chip, mask), :, pl.ds(first, cols)],
            hop(p, stage).at[zm, slot],
            hop_sem,
            (p, stage, zm, slot),
            {"fsdp": 2 * chip_at(chip, 1 << order[stage]) + core},
        )

    def line_copy(g, zm):
        k = z_low(zm)
        slot = zm >> (k + 1)
        return remote(
            got.at[chip_at(z, zm), chip, :, pl.ds(*span(pieces, groups[g]))],
            line(g, k).at[slot],
            line_sem,
            (g, k, slot),
            {"seq": chip_at(z, 1 << k)},
        )

    def total(p, zm, mask, stages, lines=0):
        first, cols, order = pieces[p]
        where = (chip_at(z, zm), chip_at(chip, mask), slice(None), pl.ds(first, cols))
        value = keep[where].astype(jnp.float32) + got[where].astype(jnp.float32)
        for stage in range(stages):
            value = value + hop(p, stage)[zm, hop_slot(order, stage, mask)].astype(jnp.float32)
        if lines:
            g = [n for n, group in enumerate(groups) if p in group][0]
            here = pl.ds(first - span(pieces, groups[g])[0], cols)
            for k in range(lines):
                value = value + line(g, k)[zm >> (k + 1), :, here].astype(jnp.float32)
        return value

    def come(g, stage, zm):
        for p in groups[g]:
            for mask in hop_masks(pieces[p][2], stage):
                hop_copy(p, stage, zm, mask).wait_recv()

    def come_line(g, zm, lines):
        for k in range(lines):
            line_copy(g, zm | (1 << k)).wait_recv()

    def start():
        for zm in (*range(1, seqs), 0):
            for mask in reversed(masks):
                core_copy(zm, mask).start()

    def hop_task(g, stage, zm):
        if stage:
            come(g, stage - 1, zm)
        elif away is not None:
            for mask in masks:
                core_copy(zm, mask).wait_recv()
        for p in groups[g]:
            first, cols, order = pieces[p]
            for mask in hop_masks(order, stage):
                got[chip_at(z, zm), chip_at(chip, mask), :, pl.ds(first, cols)] = total(p, zm, mask, stage).astype(
                    jnp.bfloat16
                )
                hop_copy(p, stage, zm, mask).start()

    def line_task(g, zm):
        k = z_low(zm)
        come(g, bits - 1, zm)
        come_line(g, zm, k)
        for p in groups[g]:
            first, cols, _ = pieces[p]
            got[chip_at(z, zm), chip, :, pl.ds(first, cols)] = total(p, zm, 0, bits, k).astype(jnp.bfloat16)
        line_copy(g, zm).start()

    def task(g, kind, zm):
        if kind == bits:
            line_task(g, zm)
        else:
            hop_task(g, kind, zm)

    def finish():
        for g, group in enumerate(groups):
            come(g, bits - 1, 0)
            come_line(g, 0, line_bits)
            for p in group:
                first, cols, _ = pieces[p]
                value = total(p, 0, 0, bits, line_bits)
                halves_ref[0, :, pl.ds(first, cols)] = value[:half]
                halves_ref[1, :, pl.ds(first, cols)] = value[half:]
        swap = remote(halves_ref.at[1 - core], swapped, swap_sem, (), sibling)
        swap.start()
        for zm in range(seqs):
            if away is not None:
                for mask in masks:
                    core_copy(zm, mask).wait_send()
            for p, (_, _, order) in enumerate(pieces):
                for stage in range(bits):
                    for mask in hop_masks(order, stage):
                        hop_copy(p, stage, zm, mask).wait_send()
            if zm:
                for g in range(len(groups)):
                    line_copy(g, zm).wait_send()
        swap.wait()

    return start, task, finish


GROUPS = ((0, 1), (2, 3))


def sum_pieces(units, tall, out, bits):
    upward, downward = tuple(range(bits)), tuple(reversed(range(bits)))
    cut = (tall + out) // 256 * 128
    half = units // 2
    return (
        (0, half, upward),
        (half, half, downward),
        (units, cut, upward),
        (units + cut, tall + out - cut, downward),
    )


def back_kernel(
    seqs, bits, pieces, plan, tiles, talls, fold, turns,
    hid_ref, att_ref, branch_ref, dff_ref, sums_ref, mixed_ref, dgate_ref, dup_ref,
    q_ref, k0, v0, k1, v1, p_ref, inv_ref, do_ref, result_hbm,
    dq_ref, own_ref, sib_ref, sum_ref, output_hbm,
    keep, got, away_wide, away_tall, away_sem, kt, va, dk, dv, sib, sib_sem, back_sem, *shared,
):
    z, chip, core = place()
    sibling = {"fsdp": 2 * chip + 1 - core}
    step = pl.program_id(0)
    last = pl.num_programs(0) - 1
    rows = keep.shape[2]
    chips = seqs << bits
    low = jnp.bfloat16
    width = att_ref.shape[1]
    tile = dgate_ref.shape[1]
    tall = fold * width // 2
    out_cols = (width + NORM_COLS) // 2
    units = 2 * tiles * tile
    first_steps = 4 * tiles + talls + 1
    per_z = 1 << bits
    _, sum_task, finish = reducer(seqs, bits, pieces, GROUPS, None, keep, got, *shared)
    seq_count, local_len = output_hbm.shape[:2]
    back_begin, back_end = returns(
        seqs, seq_count, lambda n: result_hbm.at[pl.ds(n * local_len, local_len)], output_hbm, back_sem, local_len
    )

    def wide_copy(n, slot):
        at = n * tile if n is not None else units + tall
        cols = pl.ds(pl.multiple_of(at, 128), tile)
        return pltpu.make_async_remote_copy(
            away_wide.at[slot], got.at[:, :, :, cols],
            away_sem.at[0, n if n is not None else 2 * tiles], away_sem.at[1, n if n is not None else 2 * tiles],
            device_id=sibling, device_id_type=MESH_ID,
        )

    def tall_copy(n):
        count = chips // talls
        at = n * count
        index = 2 * tiles + 1 + n
        return pltpu.make_async_remote_copy(
            away_tall.at[lax.rem(n, 2)],
            got.at[lax.div(at, per_z), pl.ds(lax.rem(at, per_z), count), :, pl.ds(units, tall)],
            away_sem.at[0, index], away_sem.at[1, index],
            device_id=sibling, device_id_type=MESH_ID,
        )

    @pl.when(step == 0)
    def _():
        greet(sum_peers(bits) + column_peers(seqs))
        for n in range(seq_count):
            back_begin(n)

    for n, ref in enumerate((dgate_ref, dup_ref)):

        @pl.when((step >= n * tiles) & (step < (n + 1) * tiles))
        def _():
            slot = lax.rem(step, 2)

            @pl.when(step >= 2)
            def _():
                wide_copy(step - 2, slot).wait_send()

            away_wide[slot] = dotf(hid_ref[...], ref[...]).astype(low).reshape(away_wide.shape[1:])
            wide_copy(step, slot).start()

        @pl.when((step >= (2 + n) * tiles) & (step < (3 + n) * tiles))
        def _():
            cols = pl.ds(pl.multiple_of((step - 2 * tiles) * tile, 128), tile)
            keep[:, :, :, cols] = dotf(hid_ref[...], ref[...]).astype(low).reshape(away_wide.shape[1:])

    n_tall = step - 4 * tiles

    def sides(halves, mine, other):
        for side, value in enumerate(halves):

            @pl.when(core == side)
            def _():
                mine(value)

            @pl.when(core != side)
            def _():
                other(value)

    @pl.when((n_tall >= 0) & (n_tall < talls))
    def _():
        @pl.when(n_tall >= 2)
        def _():
            tall_copy(n_tall - 2).wait_send()

        value = dotf(mixed_ref[...], dff_ref[...], TN)
        own = rows // 2
        count = chips // talls
        at = n_tall * count

        def folded(part):
            return jnp.concatenate(
                [
                    jnp.concatenate([part[(b * fold + a) * own : (b * fold + a + 1) * own] for a in range(fold)], 1)
                    for b in range(part.shape[0] // (fold * own))
                ],
                0,
            ).astype(low).reshape(count, rows, tall)

        def mine(value):
            keep[lax.div(at, per_z), pl.ds(lax.rem(at, per_z), count), :, units : units + tall] = value

        def other(value):
            away_tall[lax.rem(n_tall, 2)] = value

        sides([folded(value[:, : width // 2]), folded(value[:, width // 2 :])], mine, other)
        tall_copy(n_tall).start()

    @pl.when(n_tall == talls)
    def _():
        wide_copy(2 * tiles - 2, 0).wait_send()
        value = dotf(att_ref[...], branch_ref[...], TN)
        pad = jnp.zeros((NORM_COLS - sums_ref.shape[0], width), jnp.float32)
        value = jnp.concatenate([value, jnp.concatenate([sums_ref[...], pad], 0).T], 1).astype(low)

        def mine(value):
            keep[:, :, :, units + tall :] = value

        def other(value):
            away_wide[0] = value

        sides(
            [value[:, n * out_cols : (n + 1) * out_cols].reshape(away_wide.shape[1:]) for n in range(2)], mine, other
        )
        wide_copy(None, 0).start()

    @pl.when(step == 4 * tiles)
    def _():
        for n in range(2 * tiles):
            wide_copy(n, n % 2).wait_recv()

    @pl.when(step == first_steps)
    def _():
        wide_copy(2 * tiles - 1, 1).wait_send()
        wide_copy(None, 0).wait()
        for n in range(talls):
            tall_copy(n).wait_recv()
        for n in (talls - 2, talls - 1):
            tall_copy(n).wait_send()

    for at, tasks in plan.items():

        @pl.when(step == at)
        def _():
            for one in tasks:
                sum_task(*one)

    attention = step - first_steps

    @pl.when(attention >= 0)
    def _():
        attend_back_block(
            turns, lax.div(attention, turns), lax.rem(attention, turns),
            q_ref, k0, v0, k1, v1, p_ref, att_ref, inv_ref, do_ref, dq_ref, own_ref, sib_ref, kt, va, dk, dv, sib, sib_sem,
        )

    @pl.when(step == last)
    def _():
        finish()
        back_end()
        halves_ref, swapped = shared[0], shared[1]
        sum_ref[core] = halves_ref[core]
        sum_ref[1 - core] = swapped[...]
        pairs = width // 128
        for pair in range(pairs):
            if pair >= pairs - 2:
                sib_copy(sib, sib_ref, sib_sem, pair).wait_send()
            sib_copy(sib, sib_ref, sib_sem, pair).wait_recv()


def sib_copy(sib, sib_ref, sib_sem, pair):
    z, chip, core = place()
    return pltpu.make_async_remote_copy(
        sib.at[lax.rem(pair, 2)],
        sib_ref.at[:, :, pl.ds(pl.multiple_of(pair * 128, 128), 128)],
        sib_sem.at[0, pair],
        sib_sem.at[1, pair],
        device_id={"fsdp": 2 * chip + 1 - core},
        device_id_type=MESH_ID,
    )


def attend_back_block(
    turns, j, i,
    q_ref, k0, v0, k1, v1, p_ref, att_ref, inv_ref, do_ref, dq_ref, own_ref, sib_ref, kt, va, dk, dv, sib, sib_sem,
):
    part = k0.shape[0]
    unit = q_ref.shape[0]
    lane_k = lax.broadcasted_iota(jnp.int32, (part, 128), 1)

    @pl.when(i == 0)
    def _():
        for n, (k_ref, v_ref) in enumerate(((k0, v0), (k1, v1))):
            k, v = k_ref[...], v_ref[...]
            zero, one = jnp.zeros_like(v), jnp.ones_like(v)
            here = slice(n * part, (n + 1) * part)
            kt[0, :, here] = jnp.where(lane_k < HEAD_DIM, k, zero).T
            kt[1, :, here] = jnp.where(lane_k < HEAD_DIM, zero, k).T
            va[0, here] = jnp.where(lane_k < HEAD_DIM, v, jnp.where(lane_k < HEAD_DIM + 3, one, zero))
            va[1, here] = jnp.where(lane_k >= HEAD_DIM, v, jnp.where(lane_k < 3, one, zero))
        dk[...] = jnp.zeros_like(dk)
        dv[...] = jnp.zeros_like(dv)

    lane = lax.broadcasted_iota(jnp.int32, (unit, 128), 1)
    q = q_ref[...]
    o = att_ref[pl.ds(pl.multiple_of(i * unit, unit), unit), pl.ds(pl.multiple_of(j * 128, 128), 128)]
    dof = do_ref[...].astype(jnp.float32) * inv_ref[...]
    prod = dof * o.astype(jnp.float32)
    dob = dof.astype(jnp.bfloat16)
    zero = jnp.zeros_like(dob)
    turned = None
    for h in range(2):
        mine = lane < HEAD_DIM if h == 0 else lane >= HEAD_DIM
        base = HEAD_DIM if h == 0 else 0
        d = -jnp.sum(jnp.where(mine, prod, 0.0), axis=1, keepdims=True)
        d1 = d.astype(jnp.bfloat16).astype(jnp.float32)
        d2 = (d - d1).astype(jnp.bfloat16).astype(jnp.float32)
        d3 = d - d1 - d2
        extra = jnp.where(
            lane == base, d1, jnp.where(lane == base + 1, d2, jnp.where(lane == base + 2, d3, 0.0))
        ).astype(jnp.bfloat16)
        p = p_ref[h]
        ds = (p.astype(jnp.float32) * dotf(va[h], jnp.where(mine, dob, extra), NT)).astype(jnp.bfloat16)
        dv[...] += dotf(p, jnp.where(mine, dob, zero))
        dk[...] += dotf(ds, jnp.where(mine, q, zero))
        new = dotf(kt[h], ds)
        turned = new if turned is None else turned + new
    dq_ref[...] = turned.T * (1.0 / math.sqrt(HEAD_DIM))

    @pl.when(i == turns - 1)
    def _():
        @pl.when(j >= 2)
        def _():
            sib_copy(sib, sib_ref, sib_sem, j - 2).wait_send()

        for n, total in enumerate((dk, dv)):
            own_ref[n] = total[:part]
            sib[lax.rem(j, 2), n] = total[part:].astype(jnp.bfloat16)
        sib_copy(sib, sib_ref, sib_sem, j).start()


def backward(
    shape, plan, hidden_t, attended, branch, d_ff, sums, mixed, d_gate, d_up, q, own, sib, p, inv, do, result, seq_count,
    tiles=3, talls=8, unit=256,
):
    seqs, bits = shape["seq"], (shape["fsdp"] // 2).bit_length() - 1
    chips = seqs << bits
    rows, width = attended.shape
    units = mixed.shape[1]
    fold = units // width
    tile = units // 2 // tiles
    tall, out_cols = fold * width // 2, (width + NORM_COLS) // 2
    cols = units + tall + out_cols
    pieces = sum_pieces(units, tall, out_cols, bits)
    sum_rows = width // chips
    pairs, turns, part = width // 128, rows // unit, own.shape[0]
    first_steps, second_steps = 4 * tiles + talls + 1, pairs * turns
    steps = first_steps + second_steps
    low = jnp.bfloat16
    once = pl.Buffered(1)
    full = lambda array: pl.BlockSpec(array.shape, lambda s: (0, 0), pipeline_mode=once)

    def later(s):
        return lax.div(s + second_steps, steps)

    def pair_of(s):
        return lax.div((s - first_steps) * later(s), turns)

    def turn_of(s):
        return lax.rem((s - first_steps) * later(s), turns)

    def reached(s, first, count):
        return sum(lax.div(s + steps - first - k, steps) for k in range(1, count))

    def half_tile(away_at, keep_at):
        def at(s):
            core = lax.rem(lax.axis_index("fsdp"), 2)
            kept = lax.div(s + steps - keep_at, steps)
            t = reached(s, away_at, tiles) * (1 - kept) + reached(s, keep_at, tiles) * kept
            return (0, (1 - core + (2 * core - 1) * kept) * tiles + t)

        return pl.BlockSpec((rows, tile), at)

    row = pl.BlockSpec((unit, 128), lambda s: (turn_of(s), pair_of(s)))
    kv = [
        pl.BlockSpec((part, 128), lambda s: (0, 2 * pair_of(s))),
        pl.BlockSpec((part, 128), lambda s: (0, 2 * pair_of(s) + 1)),
    ]
    any_space = pl.BlockSpec(memory_space=pl.ANY)
    dma = pltpu.SemaphoreType.DMA
    form = (seqs, 1 << bits, sum_rows)
    return pl.pallas_call(
        functools.partial(back_kernel, seqs, bits, pieces, plan, tiles, talls, fold, turns),
        grid=(steps,),
        in_specs=[
            full(hidden_t), full(attended), full(branch), full(d_ff), full(sums),
            pl.BlockSpec((rows, units // talls), lambda s: (0, reached(s, 4 * tiles, talls))),
            half_tile(0, 2 * tiles), half_tile(tiles, 3 * tiles),
            row, *kv, *kv, pl.BlockSpec((2, 2 * part, unit), lambda s: (pair_of(s), 0, turn_of(s))), row, row, any_space,
        ],
        out_specs=[
            row,
            pl.BlockSpec((2, part, 128), lambda s: (0, 0, pair_of(s))),
            any_space,
            pl.BlockSpec((2, sum_rows // 2, cols), lambda s: (0, 0, 0)),
            any_space,
        ],
        out_shape=[
            jax.ShapeDtypeStruct((rows, width), jnp.float32),
            jax.ShapeDtypeStruct((2, part, width), jnp.float32),
            jax.ShapeDtypeStruct((2, part, width), low),
            jax.ShapeDtypeStruct((2, sum_rows // 2, cols), jnp.float32),
            jax.ShapeDtypeStruct((seq_count, rows // seq_count, width), low),
        ],
        scratch_shapes=[
            pltpu.VMEM((*form, cols), low),
            pltpu.VMEM((*form, cols), low),
            pltpu.VMEM((2, *form, tile), low),
            pltpu.VMEM((2, chips // talls, sum_rows, tall), low),
            dma((2, 2 * tiles + 1 + talls)),
            pltpu.VMEM((2, 128, 2 * part), low),
            pltpu.VMEM((2, 2 * part, 128), low),
            pltpu.VMEM((2 * part, 128), jnp.float32),
            pltpu.VMEM((2 * part, 128), jnp.float32),
            pltpu.VMEM((2, 2, part, 128), low),
            dma((2, pairs)),
            dma((3, seq_count)),
            *reducer_scratch(seqs, bits, pieces, GROUPS, sum_rows, cols),
        ],
        compiler_params=pltpu.CompilerParams(collective_id=1, has_side_effects=True, vmem_limit_bytes=63 << 20),
        name="backward",
    )(hidden_t, attended, branch, d_ff, sums, mixed, d_gate, d_up, q, own, own, sib, sib, p, inv, do, result)


def tail_kernel(
    seqs, bits, pieces,
    cos_ref, sin_ref, dq_ref, own_ref, got_ref, wq_ref, wk_ref, wv_ref, dr_ref, x_ref, sum_ref,
    back_ref, qsum_ref, square_ref,
    dproj, dx, keep, got, away, plane, line_sum, back_sem, plane_sem, total_sem, *shared,
):
    z, chip, core = place()
    f = 2 * chip + core
    line = 2 << bits
    block, width = dr_ref.shape
    i = pl.program_id(0)
    blocks = dx.shape[0]
    low = jnp.bfloat16
    start, sum_task, finish = reducer(seqs, bits, pieces, ((0, 1),), away, keep, got, *shared)
    back_begin, back_end = returns(seqs, back_ref.shape[0], lambda n: dx.at[n], back_ref, back_sem, block)

    @pl.when(i == 0)
    def _():
        greet(plane_peers(line) + column_peers(seqs))

    cosine, sine = cos_ref[...], -sin_ref[...]
    grads = (
        turn(dq_ref[...], cosine, sine).astype(low),
        turn(own_ref[0] + got_ref[0].astype(jnp.float32), cosine, sine).astype(low),
        (own_ref[1] + got_ref[1].astype(jnp.float32)).astype(low),
    )
    value = dr_ref[...]
    rows = pl.ds(pl.multiple_of(i * block, block), block)
    for n, (grad, w_ref) in enumerate(zip(grads, (wq_ref, wk_ref, wv_ref))):
        dproj[rows, n * width : (n + 1) * width] = grad
        value = value + dotf(grad, w_ref[...], NT)
    dx[i] = value.astype(low)
    for n in range(blocks):

        @pl.when(i == n)
        def _():
            back_begin(n)

    @pl.when(i == blocks - 1)
    def _():
        half = keep.shape[-1]
        tile = 384
        for target, side in ((away, 1 - core), (keep, core)):
            for n in range(half // tile):
                cols = pl.ds(pl.multiple_of(side * half + n * tile, 128), tile)
                grad = dotf(x_ref[...], dproj[:, cols], TN).astype(low)
                target[:, :, :, n * tile : (n + 1) * tile] = grad.reshape(target.shape[:3] + (tile,))
            if target is away:
                start()
        for task in sum_plan(seqs, bits):
            sum_task(0, *task)
        finish()
        halves_ref, swapped = shared[0], shared[1]
        qsum_ref[core] = halves_ref[core]
        qsum_ref[1 - core] = swapped[...]
        squares = jnp.sum(jnp.square(sum_ref[...])) + jnp.sum(jnp.square(qsum_ref[...]))
        plane[f] = jnp.zeros(plane.shape[1:], jnp.float32) + squares

        def plane_copy(to, source):
            return pltpu.make_async_remote_copy(
                plane.at[source], plane.at[source], plane_sem.at[0, to], plane_sem.at[1, source],
                device_id={"fsdp": to}, device_id_type=MESH_ID,
            )

        def total_copy(to, source):
            return pltpu.make_async_remote_copy(
                line_sum.at[source], line_sum.at[source], total_sem.at[0, to], total_sem.at[1, source],
                device_id={"seq": to}, device_id_type=MESH_ID,
            )

        for k in range(1, line):
            plane_copy(lax.rem(f + k, line), f).start()
        for k in range(1, line):
            plane_copy(lax.rem(f + k, line), lax.rem(f + k, line)).wait_recv()
        line_sum[z] = sum(plane[n] for n in range(line))
        for k in range(1, seqs):
            total_copy(lax.rem(z + k, seqs), z).start()
        for k in range(1, seqs):
            total_copy(lax.rem(z + k, seqs), lax.rem(z + k, seqs)).wait_recv()
        square_ref[...] = sum(line_sum[n] for n in range(seqs))
        for k in range(1, line):
            plane_copy(lax.rem(f + k, line), f).wait_send()
        for k in range(1, seqs):
            total_copy(lax.rem(z + k, seqs), z).wait_send()
        back_end()


def tail(shape, cosine, sine, d_query, own, got, wide, first, d_resid, x, sums, seq_count, block=256):
    seqs, line = shape["seq"], shape["fsdp"]
    bits = (line // 2).bit_length() - 1
    rows, width = x.shape
    low = jnp.bfloat16
    sum_rows, sum_cols = width // (seqs * line // 2), 3 * width // 2
    pieces = halves_of(sum_cols, bits)
    dma = pltpu.SemaphoreType.DMA
    row = lambda cols: pl.BlockSpec((block, cols), lambda i: (i, 0))
    pair = pl.BlockSpec((2, block, width), lambda i: (0, i, 0))
    once = pl.Buffered(1)
    weight = lambda n: pl.BlockSpec((width, width), lambda i, n=n: (0, first + n), pipeline_mode=once)
    blocks = rows // block
    return pl.pallas_call(
        functools.partial(tail_kernel, seqs, bits, pieces),
        grid=(blocks,),
        in_specs=[
            row(128), row(128), row(width), pair, pair, weight(0), weight(1), weight(2), row(width),
            pl.BlockSpec(x.shape, lambda i: (0, 0), pipeline_mode=once),
            pl.BlockSpec(sums.shape, lambda i: (0, 0, 0), pipeline_mode=once),
        ],
        out_specs=[
            pl.BlockSpec(memory_space=pl.ANY),
            pl.BlockSpec((2, sum_rows // 2, sum_cols), lambda i: (0, 0, 0)),
            pl.BlockSpec((8, 128), lambda i: (0, 0)),
        ],
        out_shape=[
            jax.ShapeDtypeStruct((seq_count, rows // seq_count, width), low),
            jax.ShapeDtypeStruct((2, sum_rows // 2, sum_cols), jnp.float32),
            jax.ShapeDtypeStruct((8, 128), jnp.float32),
        ],
        scratch_shapes=[
            pltpu.VMEM((rows, 3 * width), low),
            pltpu.VMEM((blocks, block, width), low),
            *[pltpu.VMEM((seqs, 1 << bits, sum_rows, sum_cols), low)] * 3,
            pltpu.VMEM((line, 8, 128), jnp.float32),
            pltpu.VMEM((seqs, 8, 128), jnp.float32),
            dma((3, blocks)),
            dma((2, line)),
            dma((2, seqs)),
            *reducer_scratch(seqs, bits, pieces, ((0, 1),), sum_rows, sum_cols),
        ],
        compiler_params=pltpu.CompilerParams(collective_id=2, has_side_effects=True, vmem_limit_bytes=60 << 20),
        name="tail",
    )(cosine, sine, d_query, own, got, wide, wide, wide, d_resid, x, sums)


def adam_kernel(sum_ref, qsum_ref, square_ref, back_ref, *refs):
    states, outs = refs[:18], refs[18:]
    back_out, norm_out = outs[24:]
    back_out[...] = back_ref[...].astype(jnp.float32)
    norm = jnp.sqrt(square_ref[0:1, 0:1])
    norm_out[...] = norm
    clip = jnp.minimum(1.0, MAX_NORM / (norm + 1e-06))
    rows, units = states[2].shape
    width = states[1].shape[1]
    out = (width + NORM_COLS) // 2
    take = lambda first, count: jnp.concatenate([sum_ref[n, :, first : first + count] for n in range(2)], 1)
    fold = states[4].shape[0] // rows
    tall = fold * width // 2
    red_out = take(units + tall, out)
    norms = red_out[:, width : width + 128].T[: states[5].shape[0]]
    grads = (
        jnp.concatenate([qsum_ref[0], qsum_ref[1]], 1),
        red_out[:, :width],
        take(0, units // 2),
        take(units // 2, units // 2),
        jnp.concatenate(
            [
                jnp.concatenate([sum_ref[n, :, units + a * (width // 2) : units + (a + 1) * (width // 2)] for n in range(2)], 1)
                for a in range(fold)
            ],
            0,
        ),
        norms,
    )
    for n, grad in enumerate(grads):
        rates = (0.0, NORM_RATE) if n == 5 else (WEIGHT_DECAY, LEARN_RATE)
        outs[n][...] = grad
        new, first, second = adam_update(
            states[n][...], grad, states[6 + n][...], states[12 + n][...], *rates, clip
        )
        outs[6 + n][...] = new
        outs[12 + n][...] = first
        outs[18 + n][...] = second


def adam(sums, qsums, squares, back, states):
    like = lambda array: jax.ShapeDtypeStruct(array.shape, jnp.float32)
    vmem = pl.BlockSpec(memory_space=pltpu.VMEM)
    outs = [like(array) for array in states[:6]] * 4
    outs += [like(back), jax.ShapeDtypeStruct((1, 1), jnp.float32)]
    return pl.pallas_call(
        adam_kernel,
        in_specs=[vmem] * (4 + len(states)),
        out_specs=[vmem] * len(outs),
        out_shape=outs,
        compiler_params=pltpu.CompilerParams(vmem_limit_bytes=56 << 20),
        name="adam",
    )(sums, qsums, squares, back, *states)


def sum_plan(seqs, bits):
    order = sorted(range(seqs), key=lambda zm: (z_low(zm) if zm else seqs, zm))
    found = []
    for n in range(seqs + bits):
        for stage in reversed(range(bits + 1)):
            if 0 <= n - stage < seqs and (stage < bits or order[n - stage]):
                found.append((stage, order[n - stage]))
    return found


def halves_of(cols, bits):
    cut = cols // 256 * 128
    return ((0, cut, tuple(range(bits))), (cut, cols - cut, tuple(reversed(range(bits)))))


def turn(field, cosine, sine):
    width = field.shape[-1]
    reps = width // cosine.shape[-1]
    cosine = jnp.concatenate([cosine] * reps, -1)
    sine = jnp.concatenate([sine] * reps, -1)
    lane = lax.broadcasted_iota(jnp.int32, field.shape, 1)
    half = HEAD_DIM // 2
    other = jnp.where(
        lax.rem(lane, HEAD_DIM) < half, pltpu.roll(field, width - half, 1), pltpu.roll(field, half, 1)
    )
    return field * cosine + other * sine


def project_kernel(x_ref, wq_ref, wk_ref, wv_ref, cos_ref, sin_ref, code_ref, q_ref, kv_ref):
    x, cosine, sine = x_ref[...], cos_ref[...], sin_ref[...]
    width = x.shape[-1]
    query = turn(dotf(x, wq_ref[...]), cosine, sine).astype(jnp.bfloat16)
    q_ref[...] = query * jnp.bfloat16(1.0 / math.sqrt(HEAD_DIM))
    keys = turn(dotf(x, wk_ref[...]), cosine, sine).astype(jnp.bfloat16)
    values = dotf(x, wv_ref[...]).astype(jnp.bfloat16)
    for at in range(0, width, 128):
        kv_ref[:, 2 * at : 2 * at + 128] = keys[:, at : at + 128]
        kv_ref[:, 2 * at + 128 : 2 * at + 256] = values[:, at : at + 128]
    kv_ref[:, 2 * width :] = code_ref[...]


def project(x, wide, first, cosine, sine, code, block=256):
    rows, width = x.shape
    weight = lambda n: pl.BlockSpec((width, width), lambda i, n=n: (0, first + n))
    row = lambda cols: pl.BlockSpec((block, cols), lambda i: (i, 0))
    return pl.pallas_call(
        project_kernel,
        grid=(rows // block,),
        in_specs=[row(width), weight(0), weight(1), weight(2), row(128), row(128), row(128)],
        out_specs=[row(width), row(2 * width + 128)],
        out_shape=[
            jax.ShapeDtypeStruct((rows, width), jnp.bfloat16),
            jax.ShapeDtypeStruct((rows, 2 * width + 128), jnp.bfloat16),
        ],
        compiler_params=pltpu.CompilerParams(vmem_limit_bytes=48 << 20),
        name="project",
    )(x, wide, wide, wide, cosine, sine, code)


def attend_kernel(seqs, bits, pieces, plan, unit, chunk, q_ref, qc_ref, own_ref, code_ref, own_hbm, *refs):
    p_ref, o_ref, inv_ref, sib_hbm, rest_all, down_all = refs[2:8]
    ka, vt, st_ref, sib, kv_sem, keep_sem = refs[8:14]
    own_line, own_hops, line, hops, finish_line, finish_hops = gatherer(
        seqs, bits, pieces, (None, rest_all, down_all), *refs[14:]
    )
    z, chip, core = place()
    part, rows = own_ref.shape[0], q_ref.shape[0]
    keys = 2 * part
    j, pairs = pl.program_id(0), pl.num_programs(0)
    which = range(len(pieces))

    def kv_copy(first, count, n):
        cols = pl.ds(pl.multiple_of(first, 128), count)
        return pltpu.make_async_remote_copy(
            own_hbm.at[:, cols], sib.at[:, cols], kv_sem.at[0, n], kv_sem.at[1, n],
            device_id={"fsdp": 2 * chip + 1 - core}, device_id_type=MESH_ID,
        )

    code_copy = kv_copy(256 * pairs, 128, pairs)
    pair_copy = lambda n: kv_copy(256 * n, 256, n)

    def carry(distance, level=None):
        if level is None:
            line(which, distance)
        else:
            hops(which, distance, (level,))

    @pl.when(j == 0)
    def _():
        greet(sum_peers(bits) + line_peers(seqs))
        code_copy.start()
        pair_copy(0).start()
        own_line(which)
        lax.fori_loop(1, pairs, lambda n, _: (pair_copy(n).start(), 0)[1], 0)
        code_copy.wait_recv()

    def slot(n):
        for at in [at for at in plan if at is not None and at % SLOTS == n]:

            @pl.when(j == at // SLOTS)
            def _():
                for task in plan[at]:
                    carry(*task)

    low_k = lax.broadcasted_iota(jnp.int32, (part, 128), 1) < HEAD_DIM

    pair_copy(j).wait_recv()
    sides = (
        (own_ref[:, :128], code_ref[...], own_ref[:, 128:]),
        (
            sib[:, pl.ds(pl.multiple_of(256 * j, 128), 128)],
            sib[:, sib.shape[1] - 128 :],
            sib[:, pl.ds(pl.multiple_of(256 * j + 128, 128), 128)],
        ),
    )
    for i, (k, kc, v) in enumerate(sides):
        one = jnp.ones_like(v)
        here = slice(i * part, (i + 1) * part)
        ka[0, here] = jnp.where(low_k, k, kc)
        ka[1, here] = jnp.where(low_k, kc, k)
        vt[0, :, here] = jnp.where(low_k, v, one).T
        vt[1, :, here] = jnp.where(low_k, one, v).T
    low_q = lax.broadcasted_iota(jnp.int32, (unit, 128), 1) < HEAD_DIM
    units = [(h, b) for b in range(rows // unit) for h in range(2)]
    results, before = {}, None
    for u, now in enumerate([*units, None]):
        if u < SLOTS:
            slot(u)
        if now is not None:
            h, b = now
            q, qc = q_ref[b * unit : (b + 1) * unit], qc_ref[b * unit : (b + 1) * unit]
            qa = jnp.where(low_q, q, qc) if h == 0 else jnp.where(low_q, qc, q)
        top = total = None
        for c in range(keys // chunk):
            here = slice(c * chunk, (c + 1) * chunk)
            if now is not None:
                s = dotf(ka[h, here], qa, NT)
                st_ref[u % 2, here] = s
                most = jnp.max(s.reshape(chunk // 8, 8, unit), axis=0)
                top = most if top is None else jnp.maximum(top, most)
            if before is not None:
                hb, bb, row_max = before
                p = jnp.exp(st_ref[(u - 1) % 2, here] - row_max).astype(jnp.bfloat16)
                p_ref[hb, here, bb * unit : (bb + 1) * unit] = p
                d = dotf(vt[hb, :, here], p)
                total = d if total is None else total + d
        if before is not None:
            results[before[:2]] = total.T
        before = None if now is None else (h, b, jnp.max(top, axis=0, keepdims=True))
    for b in range(rows // unit):
        r0, r1 = results[(0, b)], results[(1, b)]
        inv = 1.0 / pltpu.roll(jnp.where(low_q, r1, r0), HEAD_DIM, 1)
        inv_ref[b * unit : (b + 1) * unit] = inv
        o_ref[b * unit : (b + 1) * unit] = (jnp.where(low_q, r0, r1) * inv).astype(jnp.bfloat16)

    @pl.when(j == pairs - 1)
    def _():
        keep = pltpu.make_async_copy(sib, sib_hbm, keep_sem)
        keep.start()
        for task in plan[None]:
            carry(*task)
        finish_line(which)
        for distance in range(1, seqs):
            finish_hops(which, distance)
        code_copy.wait_send()
        lax.fori_loop(0, pairs, lambda n, _: (pair_copy(n).wait_send(), 0)[1], 0)
        keep.wait()


def attend_pallas(shape, pieces, plan, q, qc, own, rest_all, down_all, unit=512, chunk=512):
    seqs, bits = shape["seq"], (shape["fsdp"] // 2).bit_length() - 1
    rows, width = q.shape
    pairs = width // 128
    part = own.shape[0]
    low = jnp.bfloat16
    row = pl.BlockSpec((rows, 128), lambda j: (0, j))
    any_space = pl.BlockSpec(memory_space=pl.ANY)
    dma = pltpu.SemaphoreType.DMA
    like = lambda array: jax.ShapeDtypeStruct(array.shape, array.dtype)

    return pl.pallas_call(
        functools.partial(attend_kernel, seqs, bits, pieces, plan, unit, chunk),
        grid=(pairs,),
        in_specs=[
            row,
            pl.BlockSpec((rows, 128), lambda j: (0, 0)),
            pl.BlockSpec((part, 256), lambda j: (0, j)),
            pl.BlockSpec((part, 128), lambda j: (0, 2 * pairs)),
            any_space,
            any_space,
            any_space,
        ],
        out_specs=[pl.BlockSpec((2, 2 * part, rows), lambda j: (j, 0, 0)), row, row, any_space, any_space, any_space],
        out_shape=[
            jax.ShapeDtypeStruct((2 * pairs, 2 * part, rows), low),
            jax.ShapeDtypeStruct((rows, width), low),
            jax.ShapeDtypeStruct((rows, width), jnp.float32),
            like(own),
            like(rest_all),
            like(down_all),
        ],
        input_output_aliases={5: 4, 6: 5},
        scratch_shapes=[
            pltpu.VMEM((2, 2 * part, 128), low),
            pltpu.VMEM((2, 128, 2 * part), low),
            pltpu.VMEM((2, 2 * part, unit), jnp.float32),
            pltpu.VMEM(own.shape, low),
            dma((2, pairs + 1)),
            dma,
            *gatherer_scratch(seqs, bits, len(pieces)),
        ],
        compiler_params=pltpu.CompilerParams(collective_id=3, has_side_effects=True, vmem_limit_bytes=58 << 20),
        name="attend",
    )(q, qc, own, own, own, rest_all, down_all)


def mean_row(field):
    return jnp.mean(field, -1, keepdims=True)


def middle_kernel(
    seqs, seq_count, x_ref, att_ref, cot_hbm, rest_hbm, down_hbm, norms_ref,
    out_ref, dr_ref, branch_ref, datt_ref, hid_ref, mixed_ref, dgate_ref, dup_ref, dff_ref, sums_ref,
    silu_s, slope_s, dy_s, dy_sem, wo_s, wg_s, wu_s, wd_s, weight_sem,
):
    blocks, block = dy_s.shape[:2]
    subs = blocks // seq_count
    begin, came, sent = departs(
        seqs, seq_count, lambda s, sub: cot_hbm.at[s, pl.ds(sub * block, block)], lambda n: dy_s.at[n], dy_sem, subs
    )

    units, width = wd_s.shape
    step = 768
    cuts = [slice(n, n + step) for n in range(0, units, step)]
    out_at = 2 * units
    loads = [pltpu.make_async_copy(rest_hbm.at[:, pl.ds(out_at, width)], wo_s, weight_sem.at[0])]
    for n, cut in enumerate(cuts):
        for m, (source, target) in enumerate(
            (
                (rest_hbm.at[:, pl.ds(cut.start, step)], wg_s.at[:, pl.ds(cut.start, step)]),
                (rest_hbm.at[:, pl.ds(units + cut.start, step)], wu_s.at[:, pl.ds(cut.start, step)]),
                (down_hbm.at[pl.ds(cut.start, step)], wd_s.at[pl.ds(cut.start, step)]),
            )
        ):
            loads.append(pltpu.make_async_copy(source, target, weight_sem.at[1 + 3 * n + m]))

    def ready(first, count):
        @pl.when(pl.program_id(0) == 0)
        def _():
            for load in loads[first : first + count]:
                load.wait()

    @pl.when(pl.program_id(0) == 0)
    def _():
        for load in loads:
            load.start()
        greet(column_peers(seqs))
        begin()

    ready(0, 1)
    gain_one, shift_one, gain_two, shift_two = (norms_ref[n : n + 1] for n in range(4))
    resid_one = x_ref[...].astype(jnp.float32) + dotf(att_ref[...], wo_s[...])
    hidden, normed_one, inv_one = normalize(resid_one, gain_one, shift_one)
    hidden_low = hidden.astype(jnp.bfloat16)
    hid_ref[...] = hidden_low.T
    resid_two = hidden
    for n, cut in enumerate(cuts):
        ready(1 + 3 * n, 3)
        gate = dotf(hidden_low, wg_s[:, cut])
        up = dotf(hidden_low, wu_s[:, cut])
        sig = jax.nn.sigmoid(gate)
        silu = gate * sig
        mixed = (silu * up).astype(jnp.bfloat16)
        silu_s[:, cut] = silu
        slope_s[:, cut] = up * sig * (1.0 + gate * (1.0 - sig))
        mixed_ref[:, cut] = mixed
        resid_two = resid_two + dotf(mixed, wd_s[cut, :])
    result, normed_two, inv_two = normalize(resid_two, gain_two, shift_two)
    out_ref[...] = result.astype(jnp.bfloat16)
    now = row_order(seq_count, subs, pl.program_id(0))
    came(now)
    dy = dy_s[now].astype(jnp.float32)
    d_two = normalize_back(dy, normed_two, inv_two, gain_two)
    d_ff = d_two.astype(jnp.bfloat16)
    dff_ref[...] = d_ff
    d_hidden = d_two
    for cut in cuts:
        d_mixed = dotf(d_ff, wd_s[cut, :], NT)
        d_up = (d_mixed * silu_s[:, cut]).astype(jnp.bfloat16)
        d_gate = (d_mixed * slope_s[:, cut]).astype(jnp.bfloat16)
        dup_ref[:, cut] = d_up
        dgate_ref[:, cut] = d_gate
        d_hidden = d_hidden + dotf(d_gate, wg_s[:, cut], NT) + dotf(d_up, wu_s[:, cut], NT)
    d_one = normalize_back(d_hidden, normed_one, inv_one, gain_one)
    dr_ref[...] = d_one
    branch = d_one.astype(jnp.bfloat16)
    branch_ref[...] = branch
    datt_ref[...] = dotf(branch, wo_s[...], NT).astype(jnp.bfloat16)

    @pl.when(pl.program_id(0) == 0)
    def _():
        sums_ref[...] = jnp.zeros_like(sums_ref)

    for n, term in enumerate((d_hidden * normed_one, d_hidden, dy * normed_two, dy)):
        sums_ref[n : n + 1] += jnp.sum(term, 0, keepdims=True)

    @pl.when(pl.program_id(0) == blocks - 1)
    def _():
        sent()


def row_order(seq_count, subs, step):
    return lax.rem(step, seq_count) * subs + lax.div(step, seq_count)


def middle(shape, x, attended, cotangent, rest, down, norms, block=256):
    rows, width = x.shape
    units = down.shape[0]
    seq_count, local_len = cotangent.shape[:2]
    subs = local_len // block
    row = lambda cols: pl.BlockSpec((block, cols), lambda i: (row_order(seq_count, subs, i), 0))
    any_space = pl.BlockSpec(memory_space=pl.ANY)
    like = lambda cols, dtype: jax.ShapeDtypeStruct((rows, cols), dtype)
    low = jnp.bfloat16
    return pl.pallas_call(
        functools.partial(middle_kernel, shape["seq"], seq_count),
        grid=(rows // block,),
        in_specs=[
            row(width), row(width), pl.BlockSpec(memory_space=pl.ANY),
            any_space, any_space, pl.BlockSpec((8, width), lambda i: (0, 0)),
        ],
        out_specs=[
            row(width), row(width), row(width), row(width),
            pl.BlockSpec((width, block), lambda i: (0, row_order(seq_count, subs, i))),
            row(units), row(units), row(units), row(width),
            pl.BlockSpec((8, width), lambda i: (0, 0)),
        ],
        out_shape=[
            like(width, low), like(width, jnp.float32), like(width, low), like(width, low),
            jax.ShapeDtypeStruct((width, rows), low),
            like(units, low), like(units, low), like(units, low), like(width, low),
            jax.ShapeDtypeStruct((8, width), jnp.float32),
        ],
        scratch_shapes=[
            pltpu.VMEM((block, units), jnp.float32),
            pltpu.VMEM((block, units), jnp.float32),
            pltpu.VMEM((rows // block, block, width), low),
            pltpu.SemaphoreType.DMA((3, rows // block)),
            pltpu.VMEM((width, width), low),
            pltpu.VMEM((width, units), low),
            pltpu.VMEM((width, units), low),
            pltpu.VMEM((units, width), low),
            pltpu.SemaphoreType.DMA((1 + 3 * (units // 768),)),
        ],
        compiler_params=pltpu.CompilerParams(collective_id=4, has_side_effects=True, vmem_limit_bytes=61 << 20),
        name="middle",
    )(x, attended, cotangent, rest, down, norms)


NORM_COLS = 256
SLOTS = 4
GATHER_PLAN = {
    7: ((1,),), 10: ((1, 0),), 14: ((2,),), 15: ((1, 1),), 18: ((2, 0),), 20: ((3,),), 21: ((2, 1),), 23: ((3, 0),),
    None: ((3, 1),),
}
PLAN = {
    13: ((0, 0, 1),), 16: ((0, 0, 3),), 19: ((0, 0, 2),), 21: ((0, 1, 1),), 23: ((0, 0, 0),), 24: ((0, 1, 3),),
    26: ((0, 2, 1), (1, 0, 1)), 28: ((0, 1, 2), (1, 0, 3)), 29: ((0, 2, 3),), 30: ((0, 1, 0), (1, 0, 2)),
    32: ((0, 2, 2), (1, 0, 0)), 34: ((1, 1, 1),), 36: ((1, 1, 3),), 38: ((1, 2, 1), (1, 1, 2)), 40: ((1, 2, 3),),
    41: ((1, 1, 0),), 43: ((1, 2, 2),),
}


def seg_codes(segments):
    lane = jnp.arange(128) % HEAD_DIM
    low, high = lane < CODE_BITS, lane < 2 * CODE_BITS
    bit = (segments[:, None] >> jnp.where(low, lane, jnp.where(high, lane - CODE_BITS, 0))[None, :]) & 1
    query = jnp.where(low, bit, jnp.where(high, 1 - bit, 0))
    keys = jnp.where(low, 1 - bit, jnp.where(high, bit, 0)) * -FAR
    return query.astype(jnp.bfloat16), keys.astype(jnp.bfloat16)


def two_to_a_sequence(
    shape,
    tokens, segment_ids, cotangent,
    w_qkv, w_out, w_gate, w_up, w_down, norm_params,
    first_qkv, first_out, first_gate, first_up, first_down, first_norms,
    second_qkv, second_out, second_gate, second_up, second_down, second_norms,
):
    seqs = shape["seq"]
    seq_count, local_len, width = tokens.shape
    rows = seq_count * local_len
    group = seqs // seq_count
    units = w_gate.shape[1]
    z = lax.axis_index("seq")
    core = lax.axis_index("fsdp") % 2

    norm_rows = jnp.pad(norm_params.T, ((0, 0), (0, NORM_COLS - norm_params.shape[0])))
    (x, segments, qkv_all, rest_all, down_all), pieces = first_gather(
        shape, tokens, segment_ids.reshape(seq_count, 1, local_len), w_gate, w_up, w_qkv, w_out, norm_rows, w_down
    )
    x = x.reshape(rows, width)
    w_all = qkv_all.reshape(width, 3 * width)
    q_code, k_code = seg_codes(segments.reshape(rows))
    positions = ((z * 2 + core) % group * rows + jnp.arange(rows)).astype(jnp.float32)
    half_dim = HEAD_DIM // 2
    inverse = jnp.exp(jnp.arange(half_dim, dtype=jnp.float32) * (-2.0 * math.log(ROPE_BASE) / HEAD_DIM))
    angles = positions[:, None] * inverse[None, :]
    cosine, sine = jnp.cos(angles), jnp.sin(angles)
    cosine = jnp.concatenate([cosine] * 4, 1)
    sine = jnp.concatenate([-sine, sine, -sine, sine], 1)

    query, own = project(x, w_all, 0, cosine, sine, k_code)
    probs, attended, inverse_sums, sib, rest_all, down_all = attend_pallas(
        shape, pieces, GATHER_PLAN, query, q_code, own, rest_all, down_all
    )
    rest = rest_all.reshape(width, rest_all.shape[-1])
    down = down_all.reshape(units, width)
    norms = jnp.pad(rest[:, -NORM_COLS : 4 - NORM_COLS].T.astype(jnp.float32), ((0, 4), (0, 0)))
    (
        result, d_resid_one, d_branch, d_attended, hidden_low, mixed, d_gate, d_up, d_ff, sums,
    ) = middle(shape, x, attended, cotangent, rest, down, norms)

    d_query, d_own, d_got, reduced_sums, output = backward(
        shape, PLAN, hidden_low, attended, d_branch, d_ff, sums, mixed, d_gate, d_up,
        query, own, sib, probs, inverse_sums, d_attended, result, seq_count,
    )
    back, qkv_sums, squares = tail(
        shape, cosine, sine, d_query, d_own, d_got, w_all, 0, d_resid_one, x, reduced_sums, seq_count
    )
    states = (
        w_qkv, w_out, w_gate, w_up, w_down, norm_params,
        first_qkv, first_out, first_gate, first_up, first_down, first_norms,
        second_qkv, second_out, second_gate, second_up, second_down, second_norms,
    )
    *updated, input_grad, grad_norm = adam(reduced_sums, qkv_sums, squares, back, states)
    return (output, input_grad, *updated, grad_norm.reshape(()))


def device_program(shape, *arrays):
    tokens, w_gate, w_down = arrays[0], arrays[5], arrays[7]
    seqs, line = shape["seq"], shape["fsdp"]
    seq_count, local_len, width = tokens.shape
    fits = (
        seqs == 2 * seq_count
        and seqs == 4
        and line == 8
        and (seq_count * local_len) % 512 == 0
        and w_gate.shape[0] % 8 == 0
        and w_down.shape[0] % 8 == 0
    )
    return two_to_a_sequence(shape, *arrays) if fits else per_device(*arrays)


def solution(mesh):
    return jax.shard_map(
        functools.partial(device_program, dict(mesh.shape)),
        mesh=mesh,
        in_specs=(
            P("fsdp", "seq", None),
            P("fsdp", "seq"),
            P("fsdp", "seq", None),
            P(("seq", "fsdp"), None),
            P(("seq", "fsdp"), None),
            P(("seq", "fsdp"), None),
            P(("seq", "fsdp"), None),
            P(("seq", "fsdp"), None),
            P(None, ("seq", "fsdp")),
            P(("seq", "fsdp"), None),
            P(("seq", "fsdp"), None),
            P(("seq", "fsdp"), None),
            P(("seq", "fsdp"), None),
            P(("seq", "fsdp"), None),
            P(None, ("seq", "fsdp")),
            P(("seq", "fsdp"), None),
            P(("seq", "fsdp"), None),
            P(("seq", "fsdp"), None),
            P(("seq", "fsdp"), None),
            P(("seq", "fsdp"), None),
            P(None, ("seq", "fsdp")),
        ),
        out_specs=(
            P("fsdp", "seq", None),
            P("fsdp", "seq", None),
            P(("seq", "fsdp"), None),
            P(("seq", "fsdp"), None),
            P(("seq", "fsdp"), None),
            P(("seq", "fsdp"), None),
            P(("seq", "fsdp"), None),
            P(None, ("seq", "fsdp")),
            P(("seq", "fsdp"), None),
            P(("seq", "fsdp"), None),
            P(("seq", "fsdp"), None),
            P(("seq", "fsdp"), None),
            P(("seq", "fsdp"), None),
            P(None, ("seq", "fsdp")),
            P(("seq", "fsdp"), None),
            P(("seq", "fsdp"), None),
            P(("seq", "fsdp"), None),
            P(("seq", "fsdp"), None),
            P(("seq", "fsdp"), None),
            P(None, ("seq", "fsdp")),
            P(("seq", "fsdp"), None),
            P(("seq", "fsdp"), None),
            P(("seq", "fsdp"), None),
            P(("seq", "fsdp"), None),
            P(("seq", "fsdp"), None),
            P(None, ("seq", "fsdp")),
            P(),
        ),
        check_vma=False,
    )
```

```python
import functools
import math

import jax
import jax.numpy as jnp
import numpy as np
from jax import lax
from jax.experimental import pallas as pl
from jax.experimental.pallas import tpu as pltpu
from jax.sharding import PartitionSpec as P

HEADS = 12
HEAD_DIM = 64
STEP = 10


EPS_NORM = 1e-06
ROPE_BASE = 1000.0
MASKED_SCORE = -1e30
MAX_NORM = 1.0
LEARN_RATE = 0.1
NORM_RATE = 0.6
BETA_ONE = 0.9
BETA_TWO = 0.999
ADAM_EPS = 1e-08
WEIGHT_DECAY = 0.01


def rotate(field, positions, sign_rot):
    shape_in = field.shape
    heads_view = field.reshape(shape_in[:-1] + (HEADS, HEAD_DIM))
    half_dim = HEAD_DIM // 2
    inverse = jnp.exp(
        jnp.arange(half_dim, dtype=jnp.float32) * (-2.0 * math.log(ROPE_BASE) / HEAD_DIM)
    )
    angles = positions[:, None] * inverse[None, :]
    cosine = jnp.cos(angles)[:, None, :]
    sine = jnp.sin(angles)[:, None, :] * sign_rot
    first_half = heads_view[..., :half_dim]
    second_half = heads_view[..., half_dim:]
    turned = jnp.concatenate(
        [first_half * cosine - second_half * sine, second_half * cosine + first_half * sine], -1
    )
    return turned.reshape(shape_in)


def normalize(resid, gain, shift):
    mean_row = jnp.mean(resid, -1, keepdims=True)
    centered = resid - mean_row
    inv_std = lax.rsqrt(jnp.mean(centered * centered, -1, keepdims=True) + EPS_NORM)
    normed = centered * inv_std
    return (normed * gain + shift, normed, inv_std)


def normalize_back(grad_in, normed, inv_std, gain):
    scaled = grad_in * gain
    return inv_std * (
        scaled
        - jnp.mean(scaled, -1, keepdims=True)
        - normed * jnp.mean(scaled * normed, -1, keepdims=True)
    )


def attend(query, keys, values, same_doc, score_scale):
    seq_count, local_len, model_width = query.shape

    def one_head(head_index, carried):
        out_all, log_sums = carried
        col_start = head_index * HEAD_DIM
        query_head = lax.dynamic_slice_in_dim(query, col_start, HEAD_DIM, 2)
        key_head = lax.dynamic_slice_in_dim(keys, col_start, HEAD_DIM, 2)
        value_head = lax.dynamic_slice_in_dim(values, col_start, HEAD_DIM, 2)
        raw_scores = jnp.einsum(
            "sqd,skd->sqk", query_head, key_head, preferred_element_type=jnp.float32
        )
        scores = jnp.where(same_doc, raw_scores * score_scale, MASKED_SCORE)
        row_max = jnp.max(scores, -1, keepdims=True)
        exp_scores = jnp.exp(scores - row_max)
        row_sums = jnp.sum(exp_scores, -1, keepdims=True)
        attn_prob = (exp_scores / row_sums).astype(jnp.bfloat16)
        head_out = jnp.einsum(
            "sqk,skd->sqd", attn_prob, value_head, preferred_element_type=jnp.float32
        )
        out_all = lax.dynamic_update_slice_in_dim(out_all, head_out, col_start, 2)
        log_sums = lax.dynamic_update_index_in_dim(
            log_sums, (row_max + jnp.log(row_sums))[..., 0], head_index, 0
        )
        return (out_all, log_sums)

    start_state = (
        jnp.zeros((seq_count, local_len, model_width), jnp.float32),
        jnp.zeros((HEADS, seq_count, local_len), jnp.float32),
    )
    return lax.fori_loop(0, HEADS, one_head, start_state)


def attend_back(query, keys, values, same_doc, log_sums, grad_attended, score_scale):
    seq_count, local_len, model_width = query.shape
    key_len = keys.shape[1]

    def one_head(head_index, carried):
        dq_all, dk_all, dv_all = carried
        col_start = head_index * HEAD_DIM
        query_head = lax.dynamic_slice_in_dim(query, col_start, HEAD_DIM, 2)
        key_head = lax.dynamic_slice_in_dim(keys, col_start, HEAD_DIM, 2)
        value_head = lax.dynamic_slice_in_dim(values, col_start, HEAD_DIM, 2)
        grad_head = lax.dynamic_slice_in_dim(grad_attended, col_start, HEAD_DIM, 2)
        head_sums = lax.dynamic_index_in_dim(log_sums, head_index, 0, keepdims=False)
        raw_scores = jnp.einsum(
            "sqd,skd->sqk", query_head, key_head, preferred_element_type=jnp.float32
        )
        scores = jnp.where(same_doc, raw_scores * score_scale, MASKED_SCORE)
        attn_prob = jnp.exp(scores - head_sums[..., None])
        grad_prob = jnp.einsum(
            "sqd,skd->sqk", grad_head, value_head, preferred_element_type=jnp.float32
        )
        dv_head = jnp.einsum(
            "sqk,sqd->skd",
            attn_prob.astype(jnp.bfloat16),
            grad_head,
            preferred_element_type=jnp.float32,
        )
        row_dots = jnp.sum(attn_prob * grad_prob, -1, keepdims=True)
        grad_scores = (attn_prob * (grad_prob - row_dots)).astype(jnp.bfloat16)
        dq_head = (
            jnp.einsum("sqk,skd->sqd", grad_scores, key_head, preferred_element_type=jnp.float32)
            * score_scale
        )
        dk_head = (
            jnp.einsum("sqk,sqd->skd", grad_scores, query_head, preferred_element_type=jnp.float32)
            * score_scale
        )
        dq_all = lax.dynamic_update_slice_in_dim(dq_all, dq_head, col_start, 2)
        dk_all = lax.dynamic_update_slice_in_dim(dk_all, dk_head, col_start, 2)
        dv_all = lax.dynamic_update_slice_in_dim(dv_all, dv_head, col_start, 2)
        return (dq_all, dk_all, dv_all)

    start_state = (
        jnp.zeros((seq_count, local_len, model_width), jnp.float32),
        jnp.zeros((seq_count, key_len, model_width), jnp.float32),
        jnp.zeros((seq_count, key_len, model_width), jnp.float32),
    )
    return lax.fori_loop(0, HEADS, one_head, start_state)


def adam_update(weight, gradient, moment_one, moment_two, decay_rate, step_rate, clip_factor):
    clipped = gradient * clip_factor
    first_new = BETA_ONE * moment_one + (1.0 - BETA_ONE) * clipped
    second_new = BETA_TWO * moment_two + (1.0 - BETA_TWO) * clipped * clipped
    first_fix = 1.0 - BETA_ONE**STEP
    second_fix = 1.0 - BETA_TWO**STEP
    direction = (
        first_new / first_fix / (jnp.sqrt(second_new / second_fix) + ADAM_EPS) + decay_rate * weight
    )
    return (weight - step_rate * direction, first_new, second_new)


def per_device(
    tokens,
    segment_ids,
    cotangent,
    w_qkv,
    w_out,
    w_gate,
    w_up,
    w_down,
    norm_params,
    first_qkv,
    first_out,
    first_gate,
    first_up,
    first_down,
    first_norms,
    second_qkv,
    second_out,
    second_gate,
    second_up,
    second_down,
    second_norms,
):
    seq_count, local_len, model_width = tokens.shape
    row_count = seq_count * local_len
    score_scale = 1.0 / math.sqrt(HEAD_DIM)
    lowered_qkv = w_qkv.astype(jnp.bfloat16)
    lowered_out = w_out.astype(jnp.bfloat16)
    lowered_gate = w_gate.astype(jnp.bfloat16)
    lowered_up = w_up.astype(jnp.bfloat16)
    lowered_down = w_down.astype(jnp.bfloat16)
    lowered_norms = norm_params.astype(jnp.bfloat16)
    full_qkv, full_out, full_gate, full_up, full_down, full_norms = (
        lax.all_gather(lowered_qkv, ("seq", "fsdp"), axis=0, tiled=True),
        lax.all_gather(lowered_out, ("seq", "fsdp"), axis=0, tiled=True),
        lax.all_gather(lowered_gate, ("seq", "fsdp"), axis=0, tiled=True),
        lax.all_gather(lowered_up, ("seq", "fsdp"), axis=0, tiled=True),
        lax.all_gather(lowered_down, ("seq", "fsdp"), axis=0, tiled=True),
        lax.all_gather(lowered_norms, ("seq", "fsdp"), axis=1, tiled=True),
    )
    gains = full_norms.astype(jnp.float32)
    gain_one, shift_one, gain_two, shift_two = (gains[0], gains[1], gains[2], gains[3])
    positions = (lax.axis_index("seq") * local_len + jnp.arange(local_len)).astype(jnp.float32)
    flat_rows = tokens.reshape(row_count, model_width)
    projected = jnp.dot(flat_rows, full_qkv, preferred_element_type=jnp.float32).reshape(
        seq_count, local_len, 3 * model_width
    )
    query = rotate(projected[..., :model_width], positions, 1.0).astype(jnp.bfloat16)
    keys_local = rotate(projected[..., model_width : 2 * model_width], positions, 1.0).astype(
        jnp.bfloat16
    )
    values_local = projected[..., 2 * model_width :].astype(jnp.bfloat16)
    keys_all, values_all, key_segments = (
        lax.all_gather(keys_local, "seq", axis=1, tiled=True),
        lax.all_gather(values_local, "seq", axis=1, tiled=True),
        lax.all_gather(segment_ids, "seq", axis=1, tiled=True),
    )
    same_doc = segment_ids[:, :, None] == key_segments[:, None, :]
    attended, log_sums = attend(query, keys_all, values_all, same_doc, score_scale)
    attended_low = attended.astype(jnp.bfloat16).reshape(row_count, model_width)
    resid_one = flat_rows.astype(jnp.float32) + jnp.dot(
        attended_low, full_out, preferred_element_type=jnp.float32
    )
    hidden, normed_one, inv_std_one = normalize(resid_one, gain_one, shift_one)
    hidden_low = hidden.astype(jnp.bfloat16)
    gate_proj = jnp.dot(hidden_low, full_gate, preferred_element_type=jnp.float32)
    up_proj = jnp.dot(hidden_low, full_up, preferred_element_type=jnp.float32)
    sigmoid_gate = jax.nn.sigmoid(gate_proj)
    silu_gate = gate_proj * sigmoid_gate
    mixed_low = (silu_gate * up_proj).astype(jnp.bfloat16)
    resid_two = hidden + jnp.dot(mixed_low, full_down, preferred_element_type=jnp.float32)
    result, normed_two, inv_std_two = normalize(resid_two, gain_two, shift_two)
    output = result.astype(jnp.bfloat16).reshape(seq_count, local_len, model_width)
    back_qkv, back_out, back_gate, back_up, back_down = (
        lax.all_gather(lowered_qkv, ("seq", "fsdp"), axis=0, tiled=True),
        lax.all_gather(lowered_out, ("seq", "fsdp"), axis=0, tiled=True),
        lax.all_gather(lowered_gate, ("seq", "fsdp"), axis=0, tiled=True),
        lax.all_gather(lowered_up, ("seq", "fsdp"), axis=0, tiled=True),
        lax.all_gather(lowered_down, ("seq", "fsdp"), axis=0, tiled=True),
    )
    grad_result = cotangent.reshape(row_count, model_width).astype(jnp.float32)
    d_gain_two = jnp.sum(grad_result * normed_two, 0)
    d_shift_two = jnp.sum(grad_result, 0)
    d_resid_two = normalize_back(grad_result, normed_two, inv_std_two, gain_two)
    d_ff_low = d_resid_two.astype(jnp.bfloat16)
    g_down = jnp.einsum("rf,rd->fd", mixed_low, d_ff_low, preferred_element_type=jnp.float32)
    d_mixed = jnp.einsum("rd,fd->rf", d_ff_low, back_down, preferred_element_type=jnp.float32)
    d_up_low = (d_mixed * silu_gate).astype(jnp.bfloat16)
    d_gate_low = (
        d_mixed * up_proj * sigmoid_gate * (1.0 + gate_proj * (1.0 - sigmoid_gate))
    ).astype(jnp.bfloat16)
    g_gate = jnp.einsum("rd,rf->df", hidden_low, d_gate_low, preferred_element_type=jnp.float32)
    g_up = jnp.einsum("rd,rf->df", hidden_low, d_up_low, preferred_element_type=jnp.float32)
    d_hidden = (
        d_resid_two
        + jnp.einsum("rf,df->rd", d_gate_low, back_gate, preferred_element_type=jnp.float32)
        + jnp.einsum("rf,df->rd", d_up_low, back_up, preferred_element_type=jnp.float32)
    )
    d_gain_one = jnp.sum(d_hidden * normed_one, 0)
    d_shift_one = jnp.sum(d_hidden, 0)
    d_resid_one = normalize_back(d_hidden, normed_one, inv_std_one, gain_one)
    d_branch_low = d_resid_one.astype(jnp.bfloat16)
    g_out = jnp.einsum("rd,re->de", attended_low, d_branch_low, preferred_element_type=jnp.float32)
    d_attended_low = (
        jnp.einsum("re,de->rd", d_branch_low, back_out, preferred_element_type=jnp.float32)
        .astype(jnp.bfloat16)
        .reshape(seq_count, local_len, model_width)
    )
    keys_back, values_back = (
        lax.all_gather(keys_local, "seq", axis=1, tiled=True),
        lax.all_gather(values_local, "seq", axis=1, tiled=True),
    )
    d_query, d_keys, d_values = attend_back(
        query, keys_back, values_back, same_doc, log_sums, d_attended_low, score_scale
    )
    d_keys_local, d_values_local = (
        lax.psum_scatter(
            d_keys.astype(jnp.bfloat16), "seq", scatter_dimension=1, tiled=True
        ).astype(jnp.float32),
        lax.psum_scatter(
            d_values.astype(jnp.bfloat16), "seq", scatter_dimension=1, tiled=True
        ).astype(jnp.float32),
    )
    d_projected_low = (
        jnp.concatenate(
            [
                rotate(d_query, positions, -1.0),
                rotate(d_keys_local, positions, -1.0),
                d_values_local,
            ],
            -1,
        )
        .astype(jnp.bfloat16)
        .reshape(row_count, 3 * model_width)
    )
    g_qkv = jnp.einsum("rd,re->de", flat_rows, d_projected_low, preferred_element_type=jnp.float32)
    input_grad = (
        d_resid_one
        + jnp.einsum("re,de->rd", d_projected_low, back_qkv, preferred_element_type=jnp.float32)
    ).reshape(seq_count, local_len, model_width)
    g_norms = jnp.stack([d_gain_one, d_shift_one, d_gain_two, d_shift_two])
    red_qkv, red_out, red_gate, red_up, red_down, red_norms = (
        lax.psum_scatter(g_qkv, ("seq", "fsdp"), scatter_dimension=0, tiled=True),
        lax.psum_scatter(g_out, ("seq", "fsdp"), scatter_dimension=0, tiled=True),
        lax.psum_scatter(g_gate, ("seq", "fsdp"), scatter_dimension=0, tiled=True),
        lax.psum_scatter(g_up, ("seq", "fsdp"), scatter_dimension=0, tiled=True),
        lax.psum_scatter(g_down, ("seq", "fsdp"), scatter_dimension=0, tiled=True),
        lax.psum_scatter(g_norms, ("seq", "fsdp"), scatter_dimension=1, tiled=True),
    )
    local_squares = (
        jnp.sum(red_qkv * red_qkv)
        + jnp.sum(red_out * red_out)
        + jnp.sum(red_gate * red_gate)
        + jnp.sum(red_up * red_up)
        + jnp.sum(red_down * red_down)
        + jnp.sum(red_norms * red_norms)
    )
    squares_sum = lax.psum(local_squares, ("seq", "fsdp"))
    grad_norm = jnp.sqrt(squares_sum)
    clip_factor = jnp.minimum(1.0, MAX_NORM / (grad_norm + 1e-06))
    new_qkv, mom_qkv, sec_qkv = adam_update(
        w_qkv, red_qkv, first_qkv, second_qkv, WEIGHT_DECAY, LEARN_RATE, clip_factor
    )
    new_out, mom_out, sec_out = adam_update(
        w_out, red_out, first_out, second_out, WEIGHT_DECAY, LEARN_RATE, clip_factor
    )
    new_gate, mom_gate, sec_gate = adam_update(
        w_gate, red_gate, first_gate, second_gate, WEIGHT_DECAY, LEARN_RATE, clip_factor
    )
    new_up, mom_up, sec_up = adam_update(
        w_up, red_up, first_up, second_up, WEIGHT_DECAY, LEARN_RATE, clip_factor
    )
    new_down, mom_down, sec_down = adam_update(
        w_down, red_down, first_down, second_down, WEIGHT_DECAY, LEARN_RATE, clip_factor
    )
    new_norms, mom_norms, sec_norms = adam_update(
        norm_params, red_norms, first_norms, second_norms, 0.0, NORM_RATE, clip_factor
    )
    return (
        output,
        input_grad,
        red_qkv,
        red_out,
        red_gate,
        red_up,
        red_down,
        red_norms,
        new_qkv,
        new_out,
        new_gate,
        new_up,
        new_down,
        new_norms,
        mom_qkv,
        mom_out,
        mom_gate,
        mom_up,
        mom_down,
        mom_norms,
        sec_qkv,
        sec_out,
        sec_gate,
        sec_up,
        sec_down,
        sec_norms,
        grad_norm,
    )


NT = (((1,), (1,)), ((), ()))
NN = (((1,), (0,)), ((), ()))
TN = (((0,), (0,)), ((), ()))
FAR = 1e30
CODE_BITS = 7
MESH_ID = pl.DeviceIdType.MESH


def dotf(left, right, dims=NN):
    return lax.dot_general(left, right, dims, preferred_element_type=jnp.float32)


def place():
    f = lax.axis_index("fsdp")
    return lax.axis_index("seq"), lax.div(f, 2), lax.rem(f, 2)


def chip_at(chip, mask):
    at, b = chip, 0
    while mask >> b:
        if (mask >> b) & 1:
            at = at + (1 - 2 * lax.rem(lax.div(chip, 1 << b), 2)) * (1 << b)
        b += 1
    return at


def greet(peers):
    barrier = pltpu.get_barrier_semaphore()
    for peer in peers:
        pl.semaphore_signal(barrier, inc=1, device_id=peer, device_id_type=MESH_ID)
    pl.semaphore_wait(barrier, len(peers))


def column_peers(seqs):
    z, chip, core = place()
    return [{"seq": lax.rem(z + k, seqs), "fsdp": 2 * chip + c} for k in range(1, seqs) for c in range(2)]


def plane_peers(line):
    f = lax.axis_index("fsdp")
    return [{"fsdp": lax.rem(f + k, line)} for k in range(1, line)]


def sum_peers(bits):
    z, chip, core = place()
    return [{"fsdp": 2 * chip + 1 - core}] + [{"fsdp": 2 * chip_at(chip, 1 << b) + core} for b in range(bits)]


def departs(seqs, seq_count, source, target, sems, subs=1):
    z, chip, core = place()
    group = seqs // seq_count

    def copies(s, sub):
        at = (core * seq_count + s) * group + lax.div(z, seq_count)
        to_z, to_core = lax.div(at, 2), lax.rem(at, 2)
        n = lax.rem(z, seq_count) * subs + sub
        remote = pltpu.make_async_remote_copy(
            source(s, sub), target(n), sems.at[0, s * subs + sub], sems.at[1, n],
            device_id={"seq": to_z, "fsdp": 2 * chip + to_core}, device_id_type=MESH_ID,
        )
        return (to_z == z) & (to_core == core), remote, pltpu.make_async_copy(source(s, sub), target(n), sems.at[2, n])

    def begin():
        for sub in range(subs):
            for s in range(seq_count):
                mine, remote, local = copies(s, sub)

                @pl.when(mine)
                def _():
                    local.start()

                @pl.when(jnp.logical_not(mine))
                def _():
                    remote.start()

    def came(n):
        at = z * 2 + core
        from_z = lax.rem(at, group) * seq_count + lax.div(n, subs)
        mine = (from_z == z) & (lax.div(lax.div(at, group), seq_count) == core)

        @pl.when(mine)
        def _():
            pltpu.make_async_copy(source(0, 0), target(n), sems.at[2, n]).wait()

        @pl.when(jnp.logical_not(mine))
        def _():
            pltpu.make_async_remote_copy(
                source(0, 0), target(n), sems.at[0, 0], sems.at[1, n],
                device_id={"seq": z, "fsdp": 2 * chip + 1 - core}, device_id_type=MESH_ID,
            ).wait_recv()

    def sent():
        for sub in range(subs):
            for s in range(seq_count):
                mine, remote, _ = copies(s, sub)

                @pl.when(jnp.logical_not(mine))
                def _():
                    remote.wait_send()

    return begin, came, sent


def returns(seqs, seq_count, source, target, sems, rows):
    z, chip, core = place()
    group = seqs // seq_count
    at = z * 2 + core
    number = lax.div(at, group)
    slot = lax.rem(number, seq_count)
    to_core = lax.div(number, seq_count)
    local_len = target.shape[1]
    subs = local_len // rows

    def copies(n):
        t, sub = divmod(n, subs)
        to_z = lax.rem(at, group) * seq_count + t
        mine = (to_z == z) & (to_core == core)
        here = target.at[slot, pl.ds(sub * rows, rows)]
        remote = pltpu.make_async_remote_copy(
            source(n), here, sems.at[0, n], sems.at[1, slot * subs + sub],
            device_id={"seq": to_z, "fsdp": 2 * chip + to_core}, device_id_type=MESH_ID,
        )
        return mine, remote, pltpu.make_async_copy(source(n), here, sems.at[2, n])

    def begin(n):
        mine, remote, local = copies(n)

        @pl.when(mine)
        def _():
            local.start()

        @pl.when(jnp.logical_not(mine))
        def _():
            remote.start()

    def end():
        for n in range(seq_count * subs):
            mine, remote, local = copies(n)

            @pl.when(mine)
            def _():
                local.wait()

            @pl.when(jnp.logical_not(mine))
            def _():
                remote.wait_send()

        for s in range(seq_count):
            came = (core * seq_count + s) * group + lax.div(z, seq_count)
            other = jnp.logical_not((lax.div(came, 2) == z) & (lax.rem(came, 2) == core))
            for sub in range(subs):

                @pl.when(other)
                def _():
                    here = target.at[s, pl.ds(sub * rows, rows)]
                    pltpu.make_async_remote_copy(
                        source(0), here, sems.at[0, 0], sems.at[1, s * subs + sub],
                        device_id={"seq": z, "fsdp": 2 * chip + 1 - core}, device_id_type=MESH_ID,
                    ).wait_recv()

    return begin, end


def line_peers(seqs):
    z = lax.axis_index("seq")
    return [{"seq": lax.rem(z + way, seqs)} for way in (1, seqs - 1)]


def gatherer_scratch(seqs, bits, count):
    dma = pltpu.SemaphoreType.DMA
    chips = 1 << bits
    return [
        dma((count, 2, seqs)),
        dma((count, seqs)),
        dma((count, seqs, chips)),
        dma((count, seqs, chips)),
        dma((count, seqs, chips)),
        dma((count, seqs, chips)),
    ]


def gatherer(seqs, bits, pieces, wholes, line_send, line_recv, hop_send, hop_recv, swap_send, swap_recv):
    z, chip, core = place()

    def block(p, zz, mask):
        which, offset, width, _ = pieces[p]
        half = wholes[which].shape[-1] // 2
        return wholes[which].at[zz, chip_at(chip, mask), :, pl.ds(pl.multiple_of(core * half + offset, 128), width)]

    def line_copy(p, zz, way):
        return pltpu.make_async_remote_copy(
            block(p, zz, 0), block(p, zz, 0), line_send.at[p, way, zz], line_recv.at[p, zz],
            device_id={"seq": z + (1 if way else -1)}, device_id_type=MESH_ID,
        )

    def hop_copy(p, zz, mask, b):
        to = mask | (1 << b)
        return pltpu.make_async_remote_copy(
            block(p, zz, mask), block(p, zz, mask), hop_send.at[p, zz, to], hop_recv.at[p, zz, to],
            device_id={"fsdp": 2 * chip_at(chip, 1 << b) + core}, device_id_type=MESH_ID,
        )

    def swap_copy(p, zz, mask):
        return pltpu.make_async_remote_copy(
            block(p, zz, mask), block(p, zz, mask), swap_send.at[p, zz, mask], swap_recv.at[p, zz, mask],
            device_id={"fsdp": 2 * chip + 1 - core}, device_id_type=MESH_ID,
        )

    def level(p, mask):
        return max([i for i, b in enumerate(pieces[p][3]) if mask & (1 << b)], default=-1)

    def later(p, mask):
        return pieces[p][3][level(p, mask) + 1 :]

    masks = range(1 << bits)

    def pass_on(p, zz, mask, mine=False):
        for b in later(p, mask):
            hop_copy(p, zz, mask, b).start()
        if not mine:
            swap_copy(p, zz, mask).start()

    def own_line(which):
        for p in which:

            @pl.when(z > 0)
            def _():
                line_copy(p, z, 0).start()

            @pl.when(z < seqs - 1)
            def _():
                line_copy(p, z, 1).start()

    def own_hops(which):
        for p in which:
            pass_on(p, z, 0, True)

    def both(distance, task):
        for way in (1, 0) if distance else (1,):
            zz = z - distance if way else z + distance
            pl.when((zz >= 0) & (zz < seqs))(functools.partial(task, zz, way))

    def line(which, distance):
        def task(zz, way):
            for p in which:
                line_copy(p, zz, way).wait_recv()

                @pl.when((z < seqs - 1) if way else (z > 0))
                def _():
                    line_copy(p, zz, way).start()

                pass_on(p, zz, 0)

        both(distance, task)

    def hops(which, distance, levels=range(bits)):
        def task(zz, way):
            for at in levels:
                for p in which:
                    for mask in masks:
                        if level(p, mask) == at:
                            b = pieces[p][3][at]
                            hop_copy(p, zz, mask & ~(1 << b), b).wait_recv()
                            pass_on(p, zz, mask)

        both(distance, task)

    def finish_line(which):
        def task(zz, _):
            for p in which:

                @pl.when((zz <= z) & (z < seqs - 1))
                def _():
                    line_copy(p, zz, 1).wait_send()

                @pl.when((zz >= z) & (z > 0))
                def _():
                    line_copy(p, zz, 0).wait_send()

            return 0

        lax.fori_loop(0, seqs, task, 0)

    def finish_hops(which, distance):
        def task(zz, _):
            for p in which:
                for mask in masks:
                    for b in later(p, mask):
                        hop_copy(p, zz, mask, b).wait_send()
                    if mask or distance:
                        swap_copy(p, zz, mask).wait()

        both(distance, task)

    return own_line, own_hops, line, hops, finish_line, finish_hops


def first_gather_kernel(seqs, bits, pieces, early, *refs):
    tokens, segments, gate, up, qkv, out, norm, down = refs[:8]
    x_out, segments_out, qkv_all, rest_all, down_all = refs[8:13]
    qkv_two, rest_two, down_two, qkv_chip, rest_chip, down_chip, core_sem, own_sem, token_sem, segment_sem, load_sem = refs[13:24]
    z, chip, core = place()
    wholes = (qkv_all, rest_all, down_all)
    chips = (qkv_chip, rest_chip, down_chip)
    own_line, own_hops, line, hops, finish_line, finish_hops = gatherer(seqs, bits, pieces, wholes, *refs[24:])
    seq_count = tokens.shape[0]
    token_begin, token_came, token_sent = departs(
        seqs, seq_count, lambda s, _: tokens.at[s], lambda n: x_out.at[n], token_sem
    )
    segment_begin, segment_came, segment_sent = departs(
        seqs, seq_count, lambda s, _: segments.at[s], lambda n: segments_out.at[n], segment_sem
    )
    loads = [
        pltpu.make_async_copy(qkv, qkv_two.at[core], load_sem.at[0]),
        pltpu.make_async_copy(down, down_two.at[core], load_sem.at[1]),
    ]
    at = 0
    for n, part in enumerate((gate, up, out, norm)):
        cols = part.shape[1]
        loads.append(pltpu.make_async_copy(part, rest_two.at[core, :, pl.ds(at, cols)], load_sem.at[2 + n]))
        at += cols
    for load in loads:
        load.start()
    greet(sum_peers(bits) + column_peers(seqs))
    segment_begin()
    for load in loads:
        load.wait()
    twos = (qkv_two, rest_two, down_two)
    first = [
        pltpu.make_async_remote_copy(
            two.at[core], two.at[core], core_sem.at[0, i], core_sem.at[1, i],
            device_id={"fsdp": 2 * chip + 1 - core}, device_id_type=MESH_ID,
        )
        for i, two in enumerate(twos)
    ]
    for copy in first:
        copy.start()
    own = [
        pltpu.make_async_copy(chip_ref, whole.at[z, chip], own_sem.at[i])
        for i, (chip_ref, whole) in enumerate(zip(chips, wholes))
    ]
    for i, copy in enumerate(first):
        copy.wait()
        chips[i][...] = twos[i][...].reshape(chips[i].shape).astype(jnp.bfloat16)
        own[i].start()
    rest = [p for p in range(len(pieces)) if p not in early]
    own[0].wait()
    own_line(early)
    own_hops(early)
    own[1].wait()
    own[2].wait()
    own_hops(rest)
    for distance in range(1, seqs):
        line(early, distance)
        if distance == 1:
            token_begin()
        hops(early, distance - 1)
    hops(rest, 0)
    hops(early, seqs - 1)
    finish_line(early)
    for distance in range(seqs):
        finish_hops(early, distance)
    finish_hops(rest, 0)
    for n in range(seq_count):
        token_came(n)
        segment_came(n)
    token_sent()
    segment_sent()


def gather_pieces(bits, qkv, rest, down, rows):
    upward, downward = tuple(range(bits)), tuple(reversed(range(bits)))
    cut = qkv // 512 * 128
    load = down.shape[1] // 2 * down.shape[0] // rows
    other = max(128, ((rest // 2 + load) // 2 - load) // 128 * 128)
    return (
        (0, 0, cut, upward),
        (0, cut, qkv // 2 - cut, downward),
        (1, 0, other, upward),
        (2, 0, down.shape[1] // 2, upward),
        (1, other, rest // 2 - other, downward),
    )


def first_gather(shape, tokens, segments, gate, up, qkv, out, norm, down):
    seqs, chips = shape["seq"], shape["fsdp"] // 2
    bits = chips.bit_length() - 1
    rows, rows_down = gate.shape[0], down.shape[0]
    rest = sum(part.shape[1] for part in (gate, up, out, norm))
    pieces = gather_pieces(bits, qkv.shape[1], rest, down, rows)
    seq_count = tokens.shape[0]
    dma = pltpu.SemaphoreType.DMA
    low = jnp.bfloat16
    any_space = pl.BlockSpec(memory_space=pl.ANY)
    forms = ((rows, qkv.shape[1]), (rows, rest), (rows_down, down.shape[1]))
    *outs, = pl.pallas_call(
        functools.partial(first_gather_kernel, seqs, bits, pieces, (0, 1)),
        out_shape=[
            jax.ShapeDtypeStruct(tokens.shape, low),
            jax.ShapeDtypeStruct(segments.shape, jnp.int32),
            *(jax.ShapeDtypeStruct((seqs, chips, 2 * n, cols), low) for n, cols in forms),
        ],
        in_specs=[any_space] * 8,
        out_specs=[any_space] * 5,
        scratch_shapes=[
            *(pltpu.VMEM((2, *form), jnp.float32) for form in forms),
            *(pltpu.VMEM((2 * n, cols), low) for n, cols in forms),
            dma((2, 3)),
            dma((3,)),
            dma((3, seq_count)),
            dma((3, seq_count)),
            dma((6,)),
            *gatherer_scratch(seqs, bits, len(pieces)),
        ],
        compiler_params=pltpu.CompilerParams(collective_id=0, has_side_effects=True, vmem_limit_bytes=63 << 20),
        name="first_gather",
    )(tokens, segments, gate, up, qkv, out, norm, down)
    return outs, pieces[2:]


def hop_masks(order, stage):
    gone = sum(1 << b for b in order[:stage])
    return [m for m in range(1 << len(order)) if (m >> order[stage]) & 1 and not m & gone]


def hop_slot(order, stage, mask):
    return [m ^ (1 << order[stage]) for m in hop_masks(order, stage)].index(mask)


def z_low(zm):
    return (zm & -zm).bit_length() - 1


def span(pieces, group):
    return pieces[group[0]][0], sum(pieces[p][1] for p in group)


def reducer_scratch(seqs, bits, pieces, groups, rows, width):
    dma = pltpu.SemaphoreType.DMA
    low = jnp.bfloat16
    line_bits = seqs.bit_length() - 1
    hops = [
        pltpu.VMEM((seqs, len(hop_masks(order, stage)), rows, cols), low)
        for _, cols, order in pieces
        for stage in range(bits)
    ]
    lines = [
        pltpu.VMEM((seqs >> (k + 1), rows, span(pieces, group)[1]), low) for group in groups for k in range(line_bits)
    ]
    most = 1 << (bits - 1)
    return [
        pltpu.VMEM((2, rows // 2, width), jnp.float32),
        pltpu.VMEM((rows // 2, width), jnp.float32),
        dma((2, seqs, 1 << bits)),
        dma((2, len(pieces), bits, seqs, most)),
        dma((2, len(groups), line_bits, seqs)),
        dma((2,)),
        *hops,
        *lines,
    ]


def reducer(seqs, bits, pieces, groups, away, keep, got, halves_ref, swapped, core_sem, hop_sem, line_sem, swap_sem, *buffers):
    z, chip, core = place()
    rows = keep.shape[2]
    half = rows // 2
    line_bits = seqs.bit_length() - 1
    sibling = {"fsdp": 2 * chip + 1 - core}
    masks = range(1 << bits)
    hop = lambda p, stage: buffers[p * bits + stage]
    line = lambda g, k: buffers[len(pieces) * bits + g * line_bits + k]

    def remote(source, target, sems, index, device):
        return pltpu.make_async_remote_copy(
            source, target, sems.at[(0, *index)], sems.at[(1, *index)], device_id=device, device_id_type=MESH_ID
        )

    def core_copy(zm, mask):
        at = (chip_at(z, zm), chip_at(chip, mask))
        return remote(away.at[at], got.at[at], core_sem, (zm, mask), sibling)

    def hop_copy(p, stage, zm, mask):
        first, cols, order = pieces[p]
        slot = hop_slot(order, stage, mask ^ (1 << order[stage]))
        return remote(
            got.at[chip_at(z, zm), chip_at(chip, mask), :, pl.ds(first, cols)],
            hop(p, stage).at[zm, slot],
            hop_sem,
            (p, stage, zm, slot),
            {"fsdp": 2 * chip_at(chip, 1 << order[stage]) + core},
        )

    def line_copy(g, zm):
        k = z_low(zm)
        slot = zm >> (k + 1)
        return remote(
            got.at[chip_at(z, zm), chip, :, pl.ds(*span(pieces, groups[g]))],
            line(g, k).at[slot],
            line_sem,
            (g, k, slot),
            {"seq": chip_at(z, 1 << k)},
        )

    def total(p, zm, mask, stages, lines=0):
        first, cols, order = pieces[p]
        where = (chip_at(z, zm), chip_at(chip, mask), slice(None), pl.ds(first, cols))
        value = keep[where].astype(jnp.float32) + got[where].astype(jnp.float32)
        for stage in range(stages):
            value = value + hop(p, stage)[zm, hop_slot(order, stage, mask)].astype(jnp.float32)
        if lines:
            g = [n for n, group in enumerate(groups) if p in group][0]
            here = pl.ds(first - span(pieces, groups[g])[0], cols)
            for k in range(lines):
                value = value + line(g, k)[zm >> (k + 1), :, here].astype(jnp.float32)
        return value

    def come(g, stage, zm):
        for p in groups[g]:
            for mask in hop_masks(pieces[p][2], stage):
                hop_copy(p, stage, zm, mask).wait_recv()

    def come_line(g, zm, lines):
        for k in range(lines):
            line_copy(g, zm | (1 << k)).wait_recv()

    def start():
        for zm in (*range(1, seqs), 0):
            for mask in reversed(masks):
                core_copy(zm, mask).start()

    def hop_task(g, stage, zm):
        if stage:
            come(g, stage - 1, zm)
        elif away is not None:
            for mask in masks:
                core_copy(zm, mask).wait_recv()
        for p in groups[g]:
            first, cols, order = pieces[p]
            for mask in hop_masks(order, stage):
                got[chip_at(z, zm), chip_at(chip, mask), :, pl.ds(first, cols)] = total(p, zm, mask, stage).astype(
                    jnp.bfloat16
                )
                hop_copy(p, stage, zm, mask).start()

    def line_task(g, zm):
        k = z_low(zm)
        come(g, bits - 1, zm)
        come_line(g, zm, k)
        for p in groups[g]:
            first, cols, _ = pieces[p]
            got[chip_at(z, zm), chip, :, pl.ds(first, cols)] = total(p, zm, 0, bits, k).astype(jnp.bfloat16)
        line_copy(g, zm).start()

    def task(g, kind, zm):
        if kind == bits:
            line_task(g, zm)
        else:
            hop_task(g, kind, zm)

    def finish():
        for g, group in enumerate(groups):
            come(g, bits - 1, 0)
            come_line(g, 0, line_bits)
            for p in group:
                first, cols, _ = pieces[p]
                value = total(p, 0, 0, bits, line_bits)
                halves_ref[0, :, pl.ds(first, cols)] = value[:half]
                halves_ref[1, :, pl.ds(first, cols)] = value[half:]
        swap = remote(halves_ref.at[1 - core], swapped, swap_sem, (), sibling)
        swap.start()
        for zm in range(seqs):
            if away is not None:
                for mask in masks:
                    core_copy(zm, mask).wait_send()
            for p, (_, _, order) in enumerate(pieces):
                for stage in range(bits):
                    for mask in hop_masks(order, stage):
                        hop_copy(p, stage, zm, mask).wait_send()
            if zm:
                for g in range(len(groups)):
                    line_copy(g, zm).wait_send()
        swap.wait()

    return start, task, finish


GROUPS = ((0, 1), (2, 3))


def sum_pieces(units, tall, out, bits):
    upward, downward = tuple(range(bits)), tuple(reversed(range(bits)))
    cut = (tall + out) // 256 * 128
    half = units // 2
    return (
        (0, half, upward),
        (half, half, downward),
        (units, cut, upward),
        (units + cut, tall + out - cut, downward),
    )


def back_kernel(
    seqs, bits, pieces, plan, tiles, talls, fold, turns,
    hid_ref, att_ref, branch_ref, dff_ref, sums_ref, mixed_ref, dgate_ref, dup_ref,
    q_ref, k0, v0, k1, v1, p_ref, inv_ref, do_ref, result_hbm,
    dq_ref, own_ref, sib_ref, sum_ref, output_hbm,
    keep, got, away_wide, away_tall, away_sem, kt, va, dk, dv, sib, sib_sem, back_sem, *shared,
):
    z, chip, core = place()
    sibling = {"fsdp": 2 * chip + 1 - core}
    step = pl.program_id(0)
    last = pl.num_programs(0) - 1
    rows = keep.shape[2]
    chips = seqs << bits
    low = jnp.bfloat16
    width = att_ref.shape[1]
    tile = dgate_ref.shape[1]
    tall = fold * width // 2
    out_cols = (width + NORM_COLS) // 2
    units = 2 * tiles * tile
    first_steps = 4 * tiles + talls + 1
    per_z = 1 << bits
    _, sum_task, finish = reducer(seqs, bits, pieces, GROUPS, None, keep, got, *shared)
    seq_count, local_len = output_hbm.shape[:2]
    back_begin, back_end = returns(
        seqs, seq_count, lambda n: result_hbm.at[pl.ds(n * local_len, local_len)], output_hbm, back_sem, local_len
    )

    def wide_copy(n, slot):
        at = n * tile if n is not None else units + tall
        cols = pl.ds(pl.multiple_of(at, 128), tile)
        return pltpu.make_async_remote_copy(
            away_wide.at[slot], got.at[:, :, :, cols],
            away_sem.at[0, n if n is not None else 2 * tiles], away_sem.at[1, n if n is not None else 2 * tiles],
            device_id=sibling, device_id_type=MESH_ID,
        )

    def tall_copy(n):
        count = chips // talls
        at = n * count
        index = 2 * tiles + 1 + n
        return pltpu.make_async_remote_copy(
            away_tall.at[lax.rem(n, 2)],
            got.at[lax.div(at, per_z), pl.ds(lax.rem(at, per_z), count), :, pl.ds(units, tall)],
            away_sem.at[0, index], away_sem.at[1, index],
            device_id=sibling, device_id_type=MESH_ID,
        )

    @pl.when(step == 0)
    def _():
        greet(sum_peers(bits) + column_peers(seqs))
        for n in range(seq_count):
            back_begin(n)

    for n, ref in enumerate((dgate_ref, dup_ref)):

        @pl.when((step >= n * tiles) & (step < (n + 1) * tiles))
        def _():
            slot = lax.rem(step, 2)

            @pl.when(step >= 2)
            def _():
                wide_copy(step - 2, slot).wait_send()

            away_wide[slot] = dotf(hid_ref[...], ref[...]).astype(low).reshape(away_wide.shape[1:])
            wide_copy(step, slot).start()

        @pl.when((step >= (2 + n) * tiles) & (step < (3 + n) * tiles))
        def _():
            cols = pl.ds(pl.multiple_of((step - 2 * tiles) * tile, 128), tile)
            keep[:, :, :, cols] = dotf(hid_ref[...], ref[...]).astype(low).reshape(away_wide.shape[1:])

    n_tall = step - 4 * tiles

    def sides(halves, mine, other):
        for side, value in enumerate(halves):

            @pl.when(core == side)
            def _():
                mine(value)

            @pl.when(core != side)
            def _():
                other(value)

    @pl.when((n_tall >= 0) & (n_tall < talls))
    def _():
        @pl.when(n_tall >= 2)
        def _():
            tall_copy(n_tall - 2).wait_send()

        value = dotf(mixed_ref[...], dff_ref[...], TN)
        own = rows // 2
        count = chips // talls
        at = n_tall * count

        def folded(part):
            return jnp.concatenate(
                [
                    jnp.concatenate([part[(b * fold + a) * own : (b * fold + a + 1) * own] for a in range(fold)], 1)
                    for b in range(part.shape[0] // (fold * own))
                ],
                0,
            ).astype(low).reshape(count, rows, tall)

        def mine(value):
            keep[lax.div(at, per_z), pl.ds(lax.rem(at, per_z), count), :, units : units + tall] = value

        def other(value):
            away_tall[lax.rem(n_tall, 2)] = value

        sides([folded(value[:, : width // 2]), folded(value[:, width // 2 :])], mine, other)
        tall_copy(n_tall).start()

    @pl.when(n_tall == talls)
    def _():
        wide_copy(2 * tiles - 2, 0).wait_send()
        value = dotf(att_ref[...], branch_ref[...], TN)
        pad = jnp.zeros((NORM_COLS - sums_ref.shape[0], width), jnp.float32)
        value = jnp.concatenate([value, jnp.concatenate([sums_ref[...], pad], 0).T], 1).astype(low)

        def mine(value):
            keep[:, :, :, units + tall :] = value

        def other(value):
            away_wide[0] = value

        sides(
            [value[:, n * out_cols : (n + 1) * out_cols].reshape(away_wide.shape[1:]) for n in range(2)], mine, other
        )
        wide_copy(None, 0).start()

    @pl.when(step == 4 * tiles)
    def _():
        for n in range(2 * tiles):
            wide_copy(n, n % 2).wait_recv()

    @pl.when(step == first_steps)
    def _():
        wide_copy(2 * tiles - 1, 1).wait_send()
        wide_copy(None, 0).wait()
        for n in range(talls):
            tall_copy(n).wait_recv()
        for n in (talls - 2, talls - 1):
            tall_copy(n).wait_send()

    for at, tasks in plan.items():

        @pl.when(step == at)
        def _():
            for one in tasks:
                sum_task(*one)

    attention = step - first_steps

    @pl.when(attention >= 0)
    def _():
        attend_back_block(
            turns, lax.div(attention, turns), lax.rem(attention, turns),
            q_ref, k0, v0, k1, v1, p_ref, att_ref, inv_ref, do_ref, dq_ref, own_ref, sib_ref, kt, va, dk, dv, sib, sib_sem,
        )

    @pl.when(step == last)
    def _():
        finish()
        back_end()
        halves_ref, swapped = shared[0], shared[1]
        sum_ref[core] = halves_ref[core]
        sum_ref[1 - core] = swapped[...]
        pairs = width // 128
        for pair in range(pairs):
            if pair >= pairs - 2:
                sib_copy(sib, sib_ref, sib_sem, pair).wait_send()
            sib_copy(sib, sib_ref, sib_sem, pair).wait_recv()


def sib_copy(sib, sib_ref, sib_sem, pair):
    z, chip, core = place()
    return pltpu.make_async_remote_copy(
        sib.at[lax.rem(pair, 2)],
        sib_ref.at[:, :, pl.ds(pl.multiple_of(pair * 128, 128), 128)],
        sib_sem.at[0, pair],
        sib_sem.at[1, pair],
        device_id={"fsdp": 2 * chip + 1 - core},
        device_id_type=MESH_ID,
    )


def attend_back_block(
    turns, j, i,
    q_ref, k0, v0, k1, v1, p_ref, att_ref, inv_ref, do_ref, dq_ref, own_ref, sib_ref, kt, va, dk, dv, sib, sib_sem,
):
    part = k0.shape[0]
    unit = q_ref.shape[0]
    lane_k = lax.broadcasted_iota(jnp.int32, (part, 128), 1)

    @pl.when(i == 0)
    def _():
        for n, (k_ref, v_ref) in enumerate(((k0, v0), (k1, v1))):
            k, v = k_ref[...], v_ref[...]
            zero, one = jnp.zeros_like(v), jnp.ones_like(v)
            here = slice(n * part, (n + 1) * part)
            kt[0, :, here] = jnp.where(lane_k < HEAD_DIM, k, zero).T
            kt[1, :, here] = jnp.where(lane_k < HEAD_DIM, zero, k).T
            va[0, here] = jnp.where(lane_k < HEAD_DIM, v, jnp.where(lane_k < HEAD_DIM + 3, one, zero))
            va[1, here] = jnp.where(lane_k >= HEAD_DIM, v, jnp.where(lane_k < 3, one, zero))
        dk[...] = jnp.zeros_like(dk)
        dv[...] = jnp.zeros_like(dv)

    lane = lax.broadcasted_iota(jnp.int32, (unit, 128), 1)
    q = q_ref[...]
    o = att_ref[pl.ds(pl.multiple_of(i * unit, unit), unit), pl.ds(pl.multiple_of(j * 128, 128), 128)]
    dof = do_ref[...].astype(jnp.float32) * inv_ref[...]
    prod = dof * o.astype(jnp.float32)
    dob = dof.astype(jnp.bfloat16)
    zero = jnp.zeros_like(dob)
    turned = None
    for h in range(2):
        mine = lane < HEAD_DIM if h == 0 else lane >= HEAD_DIM
        base = HEAD_DIM if h == 0 else 0
        d = -jnp.sum(jnp.where(mine, prod, 0.0), axis=1, keepdims=True)
        d1 = d.astype(jnp.bfloat16).astype(jnp.float32)
        d2 = (d - d1).astype(jnp.bfloat16).astype(jnp.float32)
        d3 = d - d1 - d2
        extra = jnp.where(
            lane == base, d1, jnp.where(lane == base + 1, d2, jnp.where(lane == base + 2, d3, 0.0))
        ).astype(jnp.bfloat16)
        p = p_ref[h]
        ds = (p.astype(jnp.float32) * dotf(va[h], jnp.where(mine, dob, extra), NT)).astype(jnp.bfloat16)
        dv[...] += dotf(p, jnp.where(mine, dob, zero))
        dk[...] += dotf(ds, jnp.where(mine, q, zero))
        new = dotf(kt[h], ds)
        turned = new if turned is None else turned + new
    dq_ref[...] = turned.T * (1.0 / math.sqrt(HEAD_DIM))

    @pl.when(i == turns - 1)
    def _():
        @pl.when(j >= 2)
        def _():
            sib_copy(sib, sib_ref, sib_sem, j - 2).wait_send()

        for n, total in enumerate((dk, dv)):
            own_ref[n] = total[:part]
            sib[lax.rem(j, 2), n] = total[part:].astype(jnp.bfloat16)
        sib_copy(sib, sib_ref, sib_sem, j).start()


def backward(
    shape, plan, hidden_t, attended, branch, d_ff, sums, mixed, d_gate, d_up, q, own, sib, p, inv, do, result, seq_count,
    tiles=3, talls=8, unit=256,
):
    seqs, bits = shape["seq"], (shape["fsdp"] // 2).bit_length() - 1
    chips = seqs << bits
    rows, width = attended.shape
    units = mixed.shape[1]
    fold = units // width
    tile = units // 2 // tiles
    tall, out_cols = fold * width // 2, (width + NORM_COLS) // 2
    cols = units + tall + out_cols
    pieces = sum_pieces(units, tall, out_cols, bits)
    sum_rows = width // chips
    pairs, turns, part = width // 128, rows // unit, own.shape[0]
    first_steps, second_steps = 4 * tiles + talls + 1, pairs * turns
    steps = first_steps + second_steps
    low = jnp.bfloat16
    once = pl.Buffered(1)
    full = lambda array: pl.BlockSpec(array.shape, lambda s: (0, 0), pipeline_mode=once)

    def later(s):
        return lax.div(s + second_steps, steps)

    def pair_of(s):
        return lax.div((s - first_steps) * later(s), turns)

    def turn_of(s):
        return lax.rem((s - first_steps) * later(s), turns)

    def reached(s, first, count):
        return sum(lax.div(s + steps - first - k, steps) for k in range(1, count))

    def half_tile(away_at, keep_at):
        def at(s):
            core = lax.rem(lax.axis_index("fsdp"), 2)
            kept = lax.div(s + steps - keep_at, steps)
            t = reached(s, away_at, tiles) * (1 - kept) + reached(s, keep_at, tiles) * kept
            return (0, (1 - core + (2 * core - 1) * kept) * tiles + t)

        return pl.BlockSpec((rows, tile), at)

    row = pl.BlockSpec((unit, 128), lambda s: (turn_of(s), pair_of(s)))
    kv = [
        pl.BlockSpec((part, 128), lambda s: (0, 2 * pair_of(s))),
        pl.BlockSpec((part, 128), lambda s: (0, 2 * pair_of(s) + 1)),
    ]
    any_space = pl.BlockSpec(memory_space=pl.ANY)
    dma = pltpu.SemaphoreType.DMA
    form = (seqs, 1 << bits, sum_rows)
    return pl.pallas_call(
        functools.partial(back_kernel, seqs, bits, pieces, plan, tiles, talls, fold, turns),
        grid=(steps,),
        in_specs=[
            full(hidden_t), full(attended), full(branch), full(d_ff), full(sums),
            pl.BlockSpec((rows, units // talls), lambda s: (0, reached(s, 4 * tiles, talls))),
            half_tile(0, 2 * tiles), half_tile(tiles, 3 * tiles),
            row, *kv, *kv, pl.BlockSpec((2, 2 * part, unit), lambda s: (pair_of(s), 0, turn_of(s))), row, row, any_space,
        ],
        out_specs=[
            row,
            pl.BlockSpec((2, part, 128), lambda s: (0, 0, pair_of(s))),
            any_space,
            pl.BlockSpec((2, sum_rows // 2, cols), lambda s: (0, 0, 0)),
            any_space,
        ],
        out_shape=[
            jax.ShapeDtypeStruct((rows, width), jnp.float32),
            jax.ShapeDtypeStruct((2, part, width), jnp.float32),
            jax.ShapeDtypeStruct((2, part, width), low),
            jax.ShapeDtypeStruct((2, sum_rows // 2, cols), jnp.float32),
            jax.ShapeDtypeStruct((seq_count, rows // seq_count, width), low),
        ],
        scratch_shapes=[
            pltpu.VMEM((*form, cols), low),
            pltpu.VMEM((*form, cols), low),
            pltpu.VMEM((2, *form, tile), low),
            pltpu.VMEM((2, chips // talls, sum_rows, tall), low),
            dma((2, 2 * tiles + 1 + talls)),
            pltpu.VMEM((2, 128, 2 * part), low),
            pltpu.VMEM((2, 2 * part, 128), low),
            pltpu.VMEM((2 * part, 128), jnp.float32),
            pltpu.VMEM((2 * part, 128), jnp.float32),
            pltpu.VMEM((2, 2, part, 128), low),
            dma((2, pairs)),
            dma((3, seq_count)),
            *reducer_scratch(seqs, bits, pieces, GROUPS, sum_rows, cols),
        ],
        compiler_params=pltpu.CompilerParams(collective_id=1, has_side_effects=True, vmem_limit_bytes=63 << 20),
        name="backward",
    )(hidden_t, attended, branch, d_ff, sums, mixed, d_gate, d_up, q, own, own, sib, sib, p, inv, do, result)


def tail_kernel(
    seqs, bits, pieces,
    cos_ref, sin_ref, dq_ref, own_ref, got_ref, wq_ref, wk_ref, wv_ref, dr_ref, x_ref, sum_ref,
    back_ref, qsum_ref, square_ref,
    dproj, dx, keep, got, away, plane, line_sum, back_sem, plane_sem, total_sem, *shared,
):
    z, chip, core = place()
    f = 2 * chip + core
    line = 2 << bits
    block, width = dr_ref.shape
    i = pl.program_id(0)
    blocks = dx.shape[0]
    low = jnp.bfloat16
    start, sum_task, finish = reducer(seqs, bits, pieces, ((0, 1),), away, keep, got, *shared)
    back_begin, back_end = returns(seqs, back_ref.shape[0], lambda n: dx.at[n], back_ref, back_sem, block)

    @pl.when(i == 0)
    def _():
        greet(plane_peers(line) + column_peers(seqs))

    cosine, sine = cos_ref[...], -sin_ref[...]
    grads = (
        turn(dq_ref[...], cosine, sine).astype(low),
        turn(own_ref[0] + got_ref[0].astype(jnp.float32), cosine, sine).astype(low),
        (own_ref[1] + got_ref[1].astype(jnp.float32)).astype(low),
    )
    value = dr_ref[...]
    rows = pl.ds(pl.multiple_of(i * block, block), block)
    for n, (grad, w_ref) in enumerate(zip(grads, (wq_ref, wk_ref, wv_ref))):
        dproj[rows, n * width : (n + 1) * width] = grad
        value = value + dotf(grad, w_ref[...], NT)
    dx[i] = value.astype(low)
    for n in range(blocks):

        @pl.when(i == n)
        def _():
            back_begin(n)

    @pl.when(i == blocks - 1)
    def _():
        half = keep.shape[-1]
        tile = 384
        for target, side in ((away, 1 - core), (keep, core)):
            for n in range(half // tile):
                cols = pl.ds(pl.multiple_of(side * half + n * tile, 128), tile)
                grad = dotf(x_ref[...], dproj[:, cols], TN).astype(low)
                target[:, :, :, n * tile : (n + 1) * tile] = grad.reshape(target.shape[:3] + (tile,))
            if target is away:
                start()
        for task in sum_plan(seqs, bits):
            sum_task(0, *task)
        finish()
        halves_ref, swapped = shared[0], shared[1]
        qsum_ref[core] = halves_ref[core]
        qsum_ref[1 - core] = swapped[...]
        squares = jnp.sum(jnp.square(sum_ref[...])) + jnp.sum(jnp.square(qsum_ref[...]))
        plane[f] = jnp.zeros(plane.shape[1:], jnp.float32) + squares

        def plane_copy(to, source):
            return pltpu.make_async_remote_copy(
                plane.at[source], plane.at[source], plane_sem.at[0, to], plane_sem.at[1, source],
                device_id={"fsdp": to}, device_id_type=MESH_ID,
            )

        def total_copy(to, source):
            return pltpu.make_async_remote_copy(
                line_sum.at[source], line_sum.at[source], total_sem.at[0, to], total_sem.at[1, source],
                device_id={"seq": to}, device_id_type=MESH_ID,
            )

        for k in range(1, line):
            plane_copy(lax.rem(f + k, line), f).start()
        for k in range(1, line):
            plane_copy(lax.rem(f + k, line), lax.rem(f + k, line)).wait_recv()
        line_sum[z] = sum(plane[n] for n in range(line))
        for k in range(1, seqs):
            total_copy(lax.rem(z + k, seqs), z).start()
        for k in range(1, seqs):
            total_copy(lax.rem(z + k, seqs), lax.rem(z + k, seqs)).wait_recv()
        square_ref[...] = sum(line_sum[n] for n in range(seqs))
        for k in range(1, line):
            plane_copy(lax.rem(f + k, line), f).wait_send()
        for k in range(1, seqs):
            total_copy(lax.rem(z + k, seqs), z).wait_send()
        back_end()


def tail(shape, cosine, sine, d_query, own, got, wide, first, d_resid, x, sums, seq_count, group, block=256):
    seqs, line = shape["seq"], shape["fsdp"]
    bits = (line // 2).bit_length() - 1
    rows, width = x.shape
    low = jnp.bfloat16
    sum_rows, sum_cols = width // (seqs * line // 2), 3 * width // 2
    pieces = halves_of(sum_cols, bits)
    dma = pltpu.SemaphoreType.DMA
    row = lambda cols: pl.BlockSpec((block, cols), lambda i: (i, 0))
    pair = pl.BlockSpec((2, block, width), lambda i: (0, i, 0))
    once = pl.Buffered(1)
    weight = lambda n: pl.BlockSpec((width, width), lambda i, n=n: (0, first + n), pipeline_mode=once)
    blocks = rows // block
    turned = pl.BlockSpec((block, 128), sequence_rows(group, blocks))
    return pl.pallas_call(
        functools.partial(tail_kernel, seqs, bits, pieces),
        grid=(blocks,),
        in_specs=[
            turned, turned, row(width), pair, pair, weight(0), weight(1), weight(2), row(width),
            pl.BlockSpec(x.shape, lambda i: (0, 0), pipeline_mode=once),
            pl.BlockSpec(sums.shape, lambda i: (0, 0, 0), pipeline_mode=once),
        ],
        out_specs=[
            pl.BlockSpec(memory_space=pl.ANY),
            pl.BlockSpec((2, sum_rows // 2, sum_cols), lambda i: (0, 0, 0)),
            pl.BlockSpec((8, 128), lambda i: (0, 0)),
        ],
        out_shape=[
            jax.ShapeDtypeStruct((seq_count, rows // seq_count, width), low),
            jax.ShapeDtypeStruct((2, sum_rows // 2, sum_cols), jnp.float32),
            jax.ShapeDtypeStruct((8, 128), jnp.float32),
        ],
        scratch_shapes=[
            pltpu.VMEM((rows, 3 * width), low),
            pltpu.VMEM((blocks, block, width), low),
            *[pltpu.VMEM((seqs, 1 << bits, sum_rows, sum_cols), low)] * 3,
            pltpu.VMEM((line, 8, 128), jnp.float32),
            pltpu.VMEM((seqs, 8, 128), jnp.float32),
            dma((3, blocks)),
            dma((2, line)),
            dma((2, seqs)),
            *reducer_scratch(seqs, bits, pieces, ((0, 1),), sum_rows, sum_cols),
        ],
        compiler_params=pltpu.CompilerParams(collective_id=2, has_side_effects=True, vmem_limit_bytes=60 << 20),
        name="tail",
    )(cosine, sine, d_query, own, got, wide, wide, wide, d_resid, x, sums)


def adam_kernel(sum_ref, qsum_ref, square_ref, back_ref, *refs):
    states, outs = refs[:18], refs[18:]
    back_out, norm_out = outs[24:]
    back_out[...] = back_ref[...].astype(jnp.float32)
    norm = jnp.sqrt(square_ref[0:1, 0:1])
    norm_out[...] = norm
    clip = jnp.minimum(1.0, MAX_NORM / (norm + 1e-06))
    rows, units = states[2].shape
    width = states[1].shape[1]
    out = (width + NORM_COLS) // 2
    take = lambda first, count: jnp.concatenate([sum_ref[n, :, first : first + count] for n in range(2)], 1)
    fold = states[4].shape[0] // rows
    tall = fold * width // 2
    red_out = take(units + tall, out)
    norms = red_out[:, width : width + 128].T[: states[5].shape[0]]
    grads = (
        jnp.concatenate([qsum_ref[0], qsum_ref[1]], 1),
        red_out[:, :width],
        take(0, units // 2),
        take(units // 2, units // 2),
        jnp.concatenate(
            [
                jnp.concatenate([sum_ref[n, :, units + a * (width // 2) : units + (a + 1) * (width // 2)] for n in range(2)], 1)
                for a in range(fold)
            ],
            0,
        ),
        norms,
    )
    for n, grad in enumerate(grads):
        rates = (0.0, NORM_RATE) if n == 5 else (WEIGHT_DECAY, LEARN_RATE)
        outs[n][...] = grad
        new, first, second = adam_update(
            states[n][...], grad, states[6 + n][...], states[12 + n][...], *rates, clip
        )
        outs[6 + n][...] = new
        outs[12 + n][...] = first
        outs[18 + n][...] = second


def adam(sums, qsums, squares, back, states):
    like = lambda array: jax.ShapeDtypeStruct(array.shape, jnp.float32)
    vmem = pl.BlockSpec(memory_space=pltpu.VMEM)
    outs = [like(array) for array in states[:6]] * 4
    outs += [like(back), jax.ShapeDtypeStruct((1, 1), jnp.float32)]
    return pl.pallas_call(
        adam_kernel,
        in_specs=[vmem] * (4 + len(states)),
        out_specs=[vmem] * len(outs),
        out_shape=outs,
        compiler_params=pltpu.CompilerParams(vmem_limit_bytes=56 << 20),
        name="adam",
    )(sums, qsums, squares, back, *states)


def sum_plan(seqs, bits):
    order = sorted(range(seqs), key=lambda zm: (z_low(zm) if zm else seqs, zm))
    found = []
    for n in range(seqs + bits):
        for stage in reversed(range(bits + 1)):
            if 0 <= n - stage < seqs and (stage < bits or order[n - stage]):
                found.append((stage, order[n - stage]))
    return found


def halves_of(cols, bits):
    cut = cols // 256 * 128
    return ((0, cut, tuple(range(bits))), (cut, cols - cut, tuple(reversed(range(bits)))))


def turn(field, cosine, sine):
    width = field.shape[-1]
    reps = width // cosine.shape[-1]
    cosine = jnp.concatenate([cosine] * reps, -1)
    sine = jnp.concatenate([sine] * reps, -1)
    lane = lax.broadcasted_iota(jnp.int32, field.shape, 1)
    half = HEAD_DIM // 2
    other = jnp.where(
        lax.rem(lane, HEAD_DIM) < half, pltpu.roll(field, width - half, 1), pltpu.roll(field, half, 1)
    )
    return field * cosine + other * sine


def project_kernel(x_ref, wq_ref, wk_ref, wv_ref, cos_ref, sin_ref, code_ref, q_ref, kv_ref):
    x, cosine, sine = x_ref[...], cos_ref[...], sin_ref[...]
    width = x.shape[-1]
    query = turn(dotf(x, wq_ref[...]), cosine, sine).astype(jnp.bfloat16)
    q_ref[...] = query * jnp.bfloat16(1.0 / math.sqrt(HEAD_DIM))
    keys = turn(dotf(x, wk_ref[...]), cosine, sine).astype(jnp.bfloat16)
    values = dotf(x, wv_ref[...]).astype(jnp.bfloat16)
    for at in range(0, width, 128):
        kv_ref[:, 2 * at : 2 * at + 128] = keys[:, at : at + 128]
        kv_ref[:, 2 * at + 128 : 2 * at + 256] = values[:, at : at + 128]
    kv_ref[:, 2 * width :] = code_ref[...]


def sequence_rows(group, blocks):
    def at(i):
        part = lax.rem(2 * lax.axis_index("seq") + lax.rem(lax.axis_index("fsdp"), 2), group)
        return (part * blocks + i, 0)

    return at


def rotary_tables(positions):
    half_dim = HEAD_DIM // 2
    inverse = np.exp(np.arange(half_dim, dtype=np.float32) * np.float32(-2.0 * math.log(ROPE_BASE) / HEAD_DIM))
    angles = (np.arange(positions, dtype=np.float32)[:, None] * inverse[None, :]).astype(np.float64)
    cosine, sine = np.cos(angles), np.sin(angles)
    tables = np.concatenate([cosine] * 4, 1), np.concatenate([-sine, sine, -sine, sine], 1)
    return tuple(jnp.asarray(table.astype(np.float32)) for table in tables)


def project(x, wide, first, cosine, sine, code, group, block=256):
    rows, width = x.shape
    turned = pl.BlockSpec((block, 128), sequence_rows(group, rows // block))
    weight = lambda n: pl.BlockSpec((width, width), lambda i, n=n: (0, first + n))
    row = lambda cols: pl.BlockSpec((block, cols), lambda i: (i, 0))
    return pl.pallas_call(
        project_kernel,
        grid=(rows // block,),
        in_specs=[row(width), weight(0), weight(1), weight(2), turned, turned, row(128)],
        out_specs=[row(width), row(2 * width + 128)],
        out_shape=[
            jax.ShapeDtypeStruct((rows, width), jnp.bfloat16),
            jax.ShapeDtypeStruct((rows, 2 * width + 128), jnp.bfloat16),
        ],
        compiler_params=pltpu.CompilerParams(vmem_limit_bytes=63 << 20),
        name="project",
    )(x, wide, wide, wide, cosine, sine, code)


def attend_kernel(seqs, bits, pieces, plan, unit, chunk, q_ref, qc_ref, own_ref, code_ref, own_hbm, *refs):
    p_ref, o_ref, inv_ref, sib_hbm, rest_all, down_all = refs[2:8]
    ka, vt, st_ref, sib, kv_sem, keep_sem = refs[8:14]
    own_line, own_hops, line, hops, finish_line, finish_hops = gatherer(
        seqs, bits, pieces, (None, rest_all, down_all), *refs[14:]
    )
    z, chip, core = place()
    part, rows = own_ref.shape[0], q_ref.shape[0]
    keys = 2 * part
    j, pairs = pl.program_id(0), pl.num_programs(0)
    which = range(len(pieces))

    def kv_copy(first, count, n):
        cols = pl.ds(pl.multiple_of(first, 128), count)
        return pltpu.make_async_remote_copy(
            own_hbm.at[:, cols], sib.at[:, cols], kv_sem.at[0, n], kv_sem.at[1, n],
            device_id={"fsdp": 2 * chip + 1 - core}, device_id_type=MESH_ID,
        )

    code_copy = kv_copy(256 * pairs, 128, pairs)
    pair_copy = lambda n: kv_copy(256 * n, 256, n)

    def carry(distance, level=None):
        if level is None:
            line(which, distance)
        else:
            hops(which, distance, (level,))

    @pl.when(j == 0)
    def _():
        greet(sum_peers(bits) + line_peers(seqs))
        code_copy.start()
        pair_copy(0).start()
        own_line(which)
        lax.fori_loop(1, pairs, lambda n, _: (pair_copy(n).start(), 0)[1], 0)
        code_copy.wait_recv()

    def slot(n):
        for at in [at for at in plan if at is not None and at % SLOTS == n]:

            @pl.when(j == at // SLOTS)
            def _():
                for task in plan[at]:
                    carry(*task)

    low_k = lax.broadcasted_iota(jnp.int32, (part, 128), 1) < HEAD_DIM

    pair_copy(j).wait_recv()
    sides = (
        (own_ref[:, :128], code_ref[...], own_ref[:, 128:]),
        (
            sib[:, pl.ds(pl.multiple_of(256 * j, 128), 128)],
            sib[:, sib.shape[1] - 128 :],
            sib[:, pl.ds(pl.multiple_of(256 * j + 128, 128), 128)],
        ),
    )
    for i, (k, kc, v) in enumerate(sides):
        one = jnp.ones_like(v)
        here = slice(i * part, (i + 1) * part)
        ka[0, here] = jnp.where(low_k, k, kc)
        ka[1, here] = jnp.where(low_k, kc, k)
        vt[0, :, here] = jnp.where(low_k, v, one).T
        vt[1, :, here] = jnp.where(low_k, one, v).T
    low_q = lax.broadcasted_iota(jnp.int32, (unit, 128), 1) < HEAD_DIM
    units = [(h, b) for b in range(rows // unit) for h in range(2)]
    results, before = {}, None
    for u, now in enumerate([*units, None]):
        if u < SLOTS:
            slot(u)
        if now is not None:
            h, b = now
            q, qc = q_ref[b * unit : (b + 1) * unit], qc_ref[b * unit : (b + 1) * unit]
            qa = jnp.where(low_q, q, qc) if h == 0 else jnp.where(low_q, qc, q)
        top = total = None
        for c in range(keys // chunk):
            here = slice(c * chunk, (c + 1) * chunk)
            if now is not None:
                s = dotf(ka[h, here], qa, NT)
                st_ref[u % 2, here] = s
                most = jnp.max(s.reshape(chunk // 8, 8, unit), axis=0)
                top = most if top is None else jnp.maximum(top, most)
            if before is not None:
                hb, bb, row_max = before
                p = jnp.exp(st_ref[(u - 1) % 2, here] - row_max).astype(jnp.bfloat16)
                p_ref[hb, here, bb * unit : (bb + 1) * unit] = p
                d = dotf(vt[hb, :, here], p)
                total = d if total is None else total + d
        if before is not None:
            results[before[:2]] = total.T
        before = None if now is None else (h, b, jnp.max(top, axis=0, keepdims=True))
    for b in range(rows // unit):
        r0, r1 = results[(0, b)], results[(1, b)]
        inv = 1.0 / pltpu.roll(jnp.where(low_q, r1, r0), HEAD_DIM, 1)
        inv_ref[b * unit : (b + 1) * unit] = inv
        o_ref[b * unit : (b + 1) * unit] = (jnp.where(low_q, r0, r1) * inv).astype(jnp.bfloat16)

    @pl.when(j == pairs - 1)
    def _():
        keep = pltpu.make_async_copy(sib, sib_hbm, keep_sem)
        keep.start()
        for task in plan[None]:
            carry(*task)
        finish_line(which)
        for distance in range(1, seqs):
            finish_hops(which, distance)
        code_copy.wait_send()
        lax.fori_loop(0, pairs, lambda n, _: (pair_copy(n).wait_send(), 0)[1], 0)
        keep.wait()


def attend_pallas(shape, pieces, plan, q, qc, own, rest_all, down_all, unit=512, chunk=512):
    seqs, bits = shape["seq"], (shape["fsdp"] // 2).bit_length() - 1
    rows, width = q.shape
    pairs = width // 128
    part = own.shape[0]
    low = jnp.bfloat16
    row = pl.BlockSpec((rows, 128), lambda j: (0, j))
    any_space = pl.BlockSpec(memory_space=pl.ANY)
    dma = pltpu.SemaphoreType.DMA
    like = lambda array: jax.ShapeDtypeStruct(array.shape, array.dtype)

    return pl.pallas_call(
        functools.partial(attend_kernel, seqs, bits, pieces, plan, unit, chunk),
        grid=(pairs,),
        in_specs=[
            row,
            pl.BlockSpec((rows, 128), lambda j: (0, 0)),
            pl.BlockSpec((part, 256), lambda j: (0, j)),
            pl.BlockSpec((part, 128), lambda j: (0, 2 * pairs)),
            any_space,
            any_space,
            any_space,
        ],
        out_specs=[pl.BlockSpec((2, 2 * part, rows), lambda j: (j, 0, 0)), row, row, any_space, any_space, any_space],
        out_shape=[
            jax.ShapeDtypeStruct((2 * pairs, 2 * part, rows), low),
            jax.ShapeDtypeStruct((rows, width), low),
            jax.ShapeDtypeStruct((rows, width), jnp.float32),
            like(own),
            like(rest_all),
            like(down_all),
        ],
        input_output_aliases={5: 4, 6: 5},
        scratch_shapes=[
            pltpu.VMEM((2, 2 * part, 128), low),
            pltpu.VMEM((2, 128, 2 * part), low),
            pltpu.VMEM((2, 2 * part, unit), jnp.float32),
            pltpu.VMEM(own.shape, low),
            dma((2, pairs + 1)),
            dma,
            *gatherer_scratch(seqs, bits, len(pieces)),
        ],
        compiler_params=pltpu.CompilerParams(collective_id=3, has_side_effects=True, vmem_limit_bytes=63 << 20),
        name="attend",
    )(q, qc, own, own, own, rest_all, down_all)


def mean_row(field):
    return jnp.mean(field, -1, keepdims=True)


def middle_kernel(
    seqs, seq_count, x_ref, att_ref, cot_hbm, rest_hbm, down_hbm,
    out_ref, dr_ref, branch_ref, datt_ref, hid_ref, mixed_ref, dgate_ref, dup_ref, dff_ref, sums_ref,
    silu_s, slope_s, dy_s, dy_sem, wo_s, wg_s, wu_s, wd_s, norm_s, norms, weight_sem,
):
    blocks, block = dy_s.shape[:2]
    subs = blocks // seq_count
    begin, came, sent = departs(
        seqs, seq_count, lambda s, sub: cot_hbm.at[s, pl.ds(sub * block, block)], lambda n: dy_s.at[n], dy_sem, subs
    )

    units, width = wd_s.shape
    step = 768
    cuts = [slice(n, n + step) for n in range(0, units, step)]
    out_at = 2 * units
    loads = [
        pltpu.make_async_copy(rest_hbm.at[:, pl.ds(out_at + width, 128)], norm_s, weight_sem.at[1 + 3 * len(cuts)]),
        pltpu.make_async_copy(rest_hbm.at[:, pl.ds(out_at, width)], wo_s, weight_sem.at[0]),
    ]
    for n, cut in enumerate(cuts):
        for m, (source, target) in enumerate(
            (
                (rest_hbm.at[:, pl.ds(cut.start, step)], wg_s.at[:, pl.ds(cut.start, step)]),
                (rest_hbm.at[:, pl.ds(units + cut.start, step)], wu_s.at[:, pl.ds(cut.start, step)]),
                (down_hbm.at[pl.ds(cut.start, step)], wd_s.at[pl.ds(cut.start, step)]),
            )
        ):
            loads.append(pltpu.make_async_copy(source, target, weight_sem.at[1 + 3 * n + m]))

    def ready(first, count):
        @pl.when(pl.program_id(0) == 0)
        def _():
            for load in loads[first : first + count]:
                load.wait()

    @pl.when(pl.program_id(0) == 0)
    def _():
        for load in loads:
            load.start()
        greet(column_peers(seqs))
        begin()

    ready(0, 2)

    @pl.when(pl.program_id(0) == 0)
    def _():
        norms[...] = norm_s[...].astype(jnp.float32).T[: norms.shape[0]]

    gain_one, shift_one, gain_two, shift_two = (norms[n : n + 1] for n in range(4))
    resid_one = x_ref[...].astype(jnp.float32) + dotf(att_ref[...], wo_s[...])
    hidden, normed_one, inv_one = normalize(resid_one, gain_one, shift_one)
    hidden_low = hidden.astype(jnp.bfloat16)
    hid_ref[...] = hidden_low.T
    resid_two = hidden
    for n, cut in enumerate(cuts):
        ready(2 + 3 * n, 3)
        gate = dotf(hidden_low, wg_s[:, cut])
        up = dotf(hidden_low, wu_s[:, cut])
        sig = jax.nn.sigmoid(gate)
        silu = gate * sig
        mixed = (silu * up).astype(jnp.bfloat16)
        silu_s[:, cut] = silu
        slope_s[:, cut] = up * sig * (1.0 + gate * (1.0 - sig))
        mixed_ref[:, cut] = mixed
        resid_two = resid_two + dotf(mixed, wd_s[cut, :])
    result, normed_two, inv_two = normalize(resid_two, gain_two, shift_two)
    out_ref[...] = result.astype(jnp.bfloat16)
    now = row_order(seq_count, subs, pl.program_id(0))
    came(now)
    dy = dy_s[now].astype(jnp.float32)
    d_two = normalize_back(dy, normed_two, inv_two, gain_two)
    d_ff = d_two.astype(jnp.bfloat16)
    dff_ref[...] = d_ff
    d_hidden = d_two
    for cut in cuts:
        d_mixed = dotf(d_ff, wd_s[cut, :], NT)
        d_up = (d_mixed * silu_s[:, cut]).astype(jnp.bfloat16)
        d_gate = (d_mixed * slope_s[:, cut]).astype(jnp.bfloat16)
        dup_ref[:, cut] = d_up
        dgate_ref[:, cut] = d_gate
        d_hidden = d_hidden + dotf(d_gate, wg_s[:, cut], NT) + dotf(d_up, wu_s[:, cut], NT)
    d_one = normalize_back(d_hidden, normed_one, inv_one, gain_one)
    dr_ref[...] = d_one
    branch = d_one.astype(jnp.bfloat16)
    branch_ref[...] = branch
    datt_ref[...] = dotf(branch, wo_s[...], NT).astype(jnp.bfloat16)

    @pl.when(pl.program_id(0) == 0)
    def _():
        sums_ref[...] = jnp.zeros_like(sums_ref)

    for n, term in enumerate((d_hidden * normed_one, d_hidden, dy * normed_two, dy)):
        sums_ref[n : n + 1] += jnp.sum(term, 0, keepdims=True)

    @pl.when(pl.program_id(0) == blocks - 1)
    def _():
        sent()


def row_order(seq_count, subs, step):
    return lax.rem(step, seq_count) * subs + lax.div(step, seq_count)


def middle(shape, x, attended, cotangent, rest, down, block=256):
    rows, width = x.shape
    units = down.shape[0]
    seq_count, local_len = cotangent.shape[:2]
    subs = local_len // block
    row = lambda cols: pl.BlockSpec((block, cols), lambda i: (row_order(seq_count, subs, i), 0))
    any_space = pl.BlockSpec(memory_space=pl.ANY)
    like = lambda cols, dtype: jax.ShapeDtypeStruct((rows, cols), dtype)
    low = jnp.bfloat16
    return pl.pallas_call(
        functools.partial(middle_kernel, shape["seq"], seq_count),
        grid=(rows // block,),
        in_specs=[
            row(width), row(width), pl.BlockSpec(memory_space=pl.ANY),
            any_space, any_space,
        ],
        out_specs=[
            row(width), row(width), row(width), row(width),
            pl.BlockSpec((width, block), lambda i: (0, row_order(seq_count, subs, i))),
            row(units), row(units), row(units), row(width),
            pl.BlockSpec((8, width), lambda i: (0, 0)),
        ],
        out_shape=[
            like(width, low), like(width, jnp.float32), like(width, low), like(width, low),
            jax.ShapeDtypeStruct((width, rows), low),
            like(units, low), like(units, low), like(units, low), like(width, low),
            jax.ShapeDtypeStruct((8, width), jnp.float32),
        ],
        scratch_shapes=[
            pltpu.VMEM((block, units), jnp.float32),
            pltpu.VMEM((block, units), jnp.float32),
            pltpu.VMEM((rows // block, block, width), low),
            pltpu.SemaphoreType.DMA((3, rows // block)),
            pltpu.VMEM((width, width), low),
            pltpu.VMEM((width, units), low),
            pltpu.VMEM((width, units), low),
            pltpu.VMEM((units, width), low),
            pltpu.VMEM((width, 128), low),
            pltpu.VMEM((8, width), jnp.float32),
            pltpu.SemaphoreType.DMA((2 + 3 * (units // 768),)),
        ],
        compiler_params=pltpu.CompilerParams(collective_id=4, has_side_effects=True, vmem_limit_bytes=61 << 20),
        name="middle",
    )(x, attended, cotangent, rest, down)


NORM_COLS = 256
SLOTS = 4
GATHER_PLAN = {
    7: ((1,),), 10: ((1, 0),), 14: ((2,),), 15: ((1, 1),), 18: ((2, 0),), 20: ((3,),), 21: ((2, 1),), 23: ((3, 0),),
    None: ((3, 1),),
}
PLAN = {
    13: ((0, 0, 1),), 16: ((0, 0, 3),), 19: ((0, 0, 2),), 21: ((0, 1, 1),), 23: ((0, 0, 0),), 24: ((0, 1, 3),),
    26: ((0, 2, 1), (1, 0, 1)), 28: ((0, 1, 2), (1, 0, 3)), 29: ((0, 2, 3),), 30: ((0, 1, 0), (1, 0, 2)),
    32: ((0, 2, 2), (1, 0, 0)), 34: ((1, 1, 1),), 36: ((1, 1, 3),), 38: ((1, 2, 1), (1, 1, 2)), 40: ((1, 2, 3),),
    41: ((1, 1, 0),), 43: ((1, 2, 2),),
}


def seg_codes(segments):
    lane = jnp.arange(128) % HEAD_DIM
    low, high = lane < CODE_BITS, lane < 2 * CODE_BITS
    bit = (segments[:, None] >> jnp.where(low, lane, jnp.where(high, lane - CODE_BITS, 0))[None, :]) & 1
    query = jnp.where(low, bit, jnp.where(high, 1 - bit, 0))
    keys = jnp.where(low, 1 - bit, jnp.where(high, bit, 0)) * -FAR
    return query.astype(jnp.bfloat16), keys.astype(jnp.bfloat16)


def two_to_a_sequence(
    shape,
    tokens, segment_ids, cotangent,
    w_qkv, w_out, w_gate, w_up, w_down, norm_params,
    first_qkv, first_out, first_gate, first_up, first_down, first_norms,
    second_qkv, second_out, second_gate, second_up, second_down, second_norms,
):
    seqs = shape["seq"]
    seq_count, local_len, width = tokens.shape
    rows = seq_count * local_len
    group = seqs // seq_count
    units = w_gate.shape[1]

    norm_rows = jnp.pad(norm_params.T, ((0, 0), (0, NORM_COLS - norm_params.shape[0])))
    (x, segments, qkv_all, rest_all, down_all), pieces = first_gather(
        shape, tokens, segment_ids.reshape(seq_count, 1, local_len), w_gate, w_up, w_qkv, w_out, norm_rows, w_down
    )
    x = x.reshape(rows, width)
    w_all = qkv_all.reshape(width, 3 * width)
    q_code, k_code = seg_codes(segments.reshape(rows))
    cosine, sine = rotary_tables(rows * group)

    query, own = project(x, w_all, 0, cosine, sine, k_code, group)
    probs, attended, inverse_sums, sib, rest_all, down_all = attend_pallas(
        shape, pieces, GATHER_PLAN, query, q_code, own, rest_all, down_all
    )
    rest = rest_all.reshape(width, rest_all.shape[-1])
    down = down_all.reshape(units, width)
    (
        result, d_resid_one, d_branch, d_attended, hidden_low, mixed, d_gate, d_up, d_ff, sums,
    ) = middle(shape, x, attended, cotangent, rest, down)

    d_query, d_own, d_got, reduced_sums, output = backward(
        shape, PLAN, hidden_low, attended, d_branch, d_ff, sums, mixed, d_gate, d_up,
        query, own, sib, probs, inverse_sums, d_attended, result, seq_count,
    )
    back, qkv_sums, squares = tail(
        shape, cosine, sine, d_query, d_own, d_got, w_all, 0, d_resid_one, x, reduced_sums, seq_count, group
    )
    states = (
        w_qkv, w_out, w_gate, w_up, w_down, norm_params,
        first_qkv, first_out, first_gate, first_up, first_down, first_norms,
        second_qkv, second_out, second_gate, second_up, second_down, second_norms,
    )
    *updated, input_grad, grad_norm = adam(reduced_sums, qkv_sums, squares, back, states)
    return (output, input_grad, *updated, grad_norm.reshape(()))


def device_program(shape, *arrays):
    tokens, w_gate, w_down = arrays[0], arrays[5], arrays[7]
    seqs, line = shape["seq"], shape["fsdp"]
    seq_count, local_len, width = tokens.shape
    fits = (
        seqs == 2 * seq_count
        and seqs == 4
        and line == 8
        and (seq_count * local_len) % 512 == 0
        and w_gate.shape[0] % 8 == 0
        and w_down.shape[0] % 8 == 0
    )
    return two_to_a_sequence(shape, *arrays) if fits else per_device(*arrays)


def solution(mesh):
    return jax.shard_map(
        functools.partial(device_program, dict(mesh.shape)),
        mesh=mesh,
        in_specs=(
            P("fsdp", "seq", None),
            P("fsdp", "seq"),
            P("fsdp", "seq", None),
            P(("seq", "fsdp"), None),
            P(("seq", "fsdp"), None),
            P(("seq", "fsdp"), None),
            P(("seq", "fsdp"), None),
            P(("seq", "fsdp"), None),
            P(None, ("seq", "fsdp")),
            P(("seq", "fsdp"), None),
            P(("seq", "fsdp"), None),
            P(("seq", "fsdp"), None),
            P(("seq", "fsdp"), None),
            P(("seq", "fsdp"), None),
            P(None, ("seq", "fsdp")),
            P(("seq", "fsdp"), None),
            P(("seq", "fsdp"), None),
            P(("seq", "fsdp"), None),
            P(("seq", "fsdp"), None),
            P(("seq", "fsdp"), None),
            P(None, ("seq", "fsdp")),
        ),
        out_specs=(
            P("fsdp", "seq", None),
            P("fsdp", "seq", None),
            P(("seq", "fsdp"), None),
            P(("seq", "fsdp"), None),
            P(("seq", "fsdp"), None),
            P(("seq", "fsdp"), None),
            P(("seq", "fsdp"), None),
            P(None, ("seq", "fsdp")),
            P(("seq", "fsdp"), None),
            P(("seq", "fsdp"), None),
            P(("seq", "fsdp"), None),
            P(("seq", "fsdp"), None),
            P(("seq", "fsdp"), None),
            P(None, ("seq", "fsdp")),
            P(("seq", "fsdp"), None),
            P(("seq", "fsdp"), None),
            P(("seq", "fsdp"), None),
            P(("seq", "fsdp"), None),
            P(("seq", "fsdp"), None),
            P(None, ("seq", "fsdp")),
            P(("seq", "fsdp"), None),
            P(("seq", "fsdp"), None),
            P(("seq", "fsdp"), None),
            P(("seq", "fsdp"), None),
            P(("seq", "fsdp"), None),
            P(None, ("seq", "fsdp")),
            P(),
        ),
        check_vma=False,
    )
```
